32 devices in a mesh: strip: 4 (over y, core), depth: 8 (over z, x).
Axes of the slice: x: 2, y: 2, z: 4, core: 2. Of those that a mesh axis runs over, the one named last changes fastest.
Arguments:
- warmth_before: float32 [256, 256, 1024], P('depth', 'strip'), may hold values from -6 to 6
- stratum_category: int32 [256, 256, 1024], P('depth', 'strip'), may hold values from 0 to 7
- conductance_catalogue: float32 [8], replicated, may hold values from 0.3 to 3
- pivot_matrix_reciprocal: float32 [256, 32], P('depth'), may hold values from 0 to 1, as said below
- linkage_factor: float32 [8], P('depth'), may hold values from 0 to 1, as said below
- well_position_inside: int32 [512], P('strip'), may hold values from 0 to 65535, as said below
- well_holder_sequence: int32 [512], P('strip'), may hold values from 0 to 127, as said below
- well_reach: int32 [512], P('strip'), may hold values from 64 to 256
- entering_warmth: float32 [512], P('strip'), may hold values from -4 to 4
- well_transfer_speed: float32 [512], P('strip'), may hold values from 0.0005 to 0.03
Outputs:
- new_temperature: float32 [256, 256, 1024], P('depth', 'strip')
- leaving_warmth: float32 [512], P(('strip', 'depth'))
The draws below stay inside these ranges and needn't reach their ends.
Inputs may be any that keep to these rules, and one draw needn't show every extreme that they name: `well_position_inside`: within each strip's block of 128 entries the positions are distinct; a position counts y * 1024 + x over the strip's 64 x 1024 cells. `well_holder_sequence`: each strip's block of 128 entries is a permutation of 0 to 127. `pivot_matrix_reciprocal`: entries are positive. `linkage_factor`: entries are positive and below 1.
All inputs are finite; a program needn't handle non-finite values.
Results may differ from the reference program's by a relative error of at most 0.0003.
Values sent between devices are 32-bit elements; how exact they have to be, the bound alone decides.
No kernel may reach another device: no remote copies, remote signals or barrier semaphores. Data moves between devices by JAX's collectives and lax.ppermute only.
A program may use at most 192 MiB of HBM per device.

```python
import math
import jax
import jax.numpy as jnp
from jax import lax

CZ = 32
CY = 64
SPAN_EAST = 1024
NBS = 128
NL = 8
VERTICAL_SLABS = 256
SPAN_NORTH = 256
WELL_COUNT = 512


def draw_pivot_matrix_reciprocal(key, part):
    blocks = VERTICAL_SLABS // CZ
    scales = jax.random.uniform(key, (blocks, CZ), jnp.float32, 0.6, 1.6)
    row_index = jnp.arange(CZ, dtype=jnp.int32)[:, None]
    column_index = jnp.arange(CZ, dtype=jnp.int32)[None, :]
    lesser = jnp.minimum(row_index, column_index) + 1
    greater = jnp.maximum(row_index, column_index)
    norm_factor = float(CZ + 1) * 2.0 * float(CZ) * math.sqrt(float(CZ))
    kernel = (lesser * (CZ - greater)).astype(jnp.float32) / norm_factor
    full = scales[:, :, None] * scales[:, None, :] * kernel[None, :, :]
    return full.reshape(VERTICAL_SLABS, CZ)


def draw_linkage_factor(key, part):
    blocks = VERTICAL_SLABS // CZ
    low_gap = math.log(1.0 / (24.0 * CZ))
    high_gap = math.log(1.0 / (6.0 * CZ))
    gap = jnp.exp(jax.random.uniform(key, (blocks,), jnp.float32, low_gap, high_gap))
    return 1.0 - gap


def draw_well_position_inside(key, part):
    strips = WELL_COUNT // NBS

    def one_strip(strip_index):
        shuffled = jax.random.permutation(jax.random.fold_in(key, strip_index), CY * SPAN_EAST - 2)[:NBS - 2] + 1
        return jnp.concatenate([jnp.array([0, CY * SPAN_EAST - 1], jnp.int32), shuffled.astype(jnp.int32)])
    return jax.vmap(one_strip)(jnp.arange(strips, dtype=jnp.int32)).reshape(WELL_COUNT)


def draw_well_holder_sequence(key, part):
    strips = WELL_COUNT // NBS

    def one_strip(strip_index):
        return jax.random.permutation(jax.random.fold_in(key, strip_index + 7919), NBS).astype(jnp.int32)
    return jax.vmap(one_strip)(jnp.arange(strips, dtype=jnp.int32)).reshape(WELL_COUNT)


def draw_well_reach(key, part):
    drawn = jax.random.randint(key, (WELL_COUNT,), VERTICAL_SLABS // 4, VERTICAL_SLABS + 1, jnp.int32)
    drawn = drawn.at[0::NBS].set(VERTICAL_SLABS)
    return drawn.at[1::NBS].set(VERTICAL_SLABS // 4)


def with_ends(values, own_key, least, top_value):
    index_at = [jax.random.randint(jax.random.fold_in(own_key, axis), (), 0, length) for axis, length in enumerate(values.shape)]
    longest = values.shape.index(max(values.shape))
    neighbour = index_at[:longest] + [(index_at[longest] + 1) % values.shape[longest]] + index_at[longest + 1:]
    return values.at[tuple(index_at)].set(least).at[tuple(neighbour)].set(top_value)


def level_of(rng, dims, pieces, least, top_value):
    loudness, own = 1.0, jax.random.fold_in(rng, 6)
    for dim, blocks in pieces:
        draws = jnp.exp(jax.random.uniform(jax.random.fold_in(own, dim), (blocks,), jnp.float32, least / len(pieces), top_value / len(pieces)))
        loudness = loudness * jnp.repeat(draws, dims[dim] // blocks).reshape([-1 if axis == dim else 1 for axis in range(len(dims))])
    return loudness


def noise(own_key, shape, width, reach, cuts=(), kind=jnp.bfloat16):
    values = jax.random.normal(own_key, shape, jnp.float32) * width
    if len(cuts) > 0:
        values = level_of(own_key, shape, cuts, -0.22, 0.18) * values
    return jnp.clip(values, min=-reach, max=reach).astype(kind)


def setup_inputs(seed: int = 0) -> dict:
    keys = jax.random.split(jax.random.key(seed), 11)
    return {
        "warmth_before": noise(keys[0], (VERTICAL_SLABS, SPAN_NORTH, SPAN_EAST), 1.0, 6.0, ((0, 8), (1, 4)), jnp.float32),
        "stratum_category": with_ends(jax.random.randint(keys[1], (VERTICAL_SLABS, SPAN_NORTH, SPAN_EAST), 0, NL), jax.random.fold_in(keys[1], 1), 0, NL - 1).astype(jnp.int32),
        "conductance_catalogue": jnp.clip(jnp.exp(jax.random.uniform(keys[2], (NL,), jnp.float32, math.log(0.3), math.log(3.0))), 0.3, 3.0),
        "pivot_matrix_reciprocal": draw_pivot_matrix_reciprocal(jax.random.fold_in(keys[10], 71), 0),
        "linkage_factor": draw_linkage_factor(jax.random.fold_in(keys[10], 71), 0),
        "well_position_inside": draw_well_position_inside(jax.random.fold_in(keys[10], 71), 0),
        "well_holder_sequence": draw_well_holder_sequence(jax.random.fold_in(keys[10], 71), 0),
        "well_reach": draw_well_reach(jax.random.fold_in(keys[10], 71), 0),
        "entering_warmth": noise(keys[8], (WELL_COUNT,), 1.0, 4.0, ((0, 4),), jnp.float32),
        "well_transfer_speed": jnp.clip(jnp.exp(math.log(0.03) - 4.0943445 * jax.random.uniform(keys[9], (WELL_COUNT,), jnp.float32) ** level_of(keys[9], (WELL_COUNT,), ((0, 4),), -0.2, 0.2)), 0.0005, 0.03),
    }


backward_euler_advance = 0.2
storage_volume = 2.0

def lookup(stratum_category, conductance_catalogue):
    running = jnp.zeros(stratum_category.shape, jnp.float32)
    for level_index in range(conductance_catalogue.shape[0]):
        running = running + jnp.where(stratum_category == level_index, conductance_catalogue[level_index], jnp.zeros((), jnp.float32))
    return running

def overall_thermal_current(framed_warmth, framed_conductance):
    middle_value = framed_warmth[:, 1:-1, 1:-1]
    cond_centre = framed_conductance[:, 1:-1, 1:-1]
    vertical_extent = middle_value.shape[1]
    lateral_count = middle_value.shape[2]
    running = jnp.zeros_like(middle_value)
    for offset_north, offset_east in ((0, 1), (2, 1), (1, 0), (1, 2)):
        adjacent_value = framed_warmth[:, offset_north:offset_north + vertical_extent, offset_east:offset_east + lateral_count]
        cond_neighbour = framed_conductance[:, offset_north:offset_north + vertical_extent, offset_east:offset_east + lateral_count]
        running = running + 0.5 * (cond_centre + cond_neighbour) * (adjacent_value - middle_value)
    return running

def affine_pair(earlier, later):
    return (later[0] * earlier[0], later[0] * earlier[1] + later[1])

def liquid_circuit(stratum_lines, conductance_lines, inlets, rates, lengths):
    overall_slabs = stratum_lines.shape[1]
    levels = jnp.arange(overall_slabs, dtype=jnp.int32)[None, :]
    active = (levels < lengths[:, None]).astype(jnp.float32)
    exchange_rate = rates[:, None] * conductance_lines / (1.0 + conductance_lines) * active
    keeping = 1.0 - exchange_rate
    forcing = exchange_rate * stratum_lines
    down_coef, down_add = lax.associative_scan(affine_pair, (keeping, forcing), axis=1)
    down_after = down_coef * inlets[:, None] + down_add
    bottom = down_after[:, -1]
    down_before = jnp.concatenate([inlets[:, None], down_after[:, :-1]], axis=1)
    rise_coef, rise_add = lax.associative_scan(affine_pair, (keeping, forcing), reverse=True, axis=1)
    rise_at = rise_coef * bottom[:, None] + rise_add
    rise_below = jnp.concatenate([rise_at[:, 1:], bottom[:, None]], axis=1)
    withdrawal = exchange_rate * (2.0 * stratum_lines - down_before - rise_below)
    return (withdrawal, rise_at[:, 0])

def reduced_scalars(corners, block_size):
    corner_first = corners[:, 0]
    corner_upper = corners[:, 1]
    corner_lower = corners[:, 2]
    corner_last = corners[:, 3]
    coupling_ratio = corners[:, 4]
    blocks = corners.shape[0]
    previous_last = jnp.concatenate([jnp.ones((1,), jnp.float32), corner_last[:-1]])
    has_upper = (jnp.arange(blocks) >= 1).astype(jnp.float32)
    couple_now = has_upper * coupling_ratio * (block_size / (block_size + 1.0)) / jnp.sqrt(previous_last * corner_first)
    couple_next = jnp.concatenate([couple_now[1:], jnp.zeros((1,), jnp.float32)])
    down_first = couple_now * corner_first
    down_last = couple_now * corner_lower
    rise_first = couple_next * corner_upper
    rise_last = couple_next * corner_last

    def advance(ratio_prev, entries):
        spike_first, spike_last, next_first, next_last = entries
        pivot_value = 1.0 - spike_first * ratio_prev
        ratio_here = next_last + spike_last * ratio_prev * next_first / pivot_value
        return (ratio_here, (ratio_prev, pivot_value))
    final_ratio, (ratio_before, pivots) = lax.scan(advance, jnp.zeros((), jnp.float32), (down_first, down_last, rise_first, rise_last))
    return (couple_now, couple_next, down_first, down_last, rise_first, ratio_before, pivots)

def sweep_all(scalars, firsts, lasts):
    couple_now, couple_next, down_first, down_last, rise_first, ratio_before, pivots = scalars

    def forward(carry_prefix, entries):
        spike_first, spike_last, ratio_prev, pivot_value, value_first, value_last = entries
        prefix_here = value_last + spike_last * ratio_prev * value_first / pivot_value + spike_last / pivot_value * carry_prefix
        return (prefix_here, carry_prefix)
    final_prefix, prefix_before = lax.scan(forward, jnp.zeros_like(firsts[0]), (down_first, down_last, ratio_before, pivots, firsts, lasts))
    alpha_part = (firsts + down_first[:, None] * prefix_before) / pivots[:, None]
    beta_part = rise_first / pivots

    def backward(carry_first, entries):
        alpha_row, beta_value = entries
        first_here = alpha_row + beta_value * carry_first
        return (first_here, (first_here, carry_first))
    final_first, (first_here, first_next) = lax.scan(backward, jnp.zeros_like(firsts[0]), (alpha_part, beta_part), reverse=True)
    return (prefix_before, first_here, first_next)

def reference(warmth_before, stratum_category, conductance_catalogue, pivot_matrix_reciprocal, linkage_factor, well_position_inside, well_holder_sequence, well_reach, entering_warmth, well_transfer_speed):
    overall_slabs, overall_lines, span_eastward = warmth_before.shape
    overall_tubes = overall_lines * span_eastward
    conduct = lookup(stratum_category, conductance_catalogue)
    framed_warmth = jnp.pad(warmth_before, ((0, 0), (1, 1), (1, 1)))
    framed_conductance = jnp.pad(conduct, ((0, 0), (1, 1), (1, 1)))
    warmed_state = warmth_before + backward_euler_advance * overall_thermal_current(framed_warmth, framed_conductance)
    strip_base = jnp.arange(well_position_inside.shape[0], dtype=jnp.int32) // NBS * NBS
    sorted_values = strip_base + well_holder_sequence
    locations = jnp.take(well_position_inside, sorted_values) + strip_base // NBS * (CY * SPAN_EAST)
    linear_warmth = warmth_before.reshape(overall_slabs, overall_tubes)
    flat_cond = conduct.reshape(overall_slabs, overall_tubes)
    stratum_lines = jnp.take(linear_warmth, locations, axis=1).T
    conductance_lines = jnp.take(flat_cond, locations, axis=1).T
    withdrawal, leaving_warmth = liquid_circuit(stratum_lines, conductance_lines, jnp.take(entering_warmth, sorted_values), jnp.take(well_transfer_speed, sorted_values), jnp.take(well_reach, sorted_values))
    source_vector_linear = warmed_state.reshape(overall_slabs, overall_tubes).at[:, locations].add(-storage_volume * withdrawal.T)
    blocks = linkage_factor.shape[0]
    block_size = pivot_matrix_reciprocal.shape[1]
    inverses = pivot_matrix_reciprocal.reshape(blocks, block_size, block_size)
    local_part = jnp.einsum('jrc,jcn->jrn', inverses, source_vector_linear.reshape(blocks, block_size, overall_tubes), precision=lax.Precision.HIGHEST)
    corners = jnp.stack([inverses[:, 0, 0], inverses[:, 0, -1], inverses[:, -1, 0], inverses[:, -1, -1], linkage_factor], axis=1)
    scalars = reduced_scalars(corners, block_size)
    couple_now, couple_next = (scalars[0], scalars[1])
    ratio_before = scalars[5]
    prefix_before, first_here, first_next = sweep_all(scalars, local_part[:, 0], local_part[:, -1])
    last_before = prefix_before + ratio_before[:, None] * first_here
    solved = local_part + (couple_now[:, None] * inverses[:, :, 0])[:, :, None] * last_before[:, None, :]
    solved = solved + (couple_next[:, None] * inverses[:, :, -1])[:, :, None] * first_next[:, None, :]
    return (solved.reshape(overall_slabs, overall_lines, span_eastward), leaving_warmth)
```

```python
import functools

import jax
import jax.numpy as jnp
from jax import lax
from jax.experimental import pallas as pl
from jax.experimental.pallas import tpu as pltpu
from jax.sharding import PartitionSpec as P

backward_euler_advance = 0.2
storage_volume = 2.0
flux_scale = 0.5 * backward_euler_advance
LANES = 128
ROWS = 8
VMEM_LIMIT = 48 * 1024 * 1024
HIGHEST = lax.Precision.HIGHEST


def select_tree(category, entries):
    values = list(entries)
    bit = 1
    while len(values) > 1:
        odd = (category & bit) != 0
        values = [
            jnp.where(odd, values[k + 1], values[k]) if k + 1 < len(values) else values[k]
            for k in range(0, len(values), 2)
        ]
        bit *= 2
    return values[0]


def split_bf16(value, pieces):
    out = []
    for k in range(pieces):
        part = value.astype(jnp.bfloat16)
        out.append(part)
        if k + 1 < pieces:
            value = value - part.astype(jnp.float32)
    return out


def stencil_kernel(table, ends, w_ref, cat_ref, before, after, right_ref, fl_ref, acc):
    step = pl.program_id(0)
    planes, lines, span = w_ref.shape
    groups, tiles = lines // ROWS, span // LANES
    kinds = table.shape[0]
    entries = [flux_scale * table[k] for k in range(kinds)]
    lane = lax.broadcasted_iota(jnp.int32, (ROWS, LANES), 1)
    sub = lax.broadcasted_iota(jnp.int32, (ROWS, LANES), 0)

    @pl.when(step == 0)
    def _():
        acc[...] = jnp.zeros_like(acc)

    def plane(k, carry):
        z = step * planes + k
        end_first, end_last = ends[0, z], ends[1, z]

        def edge(ref, which, tile):
            row = ref[k, which : which + 1, tile * LANES : (tile + 1) * LANES]
            return jnp.broadcast_to(row, (ROWS, LANES))

        def finish(group, tile, value):
            rows = slice(group * ROWS, (group + 1) * ROWS)
            cols = slice(tile * LANES, (tile + 1) * LANES)
            right_ref[k, rows, cols] = value
            acc[0, rows, cols] += end_first * value
            acc[1, rows, cols] += end_last * value

        rolled_w = [edge(before, 0, t) for t in range(tiles)]
        rolled_c = [edge(before, 1, t) for t in range(tiles)]
        waiting = [None] * tiles
        waiting_roll = [None] * tiles
        for g in range(groups):
            rows = slice(g * ROWS, (g + 1) * ROWS)
            left_w = jnp.zeros((ROWS, LANES), jnp.float32)
            left_c = jnp.zeros((ROWS, LANES), jnp.float32)
            pending = None
            for t in range(tiles + 1):
                if t < tiles:
                    cols = slice(t * LANES, (t + 1) * LANES)
                    w = w_ref[k, rows, cols]
                    c = select_tree(cat_ref[k, rows, cols], entries)
                    roll_w = pltpu.roll(w, 1, 1)
                    roll_c = pltpu.roll(c, 1, 1)
                    west_w = jnp.where(lane == 0, left_w, roll_w)
                    west_c = jnp.where(lane == 0, left_c, roll_c)
                    left_w, left_c = roll_w, roll_c
                    face = (c + west_c) * (w - west_w)
                    roll_face = pltpu.roll(face, LANES - 1, 1)
                    up_w = pltpu.roll(w, 1, 0)
                    up_c = pltpu.roll(c, 1, 0)
                    north_w = jnp.where(sub == 0, rolled_w[t], up_w)
                    north_c = jnp.where(sub == 0, rolled_c[t], up_c)
                    rolled_w[t], rolled_c[t] = up_w, up_c
                    face_y = (c + north_c) * (w - north_w)
                    roll_y = pltpu.roll(face_y, ROWS - 1, 0)
                    if g > 0:
                        south = jnp.where(sub == ROWS - 1, roll_y, waiting_roll[t])
                        finish(g - 1, t, waiting[t] + south)
                    waiting_roll[t] = roll_y
                    base = w - face - face_y
                    if g == groups - 1:
                        below = (c + edge(after, 1, t)) * (edge(after, 0, t) - w)
                    else:
                        below = None
                    current = (t, base, roll_face, -c * w if t == tiles - 1 else None, below)
                    next_face = roll_face
                else:
                    current = None
                    next_face = None
                if pending is not None:
                    pt, pbase, proll, pedge, pbelow = pending
                    east = jnp.where(lane == LANES - 1, next_face if pedge is None else pedge, proll)
                    total = pbase + east
                    if pbelow is not None:
                        south = jnp.where(sub == ROWS - 1, pbelow, waiting_roll[pt])
                        finish(g, pt, total + south)
                    else:
                        waiting[pt] = total
                pending = current
        return carry

    lax.fori_loop(0, planes, plane, 0)

    @pl.when(step == pl.num_programs(0) - 1)
    def _():
        share = fl_ref.shape[-1]
        for d in range(fl_ref.shape[0]):
            fl_ref[d] = acc[:, :, d * share : (d + 1) * share]


def stencil(w, cat, table, ends, before, after, depth_count):
    slabs, lines, span = w.shape
    planes = 4
    block = pl.BlockSpec((planes, lines, span), lambda i: (i, 0, 0))
    halo = pl.BlockSpec((planes, 2, span), lambda i: (i, 0, 0))
    fl_shape = (depth_count, 2, lines, span // depth_count)
    smem = pl.BlockSpec(memory_space=pltpu.SMEM)
    return pl.pallas_call(
        stencil_kernel,
        grid=(slabs // planes,),
        in_specs=[smem, smem, block, block, halo, halo],
        out_specs=[block, pl.BlockSpec(fl_shape, lambda i: (0, 0, 0, 0))],
        out_shape=[
            jax.ShapeDtypeStruct(w.shape, jnp.float32),
            jax.ShapeDtypeStruct(fl_shape, jnp.float32),
        ],
        scratch_shapes=[pltpu.VMEM((2, lines, span), jnp.float32)],
        compiler_params=pltpu.CompilerParams(vmem_limit_bytes=VMEM_LIMIT),
        cost_estimate=pl.CostEstimate(flops=40 * w.size, bytes_accessed=12 * w.size, transcendentals=0),
        name="stencil",
    )(table, ends, w, cat, before, after)


def reduced_coefficients(info, slabs, shape):
    blocks = info.shape[0]
    full = lambda value: jnp.full(shape, value, jnp.float32)
    first = [full(info[j, 0]) for j in range(blocks)]
    upper = [full(info[j, slabs - 1]) for j in range(blocks)]
    lower = [full(info[j, slabs]) for j in range(blocks)]
    last = [full(info[j, 2 * slabs - 1]) for j in range(blocks)]
    ratio = [full(info[j, 2 * slabs]) for j in range(blocks)]
    zero = jnp.zeros(shape, jnp.float32)
    shrink = slabs / (slabs + 1.0)
    couple = [zero]
    for j in range(1, blocks):
        couple.append(ratio[j] * shrink / jnp.sqrt(last[j - 1] * first[j]))
    couple.append(zero)
    out = []
    q = zero
    for j in range(blocks):
        vf, vl = couple[j] * first[j], couple[j] * lower[j]
        wf, wl = couple[j + 1] * upper[j], couple[j + 1] * last[j]
        inverse = 1.0 / (1.0 - vf * q)
        out.append(
            dict(
                p_first=vl * q * inverse,
                p_before=vl * inverse,
                a_first=inverse,
                a_before=vf * inverse,
                a_after=wf * inverse,
                couple=couple[j],
                couple_after=couple[j + 1],
                q=q,
            )
        )
        q = wl + vl * q * wf * inverse
    return out


KINDS = ("p_first", "p_before", "a_first", "a_before", "a_after", "couple", "couple_after", "q")


def sweeps(coef, firsts, lasts):
    blocks = len(firsts)
    before = [jnp.zeros_like(firsts[0])]
    for j in range(blocks - 1):
        before.append(
            lasts[j] + coef("p_first", j) * firsts[j] + coef("p_before", j) * before[j]
        )
    above, below = [None] * blocks, [None] * blocks
    after = jnp.zeros_like(firsts[0])
    for j in reversed(range(blocks)):
        below[j] = coef("couple_after", j) * after
        here = (
            coef("a_first", j) * firsts[j]
            + coef("a_before", j) * before[j]
            + coef("a_after", j) * after
        )
        above[j] = coef("couple", j) * (before[j] + coef("q", j) * here)
        after = here
    return above, below


def middle_kernel(slabs, info, fl_ref, uv_ref, table):
    blocks, _, lines, share = fl_ref.shape
    for j, entry in enumerate(reduced_coefficients(info, slabs, (ROWS, LANES))):
        for k, kind in enumerate(KINDS):
            table[j, k] = entry[kind]
    width = min(share, LANES)

    def coef(kind, j):
        return table[j, KINDS.index(kind), :, :width]

    def group(g, carry):
        rows = pl.ds(pl.multiple_of(g * ROWS, ROWS), ROWS)
        for t in range(share // width):
            cols = slice(t * width, (t + 1) * width)
            above, below = sweeps(
                coef,
                [fl_ref[j, 0, rows, cols] for j in range(blocks)],
                [fl_ref[j, 1, rows, cols] for j in range(blocks)],
            )
            for j in range(blocks):
                uv_ref[j, 0, rows, cols] = above[j]
                uv_ref[j, 1, rows, cols] = below[j]
        return carry

    lax.fori_loop(0, lines // ROWS, group, 0)


def middle(info, fl, slabs):
    vmem = pl.BlockSpec(memory_space=pltpu.VMEM)
    return pl.pallas_call(
        functools.partial(middle_kernel, slabs),
        in_specs=[pl.BlockSpec(memory_space=pltpu.SMEM), vmem],
        out_specs=vmem,
        out_shape=jax.ShapeDtypeStruct(fl.shape, jnp.float32),
        scratch_shapes=[pltpu.VMEM((fl.shape[0], len(KINDS), ROWS, LANES), jnp.float32)],
        compiler_params=pltpu.CompilerParams(vmem_limit_bytes=VMEM_LIMIT),
        cost_estimate=pl.CostEstimate(flops=10 * fl.size, bytes_accessed=8 * fl.size, transcendentals=0),
        name="reduced",
    )(info, fl)


def well_cells_kernel(w_ref, cat_ref, place_row, place_column, out_ref, pick):
    planes, lines, span = w_ref.shape
    wells = place_row.shape[1]

    @pl.when(pl.program_id(0) == 0)
    def _():
        column = lax.broadcasted_iota(jnp.int32, (span, wells), 0)
        pick[...] = (column == place_row[...] % span).astype(jnp.float32).astype(jnp.bfloat16)

    line = lax.broadcasted_iota(jnp.int32, (lines, wells), 0)
    own_line = line == place_row[...] // span
    kinds = cat_ref[...].astype(jnp.float32).reshape(planes * lines, span).astype(jnp.bfloat16)
    sums = [jnp.zeros((planes * lines, wells), jnp.float32)] * 2
    for part in split_bf16(w_ref[...].reshape(planes * lines, span), 3):
        sums[0] = sums[0] + jnp.dot(part, pick[...], preferred_element_type=jnp.float32)
    sums[1] = jnp.dot(kinds, pick[...], preferred_element_type=jnp.float32)
    for n in range(2):
        for k in range(planes):
            cells = jnp.where(own_line, sums[n][k * lines : (k + 1) * lines], 0.0)
            out_ref[n, k : k + 1, :] = jnp.sum(cells, axis=0, keepdims=True)


def well_cells(w, cat, place_row):
    slabs, lines, span = w.shape
    wells = place_row.shape[1]
    planes = 8
    block = pl.BlockSpec((planes, lines, span), lambda i: (i, 0, 0))
    row = pl.BlockSpec((1, wells), lambda i: (0, 0))
    column = pl.BlockSpec((wells, 1), lambda i: (0, 0))
    return pl.pallas_call(
        well_cells_kernel,
        grid=(slabs // planes,),
        in_specs=[block, block, row, column],
        out_specs=pl.BlockSpec((2, planes, wells), lambda i: (0, i, 0)),
        out_shape=jax.ShapeDtypeStruct((2, slabs, wells), jnp.float32),
        scratch_shapes=[pltpu.VMEM((span, wells), jnp.bfloat16)],
        compiler_params=pltpu.CompilerParams(vmem_limit_bytes=VMEM_LIMIT),
        cost_estimate=pl.CostEstimate(
            flops=8 * w.size * wells, bytes_accessed=8 * w.size, transcendentals=0
        ),
        name="well_cells",
    )(w, cat, place_row, place_row.reshape(wells, 1))


def wells_kernel(
    table, where_am_i, info, cells, ends, inverse, well, holders, out_ref, leaving, keep, force, rate, down, rise, uv
):
    blocks, _, slabs, wells = cells.shape
    speed, inlet, reach = well[0:1], well[1:2], well[2:3]
    entries = [table[k] for k in range(table.shape[0])]
    level = lax.broadcasted_iota(jnp.int32, (slabs, wells), 0).astype(jnp.float32)
    for j in range(blocks):
        rock = cells[j, 0]
        cond = select_tree(cells[j, 1].astype(jnp.int32), entries)
        here = jnp.where(level + float(j * slabs) < reach, speed * cond / (1.0 + cond), 0.0)
        rows = slice(j * slabs, (j + 1) * slabs)
        rate[rows] = here
        keep[rows] = 1.0 - here
        force[rows] = here * rock

    chunks = blocks * slabs // ROWS

    def descend(i, value):
        rows = pl.ds(pl.multiple_of(i * ROWS, ROWS), ROWS)
        a, b = keep[rows], force[rows]
        seen = []
        for r in range(ROWS):
            seen.append(value)
            value = a[r : r + 1] * value + b[r : r + 1]
        down[rows] = jnp.concatenate(seen, axis=0)
        return value

    def ascend(i, value):
        rows = pl.ds(pl.multiple_of((chunks - 1 - i) * ROWS, ROWS), ROWS)
        a, b = keep[rows], force[rows]
        seen = []
        for r in reversed(range(ROWS)):
            seen.append(value)
            value = a[r : r + 1] * value + b[r : r + 1]
        rise[rows] = jnp.concatenate(seen[::-1], axis=0)
        return value

    bottom = lax.fori_loop(0, chunks, descend, inlet)
    top = lax.fori_loop(0, chunks, ascend, bottom)
    mine = holders[...] == lax.broadcasted_iota(jnp.int32, (holders.shape[0], wells), 1)
    leaving[...] = jnp.sum(jnp.where(mine, top, 0.0), axis=1, keepdims=True)

    for j in range(blocks):
        rows = slice(j * slabs, (j + 1) * slabs)
        taken = rate[rows] * (2.0 * cells[j, 0] - down[rows] - rise[rows])
        rise[rows] = -storage_volume * taken
    fl = jnp.dot(ends[...], rise[...], precision=HIGHEST, preferred_element_type=jnp.float32)
    coefs = reduced_coefficients(info, slabs, (1, wells))
    above, below = sweeps(
        lambda kind, j: coefs[j][kind],
        [fl[j : j + 1] for j in range(blocks)],
        [fl[blocks + j : blocks + j + 1] for j in range(blocks)],
    )
    for j in range(blocks):
        uv[j, 0:1] = above[j]
        uv[j, 1:2] = below[j]
    d = where_am_i[0]
    own = rise[pl.ds(pl.multiple_of(d * slabs, slabs), slabs)]
    row = lax.broadcasted_iota(jnp.int32, (slabs, wells), 0)
    pair = uv[d]
    own = own + jnp.where(row == 0, pair[0:1], 0.0) + jnp.where(row == slabs - 1, pair[1:2], 0.0)
    out_ref[...] = jnp.dot(inverse[...], own, precision=HIGHEST, preferred_element_type=jnp.float32)


def wells_solve(table, depth_index, info, cells, ends, inverse, well, holders):
    blocks, _, slabs, wells = cells.shape
    smem = pl.BlockSpec(memory_space=pltpu.SMEM)
    vmem = pl.BlockSpec(memory_space=pltpu.VMEM)
    column = pltpu.VMEM((blocks * slabs, wells), jnp.float32)
    return pl.pallas_call(
        wells_kernel,
        in_specs=[smem, smem, smem] + [vmem] * 5,
        out_specs=[vmem, vmem],
        out_shape=[
            jax.ShapeDtypeStruct((slabs, wells), jnp.float32),
            jax.ShapeDtypeStruct((holders.shape[0], 1), jnp.float32),
        ],
        scratch_shapes=[column] * 5 + [pltpu.VMEM((blocks, ROWS, wells), jnp.float32)],
        compiler_params=pltpu.CompilerParams(vmem_limit_bytes=VMEM_LIMIT),
        cost_estimate=pl.CostEstimate(flops=10**7, bytes_accessed=8 * cells.size, transcendentals=0),
        name="wells",
    )(table, depth_index.reshape(1), info, cells, ends, inverse, well, holders)


def solve_kernel(right, uv, inverse, place_row, place_column, solved_wells, out, high, low, pick):
    slabs, rows, span = right.shape
    wells = place_row.shape[1]
    step = pl.program_id(0)
    size = slabs * rows

    @pl.when(step == 0)
    def _():
        spread = (
            lax.broadcasted_iota(jnp.int32, (size, slabs), 0) // rows
            == lax.broadcasted_iota(jnp.int32, (size, slabs), 1)
        ).astype(jnp.float32).astype(jnp.bfloat16)
        spread_t = (
            lax.broadcasted_iota(jnp.int32, (slabs, size), 1) // rows
            == lax.broadcasted_iota(jnp.int32, (slabs, size), 0)
        ).astype(jnp.float32).astype(jnp.bfloat16)
        same = (
            lax.broadcasted_iota(jnp.int32, (size, size), 0) % rows
            == lax.broadcasted_iota(jnp.int32, (size, size), 1) % rows
        )
        for part, ref in zip(split_bf16(inverse[...], 2), (high, low)):
            tall = jnp.dot(spread, part, preferred_element_type=jnp.float32).astype(jnp.bfloat16)
            wide = jnp.dot(tall, spread_t, preferred_element_type=jnp.float32)
            ref[...] = jnp.where(same, wide, 0.0).astype(jnp.bfloat16)
        column = lax.broadcasted_iota(jnp.int32, (wells, span), 1)
        chosen = (column == place_column[...] % span).astype(jnp.float32).astype(jnp.bfloat16)
        pick[:wells] = chosen
        pick[wells:] = chosen

    line = lax.broadcasted_iota(jnp.int32, (slabs, rows, wells), 1) + step * rows
    at_wells = jnp.where(line == (place_row[...] // span)[None], solved_wells[...][:, None, :], 0.0)
    at_wells = jnp.concatenate(split_bf16(at_wells.reshape(size, wells), 2), axis=1)
    shares = uv.shape[0]
    above = jnp.concatenate([uv[d, 0] for d in range(shares)], axis=1)
    below = jnp.concatenate([uv[d, 1] for d in range(shares)], axis=1)
    tile = min(span, 256)
    dot = functools.partial(jnp.dot, preferred_element_type=jnp.float32)
    for t in range(span // tile):
        cols = slice(t * tile, (t + 1) * tile)
        value = jnp.concatenate(
            [
                right[0:1, :, cols] + above[None, :, cols],
                right[1 : slabs - 1, :, cols],
                right[slabs - 1 :, :, cols] + below[None, :, cols],
            ],
            axis=0,
        ).reshape(size, tile)
        upper, lower = split_bf16(value, 2)
        result = dot(high[...], upper)
        result = result + dot(high[...], lower)
        result = result + dot(low[...], upper)
        result = result + dot(at_wells, pick[:, cols])
        out[:, :, cols] = result.reshape(slabs, rows, tile)


def solve(right, uv, inverse, place_row, solved_wells):
    slabs, lines, span = right.shape
    wells = place_row.shape[1]
    block = pl.BlockSpec((slabs, ROWS, span), lambda g: (0, g, 0))
    shares, _, _, share = uv.shape
    whole = lambda *shape: pl.BlockSpec(shape, lambda g: (0,) * len(shape))
    size = slabs * ROWS
    return pl.pallas_call(
        solve_kernel,
        grid=(lines // ROWS,),
        in_specs=[
            block,
            pl.BlockSpec((shares, 2, ROWS, share), lambda g: (0, 0, g, 0)),
            whole(slabs, slabs),
            whole(1, wells),
            whole(wells, 1),
            whole(slabs, wells),
        ],
        out_specs=block,
        out_shape=jax.ShapeDtypeStruct(right.shape, jnp.float32),
        scratch_shapes=[
            pltpu.VMEM((size, size), jnp.bfloat16),
            pltpu.VMEM((size, size), jnp.bfloat16),
            pltpu.VMEM((2 * wells, span), jnp.bfloat16),
        ],
        compiler_params=pltpu.CompilerParams(vmem_limit_bytes=VMEM_LIMIT),
        cost_estimate=pl.CostEstimate(
            flops=8 * size * right.size, bytes_accessed=8 * right.size, transcendentals=0
        ),
        name="depth_solve",
    )(right, uv, inverse, place_row, place_row.reshape(wells, 1), solved_wells)


def body(
    warmth_before,
    stratum_category,
    conductance_catalogue,
    pivot_matrix_reciprocal,
    linkage_factor,
    well_position_inside,
    well_holder_sequence,
    well_reach,
    entering_warmth,
    well_transfer_speed,
):
    slabs, lines, span = warmth_before.shape
    depth_index = lax.axis_index("depth")
    depth_count = lax.axis_size("depth")
    wells = well_position_inside.shape[0]
    owned = wells // depth_count
    table = conductance_catalogue
    entries = [table[k] for k in range(table.shape[0])]

    ends = jnp.stack([pivot_matrix_reciprocal[0], pivot_matrix_reciprocal[-1]])
    info = jnp.concatenate([ends.reshape(-1), linkage_factor])
    info = jnp.pad(info, (0, -info.shape[0] % LANES))
    info = lax.all_gather(info[None], "depth", axis=0, tiled=True)

    warmth_edges = jnp.stack([warmth_before[:, 0], warmth_before[:, -1]])
    cond_edges = flux_scale * select_tree(
        jnp.stack([stratum_category[:, 0], stratum_category[:, -1]]), entries
    )
    count = lax.axis_size("strip")
    up = [(i, i + 1) for i in range(count - 1)]
    down = [(j, i) for i, j in up]
    before = lax.ppermute(jnp.stack([warmth_edges[1], cond_edges[1]], axis=1), "strip", up)
    after = lax.ppermute(jnp.stack([warmth_edges[0], cond_edges[0]], axis=1), "strip", down)

    right, fl = stencil(warmth_before, stratum_category, table, ends, before, after, depth_count)
    fl_all = lax.all_to_all(fl, "depth", split_axis=0, concat_axis=0, tiled=True)

    place_row = well_position_inside.reshape(1, wells)
    cells = well_cells(warmth_before, stratum_category, place_row)
    cells = lax.all_gather(cells[None], "depth", axis=0, tiled=True)

    uv = middle(info, fl_all, slabs)
    uv_own = lax.all_to_all(uv, "depth", split_axis=0, concat_axis=0, tiled=True)

    eye = jnp.eye(depth_count, dtype=jnp.float32)[:, :, None]
    all_ends = jnp.concatenate(
        [
            (eye * info[:, None, part * slabs : (part + 1) * slabs]).reshape(depth_count, -1)
            for part in range(2)
        ]
    )
    well = jnp.stack([well_transfer_speed, entering_warmth, well_reach.astype(jnp.float32)])
    well = jnp.pad(well, ((0, ROWS - 3), (0, 0)))
    holders = lax.dynamic_slice_in_dim(well_holder_sequence, depth_index * owned, owned)
    solved_wells, leaving = wells_solve(
        table, depth_index, info, cells, all_ends, pivot_matrix_reciprocal, well, holders.reshape(owned, 1)
    )
    solved = solve(right, uv_own, pivot_matrix_reciprocal, place_row, solved_wells)
    return solved, leaving.reshape(owned)


def solution(mesh):
    in_specs = (
        P("depth", "strip", None),
        P("depth", "strip", None),
        P(),
        P("depth", None),
        P("depth"),
        P("strip"),
        P("strip"),
        P("strip"),
        P("strip"),
        P("strip"),
    )
    out_specs = (P("depth", "strip", None), P(("strip", "depth")))
    return jax.shard_map(body, mesh=mesh, in_specs=in_specs, out_specs=out_specs, check_vma=False)
```

```python
import functools

import jax
import jax.numpy as jnp
from jax import lax
from jax.experimental import pallas as pl
from jax.experimental.pallas import tpu as pltpu
from jax.sharding import PartitionSpec as P

backward_euler_advance = 0.2
storage_volume = 2.0
flux_scale = 0.5 * backward_euler_advance
LANES = 128
ROWS = 8
VMEM_LIMIT = 48 * 1024 * 1024
HIGHEST = lax.Precision.HIGHEST


def select_tree(category, entries):
    values = list(entries)
    bit = 1
    while len(values) > 1:
        odd = (category & bit) != 0
        values = [
            jnp.where(odd, values[k + 1], values[k]) if k + 1 < len(values) else values[k]
            for k in range(0, len(values), 2)
        ]
        bit *= 2
    return values[0]


def split_bf16(value, pieces):
    out = []
    for k in range(pieces):
        part = value.astype(jnp.bfloat16)
        out.append(part)
        if k + 1 < pieces:
            value = value - part.astype(jnp.float32)
    return out


def edge_kernel(table, w_first, cat_first, w_last, cat_last, first, last):
    planes, rows, span = w_first.shape
    entries = [flux_scale * table[k] for k in range(table.shape[0])]
    for w_ref, cat_ref, row, out in ((w_first, cat_first, 0, first), (w_last, cat_last, rows - 1, last)):
        for k in range(planes):
            out[k, 0:1, :] = w_ref[k, row : row + 1, :]
            out[k, 1:2, :] = select_tree(cat_ref[k, row : row + 1, :], entries)


def edge_rows(w, cat, table):
    slabs, lines, span = w.shape
    planes = 8
    top = pl.BlockSpec((planes, ROWS, span), lambda i: (i, 0, 0))
    end = pl.BlockSpec((planes, ROWS, span), lambda i: (i, lines // ROWS - 1, 0))
    out = pl.BlockSpec((planes, 2, span), lambda i: (i, 0, 0))
    return pl.pallas_call(
        edge_kernel,
        grid=(slabs // planes,),
        in_specs=[pl.BlockSpec(memory_space=pltpu.SMEM), top, top, end, end],
        out_specs=[out, out],
        out_shape=[jax.ShapeDtypeStruct((slabs, 2, span), jnp.float32)] * 2,
        cost_estimate=pl.CostEstimate(flops=10**6, bytes_accessed=w.size, transcendentals=0),
        name="edge_rows",
    )(table, w, cat, w, cat)


def stencil_kernel(table, ends, w_ref, cat_ref, before, after, right_ref, fl_ref, acc, ws, cs, fs):
    step = pl.program_id(0)
    planes, lines, span = w_ref.shape
    tiles = span // LANES
    entries = [flux_scale * table[k] for k in range(table.shape[0])]
    lane = lax.broadcasted_iota(jnp.int32, (lines, LANES), 1)
    top, end = ROWS, ROWS + lines

    @pl.when(step == 0)
    def _():
        acc[...] = jnp.zeros_like(acc)

    def plane(k, carry):
        z = step * planes + k
        end_first, end_last = ends[0, z], ends[1, z]
        left_w = left_c = jnp.zeros((lines, LANES), jnp.float32)
        pending = None
        for t in range(tiles + 1):
            current, next_face = None, None
            if t < tiles:
                cols = slice(t * LANES, (t + 1) * LANES)
                w = w_ref[k, :, cols]
                c = select_tree(cat_ref[k, :, cols], entries)
                for ref, value, which in ((ws, w, 0), (cs, c, 1)):
                    ref[t, top:end] = value
                    ref[t, top - 1 : top] = before[k, which : which + 1, cols]
                    ref[t, end : end + 1] = after[k, which : which + 1, cols]
                roll_w, roll_c = pltpu.roll(w, 1, 1), pltpu.roll(c, 1, 1)
                west_w = jnp.where(lane == 0, left_w, roll_w)
                west_c = jnp.where(lane == 0, left_c, roll_c)
                left_w, left_c = roll_w, roll_c
                face = (c + west_c) * (w - west_w)
                next_face = pltpu.roll(face, LANES - 1, 1)
                north = (c + cs[t, top - 1 : end - 1]) * (w - ws[t, top - 1 : end - 1])
                fs[t, top:end] = north
                fs[t, end : end + 1] = (cs[t, end : end + 1] + cs[t, end - 1 : end]) * (
                    ws[t, end : end + 1] - ws[t, end - 1 : end]
                )
                base = w - face - north + fs[t, top + 1 : end + 1]
                current = (cols, base, next_face, -c * w)
            if pending is not None:
                cols_before, base_before, face_before, edge = pending
                east = jnp.where(lane == LANES - 1, edge if t == tiles else next_face, face_before)
                value = base_before + east
                right_ref[k, :, cols_before] = value
                acc[0, :, cols_before] += end_first * value
                acc[1, :, cols_before] += end_last * value
            pending = current
        return carry

    lax.fori_loop(0, planes, plane, 0)

    @pl.when(step == pl.num_programs(0) - 1)
    def _():
        share = fl_ref.shape[-1]
        for d in range(fl_ref.shape[0]):
            fl_ref[d] = acc[:, :, d * share : (d + 1) * share]


def stencil(w, cat, table, ends, before, after, depth_count):
    slabs, lines, span = w.shape
    planes = 4
    block = pl.BlockSpec((planes, lines, span), lambda i: (i, 0, 0))
    halo = pl.BlockSpec((planes, 2, span), lambda i: (i, 0, 0))
    fl_shape = (depth_count, 2, lines, span // depth_count)
    smem = pl.BlockSpec(memory_space=pltpu.SMEM)
    shifted = pltpu.VMEM((span // LANES, lines + 2 * ROWS, LANES), jnp.float32)
    return pl.pallas_call(
        stencil_kernel,
        grid=(slabs // planes,),
        in_specs=[smem, smem, block, block, halo, halo],
        out_specs=[block, pl.BlockSpec(fl_shape, lambda i: (0, 0, 0, 0))],
        out_shape=[
            jax.ShapeDtypeStruct(w.shape, jnp.float32),
            jax.ShapeDtypeStruct(fl_shape, jnp.float32),
        ],
        scratch_shapes=[pltpu.VMEM((2, lines, span), jnp.float32), shifted, shifted, shifted],
        compiler_params=pltpu.CompilerParams(vmem_limit_bytes=VMEM_LIMIT),
        cost_estimate=pl.CostEstimate(flops=40 * w.size, bytes_accessed=12 * w.size, transcendentals=0),
        name="stencil",
    )(table, ends, w, cat, before, after)


def reduced_coefficients(info, slabs, shape):
    blocks = info.shape[0]
    full = lambda value: jnp.full(shape, value, jnp.float32)
    first = [full(info[j, 0]) for j in range(blocks)]
    upper = [full(info[j, slabs - 1]) for j in range(blocks)]
    lower = [full(info[j, slabs]) for j in range(blocks)]
    last = [full(info[j, 2 * slabs - 1]) for j in range(blocks)]
    ratio = [full(info[j, 2 * slabs]) for j in range(blocks)]
    zero = jnp.zeros(shape, jnp.float32)
    shrink = slabs / (slabs + 1.0)
    couple = [zero]
    for j in range(1, blocks):
        couple.append(ratio[j] * shrink / jnp.sqrt(last[j - 1] * first[j]))
    couple.append(zero)
    out = []
    q = zero
    for j in range(blocks):
        vf, vl = couple[j] * first[j], couple[j] * lower[j]
        wf, wl = couple[j + 1] * upper[j], couple[j + 1] * last[j]
        inverse = 1.0 / (1.0 - vf * q)
        out.append(
            dict(
                p_first=vl * q * inverse,
                p_before=vl * inverse,
                a_first=inverse,
                a_before=vf * inverse,
                a_after=wf * inverse,
                couple=couple[j],
                couple_after=couple[j + 1],
                q=q,
            )
        )
        q = wl + vl * q * wf * inverse
    return out


KINDS = ("p_first", "p_before", "a_first", "a_before", "a_after", "couple", "couple_after", "q")


def sweeps(coef, firsts, lasts):
    blocks = len(firsts)
    before = [jnp.zeros_like(firsts[0])]
    for j in range(blocks - 1):
        before.append(
            lasts[j] + coef("p_first", j) * firsts[j] + coef("p_before", j) * before[j]
        )
    above, below = [None] * blocks, [None] * blocks
    after = jnp.zeros_like(firsts[0])
    for j in reversed(range(blocks)):
        below[j] = coef("couple_after", j) * after
        here = (
            coef("a_first", j) * firsts[j]
            + coef("a_before", j) * before[j]
            + coef("a_after", j) * after
        )
        above[j] = coef("couple", j) * (before[j] + coef("q", j) * here)
        after = here
    return above, below


def middle_kernel(slabs, info, fl_ref, uv_ref, table):
    blocks, _, lines, share = fl_ref.shape
    for j, entry in enumerate(reduced_coefficients(info, slabs, (ROWS, LANES))):
        for k, kind in enumerate(KINDS):
            table[j, k] = entry[kind]
    width = min(share, LANES)

    def coef(kind, j):
        return table[j, KINDS.index(kind), :, :width]

    def group(g, carry):
        rows = pl.ds(pl.multiple_of(g * ROWS, ROWS), ROWS)
        for t in range(share // width):
            cols = slice(t * width, (t + 1) * width)
            above, below = sweeps(
                coef,
                [fl_ref[j, 0, rows, cols] for j in range(blocks)],
                [fl_ref[j, 1, rows, cols] for j in range(blocks)],
            )
            for j in range(blocks):
                uv_ref[j, 0, rows, cols] = above[j]
                uv_ref[j, 1, rows, cols] = below[j]
        return carry

    lax.fori_loop(0, lines // ROWS, group, 0)


def middle(info, fl, slabs):
    vmem = pl.BlockSpec(memory_space=pltpu.VMEM)
    return pl.pallas_call(
        functools.partial(middle_kernel, slabs),
        in_specs=[pl.BlockSpec(memory_space=pltpu.SMEM), vmem],
        out_specs=vmem,
        out_shape=jax.ShapeDtypeStruct(fl.shape, jnp.float32),
        scratch_shapes=[pltpu.VMEM((fl.shape[0], len(KINDS), ROWS, LANES), jnp.float32)],
        compiler_params=pltpu.CompilerParams(vmem_limit_bytes=VMEM_LIMIT),
        cost_estimate=pl.CostEstimate(flops=10 * fl.size, bytes_accessed=8 * fl.size, transcendentals=0),
        name="reduced",
    )(info, fl)


def well_cells_kernel(w_ref, cat_ref, place_row, place_column, out_ref, pick):
    planes, lines, span = w_ref.shape
    wells = place_row.shape[1]

    @pl.when(pl.program_id(0) == 0)
    def _():
        column = lax.broadcasted_iota(jnp.int32, (span, wells), 0)
        pick[...] = (column == place_row[...] % span).astype(jnp.float32).astype(jnp.bfloat16)

    line = lax.broadcasted_iota(jnp.int32, (lines, wells), 0)
    own_line = line == place_row[...] // span
    kinds = cat_ref[...].astype(jnp.float32).reshape(planes * lines, span).astype(jnp.bfloat16)
    sums = [jnp.zeros((planes * lines, wells), jnp.float32)] * 2
    for part in split_bf16(w_ref[...].reshape(planes * lines, span), 3):
        sums[0] = sums[0] + jnp.dot(part, pick[...], preferred_element_type=jnp.float32)
    sums[1] = jnp.dot(kinds, pick[...], preferred_element_type=jnp.float32)
    for n in range(2):
        for k in range(planes):
            cells = jnp.where(own_line, sums[n][k * lines : (k + 1) * lines], 0.0)
            out_ref[n, k : k + 1, :] = jnp.sum(cells, axis=0, keepdims=True)


def well_cells(w, cat, place_row):
    slabs, lines, span = w.shape
    wells = place_row.shape[1]
    planes = 8
    block = pl.BlockSpec((planes, lines, span), lambda i: (i, 0, 0))
    row = pl.BlockSpec((1, wells), lambda i: (0, 0))
    column = pl.BlockSpec((wells, 1), lambda i: (0, 0))
    return pl.pallas_call(
        well_cells_kernel,
        grid=(slabs // planes,),
        in_specs=[block, block, row, column],
        out_specs=pl.BlockSpec((2, planes, wells), lambda i: (0, i, 0)),
        out_shape=jax.ShapeDtypeStruct((2, slabs, wells), jnp.float32),
        scratch_shapes=[pltpu.VMEM((span, wells), jnp.bfloat16)],
        compiler_params=pltpu.CompilerParams(vmem_limit_bytes=VMEM_LIMIT),
        cost_estimate=pl.CostEstimate(
            flops=8 * w.size * wells, bytes_accessed=8 * w.size, transcendentals=0
        ),
        name="well_cells",
    )(w, cat, place_row, place_row.reshape(wells, 1))


def wells_kernel(
    table, where_am_i, info, cells, ends, inverse, well, holders, out_ref, leaving, keep, force, rate, down, rise, uv
):
    blocks, _, slabs, wells = cells.shape
    speed, inlet, reach = well[0:1], well[1:2], well[2:3]
    entries = [table[k] for k in range(table.shape[0])]
    level = lax.broadcasted_iota(jnp.int32, (slabs, wells), 0).astype(jnp.float32)
    for j in range(blocks):
        rock = cells[j, 0]
        cond = select_tree(cells[j, 1].astype(jnp.int32), entries)
        here = jnp.where(level + float(j * slabs) < reach, speed * cond / (1.0 + cond), 0.0)
        rows = slice(j * slabs, (j + 1) * slabs)
        rate[rows] = here
        keep[rows] = 1.0 - here
        force[rows] = here * rock

    chunks = blocks * slabs // ROWS

    def descend(i, value):
        rows = pl.ds(pl.multiple_of(i * ROWS, ROWS), ROWS)
        a, b = keep[rows], force[rows]
        seen = []
        for r in range(ROWS):
            seen.append(value)
            value = a[r : r + 1] * value + b[r : r + 1]
        down[rows] = jnp.concatenate(seen, axis=0)
        return value

    def ascend(i, value):
        rows = pl.ds(pl.multiple_of((chunks - 1 - i) * ROWS, ROWS), ROWS)
        a, b = keep[rows], force[rows]
        seen = []
        for r in reversed(range(ROWS)):
            seen.append(value)
            value = a[r : r + 1] * value + b[r : r + 1]
        rise[rows] = jnp.concatenate(seen[::-1], axis=0)
        return value

    bottom = lax.fori_loop(0, chunks, descend, inlet)
    top = lax.fori_loop(0, chunks, ascend, bottom)
    mine = holders[...] == lax.broadcasted_iota(jnp.int32, (holders.shape[0], wells), 1)
    leaving[...] = jnp.sum(jnp.where(mine, top, 0.0), axis=1, keepdims=True)

    for j in range(blocks):
        rows = slice(j * slabs, (j + 1) * slabs)
        taken = rate[rows] * (2.0 * cells[j, 0] - down[rows] - rise[rows])
        rise[rows] = -storage_volume * taken
    fl = jnp.dot(ends[...], rise[...], precision=HIGHEST, preferred_element_type=jnp.float32)
    coefs = reduced_coefficients(info, slabs, (1, wells))
    above, below = sweeps(
        lambda kind, j: coefs[j][kind],
        [fl[j : j + 1] for j in range(blocks)],
        [fl[blocks + j : blocks + j + 1] for j in range(blocks)],
    )
    for j in range(blocks):
        uv[j, 0:1] = above[j]
        uv[j, 1:2] = below[j]
    d = where_am_i[0]
    own = rise[pl.ds(pl.multiple_of(d * slabs, slabs), slabs)]
    row = lax.broadcasted_iota(jnp.int32, (slabs, wells), 0)
    pair = uv[d]
    own = own + jnp.where(row == 0, pair[0:1], 0.0) + jnp.where(row == slabs - 1, pair[1:2], 0.0)
    out_ref[...] = jnp.dot(inverse[...], own, precision=HIGHEST, preferred_element_type=jnp.float32)


def wells_solve(table, depth_index, info, cells, ends, inverse, well, holders):
    blocks, _, slabs, wells = cells.shape
    smem = pl.BlockSpec(memory_space=pltpu.SMEM)
    vmem = pl.BlockSpec(memory_space=pltpu.VMEM)
    column = pltpu.VMEM((blocks * slabs, wells), jnp.float32)
    return pl.pallas_call(
        wells_kernel,
        in_specs=[smem, smem, smem] + [vmem] * 5,
        out_specs=[vmem, vmem],
        out_shape=[
            jax.ShapeDtypeStruct((slabs, wells), jnp.float32),
            jax.ShapeDtypeStruct((holders.shape[0], 1), jnp.float32),
        ],
        scratch_shapes=[column] * 5 + [pltpu.VMEM((blocks, ROWS, wells), jnp.float32)],
        compiler_params=pltpu.CompilerParams(vmem_limit_bytes=VMEM_LIMIT),
        cost_estimate=pl.CostEstimate(flops=10**7, bytes_accessed=8 * cells.size, transcendentals=0),
        name="wells",
    )(table, depth_index.reshape(1), info, cells, ends, inverse, well, holders)


def local_kernel(right, inverse, out, high, low):
    slabs, rows, span = right.shape
    size = slabs * rows

    @pl.when(pl.program_id(0) == 0)
    def _():
        spread = (
            lax.broadcasted_iota(jnp.int32, (size, slabs), 0) // rows
            == lax.broadcasted_iota(jnp.int32, (size, slabs), 1)
        ).astype(jnp.float32).astype(jnp.bfloat16)
        spread_t = (
            lax.broadcasted_iota(jnp.int32, (slabs, size), 1) // rows
            == lax.broadcasted_iota(jnp.int32, (slabs, size), 0)
        ).astype(jnp.float32).astype(jnp.bfloat16)
        same = (
            lax.broadcasted_iota(jnp.int32, (size, size), 0) % rows
            == lax.broadcasted_iota(jnp.int32, (size, size), 1) % rows
        )
        for part, ref in zip(split_bf16(inverse[...], 2), (high, low)):
            tall = jnp.dot(spread, part, preferred_element_type=jnp.float32).astype(jnp.bfloat16)
            wide = jnp.dot(tall, spread_t, preferred_element_type=jnp.float32)
            ref[...] = jnp.where(same, wide, 0.0).astype(jnp.bfloat16)

    tile = min(span, 256)
    dot = functools.partial(jnp.dot, preferred_element_type=jnp.float32)
    for t in range(span // tile):
        cols = slice(t * tile, (t + 1) * tile)
        upper, lower = split_bf16(right[:, :, cols].reshape(size, tile), 2)
        result = dot(high[...], upper)
        result = result + dot(high[...], lower)
        result = result + dot(low[...], upper)
        out[:, :, cols] = result.reshape(slabs, rows, tile)


def local_solve(right, inverse):
    slabs, lines, span = right.shape
    block = pl.BlockSpec((slabs, ROWS, span), lambda g: (0, g, 0))
    size = slabs * ROWS
    return pl.pallas_call(
        local_kernel,
        grid=(lines // ROWS,),
        in_specs=[block, pl.BlockSpec((slabs, slabs), lambda g: (0, 0))],
        out_specs=block,
        out_shape=jax.ShapeDtypeStruct(right.shape, jnp.float32),
        scratch_shapes=[pltpu.VMEM((size, size), jnp.bfloat16)] * 2,
        compiler_params=pltpu.CompilerParams(vmem_limit_bytes=VMEM_LIMIT),
        cost_estimate=pl.CostEstimate(
            flops=6 * size * right.size, bytes_accessed=8 * right.size, transcendentals=0
        ),
        name="local_solve",
    )(right, inverse)


def update_kernel(columns, local, uv, place_row, place_column, solved_wells, out, pick):
    slabs, rows, span = local.shape
    wells = place_row.shape[1]
    step = pl.program_id(0)
    size = slabs * rows

    @pl.when(step == 0)
    def _():
        column = lax.broadcasted_iota(jnp.int32, (wells, span), 1)
        chosen = (column == place_column[...] % span).astype(jnp.float32).astype(jnp.bfloat16)
        pick[:wells] = chosen
        pick[wells:] = chosen

    line = lax.broadcasted_iota(jnp.int32, (slabs, rows, wells), 1) + step * rows
    at_wells = jnp.where(line == (place_row[...] // span)[None], solved_wells[...][:, None, :], 0.0)
    at_wells = jnp.concatenate(split_bf16(at_wells.reshape(size, wells), 2), axis=1)
    shares = uv.shape[0]
    above = jnp.concatenate([uv[d, 0] for d in range(shares)], axis=1)
    below = jnp.concatenate([uv[d, 1] for d in range(shares)], axis=1)
    tile = min(span, 256)
    for t in range(span // tile):
        cols = slice(t * tile, (t + 1) * tile)
        extra = jnp.dot(at_wells, pick[:, cols], preferred_element_type=jnp.float32)
        for z in range(slabs):
            out[z, :, cols] = (
                local[z, :, cols]
                + extra[z * rows : (z + 1) * rows]
                + columns[0, z] * above[:, cols]
                + columns[1, z] * below[:, cols]
            )


def update(columns, local, uv, place_row, solved_wells):
    slabs, lines, span = local.shape
    wells = place_row.shape[1]
    block = pl.BlockSpec((slabs, ROWS, span), lambda g: (0, g, 0))
    shares, _, _, share = uv.shape
    whole = lambda *shape: pl.BlockSpec(shape, lambda g: (0,) * len(shape))
    return pl.pallas_call(
        update_kernel,
        grid=(lines // ROWS,),
        in_specs=[
            pl.BlockSpec(memory_space=pltpu.SMEM),
            block,
            pl.BlockSpec((shares, 2, ROWS, share), lambda g: (0, 0, g, 0)),
            whole(1, wells),
            whole(wells, 1),
            whole(slabs, wells),
        ],
        out_specs=block,
        out_shape=jax.ShapeDtypeStruct(local.shape, jnp.float32),
        scratch_shapes=[pltpu.VMEM((2 * wells, span), jnp.bfloat16)],
        compiler_params=pltpu.CompilerParams(vmem_limit_bytes=VMEM_LIMIT),
        cost_estimate=pl.CostEstimate(
            flops=4 * ROWS * wells * local.size, bytes_accessed=8 * local.size, transcendentals=0
        ),
        name="update",
    )(columns, local, uv, place_row, place_row.reshape(wells, 1), solved_wells)


def body(
    warmth_before,
    stratum_category,
    conductance_catalogue,
    pivot_matrix_reciprocal,
    linkage_factor,
    well_position_inside,
    well_holder_sequence,
    well_reach,
    entering_warmth,
    well_transfer_speed,
):
    slabs, lines, span = warmth_before.shape
    depth_index = lax.axis_index("depth")
    depth_count = lax.axis_size("depth")
    wells = well_position_inside.shape[0]
    owned = wells // depth_count
    table = conductance_catalogue

    def gathered(value):
        copies = jnp.broadcast_to(value[None], (depth_count,) + value.shape)
        return lax.all_to_all(copies, "depth", split_axis=0, concat_axis=0, tiled=True)

    ends = jnp.stack([pivot_matrix_reciprocal[0], pivot_matrix_reciprocal[-1]])
    info = jnp.concatenate([ends.reshape(-1), linkage_factor])
    info = jnp.pad(info, (0, -info.shape[0] % LANES))
    info = gathered(info)

    first, last = edge_rows(warmth_before, stratum_category, table)
    count = lax.axis_size("strip")
    up = [(i, i + 1) for i in range(count - 1)]
    down = [(j, i) for i, j in up]
    before = lax.ppermute(last, "strip", up)
    after = lax.ppermute(first, "strip", down)

    right, fl = stencil(warmth_before, stratum_category, table, ends, before, after, depth_count)
    fl_all = lax.all_to_all(fl, "depth", split_axis=0, concat_axis=0, tiled=True)

    place_row = well_position_inside.reshape(1, wells)
    cells = well_cells(warmth_before, stratum_category, place_row)
    cells = gathered(cells)
    local = local_solve(right, pivot_matrix_reciprocal)

    uv = middle(info, fl_all, slabs)
    uv_own = lax.all_to_all(uv, "depth", split_axis=0, concat_axis=0, tiled=True)

    eye = jnp.eye(depth_count, dtype=jnp.float32)[:, :, None]
    all_ends = jnp.concatenate(
        [
            (eye * info[:, None, part * slabs : (part + 1) * slabs]).reshape(depth_count, -1)
            for part in range(2)
        ]
    )
    well = jnp.stack([well_transfer_speed, entering_warmth, well_reach.astype(jnp.float32)])
    well = jnp.pad(well, ((0, ROWS - 3), (0, 0)))
    holders = lax.dynamic_slice_in_dim(well_holder_sequence, depth_index * owned, owned)
    solved_wells, leaving = wells_solve(
        table, depth_index, info, cells, all_ends, pivot_matrix_reciprocal, well, holders.reshape(owned, 1)
    )
    columns = jnp.stack([pivot_matrix_reciprocal[:, 0], pivot_matrix_reciprocal[:, -1]])
    solved = update(columns, local, uv_own, place_row, solved_wells)
    return solved, leaving.reshape(owned)


def solution(mesh):
    in_specs = (
        P("depth", "strip", None),
        P("depth", "strip", None),
        P(),
        P("depth", None),
        P("depth"),
        P("strip"),
        P("strip"),
        P("strip"),
        P("strip"),
        P("strip"),
    )
    out_specs = (P("depth", "strip", None), P(("strip", "depth")))
    return jax.shard_map(body, mesh=mesh, in_specs=in_specs, out_specs=out_specs, check_vma=False)
```

```python
import functools

import jax
import jax.numpy as jnp
from jax import lax
from jax.experimental import pallas as pl
from jax.experimental.pallas import tpu as pltpu
from jax.sharding import PartitionSpec as P

backward_euler_advance = 0.2
storage_volume = 2.0
flux_scale = 0.5 * backward_euler_advance
LANES = 128
ROWS = 8
VMEM_LIMIT = 48 * 1024 * 1024
HIGHEST = lax.Precision.HIGHEST


def select_tree(category, entries):
    values = list(entries)
    bit = 1
    while len(values) > 1:
        odd = (category & bit) != 0
        values = [
            jnp.where(odd, values[k + 1], values[k]) if k + 1 < len(values) else values[k]
            for k in range(0, len(values), 2)
        ]
        bit *= 2
    return values[0]


def split_bf16(value, pieces):
    out = []
    for k in range(pieces):
        part = value.astype(jnp.bfloat16)
        out.append(part)
        if k + 1 < pieces:
            value = value - part.astype(jnp.float32)
    return out


def edge_kernel(table, w_first, cat_first, w_last, cat_last, first, last, kinds):
    planes, rows, span = w_first.shape
    entries = [flux_scale * table[k] for k in range(table.shape[0])]
    for w_ref, cat_ref, row, out in ((w_first, cat_first, 0, first), (w_last, cat_last, rows - 1, last)):
        for k in range(planes):
            kinds[k : k + 1, :] = cat_ref[k, row : row + 1, :]
        cond = select_tree(kinds[...], entries)
        for k in range(planes):
            out[k, 0:1, :] = w_ref[k, row : row + 1, :]
            out[k, 1:2, :] = cond[k : k + 1]


def edge_rows(w, cat, table):
    slabs, lines, span = w.shape
    planes = 8
    top = pl.BlockSpec((planes, ROWS, span), lambda i: (i, 0, 0))
    end = pl.BlockSpec((planes, ROWS, span), lambda i: (i, lines // ROWS - 1, 0))
    out = pl.BlockSpec((planes, 2, span), lambda i: (i, 0, 0))
    return pl.pallas_call(
        edge_kernel,
        grid=(slabs // planes,),
        in_specs=[pl.BlockSpec(memory_space=pltpu.SMEM), top, top, end, end],
        out_specs=[out, out],
        out_shape=[jax.ShapeDtypeStruct((slabs, 2, span), jnp.float32)] * 2,
        scratch_shapes=[pltpu.VMEM((planes, span), jnp.int32)],
        cost_estimate=pl.CostEstimate(flops=10**6, bytes_accessed=w.size, transcendentals=0),
        name="edge_rows",
    )(table, w, cat, w, cat)


def stencil_kernel(table, ends, info, w_ref, cat_ref, before, after, right_ref, fl_ref, acc, ws, cs, fs):
    step = pl.program_id(0)
    planes, lines, span = w_ref.shape
    tiles = span // LANES
    entries = [flux_scale * table[k] for k in range(table.shape[0])]
    lane = lax.broadcasted_iota(jnp.int32, (lines, LANES), 1)
    top, end = ROWS, ROWS + lines
    together = ws.shape[0]

    @pl.when(step == 0)
    def _():
        acc[...] = jnp.zeros_like(acc)

    def faces(k, n, t, left):
        cols = slice(t * LANES, (t + 1) * LANES)
        w = w_ref[k, :, cols]
        c = select_tree(cat_ref[k, :, cols], entries)
        for ref, value, which in ((ws, w, 0), (cs, c, 1)):
            ref[n, t, top:end] = value
            ref[n, t, top - 1 : top] = before[k, which : which + 1, cols]
            ref[n, t, end : end + 1] = after[k, which : which + 1, cols]
        rolled = pltpu.roll(w, 1, 1), pltpu.roll(c, 1, 1)
        west_w = jnp.where(lane == 0, left[0], rolled[0])
        west_c = jnp.where(lane == 0, left[1], rolled[1])
        face = (c + west_c) * (w - west_w)
        north = (c + cs[n, t, top - 1 : end - 1]) * (w - ws[n, t, top - 1 : end - 1])
        fs[n, t, top:end] = north
        fs[n, t, end : end + 1] = (cs[n, t, end : end + 1] + cs[n, t, end - 1 : end]) * (
            ws[n, t, end : end + 1] - ws[n, t, end - 1 : end]
        )
        base = w - face - north + fs[n, t, top + 1 : end + 1]
        return base, pltpu.roll(face, LANES - 1, 1), rolled, -c * w

    def some_planes(m, carry):
        k = [m * together + n for n in range(together)]
        z = [step * planes + k[n] for n in range(together)]
        zero = jnp.zeros((lines, LANES), jnp.float32)
        left = [(zero, zero)] * together
        last = [None] * together
        for t in range(tiles + 1):
            now = [None] * together
            if t < tiles:
                for n in range(together):
                    now[n] = faces(k[n], n, t, left[n])
                    left[n] = now[n][2]
            if t > 0:
                cols = slice((t - 1) * LANES, t * LANES)
                first, final = acc[0, :, cols], acc[1, :, cols]
                for n in range(together):
                    base, face, _, edge = last[n]
                    east = jnp.where(lane == LANES - 1, edge if t == tiles else now[n][1], face)
                    value = base + east
                    right_ref[k[n], :, cols] = value
                    first = first + ends[0, z[n]] * value
                    final = final + ends[1, z[n]] * value
                acc[0, :, cols] = first
                acc[1, :, cols] = final
            last = now
        return carry

    lax.fori_loop(0, planes // together, some_planes, 0)

    @pl.when(step == pl.num_programs(0) - 1)
    def _():
        share = fl_ref.shape[-1]
        for d in range(fl_ref.shape[0]):
            fl_ref[d, :, :lines] = acc[:, :, d * share : (d + 1) * share]
            for n in range(2):
                fl_ref[d, n, lines:] = info[...]


def stencil(w, cat, table, ends, info, before, after, parts):
    slabs, lines, span = w.shape
    planes, together = 4, 2
    block = pl.BlockSpec((planes, lines, span), lambda i: (i, 0, 0))
    halo = pl.BlockSpec((planes, 2, span), lambda i: (i, 0, 0))
    fl_shape = (parts, 2, lines + ROWS, span // parts)
    smem = pl.BlockSpec(memory_space=pltpu.SMEM)
    shifted = pltpu.VMEM((together, span // LANES, lines + 2 * ROWS, LANES), jnp.float32)
    return pl.pallas_call(
        stencil_kernel,
        grid=(slabs // planes,),
        in_specs=[smem, smem, pl.BlockSpec(info.shape, lambda i: (0, 0)), block, block, halo, halo],
        out_specs=[block, pl.BlockSpec(fl_shape, lambda i: (0, 0, 0, 0))],
        out_shape=[
            jax.ShapeDtypeStruct(w.shape, jnp.float32),
            jax.ShapeDtypeStruct(fl_shape, jnp.float32),
        ],
        scratch_shapes=[pltpu.VMEM((2, lines, span), jnp.float32), shifted, shifted, shifted],
        compiler_params=pltpu.CompilerParams(vmem_limit_bytes=VMEM_LIMIT),
        cost_estimate=pl.CostEstimate(flops=40 * w.size, bytes_accessed=12 * w.size, transcendentals=0),
        name="stencil",
    )(table, ends, info, w, cat, before, after)


CORNERS = ((0, 0), (0, 1), (1, 0), (1, 1))


def block_scalars(tile, slabs, shape, flipped=None):
    at = lambda row, lane: jnp.broadcast_to(tile[row : row + 1, lane : lane + 1], shape)
    corner = {(r, c): at(r, c * (slabs - 1)) for r, c in CORNERS}
    if flipped is not None:
        corner = {(r, c): jnp.where(flipped, corner[1 - r, 1 - c], corner[r, c]) for r, c in CORNERS}
    return corner, at(0, slabs)


def coupling(ratio, one, other, slabs):
    return ratio * (slabs / (slabs + 1.0)) / jnp.sqrt(one * other)


def chain(corners, couple, q=None):
    out = []
    q = jnp.zeros_like(couple[0])
    for k, corner in enumerate(corners):
        vf, vl = couple[k] * corner[0, 0], couple[k] * corner[1, 0]
        wf, wl = couple[k + 1] * corner[0, 1], couple[k + 1] * corner[1, 1]
        inverse = 1.0 / (1.0 - vf * q)
        out.append(
            dict(
                p_first=vl * q * inverse,
                p_before=vl * inverse,
                a_first=inverse,
                a_before=vf * inverse,
                a_after=wf * inverse,
                couple=couple[k],
                couple_after=couple[k + 1],
                q=q,
            )
        )
        q = wl + vl * q * wf * inverse
    return out, q


KINDS = ("p_first", "p_before", "a_first", "a_before", "a_after", "couple", "couple_after", "q")


def forward(coef, firsts, lasts):
    before = [jnp.zeros_like(firsts[0])]
    for j in range(len(firsts)):
        before.append(
            lasts[j] + coef("p_first", j) * firsts[j] + coef("p_before", j) * before[j]
        )
    return before


def backward(coef, firsts, before, after):
    blocks = len(firsts)
    above, below = [None] * blocks, [None] * blocks
    for j in reversed(range(blocks)):
        below[j] = coef("couple_after", j) * after
        here = (
            coef("a_first", j) * firsts[j]
            + coef("a_before", j) * before[j]
            + coef("a_after", j) * after
        )
        above[j] = coef("couple", j) * (before[j] + coef("q", j) * here)
        after = here
    return above, below


def half_chain(tiles, slabs, flipped, middle):
    shape = (ROWS, LANES)
    scalars = [block_scalars(tile, slabs, shape, flipped) for tile in tiles]
    couple = [jnp.zeros(shape, jnp.float32)]
    for k in range(1, len(tiles)):
        ratio = jnp.where(flipped, scalars[k - 1][1], scalars[k][1])
        couple.append(coupling(ratio, scalars[k - 1][0][1, 1], scalars[k][0][0, 0], slabs))
    couple.append(middle)
    return chain([corner for corner, _ in scalars], couple)


def first_kernel(slabs, half, fl_ref, out_ref, table):
    blocks, _, lines, share = fl_ref.shape
    lines = lines - ROWS
    flip = half[0]
    flipped = flip == 1
    block = [k + flip * (blocks - 1 - 2 * k) for k in range(blocks)]
    entries, _ = half_chain(
        [fl_ref[block[k], 0, lines:, :LANES] for k in range(blocks)],
        slabs,
        flipped,
        jnp.zeros((ROWS, LANES), jnp.float32),
    )
    for k, entry in enumerate(entries):
        for n, kind in enumerate(KINDS[:2]):
            table[k, n] = entry[kind]
    coef = lambda kind, k: table[k, KINDS.index(kind)]

    def group(g, carry):
        rows = pl.ds(pl.multiple_of(g * ROWS, ROWS), ROWS)
        for t in range(share // LANES):
            cols = slice(t * LANES, (t + 1) * LANES)
            before = forward(
                coef,
                [fl_ref[block[k], flip, rows, cols] for k in range(blocks)],
                [fl_ref[block[k], 1 - flip, rows, cols] for k in range(blocks)],
            )
            out_ref[rows, cols] = before[blocks]
        return carry

    lax.fori_loop(0, lines // ROWS, group, 0)
    out_ref[lines:, :] = jnp.zeros((out_ref.shape[0] - lines, share), jnp.float32)
    for j in range(blocks):
        out_ref[lines + 2 * j : lines + 2 * j + 2, :] = fl_ref[j, 0, lines : lines + 2, :]


def first_half(half, fl, slabs):
    parts, _, lines, share = fl.shape
    vmem = pl.BlockSpec(memory_space=pltpu.VMEM)
    rows = lines - ROWS + -(-2 * parts // ROWS) * ROWS
    return pl.pallas_call(
        functools.partial(first_kernel, slabs),
        in_specs=[pl.BlockSpec(memory_space=pltpu.SMEM), vmem],
        out_specs=vmem,
        out_shape=jax.ShapeDtypeStruct((rows, share), jnp.float32),
        scratch_shapes=[pltpu.VMEM((parts, 2, ROWS, LANES), jnp.float32)],
        compiler_params=pltpu.CompilerParams(vmem_limit_bytes=VMEM_LIMIT),
        cost_estimate=pl.CostEstimate(flops=4 * fl.size, bytes_accessed=5 * fl.size, transcendentals=0),
        name="reduced_in",
    )(half, fl)


def second_kernel(slabs, half, fl_ref, mine, other, uv_ref, info_ref, table):
    blocks, _, lines, share = fl_ref.shape
    lines = lines - ROWS
    flip = half[0]
    flipped = flip == 1
    block = [k + flip * (blocks - 1 - 2 * k) for k in range(blocks)]
    for j in range(blocks):
        info_ref[flip * blocks + j] = fl_ref[j, 0, lines:, :LANES]
        info_ref[(1 - flip) * blocks + j] = jnp.zeros((ROWS, LANES), jnp.float32)
        info_ref[(1 - flip) * blocks + j, 0:2] = other[lines + 2 * j : lines + 2 * j + 2, :LANES]
    shape = (ROWS, LANES)
    above, above_ratio = block_scalars(info_ref[blocks - 1], slabs, shape)
    below, below_ratio = block_scalars(info_ref[blocks], slabs, shape)
    middle = coupling(below_ratio, above[1, 1], below[0, 0], slabs)
    tiles = lambda flip: [
        info_ref[flip * blocks + k + flip * (blocks - 1 - 2 * k)] for k in range(blocks)
    ]
    entries, q_own = half_chain(tiles(flip), slabs, flipped, middle)
    _, q_other = half_chain(tiles(1 - flip), slabs, jnp.logical_not(flipped), middle)
    for k, entry in enumerate(entries):
        for n, kind in enumerate(KINDS):
            table[k, n] = entry[kind]
    table[blocks, 0] = 1.0 / (1.0 - q_own * q_other)
    table[blocks, 1] = q_other
    coef = lambda kind, k: table[k, KINDS.index(kind)]

    def group(g, carry):
        rows = pl.ds(pl.multiple_of(g * ROWS, ROWS), ROWS)
        for t in range(share // LANES):
            cols = slice(t * LANES, (t + 1) * LANES)
            firsts = [fl_ref[block[k], flip, rows, cols] for k in range(blocks)]
            lasts = [fl_ref[block[k], 1 - flip, rows, cols] for k in range(blocks - 1)]
            before = forward(coef, firsts[:-1], lasts)
            across = table[blocks, 0] * (other[rows, cols] + table[blocks, 1] * mine[rows, cols])
            outer, inner = backward(coef, firsts, before, across)
            for k in range(blocks):
                uv_ref[block[k], flip, rows, cols] = outer[k]
                uv_ref[block[k], 1 - flip, rows, cols] = inner[k]
        return carry

    lax.fori_loop(0, lines // ROWS, group, 0)


def second_half(half, fl, mine, other, slabs):
    parts, _, lines, share = fl.shape
    vmem = pl.BlockSpec(memory_space=pltpu.VMEM)
    return pl.pallas_call(
        functools.partial(second_kernel, slabs),
        in_specs=[pl.BlockSpec(memory_space=pltpu.SMEM), vmem, vmem, vmem],
        out_specs=[vmem, vmem],
        out_shape=[
            jax.ShapeDtypeStruct((parts, 2, lines - ROWS, share), jnp.float32),
            jax.ShapeDtypeStruct((2 * parts, ROWS, LANES), jnp.float32),
        ],
        scratch_shapes=[pltpu.VMEM((parts + 1, len(KINDS), ROWS, LANES), jnp.float32)],
        compiler_params=pltpu.CompilerParams(vmem_limit_bytes=VMEM_LIMIT),
        cost_estimate=pl.CostEstimate(flops=10 * fl.size, bytes_accessed=9 * fl.size, transcendentals=0),
        name="reduced_out",
    )(half, fl, mine, other)


def well_cells_kernel(w_ref, cat_ref, place_row, place_column, out_ref, pick):
    planes, lines, span = w_ref.shape
    wells = place_row.shape[1]

    @pl.when(pl.program_id(0) == 0)
    def _():
        column = lax.broadcasted_iota(jnp.int32, (span, wells), 0)
        pick[...] = (column == place_row[...] % span).astype(jnp.float32).astype(jnp.bfloat16)

    line = lax.broadcasted_iota(jnp.int32, (lines, wells), 0)
    own_line = line == place_row[...] // span
    kinds = cat_ref[...].astype(jnp.float32).reshape(planes * lines, span).astype(jnp.bfloat16)
    sums = [jnp.zeros((planes * lines, wells), jnp.float32)] * 2
    for part in split_bf16(w_ref[...].reshape(planes * lines, span), 3):
        sums[0] = sums[0] + jnp.dot(part, pick[...], preferred_element_type=jnp.float32)
    sums[1] = jnp.dot(kinds, pick[...], preferred_element_type=jnp.float32)
    for n in range(2):
        for k in range(planes):
            cells = jnp.where(own_line, sums[n][k * lines : (k + 1) * lines], 0.0)
            out_ref[n, k : k + 1, :] = jnp.sum(cells, axis=0, keepdims=True)


def well_cells(w, cat, place_row):
    slabs, lines, span = w.shape
    wells = place_row.shape[1]
    planes = 8
    block = pl.BlockSpec((planes, lines, span), lambda i: (i, 0, 0))
    row = pl.BlockSpec((1, wells), lambda i: (0, 0))
    column = pl.BlockSpec((wells, 1), lambda i: (0, 0))
    return pl.pallas_call(
        well_cells_kernel,
        grid=(slabs // planes,),
        in_specs=[block, block, row, column],
        out_specs=pl.BlockSpec((2, planes, wells), lambda i: (0, i, 0)),
        out_shape=jax.ShapeDtypeStruct((2, slabs, wells), jnp.float32),
        scratch_shapes=[pltpu.VMEM((span, wells), jnp.bfloat16)],
        compiler_params=pltpu.CompilerParams(vmem_limit_bytes=VMEM_LIMIT),
        cost_estimate=pl.CostEstimate(
            flops=8 * w.size * wells, bytes_accessed=8 * w.size, transcendentals=0
        ),
        name="well_cells",
    )(w, cat, place_row, place_row.reshape(wells, 1))


def wells_kernel(
    table, where_am_i, info, cells, inverse, well, holders, out_ref, leaving, keep, force, rate, down, rise, uv
):
    blocks, _, slabs, wells = cells.shape
    speed, inlet, reach = well[0:1], well[1:2], well[2:3]
    entries = [table[k] for k in range(table.shape[0])]
    level = lax.broadcasted_iota(jnp.int32, (slabs, wells), 0).astype(jnp.float32)
    for j in range(blocks):
        rock = cells[j, 0]
        cond = select_tree(cells[j, 1].astype(jnp.int32), entries)
        here = jnp.where(level + float(j * slabs) < reach, speed * cond / (1.0 + cond), 0.0)
        rows = slice(j * slabs, (j + 1) * slabs)
        rate[rows] = here
        keep[rows] = 1.0 - here
        force[rows] = here * rock

    chunks = blocks * slabs // ROWS

    def descend(i, value):
        rows = pl.ds(pl.multiple_of(i * ROWS, ROWS), ROWS)
        a, b = keep[rows], force[rows]
        seen = []
        for r in range(ROWS):
            seen.append(value)
            value = a[r : r + 1] * value + b[r : r + 1]
        down[rows] = jnp.concatenate(seen, axis=0)
        return value

    def ascend(i, value):
        rows = pl.ds(pl.multiple_of((chunks - 1 - i) * ROWS, ROWS), ROWS)
        a, b = keep[rows], force[rows]
        seen = []
        for r in reversed(range(ROWS)):
            seen.append(value)
            value = a[r : r + 1] * value + b[r : r + 1]
        rise[rows] = jnp.concatenate(seen[::-1], axis=0)
        return value

    bottom = lax.fori_loop(0, chunks, descend, inlet)
    top = lax.fori_loop(0, chunks, ascend, bottom)
    mine = holders[...] == lax.broadcasted_iota(jnp.int32, (holders.shape[0], wells), 1)
    leaving[...] = jnp.sum(jnp.where(mine, top, 0.0), axis=1, keepdims=True)

    for j in range(blocks):
        rows = slice(j * slabs, (j + 1) * slabs)
        taken = rate[rows] * (2.0 * cells[j, 0] - down[rows] - rise[rows])
        rise[rows] = -storage_volume * taken
    firsts, lasts = [], []
    for j in range(blocks):
        both = jnp.dot(
            info[j, :, :slabs],
            rise[j * slabs : (j + 1) * slabs],
            precision=HIGHEST,
            preferred_element_type=jnp.float32,
        )
        firsts.append(both[0:1])
        lasts.append(both[1:2])
    scalars = [block_scalars(info[j], slabs, (1, wells)) for j in range(blocks)]
    zero = jnp.zeros((1, wells), jnp.float32)
    couple = [zero]
    for j in range(1, blocks):
        couple.append(
            coupling(scalars[j][1], scalars[j - 1][0][1, 1], scalars[j][0][0, 0], slabs)
        )
    couple.append(zero)
    coefs, _ = chain([corner for corner, _ in scalars], couple)
    coef = lambda kind, j: coefs[j][kind]
    above, below = backward(coef, firsts, forward(coef, firsts, lasts), zero)
    for j in range(blocks):
        uv[j, 0:1] = above[j]
        uv[j, 1:2] = below[j]
    d = where_am_i[0]
    own = rise[pl.ds(pl.multiple_of(d * slabs, slabs), slabs)]
    row = lax.broadcasted_iota(jnp.int32, (slabs, wells), 0)
    pair = uv[d]
    own = own + jnp.where(row == 0, pair[0:1], 0.0) + jnp.where(row == slabs - 1, pair[1:2], 0.0)
    out_ref[...] = jnp.dot(inverse[...], own, precision=HIGHEST, preferred_element_type=jnp.float32)


def wells_solve(table, depth_index, info, cells, inverse, well, holders):
    blocks, _, slabs, wells = cells.shape
    smem = pl.BlockSpec(memory_space=pltpu.SMEM)
    vmem = pl.BlockSpec(memory_space=pltpu.VMEM)
    column = pltpu.VMEM((blocks * slabs, wells), jnp.float32)
    return pl.pallas_call(
        wells_kernel,
        in_specs=[smem, smem] + [vmem] * 5,
        out_specs=[vmem, vmem],
        out_shape=[
            jax.ShapeDtypeStruct((slabs, wells), jnp.float32),
            jax.ShapeDtypeStruct((holders.shape[0], 1), jnp.float32),
        ],
        scratch_shapes=[column] * 5 + [pltpu.VMEM((blocks, ROWS, wells), jnp.float32)],
        compiler_params=pltpu.CompilerParams(vmem_limit_bytes=VMEM_LIMIT),
        cost_estimate=pl.CostEstimate(flops=10**7, bytes_accessed=8 * cells.size, transcendentals=0),
        name="wells",
    )(table, depth_index.reshape(1), info, cells, inverse, well, holders)


def solve_kernel(right, uv, inverse, place_row, place_column, solved_wells, out, factor, pick):
    slabs, rows, span = right.shape
    wells = place_row.shape[1]
    step = pl.program_id(0)
    size = slabs * rows

    @pl.when(step == 0)
    def _():
        spread = (
            lax.broadcasted_iota(jnp.int32, (size, slabs), 0) // rows
            == lax.broadcasted_iota(jnp.int32, (size, slabs), 1)
        ).astype(jnp.float32).astype(jnp.bfloat16)
        spread_t = (
            lax.broadcasted_iota(jnp.int32, (slabs, size), 1) // rows
            == lax.broadcasted_iota(jnp.int32, (slabs, size), 0)
        ).astype(jnp.float32).astype(jnp.bfloat16)
        same = (
            lax.broadcasted_iota(jnp.int32, (size, size), 0) % rows
            == lax.broadcasted_iota(jnp.int32, (size, size), 1) % rows
        )
        for n, part in enumerate(split_bf16(inverse[...], 2)):
            tall = jnp.dot(spread, part, preferred_element_type=jnp.float32).astype(jnp.bfloat16)
            wide = jnp.dot(tall, spread_t, preferred_element_type=jnp.float32)
            wide = jnp.where(same, wide, 0.0).astype(jnp.bfloat16)
            if n == 0:
                factor[:, :size] = wide
                factor[:, size : 2 * size] = wide
            else:
                factor[:, 2 * size : 3 * size] = wide
        column = lax.broadcasted_iota(jnp.int32, (wells, span), 1)
        chosen = (column == place_column[...] % span).astype(jnp.float32).astype(jnp.bfloat16)
        pick[:wells] = chosen
        pick[wells:] = chosen

    line = lax.broadcasted_iota(jnp.int32, (slabs, rows, wells), 1) + step * rows
    at_wells = jnp.where(line == (place_row[...] // span)[None], solved_wells[...][:, None, :], 0.0)
    at_wells = jnp.concatenate(split_bf16(at_wells.reshape(size, wells), 2), axis=1)
    factor[:, 3 * size :] = at_wells
    shares = uv.shape[0]
    above = jnp.concatenate([uv[d, 0] for d in range(shares)], axis=1)
    below = jnp.concatenate([uv[d, 1] for d in range(shares)], axis=1)
    tile = min(span, 256)
    for t in range(span // tile):
        cols = slice(t * tile, (t + 1) * tile)
        value = jnp.concatenate(
            [
                right[0:1, :, cols] + above[None, :, cols],
                right[1 : slabs - 1, :, cols],
                right[slabs - 1 :, :, cols] + below[None, :, cols],
            ],
            axis=0,
        ).reshape(size, tile)
        upper, lower = split_bf16(value, 2)
        result = jnp.dot(
            factor[...],
            jnp.concatenate([upper, lower, upper, pick[:, cols]], axis=0),
            preferred_element_type=jnp.float32,
        )
        out[:, :, cols] = result.reshape(slabs, rows, tile)


def solve(right, uv, inverse, place_row, solved_wells):
    slabs, lines, span = right.shape
    wells = place_row.shape[1]
    block = pl.BlockSpec((slabs, ROWS, span), lambda g: (0, g, 0))
    shares, _, _, share = uv.shape
    whole = lambda *shape: pl.BlockSpec(shape, lambda g: (0,) * len(shape))
    size = slabs * ROWS
    return pl.pallas_call(
        solve_kernel,
        grid=(lines // ROWS,),
        in_specs=[
            block,
            pl.BlockSpec((shares, 2, ROWS, share), lambda g: (0, 0, g, 0)),
            whole(slabs, slabs),
            whole(1, wells),
            whole(wells, 1),
            whole(slabs, wells),
        ],
        out_specs=block,
        out_shape=jax.ShapeDtypeStruct(right.shape, jnp.float32),
        scratch_shapes=[
            pltpu.VMEM((size, 3 * size + 2 * wells), jnp.bfloat16),
            pltpu.VMEM((2 * wells, span), jnp.bfloat16),
        ],
        compiler_params=pltpu.CompilerParams(vmem_limit_bytes=VMEM_LIMIT),
        cost_estimate=pl.CostEstimate(
            flops=8 * size * right.size, bytes_accessed=8 * right.size, transcendentals=0
        ),
        name="depth_solve",
    )(right, uv, inverse, place_row, place_row.reshape(wells, 1), solved_wells)


def body(
    warmth_before,
    stratum_category,
    conductance_catalogue,
    pivot_matrix_reciprocal,
    linkage_factor,
    well_position_inside,
    well_holder_sequence,
    well_reach,
    entering_warmth,
    well_transfer_speed,
):
    slabs, lines, span = warmth_before.shape
    depth_index = lax.axis_index("depth")
    depth_count = lax.axis_size("depth")
    wells = well_position_inside.shape[0]
    owned = wells // depth_count
    table = conductance_catalogue

    def gathered(value):
        copies = jnp.broadcast_to(value[None], (depth_count,) + value.shape)
        return lax.all_to_all(copies, "depth", split_axis=0, concat_axis=0, tiled=True)

    parts = depth_count // 2
    halves = [list(range(h * parts, (h + 1) * parts)) for h in range(2)]
    half = (depth_index // parts).astype(jnp.int32).reshape(1)
    ends = jnp.stack([pivot_matrix_reciprocal[0], pivot_matrix_reciprocal[-1]])
    info = jnp.concatenate([ends, jnp.broadcast_to(linkage_factor[:, None], (2, 1))], axis=1)
    info = jnp.pad(info, ((0, ROWS - 2), (0, span // parts - info.shape[1])))

    first, last = edge_rows(warmth_before, stratum_category, table)
    count = lax.axis_size("strip")
    up = [(i, i + 1) for i in range(count - 1)]
    down = [(j, i) for i, j in up]
    before = lax.ppermute(last, "strip", up)
    after = lax.ppermute(first, "strip", down)

    right, fl = stencil(
        warmth_before, stratum_category, table, ends, info, before, after, parts
    )
    exchange = functools.partial(
        lax.all_to_all,
        axis_name="depth",
        split_axis=0,
        concat_axis=0,
        tiled=True,
        axis_index_groups=halves,
    )
    fl_all = exchange(fl)

    place_row = well_position_inside.reshape(1, wells)
    cells = well_cells(warmth_before, stratum_category, place_row)

    mine = first_half(half, fl_all, slabs)
    other = lax.ppermute(
        mine, "depth", [(i, (i + parts) % depth_count) for i in range(depth_count)]
    )
    cells = gathered(cells)
    uv, info_all = second_half(half, fl_all, mine, other, slabs)
    uv_own = exchange(uv)

    well = jnp.stack([well_transfer_speed, entering_warmth, well_reach.astype(jnp.float32)])
    well = jnp.pad(well, ((0, ROWS - 3), (0, 0)))
    holders = lax.dynamic_slice_in_dim(well_holder_sequence, depth_index * owned, owned)
    solved_wells, leaving = wells_solve(
        table, depth_index, info_all, cells, pivot_matrix_reciprocal, well, holders.reshape(owned, 1)
    )
    solved = solve(right, uv_own, pivot_matrix_reciprocal, place_row, solved_wells)
    return solved, leaving.reshape(owned)


def solution(mesh):
    in_specs = (
        P("depth", "strip", None),
        P("depth", "strip", None),
        P(),
        P("depth", None),
        P("depth"),
        P("strip"),
        P("strip"),
        P("strip"),
        P("strip"),
        P("strip"),
    )
    out_specs = (P("depth", "strip", None), P(("strip", "depth")))
    return jax.shard_map(body, mesh=mesh, in_specs=in_specs, out_specs=out_specs, check_vma=False)
```

```python
import functools

import jax
import jax.numpy as jnp
from jax import lax
from jax.experimental import pallas as pl
from jax.experimental.pallas import tpu as pltpu
from jax.sharding import PartitionSpec as P

backward_euler_advance = 0.2
storage_volume = 2.0
flux_scale = 0.5 * backward_euler_advance
LANES = 128
ROWS = 8
VMEM_LIMIT = 48 * 1024 * 1024
HIGHEST = lax.Precision.HIGHEST


def select_tree(category, entries):
    values = list(entries)
    bit = 1
    while len(values) > 1:
        odd = (category & bit) != 0
        values = [
            jnp.where(odd, values[k + 1], values[k]) if k + 1 < len(values) else values[k]
            for k in range(0, len(values), 2)
        ]
        bit *= 2
    return values[0]


def split_bf16(value, pieces):
    out = []
    for k in range(pieces):
        part = value.astype(jnp.bfloat16)
        out.append(part)
        if k + 1 < pieces:
            value = value - part.astype(jnp.float32)
    return out


def edge_kernel(table, w_first, cat_first, w_last, cat_last, first, last, kinds):
    planes, rows, span = w_first.shape
    entries = [flux_scale * table[k] for k in range(table.shape[0])]
    for w_ref, cat_ref, row, out in ((w_first, cat_first, 0, first), (w_last, cat_last, rows - 1, last)):
        for k in range(planes):
            kinds[k : k + 1, :] = cat_ref[k, row : row + 1, :]
        cond = select_tree(kinds[...], entries)
        for k in range(planes):
            out[k, 0:1, :] = w_ref[k, row : row + 1, :]
            out[k, 1:2, :] = cond[k : k + 1]


def edge_rows(w, cat, table):
    slabs, lines, span = w.shape
    planes = 8
    top = pl.BlockSpec((planes, ROWS, span), lambda i: (i, 0, 0))
    end = pl.BlockSpec((planes, ROWS, span), lambda i: (i, lines // ROWS - 1, 0))
    out = pl.BlockSpec((planes, 2, span), lambda i: (i, 0, 0))
    return pl.pallas_call(
        edge_kernel,
        grid=(slabs // planes,),
        in_specs=[pl.BlockSpec(memory_space=pltpu.SMEM), top, top, end, end],
        out_specs=[out, out],
        out_shape=[jax.ShapeDtypeStruct((slabs, 2, span), jnp.float32)] * 2,
        scratch_shapes=[pltpu.VMEM((planes, span), jnp.int32)],
        cost_estimate=pl.CostEstimate(flops=10**6, bytes_accessed=w.size, transcendentals=0),
        name="edge_rows",
    )(table, w, cat, w, cat)


def stencil_kernel(table, ends, info, w_ref, cat_ref, before, after, right_ref, fl_ref, acc, ws, cs, fs, pieces, shift):
    step = pl.program_id(0)
    planes, lines, span = w_ref.shape
    tiles = span // LANES
    groups = lines // ROWS
    entries = [flux_scale * table[k] for k in range(table.shape[0])]
    lane = lax.broadcasted_iota(jnp.int32, (lines, LANES), 1)
    top, end = ROWS, ROWS + lines

    @pl.when(step == 0)
    def _():
        acc[...] = jnp.zeros_like(acc)
        source = lax.broadcasted_iota(jnp.int32, shift.shape, 0) % (2 * LANES)
        target = lax.broadcasted_iota(jnp.int32, shift.shape, 1)
        shift[...] = (source == target + 1).astype(jnp.float32).astype(jnp.bfloat16)

    def keep_face(k, t, face):
        rows = pl.ds(pl.multiple_of(k * lines, lines), lines)
        for n, part in enumerate(split_bf16(face, 2)):
            pieces[n, rows, t * LANES : (t + 1) * LANES] = part

    def plane(k, carry):
        left_w = left_c = jnp.zeros((lines, LANES), jnp.float32)
        for t in range(tiles):
            cols = slice(t * LANES, (t + 1) * LANES)
            w = w_ref[k, :, cols]
            c = select_tree(cat_ref[k, :, cols], entries)
            for ref, value, which in ((ws, w, 0), (cs, c, 1)):
                ref[t, top:end] = value
                ref[t, top - 1 : top] = before[k, which : which + 1, cols]
                ref[t, end : end + 1] = after[k, which : which + 1, cols]
            roll_w, roll_c = pltpu.roll(w, 1, 1), pltpu.roll(c, 1, 1)
            west_w = jnp.where(lane == 0, left_w, roll_w)
            west_c = jnp.where(lane == 0, left_c, roll_c)
            left_w, left_c = roll_w, roll_c
            face = (c + west_c) * (w - west_w)
            keep_face(k, t, face)
            if t == tiles - 1:
                keep_face(k, tiles, pltpu.roll(-c * w, 1, 1))
            north = (c + cs[t, top - 1 : end - 1]) * (w - ws[t, top - 1 : end - 1])
            fs[t, top:end] = north
            fs[t, end : end + 1] = (cs[t, end : end + 1] + cs[t, end - 1 : end]) * (
                ws[t, end : end + 1] - ws[t, end - 1 : end]
            )
            base = w - face - north + fs[t, top + 1 : end + 1]
            right_ref[:, k, :, cols] = base.reshape(groups, ROWS, LANES)
        return carry

    lax.fori_loop(0, planes, plane, 0)

    for t in range(tiles):
        cols = slice(t * LANES, (t + 1) * LANES)
        both = slice(t * LANES, (t + 2) * LANES)
        east = jnp.dot(
            jnp.concatenate([pieces[0, :, both], pieces[1, :, both]], axis=1),
            shift[...],
            preferred_element_type=jnp.float32,
        )
        first, final = acc[0, :, cols], acc[1, :, cols]
        for k in range(planes):
            z = step * planes + k
            value = right_ref[:, k, :, cols].reshape(lines, LANES) + east[k * lines : (k + 1) * lines]
            right_ref[:, k, :, cols] = value.reshape(groups, ROWS, LANES)
            first = first + ends[0, z] * value
            final = final + ends[1, z] * value
        acc[0, :, cols] = first
        acc[1, :, cols] = final

    @pl.when(step == pl.num_programs(0) - 1)
    def _():
        share = fl_ref.shape[-1]
        for d in range(fl_ref.shape[0]):
            fl_ref[d, :, :lines] = acc[:, :, d * share : (d + 1) * share]
            for n in range(2):
                fl_ref[d, n, lines:] = info[...]


def stencil(w, cat, table, ends, info, before, after, parts):
    slabs, lines, span = w.shape
    planes, groups = 4, lines // ROWS
    block = pl.BlockSpec((planes, lines, span), lambda i: (i, 0, 0))
    halo = pl.BlockSpec((planes, 2, span), lambda i: (i, 0, 0))
    fl_shape = (parts, 2, lines + ROWS, span // parts)
    smem = pl.BlockSpec(memory_space=pltpu.SMEM)
    shifted = pltpu.VMEM((span // LANES, lines + 2 * ROWS, LANES), jnp.float32)
    return pl.pallas_call(
        stencil_kernel,
        grid=(slabs // planes,),
        in_specs=[smem, smem, pl.BlockSpec(info.shape, lambda i: (0, 0)), block, block, halo, halo],
        out_specs=[
            pl.BlockSpec((groups, planes, ROWS, span), lambda i: (0, i, 0, 0)),
            pl.BlockSpec(fl_shape, lambda i: (0, 0, 0, 0)),
        ],
        out_shape=[
            jax.ShapeDtypeStruct((groups, slabs, ROWS, span), jnp.float32),
            jax.ShapeDtypeStruct(fl_shape, jnp.float32),
        ],
        scratch_shapes=[
            pltpu.VMEM((2, lines, span), jnp.float32),
            shifted,
            shifted,
            shifted,
            pltpu.VMEM((2, planes * lines, span + LANES), jnp.bfloat16),
            pltpu.VMEM((4 * LANES, LANES), jnp.bfloat16),
        ],
        compiler_params=pltpu.CompilerParams(vmem_limit_bytes=VMEM_LIMIT),
        cost_estimate=pl.CostEstimate(flops=40 * w.size, bytes_accessed=12 * w.size, transcendentals=0),
        name="stencil",
    )(table, ends, info, w, cat, before, after)


CORNERS = ((0, 0), (0, 1), (1, 0), (1, 1))


def block_scalars(tile, slabs, shape, flipped=None):
    at = lambda row, lane: jnp.broadcast_to(tile[row : row + 1, lane : lane + 1], shape)
    corner = {(r, c): at(r, c * (slabs - 1)) for r, c in CORNERS}
    if flipped is not None:
        corner = {(r, c): jnp.where(flipped, corner[1 - r, 1 - c], corner[r, c]) for r, c in CORNERS}
    return corner, at(0, slabs)


def coupling(ratio, one, other, slabs):
    return ratio * (slabs / (slabs + 1.0)) / jnp.sqrt(one * other)


def chain(corners, couple, q=None):
    out = []
    q = jnp.zeros_like(couple[0])
    for k, corner in enumerate(corners):
        vf, vl = couple[k] * corner[0, 0], couple[k] * corner[1, 0]
        wf, wl = couple[k + 1] * corner[0, 1], couple[k + 1] * corner[1, 1]
        inverse = 1.0 / (1.0 - vf * q)
        out.append(
            dict(
                p_first=vl * q * inverse,
                p_before=vl * inverse,
                a_first=inverse,
                a_before=vf * inverse,
                a_after=wf * inverse,
                couple=couple[k],
                couple_after=couple[k + 1],
                q=q,
            )
        )
        q = wl + vl * q * wf * inverse
    return out, q


KINDS = ("p_first", "p_before", "a_first", "a_before", "a_after", "couple", "couple_after", "q")


def forward(coef, firsts, lasts):
    before = [jnp.zeros_like(firsts[0])]
    for j in range(len(firsts)):
        before.append(
            lasts[j] + coef("p_first", j) * firsts[j] + coef("p_before", j) * before[j]
        )
    return before


def backward(coef, firsts, before, after):
    blocks = len(firsts)
    above, below = [None] * blocks, [None] * blocks
    for j in reversed(range(blocks)):
        below[j] = coef("couple_after", j) * after
        here = (
            coef("a_first", j) * firsts[j]
            + coef("a_before", j) * before[j]
            + coef("a_after", j) * after
        )
        above[j] = coef("couple", j) * (before[j] + coef("q", j) * here)
        after = here
    return above, below


def half_chain(tiles, slabs, flipped, middle):
    shape = (ROWS, LANES)
    scalars = [block_scalars(tile, slabs, shape, flipped) for tile in tiles]
    couple = [jnp.zeros(shape, jnp.float32)]
    for k in range(1, len(tiles)):
        ratio = jnp.where(flipped, scalars[k - 1][1], scalars[k][1])
        couple.append(coupling(ratio, scalars[k - 1][0][1, 1], scalars[k][0][0, 0], slabs))
    couple.append(middle)
    return chain([corner for corner, _ in scalars], couple)


def first_kernel(slabs, half, fl_ref, out_ref, table):
    blocks, _, lines, share = fl_ref.shape
    lines = lines - ROWS
    flip = half[0]
    flipped = flip == 1
    block = [k + flip * (blocks - 1 - 2 * k) for k in range(blocks)]
    entries, _ = half_chain(
        [fl_ref[block[k], 0, lines:, :LANES] for k in range(blocks)],
        slabs,
        flipped,
        jnp.zeros((ROWS, LANES), jnp.float32),
    )
    for k, entry in enumerate(entries):
        for n, kind in enumerate(KINDS[:2]):
            table[k, n] = entry[kind]
    coef = lambda kind, k: table[k, KINDS.index(kind)]

    def group(g, carry):
        rows = pl.ds(pl.multiple_of(g * ROWS, ROWS), ROWS)
        for t in range(share // LANES):
            cols = slice(t * LANES, (t + 1) * LANES)
            before = forward(
                coef,
                [fl_ref[block[k], flip, rows, cols] for k in range(blocks)],
                [fl_ref[block[k], 1 - flip, rows, cols] for k in range(blocks)],
            )
            out_ref[rows, cols] = before[blocks]
        return carry

    lax.fori_loop(0, lines // ROWS, group, 0)
    out_ref[lines:, :] = jnp.zeros((out_ref.shape[0] - lines, share), jnp.float32)
    for j in range(blocks):
        out_ref[lines + 2 * j : lines + 2 * j + 2, :] = fl_ref[j, 0, lines : lines + 2, :]


def first_half(half, fl, slabs):
    parts, _, lines, share = fl.shape
    vmem = pl.BlockSpec(memory_space=pltpu.VMEM)
    rows = lines - ROWS + -(-2 * parts // ROWS) * ROWS
    return pl.pallas_call(
        functools.partial(first_kernel, slabs),
        in_specs=[pl.BlockSpec(memory_space=pltpu.SMEM), vmem],
        out_specs=vmem,
        out_shape=jax.ShapeDtypeStruct((rows, share), jnp.float32),
        scratch_shapes=[pltpu.VMEM((parts, 2, ROWS, LANES), jnp.float32)],
        compiler_params=pltpu.CompilerParams(vmem_limit_bytes=VMEM_LIMIT),
        cost_estimate=pl.CostEstimate(flops=4 * fl.size, bytes_accessed=5 * fl.size, transcendentals=0),
        name="reduced_in",
    )(half, fl)


def second_kernel(slabs, half, fl_ref, mine, other, uv_ref, info_ref, table):
    blocks, _, lines, share = fl_ref.shape
    lines = lines - ROWS
    flip = half[0]
    flipped = flip == 1
    block = [k + flip * (blocks - 1 - 2 * k) for k in range(blocks)]
    for j in range(blocks):
        info_ref[flip * blocks + j] = fl_ref[j, 0, lines:, :LANES]
        info_ref[(1 - flip) * blocks + j] = jnp.zeros((ROWS, LANES), jnp.float32)
        info_ref[(1 - flip) * blocks + j, 0:2] = other[lines + 2 * j : lines + 2 * j + 2, :LANES]
    shape = (ROWS, LANES)
    above, above_ratio = block_scalars(info_ref[blocks - 1], slabs, shape)
    below, below_ratio = block_scalars(info_ref[blocks], slabs, shape)
    middle = coupling(below_ratio, above[1, 1], below[0, 0], slabs)
    tiles = lambda flip: [
        info_ref[flip * blocks + k + flip * (blocks - 1 - 2 * k)] for k in range(blocks)
    ]
    entries, q_own = half_chain(tiles(flip), slabs, flipped, middle)
    _, q_other = half_chain(tiles(1 - flip), slabs, jnp.logical_not(flipped), middle)
    for k, entry in enumerate(entries):
        for n, kind in enumerate(KINDS):
            table[k, n] = entry[kind]
    table[blocks, 0] = 1.0 / (1.0 - q_own * q_other)
    table[blocks, 1] = q_other
    coef = lambda kind, k: table[k, KINDS.index(kind)]

    def group(g, carry):
        rows = pl.ds(pl.multiple_of(g * ROWS, ROWS), ROWS)
        for t in range(share // LANES):
            cols = slice(t * LANES, (t + 1) * LANES)
            firsts = [fl_ref[block[k], flip, rows, cols] for k in range(blocks)]
            lasts = [fl_ref[block[k], 1 - flip, rows, cols] for k in range(blocks - 1)]
            before = forward(coef, firsts[:-1], lasts)
            across = table[blocks, 0] * (other[rows, cols] + table[blocks, 1] * mine[rows, cols])
            outer, inner = backward(coef, firsts, before, across)
            for k in range(blocks):
                uv_ref[block[k], flip, rows, cols] = outer[k]
                uv_ref[block[k], 1 - flip, rows, cols] = inner[k]
        return carry

    lax.fori_loop(0, lines // ROWS, group, 0)


def second_half(half, fl, mine, other, slabs):
    parts, _, lines, share = fl.shape
    vmem = pl.BlockSpec(memory_space=pltpu.VMEM)
    return pl.pallas_call(
        functools.partial(second_kernel, slabs),
        in_specs=[pl.BlockSpec(memory_space=pltpu.SMEM), vmem, vmem, vmem],
        out_specs=[vmem, vmem],
        out_shape=[
            jax.ShapeDtypeStruct((parts, 2, lines - ROWS, share), jnp.float32),
            jax.ShapeDtypeStruct((2 * parts, ROWS, LANES), jnp.float32),
        ],
        scratch_shapes=[pltpu.VMEM((parts + 1, len(KINDS), ROWS, LANES), jnp.float32)],
        compiler_params=pltpu.CompilerParams(vmem_limit_bytes=VMEM_LIMIT),
        cost_estimate=pl.CostEstimate(flops=10 * fl.size, bytes_accessed=9 * fl.size, transcendentals=0),
        name="reduced_out",
    )(half, fl, mine, other)


def well_cells_kernel(w_ref, cat_ref, place_row, place_column, out_ref, pick):
    planes, lines, span = w_ref.shape
    wells = place_row.shape[1]

    @pl.when(pl.program_id(0) == 0)
    def _():
        column = lax.broadcasted_iota(jnp.int32, (span, wells), 0)
        pick[...] = (column == place_row[...] % span).astype(jnp.float32).astype(jnp.bfloat16)

    line = lax.broadcasted_iota(jnp.int32, (lines, wells), 0)
    own_line = line == place_row[...] // span
    kinds = cat_ref[...].astype(jnp.float32).reshape(planes * lines, span).astype(jnp.bfloat16)
    sums = [jnp.zeros((planes * lines, wells), jnp.float32)] * 2
    for part in split_bf16(w_ref[...].reshape(planes * lines, span), 3):
        sums[0] = sums[0] + jnp.dot(part, pick[...], preferred_element_type=jnp.float32)
    sums[1] = jnp.dot(kinds, pick[...], preferred_element_type=jnp.float32)
    for n in range(2):
        for k in range(planes):
            cells = jnp.where(own_line, sums[n][k * lines : (k + 1) * lines], 0.0)
            out_ref[n, k : k + 1, :] = jnp.sum(cells, axis=0, keepdims=True)


def well_cells(w, cat, place_row):
    slabs, lines, span = w.shape
    wells = place_row.shape[1]
    planes = 8
    block = pl.BlockSpec((planes, lines, span), lambda i: (i, 0, 0))
    row = pl.BlockSpec((1, wells), lambda i: (0, 0))
    column = pl.BlockSpec((wells, 1), lambda i: (0, 0))
    return pl.pallas_call(
        well_cells_kernel,
        grid=(slabs // planes,),
        in_specs=[block, block, row, column],
        out_specs=pl.BlockSpec((2, planes, wells), lambda i: (0, i, 0)),
        out_shape=jax.ShapeDtypeStruct((2, slabs, wells), jnp.float32),
        scratch_shapes=[pltpu.VMEM((span, wells), jnp.bfloat16)],
        compiler_params=pltpu.CompilerParams(vmem_limit_bytes=VMEM_LIMIT),
        cost_estimate=pl.CostEstimate(
            flops=8 * w.size * wells, bytes_accessed=8 * w.size, transcendentals=0
        ),
        name="well_cells",
    )(w, cat, place_row, place_row.reshape(wells, 1))


def wells_kernel(
    table, where_am_i, info, cells, inverse, well, holders, out_ref, leaving, keep, force, rate, down, rise, uv
):
    blocks, _, slabs, wells = cells.shape
    speed, inlet, reach = well[0:1], well[1:2], well[2:3]
    entries = [table[k] for k in range(table.shape[0])]
    level = lax.broadcasted_iota(jnp.int32, (slabs, wells), 0).astype(jnp.float32)
    for j in range(blocks):
        rock = cells[j, 0]
        cond = select_tree(cells[j, 1].astype(jnp.int32), entries)
        here = jnp.where(level + float(j * slabs) < reach, speed * cond / (1.0 + cond), 0.0)
        rows = slice(j * slabs, (j + 1) * slabs)
        rate[rows] = here
        keep[rows] = 1.0 - here
        force[rows] = here * rock

    chunks = blocks * slabs // ROWS

    def descend(i, value):
        rows = pl.ds(pl.multiple_of(i * ROWS, ROWS), ROWS)
        a, b = keep[rows], force[rows]
        seen = []
        for r in range(ROWS):
            seen.append(value)
            value = a[r : r + 1] * value + b[r : r + 1]
        down[rows] = jnp.concatenate(seen, axis=0)
        return value

    def ascend(i, value):
        rows = pl.ds(pl.multiple_of((chunks - 1 - i) * ROWS, ROWS), ROWS)
        a, b = keep[rows], force[rows]
        seen = []
        for r in reversed(range(ROWS)):
            seen.append(value)
            value = a[r : r + 1] * value + b[r : r + 1]
        rise[rows] = jnp.concatenate(seen[::-1], axis=0)
        return value

    bottom = lax.fori_loop(0, chunks, descend, inlet)
    top = lax.fori_loop(0, chunks, ascend, bottom)
    own_wells = holders.shape[1]
    held = holders[...] == lax.broadcasted_iota(jnp.int32, (wells, own_wells), 0)
    leaving[...] = jnp.dot(
        jnp.broadcast_to(top, (ROWS, wells)),
        held.astype(jnp.float32),
        precision=HIGHEST,
        preferred_element_type=jnp.float32,
    )[0:1]

    for j in range(blocks):
        rows = slice(j * slabs, (j + 1) * slabs)
        taken = rate[rows] * (2.0 * cells[j, 0] - down[rows] - rise[rows])
        rise[rows] = -storage_volume * taken
    firsts, lasts = [], []
    for j in range(blocks):
        both = jnp.dot(
            info[j, :, :slabs],
            rise[j * slabs : (j + 1) * slabs],
            precision=HIGHEST,
            preferred_element_type=jnp.float32,
        )
        firsts.append(both[0:1])
        lasts.append(both[1:2])
    scalars = [block_scalars(info[j], slabs, (1, wells)) for j in range(blocks)]
    zero = jnp.zeros((1, wells), jnp.float32)
    couple = [zero]
    for j in range(1, blocks):
        couple.append(
            coupling(scalars[j][1], scalars[j - 1][0][1, 1], scalars[j][0][0, 0], slabs)
        )
    couple.append(zero)
    coefs, _ = chain([corner for corner, _ in scalars], couple)
    coef = lambda kind, j: coefs[j][kind]
    above, below = backward(coef, firsts, forward(coef, firsts, lasts), zero)
    for j in range(blocks):
        uv[j, 0:1] = above[j]
        uv[j, 1:2] = below[j]
    d = where_am_i[0]
    own = rise[pl.ds(pl.multiple_of(d * slabs, slabs), slabs)]
    row = lax.broadcasted_iota(jnp.int32, (slabs, wells), 0)
    pair = uv[d]
    own = own + jnp.where(row == 0, pair[0:1], 0.0) + jnp.where(row == slabs - 1, pair[1:2], 0.0)
    out_ref[...] = jnp.dot(inverse[...], own, precision=HIGHEST, preferred_element_type=jnp.float32)


def wells_solve(table, depth_index, info, cells, inverse, well, holders):
    blocks, _, slabs, wells = cells.shape
    smem = pl.BlockSpec(memory_space=pltpu.SMEM)
    vmem = pl.BlockSpec(memory_space=pltpu.VMEM)
    column = pltpu.VMEM((blocks * slabs, wells), jnp.float32)
    return pl.pallas_call(
        wells_kernel,
        in_specs=[smem, smem] + [vmem] * 5,
        out_specs=[vmem, vmem],
        out_shape=[
            jax.ShapeDtypeStruct((slabs, wells), jnp.float32),
            jax.ShapeDtypeStruct((1, holders.shape[1]), jnp.float32),
        ],
        scratch_shapes=[column] * 5 + [pltpu.VMEM((blocks, ROWS, wells), jnp.float32)],
        compiler_params=pltpu.CompilerParams(vmem_limit_bytes=VMEM_LIMIT),
        cost_estimate=pl.CostEstimate(flops=10**7, bytes_accessed=8 * cells.size, transcendentals=0),
        name="wells",
    )(table, depth_index.reshape(1), info, cells, inverse, well, holders)


def solve_kernel(right, uv, inverse, place_row, place_column, solved_wells, out, factor, pick):
    together, slabs, rows, span = right.shape
    wells = place_row.shape[1]
    step = pl.program_id(0)
    size = slabs * rows

    @pl.when(step == 0)
    def _():
        spread = (
            lax.broadcasted_iota(jnp.int32, (size, slabs), 0) // rows
            == lax.broadcasted_iota(jnp.int32, (size, slabs), 1)
        ).astype(jnp.float32).astype(jnp.bfloat16)
        spread_t = (
            lax.broadcasted_iota(jnp.int32, (slabs, size), 1) // rows
            == lax.broadcasted_iota(jnp.int32, (slabs, size), 0)
        ).astype(jnp.float32).astype(jnp.bfloat16)
        same = (
            lax.broadcasted_iota(jnp.int32, (size, size), 0) % rows
            == lax.broadcasted_iota(jnp.int32, (size, size), 1) % rows
        )
        for n, part in enumerate(split_bf16(inverse[...], 2)):
            tall = jnp.dot(spread, part, preferred_element_type=jnp.float32).astype(jnp.bfloat16)
            wide = jnp.dot(tall, spread_t, preferred_element_type=jnp.float32)
            wide = jnp.where(same, wide, 0.0).astype(jnp.bfloat16)
            if n == 0:
                factor[:, :size] = wide
                factor[:, size : 2 * size] = wide
            else:
                factor[:, 2 * size : 3 * size] = wide
        column = lax.broadcasted_iota(jnp.int32, (wells, span), 1)
        chosen = (column == place_column[...] % span).astype(jnp.float32).astype(jnp.bfloat16)
        pick[:wells] = chosen
        pick[wells:] = chosen

    tile = min(span, 256)
    for n in range(together):
        line = lax.broadcasted_iota(jnp.int32, (slabs, rows, wells), 1) + (step * together + n) * rows
        at_wells = jnp.where(line == (place_row[...] // span)[None], solved_wells[...][:, None, :], 0.0)
        at_wells = jnp.concatenate(split_bf16(at_wells.reshape(size, wells), 2), axis=1)
        factor[:, 3 * size :] = at_wells
        lines = slice(n * rows, (n + 1) * rows)
        above = jnp.concatenate([uv[d, 0, lines] for d in range(uv.shape[0])], axis=1)
        below = jnp.concatenate([uv[d, 1, lines] for d in range(uv.shape[0])], axis=1)
        for t in range(span // tile):
            cols = slice(t * tile, (t + 1) * tile)
            value = jnp.concatenate(
                [
                    right[n, 0:1, :, cols] + above[None, :, cols],
                    right[n, 1 : slabs - 1, :, cols],
                    right[n, slabs - 1 :, :, cols] + below[None, :, cols],
                ],
                axis=0,
            ).reshape(size, tile)
            upper, lower = split_bf16(value, 2)
            result = jnp.dot(
                factor[...],
                jnp.concatenate([upper, lower, upper, pick[:, cols]], axis=0),
                preferred_element_type=jnp.float32,
            )
            out[:, lines, cols] = result.reshape(slabs, rows, tile)


def solve(right, uv, inverse, place_row, solved_wells):
    groups, slabs, _, span = right.shape
    wells = place_row.shape[1]
    together = 2
    lines = together * ROWS
    shares, _, _, share = uv.shape
    whole = lambda *shape: pl.BlockSpec(shape, lambda g: (0,) * len(shape))
    size = slabs * ROWS
    return pl.pallas_call(
        solve_kernel,
        grid=(groups // together,),
        in_specs=[
            pl.BlockSpec((together, slabs, ROWS, span), lambda g: (g, 0, 0, 0)),
            pl.BlockSpec((shares, 2, lines, share), lambda g: (0, 0, g, 0)),
            whole(slabs, slabs),
            whole(1, wells),
            whole(wells, 1),
            whole(slabs, wells),
        ],
        out_specs=pl.BlockSpec((slabs, lines, span), lambda g: (0, g, 0)),
        out_shape=jax.ShapeDtypeStruct((slabs, groups * ROWS, span), jnp.float32),
        scratch_shapes=[
            pltpu.VMEM((size, 3 * size + 2 * wells), jnp.bfloat16),
            pltpu.VMEM((2 * wells, span), jnp.bfloat16),
        ],
        compiler_params=pltpu.CompilerParams(vmem_limit_bytes=VMEM_LIMIT),
        cost_estimate=pl.CostEstimate(
            flops=8 * size * right.size, bytes_accessed=8 * right.size, transcendentals=0
        ),
        name="depth_solve",
    )(right, uv, inverse, place_row, place_row.reshape(wells, 1), solved_wells)


def body(
    warmth_before,
    stratum_category,
    conductance_catalogue,
    pivot_matrix_reciprocal,
    linkage_factor,
    well_position_inside,
    well_holder_sequence,
    well_reach,
    entering_warmth,
    well_transfer_speed,
):
    slabs, lines, span = warmth_before.shape
    depth_index = lax.axis_index("depth")
    depth_count = lax.axis_size("depth")
    wells = well_position_inside.shape[0]
    owned = wells // depth_count
    table = conductance_catalogue

    def gathered(value):
        copies = jnp.broadcast_to(value[None], (depth_count,) + value.shape)
        return lax.all_to_all(copies, "depth", split_axis=0, concat_axis=0, tiled=True)

    parts = depth_count // 2
    halves = [list(range(h * parts, (h + 1) * parts)) for h in range(2)]
    half = (depth_index // parts).astype(jnp.int32).reshape(1)
    ends = jnp.stack([pivot_matrix_reciprocal[0], pivot_matrix_reciprocal[-1]])
    info = jnp.concatenate([ends, jnp.broadcast_to(linkage_factor[:, None], (2, 1))], axis=1)
    info = jnp.pad(info, ((0, ROWS - 2), (0, span // parts - info.shape[1])))

    first, last = edge_rows(warmth_before, stratum_category, table)
    count = lax.axis_size("strip")
    up = [(i, i + 1) for i in range(count - 1)]
    down = [(j, i) for i, j in up]
    before = lax.ppermute(last, "strip", up)
    after = lax.ppermute(first, "strip", down)

    right, fl = stencil(
        warmth_before, stratum_category, table, ends, info, before, after, parts
    )
    exchange = functools.partial(
        lax.all_to_all,
        axis_name="depth",
        split_axis=0,
        concat_axis=0,
        tiled=True,
        axis_index_groups=halves,
    )
    fl_all = exchange(fl)

    place_row = well_position_inside.reshape(1, wells)
    cells = well_cells(warmth_before, stratum_category, place_row)

    mine = first_half(half, fl_all, slabs)
    other = lax.ppermute(
        mine, "depth", [(i, (i + parts) % depth_count) for i in range(depth_count)]
    )
    uv, info_all = second_half(half, fl_all, mine, other, slabs)
    uv, cells = lax.optimization_barrier((uv, cells))
    uv_own = exchange(uv)
    cells = gathered(cells)

    well = jnp.stack([well_transfer_speed, entering_warmth, well_reach.astype(jnp.float32)])
    well = jnp.pad(well, ((0, ROWS - 3), (0, 0)))
    holders = lax.dynamic_slice_in_dim(well_holder_sequence, depth_index * owned, owned)
    solved_wells, leaving = wells_solve(
        table, depth_index, info_all, cells, pivot_matrix_reciprocal, well, holders.reshape(1, owned)
    )
    solved = solve(right, uv_own, pivot_matrix_reciprocal, place_row, solved_wells)
    return solved, leaving.reshape(owned)


def solution(mesh):
    in_specs = (
        P("depth", "strip", None),
        P("depth", "strip", None),
        P(),
        P("depth", None),
        P("depth"),
        P("strip"),
        P("strip"),
        P("strip"),
        P("strip"),
        P("strip"),
    )
    out_specs = (P("depth", "strip", None), P(("strip", "depth")))
    return jax.shard_map(body, mesh=mesh, in_specs=in_specs, out_specs=out_specs, check_vma=False)
```

```python
import functools

import jax
import jax.numpy as jnp
from jax import lax
from jax.experimental import pallas as pl
from jax.experimental.pallas import tpu as pltpu
from jax.sharding import PartitionSpec as P

backward_euler_advance = 0.2
storage_volume = 2.0
flux_scale = 0.5 * backward_euler_advance
LANES = 128
ROWS = 8
VMEM_LIMIT = 48 * 1024 * 1024
HIGHEST = lax.Precision.HIGHEST


def select_tree(category, entries):
    values = list(entries)
    bit = 1
    while len(values) > 1:
        odd = (category & bit) != 0
        values = [
            jnp.where(odd, values[k + 1], values[k]) if k + 1 < len(values) else values[k]
            for k in range(0, len(values), 2)
        ]
        bit *= 2
    return values[0]


def split_bf16(value, pieces):
    out = []
    for k in range(pieces):
        part = value.astype(jnp.bfloat16)
        out.append(part)
        if k + 1 < pieces:
            value = value - part.astype(jnp.float32)
    return out


def outset_kernel(table, w_ref, cat_ref, place, first, last, cells, pick, edge_kinds):
    planes, lines, span = w_ref.shape
    wells = place.shape[1]
    entries = [flux_scale * table[k] for k in range(table.shape[0])]

    @pl.when(pl.program_id(0) == 0)
    def _():
        column = lax.broadcasted_iota(jnp.int32, (span, wells), 0)
        pick[...] = (column == place[...] % span).astype(jnp.float32).astype(jnp.bfloat16)

    for n, (row, out) in enumerate(((0, first), (lines - 1, last))):
        for k in range(planes):
            edge_kinds[n, k : k + 1, :] = cat_ref[k, row : row + 1, :]
        cond = select_tree(edge_kinds[n], entries)
        for k in range(planes):
            out[k, 0:1, :] = w_ref[k, row : row + 1, :]
            out[k, 1:2, :] = cond[k : k + 1]

    dot = functools.partial(jnp.dot, preferred_element_type=jnp.float32)
    own_line = lax.broadcasted_iota(jnp.int32, (lines, wells), 0) == place[...] // span
    upper, lower = split_bf16(w_ref[...].reshape(planes * lines, span), 2)
    kinds = cat_ref[...].astype(jnp.float32).reshape(planes * lines, span).astype(jnp.bfloat16)
    sums = [dot(upper, pick[...]) + dot(lower, pick[...]), dot(kinds, pick[...])]
    for n in range(2):
        for k in range(planes):
            mine = jnp.where(own_line, sums[n][k * lines : (k + 1) * lines], 0.0)
            cells[n, k : k + 1, :] = jnp.sum(mine, axis=0, keepdims=True)


def outset(w, cat, table, place_row):
    slabs, lines, span = w.shape
    wells = place_row.shape[1]
    planes = 8
    block = pl.BlockSpec((planes, lines, span), lambda i: (i, 0, 0))
    edge = pl.BlockSpec((planes, 2, span), lambda i: (i, 0, 0))
    return pl.pallas_call(
        outset_kernel,
        grid=(slabs // planes,),
        in_specs=[
            pl.BlockSpec(memory_space=pltpu.SMEM),
            block,
            block,
            pl.BlockSpec((1, wells), lambda i: (0, 0)),
        ],
        out_specs=[edge, edge, pl.BlockSpec((2, planes, wells), lambda i: (0, i, 0))],
        out_shape=[jax.ShapeDtypeStruct((slabs, 2, span), jnp.float32)] * 2
        + [jax.ShapeDtypeStruct((2, slabs, wells), jnp.float32)],
        scratch_shapes=[
            pltpu.VMEM((span, wells), jnp.bfloat16),
            pltpu.VMEM((2, planes, span), jnp.int32),
        ],
        compiler_params=pltpu.CompilerParams(vmem_limit_bytes=VMEM_LIMIT),
        cost_estimate=pl.CostEstimate(
            flops=6 * w.size * wells, bytes_accessed=8 * w.size, transcendentals=0
        ),
        name="edges_and_cells",
    )(table, w, cat, place_row)


def stencil_kernel(table, ends, info, w_ref, cat_ref, before, after, right_ref, fl_ref, acc, ws, cs, fs, pieces, shift):
    step = pl.program_id(0)
    planes, lines, span = w_ref.shape
    tiles = span // LANES
    groups = lines // ROWS
    entries = [flux_scale * table[k] for k in range(table.shape[0])]
    lane = lax.broadcasted_iota(jnp.int32, (lines, LANES), 1)
    top, end = ROWS, ROWS + lines

    @pl.when(step == 0)
    def _():
        acc[...] = jnp.zeros_like(acc)
        source = lax.broadcasted_iota(jnp.int32, shift.shape, 0) % (2 * LANES)
        target = lax.broadcasted_iota(jnp.int32, shift.shape, 1)
        shift[...] = (source == target + 1).astype(jnp.float32).astype(jnp.bfloat16)

    def keep_face(k, t, face):
        rows = pl.ds(pl.multiple_of(k * lines, lines), lines)
        for n, part in enumerate(split_bf16(face, 2)):
            pieces[n, rows, t * LANES : (t + 1) * LANES] = part

    def plane(k, carry):
        left_w = left_c = jnp.zeros((lines, LANES), jnp.float32)
        for t in range(tiles):
            cols = slice(t * LANES, (t + 1) * LANES)
            w = w_ref[k, :, cols]
            c = select_tree(cat_ref[k, :, cols], entries)
            for ref, value, which in ((ws, w, 0), (cs, c, 1)):
                ref[t, top:end] = value
                ref[t, top - 1 : top] = before[k, which : which + 1, cols]
                ref[t, end : end + 1] = after[k, which : which + 1, cols]
            roll_w, roll_c = pltpu.roll(w, 1, 1), pltpu.roll(c, 1, 1)
            west_w = jnp.where(lane == 0, left_w, roll_w)
            west_c = jnp.where(lane == 0, left_c, roll_c)
            left_w, left_c = roll_w, roll_c
            face = (c + west_c) * (w - west_w)
            keep_face(k, t, face)
            if t == tiles - 1:
                keep_face(k, tiles, pltpu.roll(-c * w, 1, 1))
            north = (c + cs[t, top - 1 : end - 1]) * (w - ws[t, top - 1 : end - 1])
            fs[t, top:end] = north
            fs[t, end : end + 1] = (cs[t, end : end + 1] + cs[t, end - 1 : end]) * (
                ws[t, end : end + 1] - ws[t, end - 1 : end]
            )
            base = w - face - north + fs[t, top + 1 : end + 1]
            right_ref[:, k, :, cols] = base.reshape(groups, ROWS, LANES)
        return carry

    lax.fori_loop(0, planes, plane, 0)

    for t in range(tiles):
        cols = slice(t * LANES, (t + 1) * LANES)
        both = slice(t * LANES, (t + 2) * LANES)
        east = jnp.dot(
            jnp.concatenate([pieces[0, :, both], pieces[1, :, both]], axis=1),
            shift[...],
            preferred_element_type=jnp.float32,
        )
        first, final = acc[0, :, cols], acc[1, :, cols]
        for k in range(planes):
            z = step * planes + k
            value = right_ref[:, k, :, cols].reshape(lines, LANES) + east[k * lines : (k + 1) * lines]
            right_ref[:, k, :, cols] = value.reshape(groups, ROWS, LANES)
            first = first + ends[0, z] * value
            final = final + ends[1, z] * value
        acc[0, :, cols] = first
        acc[1, :, cols] = final

    @pl.when(step == pl.num_programs(0) - 1)
    def _():
        share = fl_ref.shape[-1]
        for d in range(fl_ref.shape[0]):
            fl_ref[d, :, :lines] = acc[:, :, d * share : (d + 1) * share]
            for n in range(2):
                fl_ref[d, n, lines:] = info[...]


def stencil(w, cat, table, ends, info, before, after, parts):
    slabs, lines, span = w.shape
    planes, groups = 4, lines // ROWS
    block = pl.BlockSpec((planes, lines, span), lambda i: (i, 0, 0))
    halo = pl.BlockSpec((planes, 2, span), lambda i: (i, 0, 0))
    fl_shape = (parts, 2, lines + ROWS, span // parts)
    smem = pl.BlockSpec(memory_space=pltpu.SMEM)
    shifted = pltpu.VMEM((span // LANES, lines + 2 * ROWS, LANES), jnp.float32)
    return pl.pallas_call(
        stencil_kernel,
        grid=(slabs // planes,),
        in_specs=[smem, smem, pl.BlockSpec(info.shape, lambda i: (0, 0)), block, block, halo, halo],
        out_specs=[
            pl.BlockSpec((groups, planes, ROWS, span), lambda i: (0, i, 0, 0)),
            pl.BlockSpec(fl_shape, lambda i: (0, 0, 0, 0)),
        ],
        out_shape=[
            jax.ShapeDtypeStruct((groups, slabs, ROWS, span), jnp.float32),
            jax.ShapeDtypeStruct(fl_shape, jnp.float32),
        ],
        scratch_shapes=[
            pltpu.VMEM((2, lines, span), jnp.float32),
            shifted,
            shifted,
            shifted,
            pltpu.VMEM((2, planes * lines, span + LANES), jnp.bfloat16),
            pltpu.VMEM((4 * LANES, LANES), jnp.bfloat16),
        ],
        compiler_params=pltpu.CompilerParams(vmem_limit_bytes=VMEM_LIMIT),
        cost_estimate=pl.CostEstimate(flops=40 * w.size, bytes_accessed=12 * w.size, transcendentals=0),
        name="stencil",
    )(table, ends, info, w, cat, before, after)


CORNERS = ((0, 0), (0, 1), (1, 0), (1, 1))


def block_scalars(tile, slabs, shape, flipped=None):
    at = lambda row, lane: jnp.broadcast_to(tile[row : row + 1, lane : lane + 1], shape)
    corner = {(r, c): at(r, c * (slabs - 1)) for r, c in CORNERS}
    if flipped is not None:
        corner = {(r, c): jnp.where(flipped, corner[1 - r, 1 - c], corner[r, c]) for r, c in CORNERS}
    return corner, at(0, slabs)


def coupling(ratio, one, other, slabs):
    return ratio * (slabs / (slabs + 1.0)) / jnp.sqrt(one * other)


def chain(corners, couple, q=None):
    out = []
    q = jnp.zeros_like(couple[0])
    for k, corner in enumerate(corners):
        vf, vl = couple[k] * corner[0, 0], couple[k] * corner[1, 0]
        wf, wl = couple[k + 1] * corner[0, 1], couple[k + 1] * corner[1, 1]
        inverse = 1.0 / (1.0 - vf * q)
        out.append(
            dict(
                p_first=vl * q * inverse,
                p_before=vl * inverse,
                a_first=inverse,
                a_before=vf * inverse,
                a_after=wf * inverse,
                couple=couple[k],
                couple_after=couple[k + 1],
                q=q,
            )
        )
        q = wl + vl * q * wf * inverse
    return out, q


KINDS = ("p_first", "p_before", "a_first", "a_before", "a_after", "couple", "couple_after", "q")


def forward(coef, firsts, lasts):
    before = [jnp.zeros_like(firsts[0])]
    for j in range(len(firsts)):
        before.append(
            lasts[j] + coef("p_first", j) * firsts[j] + coef("p_before", j) * before[j]
        )
    return before


def backward(coef, firsts, before, after):
    blocks = len(firsts)
    above, below = [None] * blocks, [None] * blocks
    for j in reversed(range(blocks)):
        below[j] = coef("couple_after", j) * after
        here = (
            coef("a_first", j) * firsts[j]
            + coef("a_before", j) * before[j]
            + coef("a_after", j) * after
        )
        above[j] = coef("couple", j) * (before[j] + coef("q", j) * here)
        after = here
    return above, below


def half_chain(tiles, slabs, flipped, middle):
    shape = (ROWS, LANES)
    scalars = [block_scalars(tile, slabs, shape, flipped) for tile in tiles]
    couple = [jnp.zeros(shape, jnp.float32)]
    for k in range(1, len(tiles)):
        ratio = jnp.where(flipped, scalars[k - 1][1], scalars[k][1])
        couple.append(coupling(ratio, scalars[k - 1][0][1, 1], scalars[k][0][0, 0], slabs))
    couple.append(middle)
    return chain([corner for corner, _ in scalars], couple)


def first_kernel(slabs, half, fl_ref, out_ref, table):
    blocks, _, lines, share = fl_ref.shape
    lines = lines - ROWS
    flip = half[0]
    flipped = flip == 1
    block = [k + flip * (blocks - 1 - 2 * k) for k in range(blocks)]
    entries, _ = half_chain(
        [fl_ref[block[k], 0, lines:, :LANES] for k in range(blocks)],
        slabs,
        flipped,
        jnp.zeros((ROWS, LANES), jnp.float32),
    )
    for k, entry in enumerate(entries):
        for n, kind in enumerate(KINDS[:2]):
            table[k, n] = entry[kind]
    coef = lambda kind, k: table[k, KINDS.index(kind)]

    def group(g, carry):
        rows = pl.ds(pl.multiple_of(g * ROWS, ROWS), ROWS)
        for t in range(share // LANES):
            cols = slice(t * LANES, (t + 1) * LANES)
            before = forward(
                coef,
                [fl_ref[block[k], flip, rows, cols] for k in range(blocks)],
                [fl_ref[block[k], 1 - flip, rows, cols] for k in range(blocks)],
            )
            out_ref[rows, cols] = before[blocks]
        return carry

    lax.fori_loop(0, lines // ROWS, group, 0)
    out_ref[lines:, :] = jnp.zeros((out_ref.shape[0] - lines, share), jnp.float32)
    for j in range(blocks):
        out_ref[lines + 2 * j : lines + 2 * j + 2, :] = fl_ref[j, 0, lines : lines + 2, :]


def first_half(half, fl, slabs):
    parts, _, lines, share = fl.shape
    vmem = pl.BlockSpec(memory_space=pltpu.VMEM)
    rows = lines - ROWS + -(-2 * parts // ROWS) * ROWS
    return pl.pallas_call(
        functools.partial(first_kernel, slabs),
        in_specs=[pl.BlockSpec(memory_space=pltpu.SMEM), vmem],
        out_specs=vmem,
        out_shape=jax.ShapeDtypeStruct((rows, share), jnp.float32),
        scratch_shapes=[pltpu.VMEM((parts, 2, ROWS, LANES), jnp.float32)],
        compiler_params=pltpu.CompilerParams(vmem_limit_bytes=VMEM_LIMIT),
        cost_estimate=pl.CostEstimate(flops=4 * fl.size, bytes_accessed=5 * fl.size, transcendentals=0),
        name="reduced_in",
    )(half, fl)


def second_kernel(slabs, half, fl_ref, mine, other, uv_ref, info_ref, table):
    blocks, _, lines, share = fl_ref.shape
    lines = lines - ROWS
    flip = half[0]
    flipped = flip == 1
    block = [k + flip * (blocks - 1 - 2 * k) for k in range(blocks)]
    for j in range(blocks):
        info_ref[flip * blocks + j] = fl_ref[j, 0, lines:, :LANES]
        info_ref[(1 - flip) * blocks + j] = jnp.zeros((ROWS, LANES), jnp.float32)
        info_ref[(1 - flip) * blocks + j, 0:2] = other[lines + 2 * j : lines + 2 * j + 2, :LANES]
    shape = (ROWS, LANES)
    above, above_ratio = block_scalars(info_ref[blocks - 1], slabs, shape)
    below, below_ratio = block_scalars(info_ref[blocks], slabs, shape)
    middle = coupling(below_ratio, above[1, 1], below[0, 0], slabs)
    tiles = lambda flip: [
        info_ref[flip * blocks + k + flip * (blocks - 1 - 2 * k)] for k in range(blocks)
    ]
    entries, q_own = half_chain(tiles(flip), slabs, flipped, middle)
    _, q_other = half_chain(tiles(1 - flip), slabs, jnp.logical_not(flipped), middle)
    for k, entry in enumerate(entries):
        for n, kind in enumerate(KINDS):
            table[k, n] = entry[kind]
    table[blocks, 0] = 1.0 / (1.0 - q_own * q_other)
    table[blocks, 1] = q_other
    coef = lambda kind, k: table[k, KINDS.index(kind)]

    def group(g, carry):
        rows = pl.ds(pl.multiple_of(g * ROWS, ROWS), ROWS)
        for t in range(share // LANES):
            cols = slice(t * LANES, (t + 1) * LANES)
            firsts = [fl_ref[block[k], flip, rows, cols] for k in range(blocks)]
            lasts = [fl_ref[block[k], 1 - flip, rows, cols] for k in range(blocks - 1)]
            before = forward(coef, firsts[:-1], lasts)
            across = table[blocks, 0] * (other[rows, cols] + table[blocks, 1] * mine[rows, cols])
            outer, inner = backward(coef, firsts, before, across)
            for k in range(blocks):
                uv_ref[block[k], flip, rows, cols] = outer[k]
                uv_ref[block[k], 1 - flip, rows, cols] = inner[k]
        return carry

    lax.fori_loop(0, lines // ROWS, group, 0)


def second_half(half, fl, mine, other, slabs):
    parts, _, lines, share = fl.shape
    vmem = pl.BlockSpec(memory_space=pltpu.VMEM)
    return pl.pallas_call(
        functools.partial(second_kernel, slabs),
        in_specs=[pl.BlockSpec(memory_space=pltpu.SMEM), vmem, vmem, vmem],
        out_specs=[vmem, vmem],
        out_shape=[
            jax.ShapeDtypeStruct((parts, 2, lines - ROWS, share), jnp.float32),
            jax.ShapeDtypeStruct((2 * parts, ROWS, LANES), jnp.float32),
        ],
        scratch_shapes=[pltpu.VMEM((parts + 1, len(KINDS), ROWS, LANES), jnp.float32)],
        compiler_params=pltpu.CompilerParams(vmem_limit_bytes=VMEM_LIMIT),
        cost_estimate=pl.CostEstimate(flops=10 * fl.size, bytes_accessed=9 * fl.size, transcendentals=0),
        name="reduced_out",
    )(half, fl, mine, other)


def wells_kernel(
    table, where_am_i, info, cells, inverse, well, holders, out_ref, leaving, keep, force, rate, down, rise, uv
):
    blocks, _, slabs, wells = cells.shape
    speed, inlet, reach = well[0:1], well[1:2], well[2:3]
    entries = [table[k] for k in range(table.shape[0])]
    level = lax.broadcasted_iota(jnp.int32, (slabs, wells), 0).astype(jnp.float32)
    for j in range(blocks):
        rock = cells[j, 0]
        cond = select_tree(cells[j, 1].astype(jnp.int32), entries)
        here = jnp.where(level + float(j * slabs) < reach, speed * cond / (1.0 + cond), 0.0)
        rows = slice(j * slabs, (j + 1) * slabs)
        rate[rows] = here
        keep[rows] = 1.0 - here
        force[rows] = here * rock

    chunks = blocks * slabs // ROWS

    def descend(i, value):
        rows = pl.ds(pl.multiple_of(i * ROWS, ROWS), ROWS)
        a, b = keep[rows], force[rows]
        seen = []
        for r in range(ROWS):
            seen.append(value)
            value = a[r : r + 1] * value + b[r : r + 1]
        down[rows] = jnp.concatenate(seen, axis=0)
        return value

    def ascend(i, value):
        rows = pl.ds(pl.multiple_of((chunks - 1 - i) * ROWS, ROWS), ROWS)
        a, b = keep[rows], force[rows]
        seen = []
        for r in reversed(range(ROWS)):
            seen.append(value)
            value = a[r : r + 1] * value + b[r : r + 1]
        rise[rows] = jnp.concatenate(seen[::-1], axis=0)
        return value

    bottom = lax.fori_loop(0, chunks, descend, inlet)
    top = lax.fori_loop(0, chunks, ascend, bottom)
    own_wells = holders.shape[1]
    held = holders[...] == lax.broadcasted_iota(jnp.int32, (wells, own_wells), 0)
    leaving[...] = jnp.dot(
        jnp.broadcast_to(top, (ROWS, wells)),
        held.astype(jnp.float32),
        precision=HIGHEST,
        preferred_element_type=jnp.float32,
    )[0:1]

    for j in range(blocks):
        rows = slice(j * slabs, (j + 1) * slabs)
        taken = rate[rows] * (2.0 * cells[j, 0] - down[rows] - rise[rows])
        rise[rows] = -storage_volume * taken
    firsts, lasts = [], []
    for j in range(blocks):
        both = jnp.dot(
            info[j, :, :slabs],
            rise[j * slabs : (j + 1) * slabs],
            precision=HIGHEST,
            preferred_element_type=jnp.float32,
        )
        firsts.append(both[0:1])
        lasts.append(both[1:2])
    scalars = [block_scalars(info[j], slabs, (1, wells)) for j in range(blocks)]
    zero = jnp.zeros((1, wells), jnp.float32)
    couple = [zero]
    for j in range(1, blocks):
        couple.append(
            coupling(scalars[j][1], scalars[j - 1][0][1, 1], scalars[j][0][0, 0], slabs)
        )
    couple.append(zero)
    coefs, _ = chain([corner for corner, _ in scalars], couple)
    coef = lambda kind, j: coefs[j][kind]
    above, below = backward(coef, firsts, forward(coef, firsts, lasts), zero)
    for j in range(blocks):
        uv[j, 0:1] = above[j]
        uv[j, 1:2] = below[j]
    d = where_am_i[0]
    own = rise[pl.ds(pl.multiple_of(d * slabs, slabs), slabs)]
    row = lax.broadcasted_iota(jnp.int32, (slabs, wells), 0)
    pair = uv[d]
    own = own + jnp.where(row == 0, pair[0:1], 0.0) + jnp.where(row == slabs - 1, pair[1:2], 0.0)
    out_ref[...] = jnp.dot(inverse[...], own, precision=HIGHEST, preferred_element_type=jnp.float32)


def wells_solve(table, depth_index, info, cells, inverse, well, holders):
    blocks, _, slabs, wells = cells.shape
    smem = pl.BlockSpec(memory_space=pltpu.SMEM)
    vmem = pl.BlockSpec(memory_space=pltpu.VMEM)
    column = pltpu.VMEM((blocks * slabs, wells), jnp.float32)
    return pl.pallas_call(
        wells_kernel,
        in_specs=[smem, smem] + [vmem] * 5,
        out_specs=[vmem, vmem],
        out_shape=[
            jax.ShapeDtypeStruct((slabs, wells), jnp.float32),
            jax.ShapeDtypeStruct((1, holders.shape[1]), jnp.float32),
        ],
        scratch_shapes=[column] * 5 + [pltpu.VMEM((blocks, ROWS, wells), jnp.float32)],
        compiler_params=pltpu.CompilerParams(vmem_limit_bytes=VMEM_LIMIT),
        cost_estimate=pl.CostEstimate(flops=10**7, bytes_accessed=8 * cells.size, transcendentals=0),
        name="wells",
    )(table, depth_index.reshape(1), info, cells, inverse, well, holders)


def solve_kernel(right, uv, inverse, place_row, place_column, solved_wells, out, factor, pick):
    together, slabs, rows, span = right.shape
    wells = place_row.shape[1]
    step = pl.program_id(0)
    size = slabs * rows

    @pl.when(step == 0)
    def _():
        spread = (
            lax.broadcasted_iota(jnp.int32, (size, slabs), 0) // rows
            == lax.broadcasted_iota(jnp.int32, (size, slabs), 1)
        ).astype(jnp.float32).astype(jnp.bfloat16)
        spread_t = (
            lax.broadcasted_iota(jnp.int32, (slabs, size), 1) // rows
            == lax.broadcasted_iota(jnp.int32, (slabs, size), 0)
        ).astype(jnp.float32).astype(jnp.bfloat16)
        same = (
            lax.broadcasted_iota(jnp.int32, (size, size), 0) % rows
            == lax.broadcasted_iota(jnp.int32, (size, size), 1) % rows
        )
        for n, part in enumerate(split_bf16(inverse[...], 2)):
            tall = jnp.dot(spread, part, preferred_element_type=jnp.float32).astype(jnp.bfloat16)
            wide = jnp.dot(tall, spread_t, preferred_element_type=jnp.float32)
            wide = jnp.where(same, wide, 0.0).astype(jnp.bfloat16)
            if n == 0:
                factor[:, :size] = wide
                factor[:, size : 2 * size] = wide
            else:
                factor[:, 2 * size : 3 * size] = wide
        column = lax.broadcasted_iota(jnp.int32, (wells, span), 1)
        chosen = (column == place_column[...] % span).astype(jnp.float32).astype(jnp.bfloat16)
        pick[:wells] = chosen
        pick[wells:] = chosen

    tile = min(span, 256)
    for n in range(together):
        line = lax.broadcasted_iota(jnp.int32, (slabs, rows, wells), 1) + (step * together + n) * rows
        at_wells = jnp.where(line == (place_row[...] // span)[None], solved_wells[...][:, None, :], 0.0)
        at_wells = jnp.concatenate(split_bf16(at_wells.reshape(size, wells), 2), axis=1)
        factor[:, 3 * size :] = at_wells
        lines = slice(n * rows, (n + 1) * rows)
        above = jnp.concatenate([uv[d, 0, lines] for d in range(uv.shape[0])], axis=1)
        below = jnp.concatenate([uv[d, 1, lines] for d in range(uv.shape[0])], axis=1)
        for t in range(span // tile):
            cols = slice(t * tile, (t + 1) * tile)
            value = jnp.concatenate(
                [
                    right[n, 0:1, :, cols] + above[None, :, cols],
                    right[n, 1 : slabs - 1, :, cols],
                    right[n, slabs - 1 :, :, cols] + below[None, :, cols],
                ],
                axis=0,
            ).reshape(size, tile)
            upper, lower = split_bf16(value, 2)
            result = jnp.dot(
                factor[...],
                jnp.concatenate([upper, lower, upper, pick[:, cols]], axis=0),
                preferred_element_type=jnp.float32,
            )
            out[:, lines, cols] = result.reshape(slabs, rows, tile)


def solve(right, uv, inverse, place_row, solved_wells):
    groups, slabs, _, span = right.shape
    wells = place_row.shape[1]
    together = 2
    lines = together * ROWS
    shares, _, _, share = uv.shape
    whole = lambda *shape: pl.BlockSpec(shape, lambda g: (0,) * len(shape))
    size = slabs * ROWS
    return pl.pallas_call(
        solve_kernel,
        grid=(groups // together,),
        in_specs=[
            pl.BlockSpec((together, slabs, ROWS, span), lambda g: (g, 0, 0, 0)),
            pl.BlockSpec((shares, 2, lines, share), lambda g: (0, 0, g, 0)),
            whole(slabs, slabs),
            whole(1, wells),
            whole(wells, 1),
            whole(slabs, wells),
        ],
        out_specs=pl.BlockSpec((slabs, lines, span), lambda g: (0, g, 0)),
        out_shape=jax.ShapeDtypeStruct((slabs, groups * ROWS, span), jnp.float32),
        scratch_shapes=[
            pltpu.VMEM((size, 3 * size + 2 * wells), jnp.bfloat16),
            pltpu.VMEM((2 * wells, span), jnp.bfloat16),
        ],
        compiler_params=pltpu.CompilerParams(vmem_limit_bytes=VMEM_LIMIT),
        cost_estimate=pl.CostEstimate(
            flops=8 * size * right.size, bytes_accessed=8 * right.size, transcendentals=0
        ),
        name="depth_solve",
    )(right, uv, inverse, place_row, place_row.reshape(wells, 1), solved_wells)


def body(
    warmth_before,
    stratum_category,
    conductance_catalogue,
    pivot_matrix_reciprocal,
    linkage_factor,
    well_position_inside,
    well_holder_sequence,
    well_reach,
    entering_warmth,
    well_transfer_speed,
):
    slabs, lines, span = warmth_before.shape
    depth_index = lax.axis_index("depth")
    depth_count = lax.axis_size("depth")
    wells = well_position_inside.shape[0]
    owned = wells // depth_count
    table = conductance_catalogue

    def gathered(value):
        copies = jnp.broadcast_to(value[None], (depth_count,) + value.shape)
        return lax.all_to_all(copies, "depth", split_axis=0, concat_axis=0, tiled=True)

    parts = depth_count // 2
    halves = [list(range(h * parts, (h + 1) * parts)) for h in range(2)]
    half = (depth_index // parts).astype(jnp.int32).reshape(1)
    ends = jnp.stack([pivot_matrix_reciprocal[0], pivot_matrix_reciprocal[-1]])
    info = jnp.concatenate([ends, jnp.broadcast_to(linkage_factor[:, None], (2, 1))], axis=1)
    info = jnp.pad(info, ((0, ROWS - 2), (0, span // parts - info.shape[1])))

    place_row = well_position_inside.reshape(1, wells)
    first, last, cells = outset(warmth_before, stratum_category, table, place_row)
    count = lax.axis_size("strip")
    up = [(i, i + 1) for i in range(count - 1)]
    down = [(j, i) for i, j in up]
    before = lax.ppermute(last, "strip", up)
    after = lax.ppermute(first, "strip", down)

    cells = gathered(cells)
    right, fl = stencil(
        warmth_before, stratum_category, table, ends, info, before, after, parts
    )
    exchange = functools.partial(
        lax.all_to_all,
        axis_name="depth",
        split_axis=0,
        concat_axis=0,
        tiled=True,
        axis_index_groups=halves,
    )
    fl_all = exchange(fl)

    mine = first_half(half, fl_all, slabs)
    other = lax.ppermute(
        mine, "depth", [(i, (i + parts) % depth_count) for i in range(depth_count)]
    )
    uv, info_all = second_half(half, fl_all, mine, other, slabs)
    uv_own = exchange(uv)

    well = jnp.stack([well_transfer_speed, entering_warmth, well_reach.astype(jnp.float32)])
    well = jnp.pad(well, ((0, ROWS - 3), (0, 0)))
    holders = lax.dynamic_slice_in_dim(well_holder_sequence, depth_index * owned, owned)
    solved_wells, leaving = wells_solve(
        table, depth_index, info_all, cells, pivot_matrix_reciprocal, well, holders.reshape(1, owned)
    )
    solved = solve(right, uv_own, pivot_matrix_reciprocal, place_row, solved_wells)
    return solved, leaving.reshape(owned)


def solution(mesh):
    in_specs = (
        P("depth", "strip", None),
        P("depth", "strip", None),
        P(),
        P("depth", None),
        P("depth"),
        P("strip"),
        P("strip"),
        P("strip"),
        P("strip"),
        P("strip"),
    )
    out_specs = (P("depth", "strip", None), P(("strip", "depth")))
    return jax.shard_map(body, mesh=mesh, in_specs=in_specs, out_specs=out_specs, check_vma=False)
```

```python
import functools

import jax
import jax.numpy as jnp
from jax import lax
from jax.experimental import pallas as pl
from jax.experimental.pallas import tpu as pltpu
from jax.sharding import PartitionSpec as P

backward_euler_advance = 0.2
storage_volume = 2.0
flux_scale = 0.5 * backward_euler_advance
LANES = 128
ROWS = 8
VMEM_LIMIT = 48 * 1024 * 1024
HIGHEST = lax.Precision.HIGHEST


def select_tree(category, entries):
    values = list(entries)
    bit = 1
    while len(values) > 1:
        odd = (category & bit) != 0
        values = [
            jnp.where(odd, values[k + 1], values[k]) if k + 1 < len(values) else values[k]
            for k in range(0, len(values), 2)
        ]
        bit *= 2
    return values[0]


def split_bf16(value, pieces):
    out = []
    for k in range(pieces):
        part = value.astype(jnp.bfloat16)
        out.append(part)
        if k + 1 < pieces:
            value = value - part.astype(jnp.float32)
    return out


def outset_kernel(table, w_ref, cat_ref, place, first, last, cells, pick, edge_kinds):
    planes, lines, span = w_ref.shape
    wells = place.shape[1]
    entries = [flux_scale * table[k] for k in range(table.shape[0])]

    @pl.when(pl.program_id(0) == 0)
    def _():
        column = lax.broadcasted_iota(jnp.int32, (span, wells), 0)
        pick[...] = (column == place[...] % span).astype(jnp.float32).astype(jnp.bfloat16)

    for n, (row, out) in enumerate(((0, first), (lines - 1, last))):
        for k in range(planes):
            edge_kinds[n, k : k + 1, :] = cat_ref[k, row : row + 1, :]
        cond = select_tree(edge_kinds[n], entries)
        for k in range(planes):
            out[k, 0:1, :] = w_ref[k, row : row + 1, :]
            out[k, 1:2, :] = cond[k : k + 1]

    dot = functools.partial(jnp.dot, preferred_element_type=jnp.float32)
    own_line = lax.broadcasted_iota(jnp.int32, (lines, wells), 0) == place[...] // span
    upper, lower = split_bf16(w_ref[...].reshape(planes * lines, span), 2)
    kinds = cat_ref[...].astype(jnp.float32).reshape(planes * lines, span).astype(jnp.bfloat16)
    sums = [dot(upper, pick[...]) + dot(lower, pick[...]), dot(kinds, pick[...])]
    for n in range(2):
        for k in range(planes):
            mine = jnp.where(own_line, sums[n][k * lines : (k + 1) * lines], 0.0)
            cells[n, k : k + 1, :] = jnp.sum(mine, axis=0, keepdims=True)


def outset(w, cat, table, place_row):
    slabs, lines, span = w.shape
    wells = place_row.shape[1]
    planes = 8
    block = pl.BlockSpec((planes, lines, span), lambda i: (i, 0, 0))
    edge = pl.BlockSpec((planes, 2, span), lambda i: (i, 0, 0))
    return pl.pallas_call(
        outset_kernel,
        grid=(slabs // planes,),
        in_specs=[
            pl.BlockSpec(memory_space=pltpu.SMEM),
            block,
            block,
            pl.BlockSpec((1, wells), lambda i: (0, 0)),
        ],
        out_specs=[edge, edge, pl.BlockSpec((2, planes, wells), lambda i: (0, i, 0))],
        out_shape=[jax.ShapeDtypeStruct((slabs, 2, span), jnp.float32)] * 2
        + [jax.ShapeDtypeStruct((2, slabs, wells), jnp.float32)],
        scratch_shapes=[
            pltpu.VMEM((span, wells), jnp.bfloat16),
            pltpu.VMEM((2, planes, span), jnp.int32),
        ],
        compiler_params=pltpu.CompilerParams(vmem_limit_bytes=VMEM_LIMIT),
        cost_estimate=pl.CostEstimate(
            flops=6 * w.size * wells, bytes_accessed=8 * w.size, transcendentals=0
        ),
        name="edges_and_cells",
    )(table, w, cat, place_row)


def stencil_kernel(table, ends, info, w_ref, cat_ref, before, after, right_ref, fl_ref, acc, ws, cs, fs, pieces, shift):
    step = pl.program_id(0)
    planes, lines, span = w_ref.shape
    tiles = span // LANES
    groups = lines // ROWS
    entries = [flux_scale * table[k] for k in range(table.shape[0])]
    lane = lax.broadcasted_iota(jnp.int32, (lines, LANES), 1)
    top, end = ROWS, ROWS + lines

    @pl.when(step == 0)
    def _():
        acc[...] = jnp.zeros_like(acc)
        source = lax.broadcasted_iota(jnp.int32, shift.shape, 0) % (2 * LANES)
        target = lax.broadcasted_iota(jnp.int32, shift.shape, 1)
        shift[...] = (source == target + 1).astype(jnp.float32).astype(jnp.bfloat16)

    def keep_face(k, t, face):
        rows = pl.ds(pl.multiple_of(k * lines, lines), lines)
        for n, part in enumerate(split_bf16(face, 2)):
            pieces[n, rows, t * LANES : (t + 1) * LANES] = part

    def plane(k, carry):
        left_w = left_c = jnp.zeros((lines, LANES), jnp.float32)
        for t in range(tiles):
            cols = slice(t * LANES, (t + 1) * LANES)
            w = w_ref[k, :, cols]
            c = select_tree(cat_ref[k, :, cols], entries)
            for ref, value, which in ((ws, w, 0), (cs, c, 1)):
                ref[t, top:end] = value
                ref[t, top - 1 : top] = before[k, which : which + 1, cols]
                ref[t, end : end + 1] = after[k, which : which + 1, cols]
            roll_w, roll_c = pltpu.roll(w, 1, 1), pltpu.roll(c, 1, 1)
            west_w = jnp.where(lane == 0, left_w, roll_w)
            west_c = jnp.where(lane == 0, left_c, roll_c)
            left_w, left_c = roll_w, roll_c
            face = (c + west_c) * (w - west_w)
            keep_face(k, t, face)
            if t == tiles - 1:
                keep_face(k, tiles, pltpu.roll(-c * w, 1, 1))
            north = (c + cs[t, top - 1 : end - 1]) * (w - ws[t, top - 1 : end - 1])
            fs[t, top:end] = north
            fs[t, end : end + 1] = (cs[t, end : end + 1] + cs[t, end - 1 : end]) * (
                ws[t, end : end + 1] - ws[t, end - 1 : end]
            )
            base = w - face - north + fs[t, top + 1 : end + 1]
            right_ref[:, k, :, cols] = base.reshape(groups, ROWS, LANES)
        return carry

    lax.fori_loop(0, planes, plane, 0)

    for t in range(tiles):
        cols = slice(t * LANES, (t + 1) * LANES)
        both = slice(t * LANES, (t + 2) * LANES)
        east = jnp.dot(
            jnp.concatenate([pieces[0, :, both], pieces[1, :, both]], axis=1),
            shift[...],
            preferred_element_type=jnp.float32,
        )
        first, final = acc[0, :, cols], acc[1, :, cols]
        for k in range(planes):
            z = step * planes + k
            value = right_ref[:, k, :, cols].reshape(lines, LANES) + east[k * lines : (k + 1) * lines]
            right_ref[:, k, :, cols] = value.reshape(groups, ROWS, LANES)
            first = first + ends[0, z] * value
            final = final + ends[1, z] * value
        acc[0, :, cols] = first
        acc[1, :, cols] = final

    @pl.when(step == pl.num_programs(0) - 1)
    def _():
        share = fl_ref.shape[-1]
        for d in range(fl_ref.shape[0]):
            fl_ref[d, :, :lines] = acc[:, :, d * share : (d + 1) * share]
            for n in range(2):
                fl_ref[d, n, lines:] = info[...]


def stencil(w, cat, table, ends, info, before, after, parts):
    slabs, lines, span = w.shape
    planes, groups = 4, lines // ROWS
    block = pl.BlockSpec((planes, lines, span), lambda i: (i, 0, 0))
    halo = pl.BlockSpec((planes, 2, span), lambda i: (i, 0, 0))
    fl_shape = (parts, 2, lines + ROWS, span // parts)
    smem = pl.BlockSpec(memory_space=pltpu.SMEM)
    shifted = pltpu.VMEM((span // LANES, lines + 2 * ROWS, LANES), jnp.float32)
    return pl.pallas_call(
        stencil_kernel,
        grid=(slabs // planes,),
        in_specs=[smem, smem, pl.BlockSpec(info.shape, lambda i: (0, 0)), block, block, halo, halo],
        out_specs=[
            pl.BlockSpec((groups, planes, ROWS, span), lambda i: (0, i, 0, 0)),
            pl.BlockSpec(fl_shape, lambda i: (0, 0, 0, 0)),
        ],
        out_shape=[
            jax.ShapeDtypeStruct((groups, slabs, ROWS, span), jnp.float32),
            jax.ShapeDtypeStruct(fl_shape, jnp.float32),
        ],
        scratch_shapes=[
            pltpu.VMEM((2, lines, span), jnp.float32),
            shifted,
            shifted,
            shifted,
            pltpu.VMEM((2, planes * lines, span + LANES), jnp.bfloat16),
            pltpu.VMEM((4 * LANES, LANES), jnp.bfloat16),
        ],
        compiler_params=pltpu.CompilerParams(vmem_limit_bytes=VMEM_LIMIT),
        cost_estimate=pl.CostEstimate(flops=40 * w.size, bytes_accessed=12 * w.size, transcendentals=0),
        name="stencil",
    )(table, ends, info, w, cat, before, after)


CORNERS = ((0, 0), (0, 1), (1, 0), (1, 1))


def block_scalars(tile, slabs, shape, flipped=None):
    at = lambda row, lane: jnp.broadcast_to(tile[row : row + 1, lane : lane + 1], shape)
    corner = {(r, c): at(r, c * (slabs - 1)) for r, c in CORNERS}
    if flipped is not None:
        corner = {(r, c): jnp.where(flipped, corner[1 - r, 1 - c], corner[r, c]) for r, c in CORNERS}
    return corner, at(0, slabs)


def coupling(ratio, one, other, slabs):
    return ratio * (slabs / (slabs + 1.0)) / jnp.sqrt(one * other)


def chain(corners, couple, q=None):
    out = []
    q = jnp.zeros_like(couple[0])
    for k, corner in enumerate(corners):
        vf, vl = couple[k] * corner[0, 0], couple[k] * corner[1, 0]
        wf, wl = couple[k + 1] * corner[0, 1], couple[k + 1] * corner[1, 1]
        inverse = 1.0 / (1.0 - vf * q)
        out.append(
            dict(
                p_first=vl * q * inverse,
                p_before=vl * inverse,
                a_first=inverse,
                a_before=vf * inverse,
                a_after=wf * inverse,
                couple=couple[k],
                couple_after=couple[k + 1],
                q=q,
            )
        )
        q = wl + vl * q * wf * inverse
    return out, q


KINDS = ("p_first", "p_before", "a_first", "a_before", "a_after", "couple", "couple_after", "q")


def forward(coef, firsts, lasts):
    before = [jnp.zeros_like(firsts[0])]
    for j in range(len(firsts)):
        before.append(
            lasts[j] + coef("p_first", j) * firsts[j] + coef("p_before", j) * before[j]
        )
    return before


def backward(coef, firsts, before, after):
    blocks = len(firsts)
    above, below = [None] * blocks, [None] * blocks
    for j in reversed(range(blocks)):
        below[j] = coef("couple_after", j) * after
        here = (
            coef("a_first", j) * firsts[j]
            + coef("a_before", j) * before[j]
            + coef("a_after", j) * after
        )
        above[j] = coef("couple", j) * (before[j] + coef("q", j) * here)
        after = here
    return above, below


def half_chain(tiles, slabs, flipped, middle):
    shape = (ROWS, LANES)
    scalars = [block_scalars(tile, slabs, shape, flipped) for tile in tiles]
    couple = [jnp.zeros(shape, jnp.float32)]
    for k in range(1, len(tiles)):
        ratio = jnp.where(flipped, scalars[k - 1][1], scalars[k][1])
        couple.append(coupling(ratio, scalars[k - 1][0][1, 1], scalars[k][0][0, 0], slabs))
    couple.append(middle)
    return chain([corner for corner, _ in scalars], couple)


def first_kernel(slabs, half, fl_ref, out_ref, table):
    blocks, _, lines, share = fl_ref.shape
    lines = lines - ROWS
    flip = half[0]
    flipped = flip == 1
    block = [k + flip * (blocks - 1 - 2 * k) for k in range(blocks)]
    entries, _ = half_chain(
        [fl_ref[block[k], 0, lines:, :LANES] for k in range(blocks)],
        slabs,
        flipped,
        jnp.zeros((ROWS, LANES), jnp.float32),
    )
    for k, entry in enumerate(entries):
        for n, kind in enumerate(KINDS[:2]):
            table[k, n] = entry[kind]
    coef = lambda kind, k: table[k, KINDS.index(kind)]

    def group(g, carry):
        rows = pl.ds(pl.multiple_of(g * ROWS, ROWS), ROWS)
        for t in range(share // LANES):
            cols = slice(t * LANES, (t + 1) * LANES)
            before = forward(
                coef,
                [fl_ref[block[k], flip, rows, cols] for k in range(blocks)],
                [fl_ref[block[k], 1 - flip, rows, cols] for k in range(blocks)],
            )
            out_ref[rows, cols] = before[blocks]
        return carry

    lax.fori_loop(0, lines // ROWS, group, 0)
    out_ref[lines:, :] = jnp.zeros((out_ref.shape[0] - lines, share), jnp.float32)
    for j in range(blocks):
        out_ref[lines + 2 * j : lines + 2 * j + 2, :] = fl_ref[j, 0, lines : lines + 2, :]


def first_half(half, fl, slabs):
    parts, _, lines, share = fl.shape
    vmem = pl.BlockSpec(memory_space=pltpu.VMEM)
    rows = lines - ROWS + -(-2 * parts // ROWS) * ROWS
    return pl.pallas_call(
        functools.partial(first_kernel, slabs),
        in_specs=[pl.BlockSpec(memory_space=pltpu.SMEM), vmem],
        out_specs=vmem,
        out_shape=jax.ShapeDtypeStruct((rows, share), jnp.float32),
        scratch_shapes=[pltpu.VMEM((parts, 2, ROWS, LANES), jnp.float32)],
        compiler_params=pltpu.CompilerParams(vmem_limit_bytes=VMEM_LIMIT),
        cost_estimate=pl.CostEstimate(flops=4 * fl.size, bytes_accessed=5 * fl.size, transcendentals=0),
        name="reduced_in",
    )(half, fl)


def second_kernel(slabs, half, fl_ref, mine, other, uv_ref, info_ref, table):
    blocks, _, lines, share = fl_ref.shape
    lines = lines - ROWS
    flip = half[0]
    flipped = flip == 1
    block = [k + flip * (blocks - 1 - 2 * k) for k in range(blocks)]
    for j in range(blocks):
        info_ref[flip * blocks + j] = fl_ref[j, 0, lines:, :LANES]
        info_ref[(1 - flip) * blocks + j] = jnp.zeros((ROWS, LANES), jnp.float32)
        info_ref[(1 - flip) * blocks + j, 0:2] = other[lines + 2 * j : lines + 2 * j + 2, :LANES]
    shape = (ROWS, LANES)
    above, above_ratio = block_scalars(info_ref[blocks - 1], slabs, shape)
    below, below_ratio = block_scalars(info_ref[blocks], slabs, shape)
    middle = coupling(below_ratio, above[1, 1], below[0, 0], slabs)
    tiles = lambda flip: [
        info_ref[flip * blocks + k + flip * (blocks - 1 - 2 * k)] for k in range(blocks)
    ]
    entries, q_own = half_chain(tiles(flip), slabs, flipped, middle)
    _, q_other = half_chain(tiles(1 - flip), slabs, jnp.logical_not(flipped), middle)
    for k, entry in enumerate(entries):
        for n, kind in enumerate(KINDS):
            table[k, n] = entry[kind]
    table[blocks, 0] = 1.0 / (1.0 - q_own * q_other)
    table[blocks, 1] = q_other
    coef = lambda kind, k: table[k, KINDS.index(kind)]

    def group(g, carry):
        rows = pl.ds(pl.multiple_of(g * ROWS, ROWS), ROWS)
        for t in range(share // LANES):
            cols = slice(t * LANES, (t + 1) * LANES)
            firsts = [fl_ref[block[k], flip, rows, cols] for k in range(blocks)]
            lasts = [fl_ref[block[k], 1 - flip, rows, cols] for k in range(blocks - 1)]
            before = forward(coef, firsts[:-1], lasts)
            across = table[blocks, 0] * (other[rows, cols] + table[blocks, 1] * mine[rows, cols])
            outer, inner = backward(coef, firsts, before, across)
            for k in range(blocks):
                uv_ref[block[k], flip, rows, cols] = outer[k]
                uv_ref[block[k], 1 - flip, rows, cols] = inner[k]
        return carry

    lax.fori_loop(0, lines // ROWS, group, 0)


def second_half(half, fl, mine, other, slabs):
    parts, _, lines, share = fl.shape
    vmem = pl.BlockSpec(memory_space=pltpu.VMEM)
    return pl.pallas_call(
        functools.partial(second_kernel, slabs),
        in_specs=[pl.BlockSpec(memory_space=pltpu.SMEM), vmem, vmem, vmem],
        out_specs=[vmem, vmem],
        out_shape=[
            jax.ShapeDtypeStruct((parts, 2, lines - ROWS, share), jnp.float32),
            jax.ShapeDtypeStruct((2 * parts, ROWS, LANES), jnp.float32),
        ],
        scratch_shapes=[pltpu.VMEM((parts + 1, len(KINDS), ROWS, LANES), jnp.float32)],
        compiler_params=pltpu.CompilerParams(vmem_limit_bytes=VMEM_LIMIT),
        cost_estimate=pl.CostEstimate(flops=10 * fl.size, bytes_accessed=9 * fl.size, transcendentals=0),
        name="reduced_out",
    )(half, fl, mine, other)


def circuits_kernel(table, cells, well, holders, source, leaving, keep, force, rate, down, rise):
    blocks, _, slabs, wells = cells.shape
    speed, inlet, reach = well[0:1], well[1:2], well[2:3]
    entries = [table[k] for k in range(table.shape[0])]
    level = lax.broadcasted_iota(jnp.int32, (slabs, wells), 0).astype(jnp.float32)
    for j in range(blocks):
        rock = cells[j, 0]
        cond = select_tree(cells[j, 1].astype(jnp.int32), entries)
        here = jnp.where(level + float(j * slabs) < reach, speed * cond / (1.0 + cond), 0.0)
        rows = slice(j * slabs, (j + 1) * slabs)
        rate[rows] = here
        keep[rows] = 1.0 - here
        force[rows] = here * rock

    chunks = blocks * slabs // ROWS

    def descend(i, value):
        rows = pl.ds(pl.multiple_of(i * ROWS, ROWS), ROWS)
        a, b = keep[rows], force[rows]
        seen = []
        for r in range(ROWS):
            seen.append(value)
            value = a[r : r + 1] * value + b[r : r + 1]
        down[rows] = jnp.concatenate(seen, axis=0)
        return value

    def ascend(i, value):
        rows = pl.ds(pl.multiple_of((chunks - 1 - i) * ROWS, ROWS), ROWS)
        a, b = keep[rows], force[rows]
        seen = []
        for r in reversed(range(ROWS)):
            seen.append(value)
            value = a[r : r + 1] * value + b[r : r + 1]
        rise[rows] = jnp.concatenate(seen[::-1], axis=0)
        return value

    bottom = lax.fori_loop(0, chunks, descend, inlet)
    top = lax.fori_loop(0, chunks, ascend, bottom)
    held = holders[...] == lax.broadcasted_iota(jnp.int32, (wells, holders.shape[1]), 0)
    leaving[...] = jnp.dot(
        jnp.broadcast_to(top, (ROWS, wells)),
        held.astype(jnp.float32),
        precision=HIGHEST,
        preferred_element_type=jnp.float32,
    )[0:1]
    for j in range(blocks):
        rows = slice(j * slabs, (j + 1) * slabs)
        taken = rate[rows] * (2.0 * cells[j, 0] - down[rows] - rise[rows])
        source[rows] = -storage_volume * taken


def circuits(table, cells, well, holders):
    blocks, _, slabs, wells = cells.shape
    smem = pl.BlockSpec(memory_space=pltpu.SMEM)
    vmem = pl.BlockSpec(memory_space=pltpu.VMEM)
    column = pltpu.VMEM((blocks * slabs, wells), jnp.float32)
    return pl.pallas_call(
        circuits_kernel,
        in_specs=[smem, vmem, vmem, vmem],
        out_specs=[vmem, vmem],
        out_shape=[
            jax.ShapeDtypeStruct((blocks * slabs, wells), jnp.float32),
            jax.ShapeDtypeStruct((1, holders.shape[1]), jnp.float32),
        ],
        scratch_shapes=[column] * 5,
        cost_estimate=pl.CostEstimate(flops=10**7, bytes_accessed=8 * cells.size, transcendentals=0),
        name="circuits",
    )(table, cells, well, holders)


def coupled_kernel(where_am_i, info, source, inverse, out_ref, uv):
    blocks = info.shape[0]
    slabs, wells = out_ref.shape
    firsts, lasts = [], []
    for j in range(blocks):
        both = jnp.dot(
            info[j, :, :slabs],
            source[j * slabs : (j + 1) * slabs],
            precision=HIGHEST,
            preferred_element_type=jnp.float32,
        )
        firsts.append(both[0:1])
        lasts.append(both[1:2])
    scalars = [block_scalars(info[j], slabs, (1, wells)) for j in range(blocks)]
    zero = jnp.zeros((1, wells), jnp.float32)
    couple = [zero]
    for j in range(1, blocks):
        couple.append(
            coupling(scalars[j][1], scalars[j - 1][0][1, 1], scalars[j][0][0, 0], slabs)
        )
    couple.append(zero)
    coefs, _ = chain([corner for corner, _ in scalars], couple)
    coef = lambda kind, j: coefs[j][kind]
    above, below = backward(coef, firsts, forward(coef, firsts, lasts), zero)
    for j in range(blocks):
        uv[j, 0:1] = above[j]
        uv[j, 1:2] = below[j]
    d = where_am_i[0]
    own = source[pl.ds(pl.multiple_of(d * slabs, slabs), slabs)]
    row = lax.broadcasted_iota(jnp.int32, (slabs, wells), 0)
    pair = uv[d]
    own = own + jnp.where(row == 0, pair[0:1], 0.0) + jnp.where(row == slabs - 1, pair[1:2], 0.0)
    out_ref[...] = jnp.dot(inverse[...], own, precision=HIGHEST, preferred_element_type=jnp.float32)


def coupled_wells(depth_index, info, source, inverse):
    blocks = info.shape[0]
    slabs, wells = inverse.shape[0], source.shape[1]
    smem = pl.BlockSpec(memory_space=pltpu.SMEM)
    vmem = pl.BlockSpec(memory_space=pltpu.VMEM)
    return pl.pallas_call(
        coupled_kernel,
        in_specs=[smem, vmem, vmem, vmem],
        out_specs=vmem,
        out_shape=jax.ShapeDtypeStruct((slabs, wells), jnp.float32),
        scratch_shapes=[pltpu.VMEM((blocks, ROWS, wells), jnp.float32)],
        cost_estimate=pl.CostEstimate(flops=10**6, bytes_accessed=4 * source.size, transcendentals=0),
        name="coupled_wells",
    )(depth_index.reshape(1), info, source, inverse)


def solve_kernel(right, uv, inverse, place_row, place_column, solved_wells, out, factor, pick):
    together, slabs, rows, span = right.shape
    wells = place_row.shape[1]
    step = pl.program_id(0)
    size = slabs * rows

    @pl.when(step == 0)
    def _():
        spread = (
            lax.broadcasted_iota(jnp.int32, (size, slabs), 0) // rows
            == lax.broadcasted_iota(jnp.int32, (size, slabs), 1)
        ).astype(jnp.float32).astype(jnp.bfloat16)
        spread_t = (
            lax.broadcasted_iota(jnp.int32, (slabs, size), 1) // rows
            == lax.broadcasted_iota(jnp.int32, (slabs, size), 0)
        ).astype(jnp.float32).astype(jnp.bfloat16)
        same = (
            lax.broadcasted_iota(jnp.int32, (size, size), 0) % rows
            == lax.broadcasted_iota(jnp.int32, (size, size), 1) % rows
        )
        for n, part in enumerate(split_bf16(inverse[...], 2)):
            tall = jnp.dot(spread, part, preferred_element_type=jnp.float32).astype(jnp.bfloat16)
            wide = jnp.dot(tall, spread_t, preferred_element_type=jnp.float32)
            wide = jnp.where(same, wide, 0.0).astype(jnp.bfloat16)
            if n == 0:
                factor[:, :size] = wide
                factor[:, size : 2 * size] = wide
            else:
                factor[:, 2 * size : 3 * size] = wide
        column = lax.broadcasted_iota(jnp.int32, (wells, span), 1)
        chosen = (column == place_column[...] % span).astype(jnp.float32).astype(jnp.bfloat16)
        pick[:wells] = chosen
        pick[wells:] = chosen

    tile = min(span, 256)
    for n in range(together):
        line = lax.broadcasted_iota(jnp.int32, (slabs, rows, wells), 1) + (step * together + n) * rows
        at_wells = jnp.where(line == (place_row[...] // span)[None], solved_wells[...][:, None, :], 0.0)
        at_wells = jnp.concatenate(split_bf16(at_wells.reshape(size, wells), 2), axis=1)
        factor[:, 3 * size :] = at_wells
        lines = slice(n * rows, (n + 1) * rows)
        above = jnp.concatenate([uv[d, 0, lines] for d in range(uv.shape[0])], axis=1)
        below = jnp.concatenate([uv[d, 1, lines] for d in range(uv.shape[0])], axis=1)
        for t in range(span // tile):
            cols = slice(t * tile, (t + 1) * tile)
            value = jnp.concatenate(
                [
                    right[n, 0:1, :, cols] + above[None, :, cols],
                    right[n, 1 : slabs - 1, :, cols],
                    right[n, slabs - 1 :, :, cols] + below[None, :, cols],
                ],
                axis=0,
            ).reshape(size, tile)
            upper, lower = split_bf16(value, 2)
            result = jnp.dot(
                factor[...],
                jnp.concatenate([upper, lower, upper, pick[:, cols]], axis=0),
                preferred_element_type=jnp.float32,
            )
            out[:, lines, cols] = result.reshape(slabs, rows, tile)


def solve(right, uv, inverse, place_row, solved_wells):
    groups, slabs, _, span = right.shape
    wells = place_row.shape[1]
    together = 2
    lines = together * ROWS
    shares, _, _, share = uv.shape
    whole = lambda *shape: pl.BlockSpec(shape, lambda g: (0,) * len(shape))
    size = slabs * ROWS
    return pl.pallas_call(
        solve_kernel,
        grid=(groups // together,),
        in_specs=[
            pl.BlockSpec((together, slabs, ROWS, span), lambda g: (g, 0, 0, 0)),
            pl.BlockSpec((shares, 2, lines, share), lambda g: (0, 0, g, 0)),
            whole(slabs, slabs),
            whole(1, wells),
            whole(wells, 1),
            whole(slabs, wells),
        ],
        out_specs=pl.BlockSpec((slabs, lines, span), lambda g: (0, g, 0)),
        out_shape=jax.ShapeDtypeStruct((slabs, groups * ROWS, span), jnp.float32),
        scratch_shapes=[
            pltpu.VMEM((size, 3 * size + 2 * wells), jnp.bfloat16),
            pltpu.VMEM((2 * wells, span), jnp.bfloat16),
        ],
        compiler_params=pltpu.CompilerParams(vmem_limit_bytes=VMEM_LIMIT),
        cost_estimate=pl.CostEstimate(
            flops=8 * size * right.size, bytes_accessed=8 * right.size, transcendentals=0
        ),
        name="depth_solve",
    )(right, uv, inverse, place_row, place_row.reshape(wells, 1), solved_wells)


def body(
    warmth_before,
    stratum_category,
    conductance_catalogue,
    pivot_matrix_reciprocal,
    linkage_factor,
    well_position_inside,
    well_holder_sequence,
    well_reach,
    entering_warmth,
    well_transfer_speed,
):
    slabs, lines, span = warmth_before.shape
    depth_index = lax.axis_index("depth")
    depth_count = lax.axis_size("depth")
    wells = well_position_inside.shape[0]
    owned = wells // depth_count
    table = conductance_catalogue

    def gathered(value):
        copies = jnp.broadcast_to(value[None], (depth_count,) + value.shape)
        return lax.all_to_all(copies, "depth", split_axis=0, concat_axis=0, tiled=True)

    parts = depth_count // 2
    halves = [list(range(h * parts, (h + 1) * parts)) for h in range(2)]
    half = (depth_index // parts).astype(jnp.int32).reshape(1)
    ends = jnp.stack([pivot_matrix_reciprocal[0], pivot_matrix_reciprocal[-1]])
    info = jnp.concatenate([ends, jnp.broadcast_to(linkage_factor[:, None], (2, 1))], axis=1)
    info = jnp.pad(info, ((0, ROWS - 2), (0, span // parts - info.shape[1])))

    place_row = well_position_inside.reshape(1, wells)
    first, last, cells = outset(warmth_before, stratum_category, table, place_row)
    count = lax.axis_size("strip")
    up = [(i, i + 1) for i in range(count - 1)]
    down = [(j, i) for i, j in up]
    before = lax.ppermute(last, "strip", up)
    after = lax.ppermute(first, "strip", down)

    cells = gathered(cells)
    right, fl = stencil(
        warmth_before, stratum_category, table, ends, info, before, after, parts
    )
    exchange = functools.partial(
        lax.all_to_all,
        axis_name="depth",
        split_axis=0,
        concat_axis=0,
        tiled=True,
        axis_index_groups=halves,
    )
    fl, cells = lax.optimization_barrier((fl, cells))
    fl_all = exchange(fl)

    well = jnp.stack([well_transfer_speed, entering_warmth, well_reach.astype(jnp.float32)])
    well = jnp.pad(well, ((0, ROWS - 3), (0, 0)))
    holders = lax.dynamic_slice_in_dim(well_holder_sequence, depth_index * owned, owned)
    source, leaving = circuits(table, cells, well, holders.reshape(1, owned))

    mine = first_half(half, fl_all, slabs)
    other = lax.ppermute(
        mine, "depth", [(i, (i + parts) % depth_count) for i in range(depth_count)]
    )
    uv, info_all = second_half(half, fl_all, mine, other, slabs)
    uv_own = exchange(uv)
    solved_wells = coupled_wells(depth_index, info_all, source, pivot_matrix_reciprocal)
    solved = solve(right, uv_own, pivot_matrix_reciprocal, place_row, solved_wells)
    return solved, leaving.reshape(owned)


def solution(mesh):
    in_specs = (
        P("depth", "strip", None),
        P("depth", "strip", None),
        P(),
        P("depth", None),
        P("depth"),
        P("strip"),
        P("strip"),
        P("strip"),
        P("strip"),
        P("strip"),
    )
    out_specs = (P("depth", "strip", None), P(("strip", "depth")))
    return jax.shard_map(body, mesh=mesh, in_specs=in_specs, out_specs=out_specs, check_vma=False)
```

```python
import functools

import jax
import jax.numpy as jnp
from jax import lax
from jax.experimental import pallas as pl
from jax.experimental.pallas import tpu as pltpu
from jax.sharding import PartitionSpec as P

backward_euler_advance = 0.2
storage_volume = 2.0
flux_scale = 0.5 * backward_euler_advance
LANES = 128
ROWS = 8
VMEM_LIMIT = 48 * 1024 * 1024
HIGHEST = lax.Precision.HIGHEST


def select_tree(category, entries):
    values = list(entries)
    bit = 1
    while len(values) > 1:
        odd = (category & bit) != 0
        values = [
            jnp.where(odd, values[k + 1], values[k]) if k + 1 < len(values) else values[k]
            for k in range(0, len(values), 2)
        ]
        bit *= 2
    return values[0]


def split_bf16(value, pieces):
    out = []
    for k in range(pieces):
        part = value.astype(jnp.bfloat16)
        out.append(part)
        if k + 1 < pieces:
            value = value - part.astype(jnp.float32)
    return out


def stencil_kernel(
    table,
    ends,
    info,
    w_ref,
    cat_ref,
    place,
    right_ref,
    fl_ref,
    first_ref,
    last_ref,
    cells_ref,
    acc,
    ws,
    cs,
    fs,
    pieces,
    shift,
    pick,
    edges,
):
    step = pl.program_id(0)
    planes, lines, span = w_ref.shape
    tiles = span // LANES
    groups = lines // ROWS
    wells = place.shape[1]
    entries = [flux_scale * table[k] for k in range(table.shape[0])]
    lane = lax.broadcasted_iota(jnp.int32, (lines, LANES), 1)
    top, end = ROWS, ROWS + lines

    @pl.when(step == 0)
    def _():
        acc[...] = jnp.zeros_like(acc)
        source = lax.broadcasted_iota(jnp.int32, shift.shape, 0) % (2 * LANES)
        target = lax.broadcasted_iota(jnp.int32, shift.shape, 1)
        shift[...] = (source == target + 1).astype(jnp.float32).astype(jnp.bfloat16)
        column = lax.broadcasted_iota(jnp.int32, (span, wells), 0)
        pick[...] = (column == place[...] % span).astype(jnp.float32).astype(jnp.bfloat16)

    def keep_face(k, t, face):
        rows = pl.ds(pl.multiple_of(k * lines, lines), lines)
        for n, part in enumerate(split_bf16(face, 2)):
            pieces[n, rows, t * LANES : (t + 1) * LANES] = part

    def plane(k, carry):
        left_w = left_c = jnp.zeros((lines, LANES), jnp.float32)
        for t in range(tiles):
            cols = slice(t * LANES, (t + 1) * LANES)
            w = w_ref[k, :, cols]
            c = select_tree(cat_ref[k, :, cols], entries)
            for n, (ref, value) in enumerate(((ws, w), (cs, c))):
                ref[t, top:end] = value
                edge_first, edge_last = value[0:1], value[lines - 1 : lines]
                ref[t, top - 1 : top] = edge_first
                ref[t, end : end + 1] = edge_last
                edges[k, n : n + 1, cols] = edge_first
                edges[k, n + 2 : n + 3, cols] = edge_last
            roll_w, roll_c = pltpu.roll(w, 1, 1), pltpu.roll(c, 1, 1)
            west_w = jnp.where(lane == 0, left_w, roll_w)
            west_c = jnp.where(lane == 0, left_c, roll_c)
            left_w, left_c = roll_w, roll_c
            face = (c + west_c) * (w - west_w)
            keep_face(k, t, face)
            if t == tiles - 1:
                keep_face(k, tiles, pltpu.roll(-c * w, 1, 1))
            north = (c + cs[t, top - 1 : end - 1]) * (w - ws[t, top - 1 : end - 1])
            fs[t, top:end] = north
            fs[t, end : end + 1] = jnp.zeros((1, LANES), jnp.float32)
            base = w - face - north + fs[t, top + 1 : end + 1]
            right_ref[:, k, :, cols] = base.reshape(groups, ROWS, LANES)
        return carry

    lax.fori_loop(0, planes, plane, 0)

    for t in range(tiles):
        cols = slice(t * LANES, (t + 1) * LANES)
        both = slice(t * LANES, (t + 2) * LANES)
        east = jnp.dot(
            jnp.concatenate([pieces[0, :, both], pieces[1, :, both]], axis=1),
            shift[...],
            preferred_element_type=jnp.float32,
        )
        first, final = acc[0, :, cols], acc[1, :, cols]
        for k in range(planes):
            z = step * planes + k
            value = right_ref[:, k, :, cols].reshape(lines, LANES) + east[k * lines : (k + 1) * lines]
            right_ref[:, k, :, cols] = value.reshape(groups, ROWS, LANES)
            first = first + ends[0, z] * value
            final = final + ends[1, z] * value
        acc[0, :, cols] = first
        acc[1, :, cols] = final

    for k in range(planes):
        for n in range(2):
            first_ref[n, k : k + 1, :] = edges[k, n : n + 1, :]
            last_ref[n, k : k + 1, :] = edges[k, n + 2 : n + 3, :]

    dot = functools.partial(jnp.dot, preferred_element_type=jnp.float32)
    own_line = lax.broadcasted_iota(jnp.int32, (lines, wells), 0) == place[...] // span
    upper, lower = split_bf16(w_ref[...].reshape(planes * lines, span), 2)
    kinds = cat_ref[...].astype(jnp.float32).reshape(planes * lines, span).astype(jnp.bfloat16)
    sums = [dot(upper, pick[...]) + dot(lower, pick[...]), dot(kinds, pick[...])]
    for n in range(2):
        for k in range(planes):
            mine = jnp.where(own_line, sums[n][k * lines : (k + 1) * lines], 0.0)
            cells_ref[n, k : k + 1, :] = jnp.sum(mine, axis=0, keepdims=True)

    @pl.when(step == pl.num_programs(0) - 1)
    def _():
        share = fl_ref.shape[-1]
        for d in range(fl_ref.shape[0]):
            fl_ref[d, :, :lines] = acc[:, :, d * share : (d + 1) * share]
            for n in range(2):
                fl_ref[d, n, lines:] = info[...]


def stencil(w, cat, table, ends, info, place_row, parts):
    slabs, lines, span = w.shape
    planes, groups = 8, lines // ROWS
    wells = place_row.shape[1]
    block = pl.BlockSpec((planes, lines, span), lambda i: (i, 0, 0))
    edge = pl.BlockSpec((2, planes, span), lambda i: (0, i, 0))
    fl_shape = (parts, 2, lines + ROWS, span // parts)
    smem = pl.BlockSpec(memory_space=pltpu.SMEM)
    shifted = pltpu.VMEM((span // LANES, lines + 2 * ROWS, LANES), jnp.float32)
    return pl.pallas_call(
        stencil_kernel,
        grid=(slabs // planes,),
        in_specs=[
            smem,
            smem,
            pl.BlockSpec(info.shape, lambda i: (0, 0)),
            block,
            block,
            pl.BlockSpec((1, wells), lambda i: (0, 0)),
        ],
        out_specs=[
            pl.BlockSpec((groups, planes, ROWS, span), lambda i: (0, i, 0, 0)),
            pl.BlockSpec(fl_shape, lambda i: (0, 0, 0, 0)),
            edge,
            edge,
            pl.BlockSpec((2, planes, wells), lambda i: (0, i, 0)),
        ],
        out_shape=[
            jax.ShapeDtypeStruct((groups, slabs, ROWS, span), jnp.float32),
            jax.ShapeDtypeStruct(fl_shape, jnp.float32),
            jax.ShapeDtypeStruct((2, slabs, span), jnp.float32),
            jax.ShapeDtypeStruct((2, slabs, span), jnp.float32),
            jax.ShapeDtypeStruct((2, slabs, wells), jnp.float32),
        ],
        scratch_shapes=[
            pltpu.VMEM((2, lines, span), jnp.float32),
            shifted,
            shifted,
            shifted,
            pltpu.VMEM((2, planes * lines, span + LANES), jnp.bfloat16),
            pltpu.VMEM((4 * LANES, LANES), jnp.bfloat16),
            pltpu.VMEM((span, wells), jnp.bfloat16),
            pltpu.VMEM((planes, 4, span), jnp.float32),
        ],
        compiler_params=pltpu.CompilerParams(vmem_limit_bytes=VMEM_LIMIT),
        cost_estimate=pl.CostEstimate(flops=40 * w.size, bytes_accessed=12 * w.size, transcendentals=0),
        name="stencil",
    )(table, ends, info, w, cat, place_row)


def outer_flux_kernel(first, last, before, after, ends, cells, flux_ref, out_ref):
    copies, _, lanes = out_ref.shape
    slabs, span = first.shape[1:]
    tiles = span // lanes
    out_ref[0, : 2 * slabs] = cells[...].reshape(2 * slabs, lanes)
    for n, (own, other) in enumerate(((first, before), (last, after))):
        flux = (own[1] + other[1]) * (other[0] - own[0])
        flux_ref[n] = flux
        sums = jnp.dot(ends[...], flux, precision=HIGHEST, preferred_element_type=jnp.float32)
        for q in range(2):
            for t in range(tiles):
                row = 2 * slabs + (2 * q + n) * tiles + t
                out_ref[0, row : row + 1] = sums[q : q + 1, t * lanes : (t + 1) * lanes]
    for d in range(1, copies):
        out_ref[d] = out_ref[0]


def outer_flux(first, last, before, after, ends, cells, copies):
    _, slabs, span = first.shape
    lanes = cells.shape[-1]
    rows = 2 * slabs + 4 * (span // lanes)
    vmem = pl.BlockSpec(memory_space=pltpu.VMEM)
    return pl.pallas_call(
        outer_flux_kernel,
        in_specs=[vmem] * 6,
        out_specs=[vmem] * 2,
        out_shape=[
            jax.ShapeDtypeStruct((2, slabs, span), jnp.float32),
            jax.ShapeDtypeStruct((copies, rows, lanes), jnp.float32),
        ],
        cost_estimate=pl.CostEstimate(flops=10**6, bytes_accessed=10**6, transcendentals=0),
        name="outer_flux",
    )(first, last, before, after, ends, cells)


CORNERS = ((0, 0), (0, 1), (1, 0), (1, 1))


def block_scalars(tile, slabs, shape, flipped=None):
    at = lambda row, lane: jnp.broadcast_to(tile[row : row + 1, lane : lane + 1], shape)
    corner = {(r, c): at(r, c * (slabs - 1)) for r, c in CORNERS}
    if flipped is not None:
        corner = {(r, c): jnp.where(flipped, corner[1 - r, 1 - c], corner[r, c]) for r, c in CORNERS}
    return corner, at(0, slabs)


def coupling(ratio, one, other, slabs):
    return ratio * (slabs / (slabs + 1.0)) / jnp.sqrt(one * other)


def chain(corners, couple, q=None):
    out = []
    q = jnp.zeros_like(couple[0])
    for k, corner in enumerate(corners):
        vf, vl = couple[k] * corner[0, 0], couple[k] * corner[1, 0]
        wf, wl = couple[k + 1] * corner[0, 1], couple[k + 1] * corner[1, 1]
        inverse = 1.0 / (1.0 - vf * q)
        out.append(
            dict(
                p_first=vl * q * inverse,
                p_before=vl * inverse,
                a_first=inverse,
                a_before=vf * inverse,
                a_after=wf * inverse,
                couple=couple[k],
                couple_after=couple[k + 1],
                q=q,
            )
        )
        q = wl + vl * q * wf * inverse
    return out, q


KINDS = ("p_first", "p_before", "a_first", "a_before", "a_after", "couple", "couple_after", "q")


def forward(coef, firsts, lasts):
    before = [jnp.zeros_like(firsts[0])]
    for j in range(len(firsts)):
        before.append(
            lasts[j] + coef("p_first", j) * firsts[j] + coef("p_before", j) * before[j]
        )
    return before


def backward(coef, firsts, before, after):
    blocks = len(firsts)
    above, below = [None] * blocks, [None] * blocks
    for j in reversed(range(blocks)):
        below[j] = coef("couple_after", j) * after
        here = (
            coef("a_first", j) * firsts[j]
            + coef("a_before", j) * before[j]
            + coef("a_after", j) * after
        )
        above[j] = coef("couple", j) * (before[j] + coef("q", j) * here)
        after = here
    return above, below


def half_chain(tiles, slabs, flipped, middle):
    shape = (ROWS, LANES)
    scalars = [block_scalars(tile, slabs, shape, flipped) for tile in tiles]
    couple = [jnp.zeros(shape, jnp.float32)]
    for k in range(1, len(tiles)):
        ratio = jnp.where(flipped, scalars[k - 1][1], scalars[k][1])
        couple.append(coupling(ratio, scalars[k - 1][0][1, 1], scalars[k][0][0, 0], slabs))
    couple.append(middle)
    return chain([corner for corner, _ in scalars], couple)


def first_kernel(slabs, half, fl_ref, out_ref, table):
    blocks, _, lines, share = fl_ref.shape
    lines = lines - ROWS
    flip = half[0]
    flipped = flip == 1
    block = [k + flip * (blocks - 1 - 2 * k) for k in range(blocks)]
    entries, _ = half_chain(
        [fl_ref[block[k], 0, lines:, :LANES] for k in range(blocks)],
        slabs,
        flipped,
        jnp.zeros((ROWS, LANES), jnp.float32),
    )
    for k, entry in enumerate(entries):
        for n, kind in enumerate(KINDS[:2]):
            table[k, n] = entry[kind]
    coef = lambda kind, k: table[k, KINDS.index(kind)]

    def group(g, carry):
        rows = pl.ds(pl.multiple_of(g * ROWS, ROWS), ROWS)
        for t in range(share // LANES):
            cols = slice(t * LANES, (t + 1) * LANES)
            before = forward(
                coef,
                [fl_ref[block[k], flip, rows, cols] for k in range(blocks)],
                [fl_ref[block[k], 1 - flip, rows, cols] for k in range(blocks)],
            )
            out_ref[rows, cols] = before[blocks]
        return carry

    lax.fori_loop(0, lines // ROWS, group, 0)
    out_ref[lines:, :] = jnp.zeros((out_ref.shape[0] - lines, share), jnp.float32)
    for j in range(blocks):
        out_ref[lines + 2 * j : lines + 2 * j + 2, :] = fl_ref[j, 0, lines : lines + 2, :]


def first_half(half, fl, slabs):
    parts, _, lines, share = fl.shape
    vmem = pl.BlockSpec(memory_space=pltpu.VMEM)
    rows = lines - ROWS + -(-2 * parts // ROWS) * ROWS
    return pl.pallas_call(
        functools.partial(first_kernel, slabs),
        in_specs=[pl.BlockSpec(memory_space=pltpu.SMEM), vmem],
        out_specs=vmem,
        out_shape=jax.ShapeDtypeStruct((rows, share), jnp.float32),
        scratch_shapes=[pltpu.VMEM((parts, 2, ROWS, LANES), jnp.float32)],
        compiler_params=pltpu.CompilerParams(vmem_limit_bytes=VMEM_LIMIT),
        cost_estimate=pl.CostEstimate(flops=4 * fl.size, bytes_accessed=5 * fl.size, transcendentals=0),
        name="reduced_in",
    )(half, fl)


def second_kernel(slabs, half, fl_ref, mine, other, uv_ref, info_ref, table):
    blocks, _, lines, share = fl_ref.shape
    lines = lines - ROWS
    flip = half[0]
    flipped = flip == 1
    block = [k + flip * (blocks - 1 - 2 * k) for k in range(blocks)]
    for j in range(blocks):
        info_ref[flip * blocks + j] = fl_ref[j, 0, lines:, :LANES]
        info_ref[(1 - flip) * blocks + j] = jnp.zeros((ROWS, LANES), jnp.float32)
        info_ref[(1 - flip) * blocks + j, 0:2] = other[lines + 2 * j : lines + 2 * j + 2, :LANES]
    shape = (ROWS, LANES)
    above, above_ratio = block_scalars(info_ref[blocks - 1], slabs, shape)
    below, below_ratio = block_scalars(info_ref[blocks], slabs, shape)
    middle = coupling(below_ratio, above[1, 1], below[0, 0], slabs)
    tiles = lambda flip: [
        info_ref[flip * blocks + k + flip * (blocks - 1 - 2 * k)] for k in range(blocks)
    ]
    entries, q_own = half_chain(tiles(flip), slabs, flipped, middle)
    _, q_other = half_chain(tiles(1 - flip), slabs, jnp.logical_not(flipped), middle)
    for k, entry in enumerate(entries):
        for n, kind in enumerate(KINDS):
            table[k, n] = entry[kind]
    table[blocks, 0] = 1.0 / (1.0 - q_own * q_other)
    table[blocks, 1] = q_other
    coef = lambda kind, k: table[k, KINDS.index(kind)]

    def group(g, carry):
        rows = pl.ds(pl.multiple_of(g * ROWS, ROWS), ROWS)
        for t in range(share // LANES):
            cols = slice(t * LANES, (t + 1) * LANES)
            firsts = [fl_ref[block[k], flip, rows, cols] for k in range(blocks)]
            lasts = [fl_ref[block[k], 1 - flip, rows, cols] for k in range(blocks - 1)]
            before = forward(coef, firsts[:-1], lasts)
            across = table[blocks, 0] * (other[rows, cols] + table[blocks, 1] * mine[rows, cols])
            outer, inner = backward(coef, firsts, before, across)
            for k in range(blocks):
                uv_ref[block[k], flip, rows, cols] = outer[k]
                uv_ref[block[k], 1 - flip, rows, cols] = inner[k]
        return carry

    lax.fori_loop(0, lines // ROWS, group, 0)


def second_half(half, fl, mine, other, slabs):
    parts, _, lines, share = fl.shape
    vmem = pl.BlockSpec(memory_space=pltpu.VMEM)
    return pl.pallas_call(
        functools.partial(second_kernel, slabs),
        in_specs=[pl.BlockSpec(memory_space=pltpu.SMEM), vmem, vmem, vmem],
        out_specs=[vmem, vmem],
        out_shape=[
            jax.ShapeDtypeStruct((parts, 2, lines - ROWS, share), jnp.float32),
            jax.ShapeDtypeStruct((2 * parts, ROWS, LANES), jnp.float32),
        ],
        scratch_shapes=[pltpu.VMEM((parts + 1, len(KINDS), ROWS, LANES), jnp.float32)],
        compiler_params=pltpu.CompilerParams(vmem_limit_bytes=VMEM_LIMIT),
        cost_estimate=pl.CostEstimate(flops=10 * fl.size, bytes_accessed=9 * fl.size, transcendentals=0),
        name="reduced_out",
    )(half, fl, mine, other)


def extras_kernel(
    table,
    where_am_i,
    info,
    shared,
    flux,
    inverse,
    well,
    holders,
    wells_ref,
    rows_ref,
    leaving,
    keep,
    force,
    rate,
    down,
    rise,
    pairs,
):
    blocks = shared.shape[0]
    slabs, wells = wells_ref.shape
    speed, inlet, reach = well[0:1], well[1:2], well[2:3]
    entries = [table[k] for k in range(table.shape[0])]
    level = lax.broadcasted_iota(jnp.int32, (slabs, wells), 0).astype(jnp.float32)
    for j in range(blocks):
        rock = shared[j, :slabs]
        cond = select_tree(shared[j, slabs : 2 * slabs].astype(jnp.int32), entries)
        here = jnp.where(level + float(j * slabs) < reach, speed * cond / (1.0 + cond), 0.0)
        rows = slice(j * slabs, (j + 1) * slabs)
        rate[rows] = here
        keep[rows] = 1.0 - here
        force[rows] = here * rock

    chunks = blocks * slabs // ROWS

    def descend(i, value):
        rows = pl.ds(pl.multiple_of(i * ROWS, ROWS), ROWS)
        a, b = keep[rows], force[rows]
        seen = []
        for r in range(ROWS):
            seen.append(value)
            value = a[r : r + 1] * value + b[r : r + 1]
        down[rows] = jnp.concatenate(seen, axis=0)
        return value

    def ascend(i, value):
        rows = pl.ds(pl.multiple_of((chunks - 1 - i) * ROWS, ROWS), ROWS)
        a, b = keep[rows], force[rows]
        seen = []
        for r in reversed(range(ROWS)):
            seen.append(value)
            value = a[r : r + 1] * value + b[r : r + 1]
        rise[rows] = jnp.concatenate(seen[::-1], axis=0)
        return value

    bottom = lax.fori_loop(0, chunks, descend, inlet)
    surface = lax.fori_loop(0, chunks, ascend, bottom)
    held = holders[...] == lax.broadcasted_iota(jnp.int32, (wells, holders.shape[1]), 0)
    leaving[...] = jnp.dot(
        jnp.broadcast_to(surface, (ROWS, wells)),
        held.astype(jnp.float32),
        precision=HIGHEST,
        preferred_element_type=jnp.float32,
    )[0:1]

    firsts, lasts = [], []
    for j in range(blocks):
        rows = slice(j * slabs, (j + 1) * slabs)
        taken = rate[rows] * (2.0 * shared[j, :slabs] - down[rows] - rise[rows])
        source = -storage_volume * taken
        force[rows] = source
        both = jnp.dot(
            info[j, :, :slabs], source, precision=HIGHEST, preferred_element_type=jnp.float32
        )
        firsts.append(both[0:1])
        lasts.append(both[1:2])

    scalars = [block_scalars(info[j], slabs, (1, wells)) for j in range(blocks)]
    zero = jnp.zeros((1, wells), jnp.float32)
    couple = [zero]
    for j in range(1, blocks):
        couple.append(
            coupling(scalars[j][1], scalars[j - 1][0][1, 1], scalars[j][0][0, 0], slabs)
        )
    couple.append(zero)
    coefs, _ = chain([corner for corner, _ in scalars], couple)
    coef = lambda kind, j: coefs[j][kind]
    d = where_am_i[0]
    row = lax.broadcasted_iota(jnp.int32, (slabs, wells), 0)

    def with_ends(value, above, below):
        return value + jnp.where(row == 0, above, 0.0) + jnp.where(row == slabs - 1, below, 0.0)

    dot = functools.partial(
        jnp.dot, precision=HIGHEST, preferred_element_type=jnp.float32
    )
    above, below = backward(coef, firsts, forward(coef, firsts, lasts), zero)
    for j in range(blocks):
        pairs[j, 0, 0:1] = above[j]
        pairs[j, 1, 0:1] = below[j]
    own = force[pl.ds(pl.multiple_of(d * slabs, slabs), slabs)]
    wells_ref[...] = dot(inverse[...], with_ends(own, pairs[d, 0, 0:1], pairs[d, 1, 0:1]))

    tiles = flux.shape[2] // wells
    start, count = 2 * slabs, 2 * tiles
    firsts = [shared[j, start : start + count] for j in range(blocks)]
    lasts = [shared[j, start + count : start + 2 * count] for j in range(blocks)]
    above, below = backward(coef, firsts, forward(coef, firsts, lasts), jnp.zeros_like(firsts[0]))
    for j in range(blocks):
        pairs[j, 0, :count] = above[j]
        pairs[j, 1, :count] = below[j]
    for n in range(2):
        for t in range(tiles):
            cols = slice(t * wells, (t + 1) * wells)
            at = n * tiles + t
            rows_ref[n, :, cols] = dot(
                inverse[...],
                with_ends(flux[n, :, cols], pairs[d, 0, at : at + 1], pairs[d, 1, at : at + 1]),
            )


def extras(table, depth_index, info, shared, flux, inverse, well, holders):
    blocks, _, wells = shared.shape
    _, slabs, span = flux.shape
    smem = pl.BlockSpec(memory_space=pltpu.SMEM)
    vmem = pl.BlockSpec(memory_space=pltpu.VMEM)
    column = pltpu.VMEM((blocks * slabs, wells), jnp.float32)
    count = -(-2 * (span // wells) // ROWS) * ROWS
    return pl.pallas_call(
        extras_kernel,
        in_specs=[smem, smem] + [vmem] * 6,
        out_specs=[vmem] * 3,
        out_shape=[
            jax.ShapeDtypeStruct((slabs, wells), jnp.float32),
            jax.ShapeDtypeStruct((2, slabs, span), jnp.float32),
            jax.ShapeDtypeStruct((1, holders.shape[1]), jnp.float32),
        ],
        scratch_shapes=[column] * 5 + [pltpu.VMEM((blocks, 2, count, wells), jnp.float32)],
        cost_estimate=pl.CostEstimate(flops=10**7, bytes_accessed=8 * shared.size, transcendentals=0),
        name="extras",
    )(table, depth_index.reshape(1), info, shared, flux, inverse, well, holders)


def solve_kernel(right, uv, inverse, place_row, place_column, solved_wells, outer, out, factor, pick):
    together, slabs, rows, span = right.shape
    wells = place_row.shape[1]
    step = pl.program_id(0)
    size = slabs * rows

    @pl.when(step == 0)
    def _():
        spread = (
            lax.broadcasted_iota(jnp.int32, (size, slabs), 0) // rows
            == lax.broadcasted_iota(jnp.int32, (size, slabs), 1)
        ).astype(jnp.float32).astype(jnp.bfloat16)
        spread_t = (
            lax.broadcasted_iota(jnp.int32, (slabs, size), 1) // rows
            == lax.broadcasted_iota(jnp.int32, (slabs, size), 0)
        ).astype(jnp.float32).astype(jnp.bfloat16)
        same = (
            lax.broadcasted_iota(jnp.int32, (size, size), 0) % rows
            == lax.broadcasted_iota(jnp.int32, (size, size), 1) % rows
        )
        for n, part in enumerate(split_bf16(inverse[...], 2)):
            tall = jnp.dot(spread, part, preferred_element_type=jnp.float32).astype(jnp.bfloat16)
            wide = jnp.dot(tall, spread_t, preferred_element_type=jnp.float32)
            wide = jnp.where(same, wide, 0.0).astype(jnp.bfloat16)
            if n == 0:
                factor[:, :size] = wide
                factor[:, size : 2 * size] = wide
            else:
                factor[:, 2 * size : 3 * size] = wide
        column = lax.broadcasted_iota(jnp.int32, (wells, span), 1)
        chosen = (column == place_column[...] % span).astype(jnp.float32).astype(jnp.bfloat16)
        pick[:wells] = chosen
        pick[wells:] = chosen

    tile = min(span, 256)
    for n in range(together):
        line = lax.broadcasted_iota(jnp.int32, (slabs, rows, wells), 1) + (step * together + n) * rows
        at_wells = jnp.where(line == (place_row[...] // span)[None], solved_wells[...][:, None, :], 0.0)
        at_wells = jnp.concatenate(split_bf16(at_wells.reshape(size, wells), 2), axis=1)
        factor[:, 3 * size :] = at_wells
        lines = slice(n * rows, (n + 1) * rows)
        above = jnp.concatenate([uv[d, 0, lines] for d in range(uv.shape[0])], axis=1)
        below = jnp.concatenate([uv[d, 1, lines] for d in range(uv.shape[0])], axis=1)
        for t in range(span // tile):
            cols = slice(t * tile, (t + 1) * tile)
            value = jnp.concatenate(
                [
                    right[n, 0:1, :, cols] + above[None, :, cols],
                    right[n, 1 : slabs - 1, :, cols],
                    right[n, slabs - 1 :, :, cols] + below[None, :, cols],
                ],
                axis=0,
            ).reshape(size, tile)
            upper, lower = split_bf16(value, 2)
            result = jnp.dot(
                factor[...],
                jnp.concatenate([upper, lower, upper, pick[:, cols]], axis=0),
                preferred_element_type=jnp.float32,
            )
            out[:, lines, cols] = result.reshape(slabs, rows, tile)

    for n, (when, line) in enumerate(((0, 0), (pl.num_programs(0) - 1, together * rows - 1))):

        @pl.when(step == when)
        def _():
            for z in range(slabs):
                out[z, line : line + 1, :] += outer[n, z : z + 1, :]


def solve(right, uv, inverse, place_row, solved_wells, outer):
    groups, slabs, _, span = right.shape
    wells = place_row.shape[1]
    together = 2
    lines = together * ROWS
    shares, _, _, share = uv.shape
    whole = lambda *shape: pl.BlockSpec(shape, lambda g: (0,) * len(shape))
    size = slabs * ROWS
    return pl.pallas_call(
        solve_kernel,
        grid=(groups // together,),
        in_specs=[
            pl.BlockSpec((together, slabs, ROWS, span), lambda g: (g, 0, 0, 0)),
            pl.BlockSpec((shares, 2, lines, share), lambda g: (0, 0, g, 0)),
            whole(slabs, slabs),
            whole(1, wells),
            whole(wells, 1),
            whole(slabs, wells),
            whole(*outer.shape),
        ],
        out_specs=pl.BlockSpec((slabs, lines, span), lambda g: (0, g, 0)),
        out_shape=jax.ShapeDtypeStruct((slabs, groups * ROWS, span), jnp.float32),
        scratch_shapes=[
            pltpu.VMEM((size, 3 * size + 2 * wells), jnp.bfloat16),
            pltpu.VMEM((2 * wells, span), jnp.bfloat16),
        ],
        compiler_params=pltpu.CompilerParams(vmem_limit_bytes=VMEM_LIMIT),
        cost_estimate=pl.CostEstimate(
            flops=8 * size * right.size, bytes_accessed=8 * right.size, transcendentals=0
        ),
        name="depth_solve",
    )(right, uv, inverse, place_row, place_row.reshape(wells, 1), solved_wells, outer)


def body(
    warmth_before,
    stratum_category,
    conductance_catalogue,
    pivot_matrix_reciprocal,
    linkage_factor,
    well_position_inside,
    well_holder_sequence,
    well_reach,
    entering_warmth,
    well_transfer_speed,
):
    slabs, lines, span = warmth_before.shape
    depth_index = lax.axis_index("depth")
    depth_count = lax.axis_size("depth")
    wells = well_position_inside.shape[0]
    owned = wells // depth_count
    table = conductance_catalogue

    parts = depth_count // 2
    halves = [list(range(h * parts, (h + 1) * parts)) for h in range(2)]
    half = (depth_index // parts).astype(jnp.int32).reshape(1)
    ends = jnp.stack([pivot_matrix_reciprocal[0], pivot_matrix_reciprocal[-1]])
    info = jnp.concatenate([ends, jnp.broadcast_to(linkage_factor[:, None], (2, 1))], axis=1)
    info = jnp.pad(info, ((0, ROWS - 2), (0, span // parts - info.shape[1])))

    place_row = well_position_inside.reshape(1, wells)
    right, fl, first, last, cells = stencil(
        warmth_before, stratum_category, table, ends, info, place_row, parts
    )
    exchange = functools.partial(
        lax.all_to_all, axis_name="depth", split_axis=0, concat_axis=0, tiled=True
    )
    fl_all = exchange(fl, axis_index_groups=halves)

    count = lax.axis_size("strip")
    up = [(i, i + 1) for i in range(count - 1)]
    down = [(j, i) for i, j in up]
    before = lax.ppermute(last, "strip", up)
    after = lax.ppermute(first, "strip", down)
    flux, shared = outer_flux(first, last, before, after, ends, cells, depth_count)
    fl_all, shared = lax.optimization_barrier((fl_all, shared))

    mine = first_half(half, fl_all, slabs)
    other = lax.ppermute(
        mine, "depth", [(i, (i + parts) % depth_count) for i in range(depth_count)]
    )
    shared = exchange(shared)
    uv, info_all = second_half(half, fl_all, mine, other, slabs)
    uv_own = exchange(uv, axis_index_groups=halves)

    well = jnp.stack([well_transfer_speed, entering_warmth, well_reach.astype(jnp.float32)])
    well = jnp.pad(well, ((0, ROWS - 3), (0, 0)))
    holders = lax.dynamic_slice_in_dim(well_holder_sequence, depth_index * owned, owned)
    solved_wells, outer, leaving = extras(
        table, depth_index, info_all, shared, flux, pivot_matrix_reciprocal, well, holders.reshape(1, owned)
    )
    solved = solve(right, uv_own, pivot_matrix_reciprocal, place_row, solved_wells, outer)
    return solved, leaving.reshape(owned)


def solution(mesh):
    in_specs = (
        P("depth", "strip", None),
        P("depth", "strip", None),
        P(),
        P("depth", None),
        P("depth"),
        P("strip"),
        P("strip"),
        P("strip"),
        P("strip"),
        P("strip"),
    )
    out_specs = (P("depth", "strip", None), P(("strip", "depth")))
    return jax.shard_map(body, mesh=mesh, in_specs=in_specs, out_specs=out_specs, check_vma=False)
```

```python
import functools

import jax
import jax.numpy as jnp
from jax import lax
from jax.experimental import pallas as pl
from jax.experimental.pallas import tpu as pltpu
from jax.sharding import PartitionSpec as P

backward_euler_advance = 0.2
storage_volume = 2.0
flux_scale = 0.5 * backward_euler_advance
LANES = 128
ROWS = 8
VMEM_LIMIT = 48 * 1024 * 1024
SOLVE_VMEM = 32 * 1024 * 1024
SMALL_VMEM = 12 * 1024 * 1024
HIGHEST = lax.Precision.HIGHEST


def select_tree(category, entries):
    values = list(entries)
    bit = 1
    while len(values) > 1:
        odd = (category & bit) != 0
        values = [
            jnp.where(odd, values[k + 1], values[k]) if k + 1 < len(values) else values[k]
            for k in range(0, len(values), 2)
        ]
        bit *= 2
    return values[0]


def split_bf16(value, pieces):
    out = []
    for k in range(pieces):
        part = value.astype(jnp.bfloat16)
        out.append(part)
        if k + 1 < pieces:
            value = value - part.astype(jnp.float32)
    return out


def stencil_kernel(
    table,
    ends,
    ratio,
    w_ref,
    cat_ref,
    place,
    inverse,
    right_ref,
    fl_ref,
    first_ref,
    last_ref,
    cells_ref,
    acc,
    ws,
    cs,
    fs,
    pieces,
    shift,
    pick,
    edges,
):
    step = pl.program_id(0)
    planes, lines, span = w_ref.shape
    tiles = span // LANES
    groups = lines // ROWS
    wells = place.shape[1]
    entries = [flux_scale * table[k] for k in range(table.shape[0])]
    lane = lax.broadcasted_iota(jnp.int32, (lines, LANES), 1)
    top, end = ROWS, ROWS + lines

    @pl.when(step == 0)
    def _():
        acc[...] = jnp.zeros_like(acc)
        source = lax.broadcasted_iota(jnp.int32, shift.shape, 0) % (2 * LANES)
        target = lax.broadcasted_iota(jnp.int32, shift.shape, 1)
        shift[...] = (source == target + 1).astype(jnp.float32).astype(jnp.bfloat16)
        column = lax.broadcasted_iota(jnp.int32, (span, wells), 0)
        pick[...] = (column == place[...] % span).astype(jnp.float32).astype(jnp.bfloat16)

    def keep_face(k, t, face):
        rows = pl.ds(pl.multiple_of(k * lines, lines), lines)
        for n, part in enumerate(split_bf16(face, 2)):
            pieces[n, rows, t * LANES : (t + 1) * LANES] = part

    def plane(k, carry):
        left_w = left_c = jnp.zeros((lines, LANES), jnp.float32)
        for t in range(tiles):
            cols = slice(t * LANES, (t + 1) * LANES)
            w = w_ref[k, :, cols]
            c = select_tree(cat_ref[k, :, cols], entries)
            for n, (ref, value) in enumerate(((ws, w), (cs, c))):
                ref[t, top:end] = value
                edge_first, edge_last = value[0:1], value[lines - 1 : lines]
                ref[t, top - 1 : top] = edge_first
                ref[t, end : end + 1] = edge_last
                edges[k, n : n + 1, cols] = edge_first
                edges[k, n + 2 : n + 3, cols] = edge_last
            roll_w, roll_c = pltpu.roll(w, 1, 1), pltpu.roll(c, 1, 1)
            west_w = jnp.where(lane == 0, left_w, roll_w)
            west_c = jnp.where(lane == 0, left_c, roll_c)
            left_w, left_c = roll_w, roll_c
            face = (c + west_c) * (w - west_w)
            keep_face(k, t, face)
            if t == tiles - 1:
                keep_face(k, tiles, pltpu.roll(-c * w, 1, 1))
            north = (c + cs[t, top - 1 : end - 1]) * (w - ws[t, top - 1 : end - 1])
            fs[t, top:end] = north
            fs[t, end : end + 1] = jnp.zeros((1, LANES), jnp.float32)
            base = w - face - north + fs[t, top + 1 : end + 1]
            right_ref[:, k, :, cols] = base.reshape(groups, ROWS, LANES)
        return carry

    lax.fori_loop(0, planes, plane, 0)

    for t in range(tiles):
        cols = slice(t * LANES, (t + 1) * LANES)
        both = slice(t * LANES, (t + 2) * LANES)
        east = jnp.dot(
            jnp.concatenate([pieces[0, :, both], pieces[1, :, both]], axis=1),
            shift[...],
            preferred_element_type=jnp.float32,
        )
        first, final = acc[0, :, cols], acc[1, :, cols]
        for k in range(planes):
            z = step * planes + k
            value = right_ref[:, k, :, cols].reshape(lines, LANES) + east[k * lines : (k + 1) * lines]
            right_ref[:, k, :, cols] = value.reshape(groups, ROWS, LANES)
            first = first + ends[0, z] * value
            final = final + ends[ends.shape[0] - 1, z] * value
        acc[0, :, cols] = first
        acc[1, :, cols] = final

    for k in range(planes):
        for n in range(2):
            first_ref[n, k : k + 1, :] = edges[k, n : n + 1, :]
            last_ref[n, k : k + 1, :] = edges[k, n + 2 : n + 3, :]

    dot = functools.partial(jnp.dot, preferred_element_type=jnp.float32)
    own_line = lax.broadcasted_iota(jnp.int32, (lines, wells), 0) == place[...] // span
    upper, lower = split_bf16(w_ref[...].reshape(planes * lines, span), 2)
    kinds = cat_ref[...].astype(jnp.float32).reshape(planes * lines, span).astype(jnp.bfloat16)
    sums = [dot(upper, pick[...]) + dot(lower, pick[...]), dot(kinds, pick[...])]
    for n in range(2):
        for k in range(planes):
            mine = jnp.where(own_line, sums[n][k * lines : (k + 1) * lines], 0.0)
            cells_ref[0, n, k : k + 1, :] = jnp.sum(mine, axis=0, keepdims=True)
    for d in range(1, cells_ref.shape[0]):
        cells_ref[d] = cells_ref[0]

    @pl.when(step == pl.num_programs(0) - 1)
    def _():
        share = fl_ref.shape[-1]
        slabs = inverse.shape[0]
        for d in range(fl_ref.shape[0]):
            fl_ref[d, :, :lines] = acc[:, :, d * share : (d + 1) * share]
            fl_ref[d, :, lines:] = jnp.zeros((2, ROWS, share), jnp.float32)
            fl_ref[d, 0, lines : lines + 1, :slabs] = inverse[0:1]
            fl_ref[d, 0, lines + 1 : lines + 2, :slabs] = inverse[slabs - 1 : slabs]
            fl_ref[d, 0, lines : lines + 1, slabs : slabs + 1] = jnp.full((1, 1), ratio[0])


def stencil(w, cat, table, inverse, ratio, place_row, parts):
    slabs, lines, span = w.shape
    planes, groups = 8, lines // ROWS
    wells = place_row.shape[1]
    block = pl.BlockSpec((planes, lines, span), lambda i: (i, 0, 0))
    edge = pl.BlockSpec((2, planes, span), lambda i: (0, i, 0))
    fl_shape = (parts, 2, lines + ROWS, span // parts)
    smem = pl.BlockSpec(memory_space=pltpu.SMEM)
    shifted = pltpu.VMEM((span // LANES, lines + 2 * ROWS, LANES), jnp.float32)
    return pl.pallas_call(
        stencil_kernel,
        grid=(slabs // planes,),
        in_specs=[
            smem,
            smem,
            smem,
            block,
            block,
            pl.BlockSpec((1, wells), lambda i: (0, 0)),
            pl.BlockSpec(inverse.shape, lambda i: (0, 0)),
        ],
        out_specs=[
            pl.BlockSpec((groups, planes, ROWS, span), lambda i: (0, i, 0, 0)),
            pl.BlockSpec(fl_shape, lambda i: (0, 0, 0, 0)),
            edge,
            edge,
            pl.BlockSpec((2 * parts, 2, planes, wells), lambda i: (0, 0, i, 0)),
        ],
        out_shape=[
            jax.ShapeDtypeStruct((groups, slabs, ROWS, span), jnp.float32),
            jax.ShapeDtypeStruct(fl_shape, jnp.float32),
            jax.ShapeDtypeStruct((2, slabs, span), jnp.float32),
            jax.ShapeDtypeStruct((2, slabs, span), jnp.float32),
            jax.ShapeDtypeStruct((2 * parts, 2, slabs, wells), jnp.float32),
        ],
        scratch_shapes=[
            pltpu.VMEM((2, lines, span), jnp.float32),
            shifted,
            shifted,
            shifted,
            pltpu.VMEM((2, planes * lines, span + LANES), jnp.bfloat16),
            pltpu.VMEM((4 * LANES, LANES), jnp.bfloat16),
            pltpu.VMEM((span, wells), jnp.bfloat16),
            pltpu.VMEM((planes, 4, span), jnp.float32),
        ],
        compiler_params=pltpu.CompilerParams(vmem_limit_bytes=VMEM_LIMIT),
        cost_estimate=pl.CostEstimate(flops=40 * w.size, bytes_accessed=12 * w.size, transcendentals=0),
        name="stencil",
    )(table, inverse, ratio, w, cat, place_row, inverse)


def outer_flux_kernel(first, last, before, after, inverse, flux_ref, out_ref):
    copies, _, lanes = out_ref.shape
    slabs, span = first.shape[1:]
    tiles = span // lanes
    ends = jnp.concatenate([inverse[0:1], inverse[slabs - 1 : slabs]], axis=0)
    for n, (own, other) in enumerate(((first, before), (last, after))):
        flux = (own[1] + other[1]) * (other[0] - own[0])
        flux_ref[n] = flux
        sums = jnp.dot(ends, flux, precision=HIGHEST, preferred_element_type=jnp.float32)
        for q in range(2):
            for t in range(tiles):
                row = (2 * q + n) * tiles + t
                out_ref[0, row : row + 1] = sums[q : q + 1, t * lanes : (t + 1) * lanes]
    for d in range(1, copies):
        out_ref[d] = out_ref[0]


def outer_flux(first, last, before, after, inverse, copies):
    _, slabs, span = first.shape
    vmem = pl.BlockSpec(memory_space=pltpu.VMEM)
    return pl.pallas_call(
        outer_flux_kernel,
        in_specs=[vmem] * 5,
        out_specs=[vmem] * 2,
        out_shape=[
            jax.ShapeDtypeStruct((2, slabs, span), jnp.float32),
            jax.ShapeDtypeStruct((copies, 4 * (span // LANES), LANES), jnp.float32),
        ],
        compiler_params=pltpu.CompilerParams(vmem_limit_bytes=SMALL_VMEM),
        cost_estimate=pl.CostEstimate(flops=10**6, bytes_accessed=10**6, transcendentals=0),
        name="outer_flux",
    )(first, last, before, after, inverse)


CORNERS = ((0, 0), (0, 1), (1, 0), (1, 1))


def block_scalars(tile, slabs, shape, flipped=None):
    at = lambda row, lane: jnp.broadcast_to(tile[row : row + 1, lane : lane + 1], shape)
    corner = {(r, c): at(r, c * (slabs - 1)) for r, c in CORNERS}
    if flipped is not None:
        corner = {(r, c): jnp.where(flipped, corner[1 - r, 1 - c], corner[r, c]) for r, c in CORNERS}
    return corner, at(0, slabs)


def coupling(ratio, one, other, slabs):
    return ratio * (slabs / (slabs + 1.0)) / jnp.sqrt(one * other)


def chain(corners, couple, q=None):
    out = []
    q = jnp.zeros_like(couple[0])
    for k, corner in enumerate(corners):
        vf, vl = couple[k] * corner[0, 0], couple[k] * corner[1, 0]
        wf, wl = couple[k + 1] * corner[0, 1], couple[k + 1] * corner[1, 1]
        inverse = 1.0 / (1.0 - vf * q)
        out.append(
            dict(
                p_first=vl * q * inverse,
                p_before=vl * inverse,
                a_first=inverse,
                a_before=vf * inverse,
                a_after=wf * inverse,
                couple=couple[k],
                couple_after=couple[k + 1],
                q=q,
            )
        )
        q = wl + vl * q * wf * inverse
    return out, q


KINDS = ("p_first", "p_before", "a_first", "a_before", "a_after", "couple", "couple_after", "q")


def forward(coef, firsts, lasts):
    before = [jnp.zeros_like(firsts[0])]
    for j in range(len(firsts)):
        before.append(
            lasts[j] + coef("p_first", j) * firsts[j] + coef("p_before", j) * before[j]
        )
    return before


def backward(coef, firsts, before, after):
    blocks = len(firsts)
    above, below = [None] * blocks, [None] * blocks
    for j in reversed(range(blocks)):
        below[j] = coef("couple_after", j) * after
        here = (
            coef("a_first", j) * firsts[j]
            + coef("a_before", j) * before[j]
            + coef("a_after", j) * after
        )
        above[j] = coef("couple", j) * (before[j] + coef("q", j) * here)
        after = here
    return above, below


def half_chain(tiles, slabs, flipped, middle):
    shape = (ROWS, LANES)
    scalars = [block_scalars(tile, slabs, shape, flipped) for tile in tiles]
    couple = [jnp.zeros(shape, jnp.float32)]
    for k in range(1, len(tiles)):
        ratio = jnp.where(flipped, scalars[k - 1][1], scalars[k][1])
        couple.append(coupling(ratio, scalars[k - 1][0][1, 1], scalars[k][0][0, 0], slabs))
    couple.append(middle)
    return chain([corner for corner, _ in scalars], couple)


def first_kernel(slabs, half, fl_ref, out_ref, table):
    blocks, _, lines, share = fl_ref.shape
    lines = lines - ROWS
    flip = half[0]
    flipped = flip == 1
    block = [k + flip * (blocks - 1 - 2 * k) for k in range(blocks)]
    entries, _ = half_chain(
        [fl_ref[block[k], 0, lines:, :LANES] for k in range(blocks)],
        slabs,
        flipped,
        jnp.zeros((ROWS, LANES), jnp.float32),
    )
    for k, entry in enumerate(entries):
        for n, kind in enumerate(KINDS[:2]):
            table[k, n] = entry[kind]
    coef = lambda kind, k: table[k, KINDS.index(kind)]

    def group(g, carry):
        rows = pl.ds(pl.multiple_of(g * ROWS, ROWS), ROWS)
        for t in range(share // LANES):
            cols = slice(t * LANES, (t + 1) * LANES)
            before = forward(
                coef,
                [fl_ref[block[k], flip, rows, cols] for k in range(blocks)],
                [fl_ref[block[k], 1 - flip, rows, cols] for k in range(blocks)],
            )
            out_ref[rows, cols] = before[blocks]
        return carry

    lax.fori_loop(0, lines // ROWS, group, 0)
    out_ref[lines:, :] = jnp.zeros((out_ref.shape[0] - lines, share), jnp.float32)
    for j in range(blocks):
        out_ref[lines + 2 * j : lines + 2 * j + 2, :] = fl_ref[j, 0, lines : lines + 2, :]


def first_half(half, fl, slabs):
    parts, _, lines, share = fl.shape
    vmem = pl.BlockSpec(memory_space=pltpu.VMEM)
    rows = lines - ROWS + -(-2 * parts // ROWS) * ROWS
    return pl.pallas_call(
        functools.partial(first_kernel, slabs),
        in_specs=[pl.BlockSpec(memory_space=pltpu.SMEM), vmem],
        out_specs=vmem,
        out_shape=jax.ShapeDtypeStruct((rows, share), jnp.float32),
        scratch_shapes=[pltpu.VMEM((parts, 2, ROWS, LANES), jnp.float32)],
        compiler_params=pltpu.CompilerParams(vmem_limit_bytes=SMALL_VMEM),
        cost_estimate=pl.CostEstimate(flops=4 * fl.size, bytes_accessed=5 * fl.size, transcendentals=0),
        name="reduced_in",
    )(half, fl)


def second_kernel(slabs, half, fl_ref, mine, other, uv_ref, info_ref, table):
    blocks, _, lines, share = fl_ref.shape
    lines = lines - ROWS
    flip = half[0]
    flipped = flip == 1
    block = [k + flip * (blocks - 1 - 2 * k) for k in range(blocks)]
    for j in range(blocks):
        info_ref[flip * blocks + j] = fl_ref[j, 0, lines:, :LANES]
        info_ref[(1 - flip) * blocks + j] = jnp.zeros((ROWS, LANES), jnp.float32)
        info_ref[(1 - flip) * blocks + j, 0:2] = other[lines + 2 * j : lines + 2 * j + 2, :LANES]
    shape = (ROWS, LANES)
    above, above_ratio = block_scalars(info_ref[blocks - 1], slabs, shape)
    below, below_ratio = block_scalars(info_ref[blocks], slabs, shape)
    middle = coupling(below_ratio, above[1, 1], below[0, 0], slabs)
    tiles = lambda flip: [
        info_ref[flip * blocks + k + flip * (blocks - 1 - 2 * k)] for k in range(blocks)
    ]
    entries, q_own = half_chain(tiles(flip), slabs, flipped, middle)
    _, q_other = half_chain(tiles(1 - flip), slabs, jnp.logical_not(flipped), middle)
    for k, entry in enumerate(entries):
        for n, kind in enumerate(KINDS):
            table[k, n] = entry[kind]
    table[blocks, 0] = 1.0 / (1.0 - q_own * q_other)
    table[blocks, 1] = q_other
    coef = lambda kind, k: table[k, KINDS.index(kind)]

    def group(g, carry):
        rows = pl.ds(pl.multiple_of(g * ROWS, ROWS), ROWS)
        for t in range(share // LANES):
            cols = slice(t * LANES, (t + 1) * LANES)
            firsts = [fl_ref[block[k], flip, rows, cols] for k in range(blocks)]
            lasts = [fl_ref[block[k], 1 - flip, rows, cols] for k in range(blocks - 1)]
            before = forward(coef, firsts[:-1], lasts)
            across = table[blocks, 0] * (other[rows, cols] + table[blocks, 1] * mine[rows, cols])
            outer, inner = backward(coef, firsts, before, across)
            for k in range(blocks):
                uv_ref[block[k], flip, rows, cols] = outer[k]
                uv_ref[block[k], 1 - flip, rows, cols] = inner[k]
        return carry

    lax.fori_loop(0, lines // ROWS, group, 0)


def second_half(half, fl, mine, other, slabs):
    parts, _, lines, share = fl.shape
    vmem = pl.BlockSpec(memory_space=pltpu.VMEM)
    return pl.pallas_call(
        functools.partial(second_kernel, slabs),
        in_specs=[pl.BlockSpec(memory_space=pltpu.SMEM), vmem, vmem, vmem],
        out_specs=[vmem, vmem],
        out_shape=[
            jax.ShapeDtypeStruct((parts, 2, lines - ROWS, share), jnp.float32),
            jax.ShapeDtypeStruct((2 * parts, ROWS, LANES), jnp.float32),
        ],
        scratch_shapes=[pltpu.VMEM((parts + 1, len(KINDS), ROWS, LANES), jnp.float32)],
        compiler_params=pltpu.CompilerParams(vmem_limit_bytes=SMALL_VMEM),
        cost_estimate=pl.CostEstimate(flops=10 * fl.size, bytes_accessed=9 * fl.size, transcendentals=0),
        name="reduced_out",
    )(half, fl, mine, other)


def extras_kernel(
    table,
    where_am_i,
    info,
    cells,
    outside,
    flux,
    inverse,
    well,
    holders,
    wells_ref,
    rows_ref,
    leaving,
    keep,
    force,
    rate,
    down,
    rise,
    pairs,
):
    blocks = cells.shape[0]
    slabs, wells = wells_ref.shape
    speed, inlet, reach = well[0:1], well[1:2], well[2:3]
    entries = [table[k] for k in range(table.shape[0])]
    level = lax.broadcasted_iota(jnp.int32, (slabs, wells), 0).astype(jnp.float32)
    for j in range(blocks):
        rock = cells[j, 0]
        cond = select_tree(cells[j, 1].astype(jnp.int32), entries)
        here = jnp.where(level + float(j * slabs) < reach, speed * cond / (1.0 + cond), 0.0)
        rows = slice(j * slabs, (j + 1) * slabs)
        rate[rows] = here
        keep[rows] = 1.0 - here
        force[rows] = here * rock

    chunks = blocks * slabs // ROWS

    def descend(i, value):
        rows = pl.ds(pl.multiple_of(i * ROWS, ROWS), ROWS)
        a, b = keep[rows], force[rows]
        seen = []
        for r in range(ROWS):
            seen.append(value)
            value = a[r : r + 1] * value + b[r : r + 1]
        down[rows] = jnp.concatenate(seen, axis=0)
        return value

    def ascend(i, value):
        rows = pl.ds(pl.multiple_of((chunks - 1 - i) * ROWS, ROWS), ROWS)
        a, b = keep[rows], force[rows]
        seen = []
        for r in reversed(range(ROWS)):
            seen.append(value)
            value = a[r : r + 1] * value + b[r : r + 1]
        rise[rows] = jnp.concatenate(seen[::-1], axis=0)
        return value

    bottom = lax.fori_loop(0, chunks, descend, inlet)
    surface = lax.fori_loop(0, chunks, ascend, bottom)
    held = holders[...] == lax.broadcasted_iota(jnp.int32, (wells, holders.shape[1]), 0)
    leaving[...] = jnp.dot(
        jnp.broadcast_to(surface, (ROWS, wells)),
        held.astype(jnp.float32),
        precision=HIGHEST,
        preferred_element_type=jnp.float32,
    )[0:1]

    firsts, lasts = [], []
    for j in range(blocks):
        rows = slice(j * slabs, (j + 1) * slabs)
        taken = rate[rows] * (2.0 * cells[j, 0] - down[rows] - rise[rows])
        source = -storage_volume * taken
        force[rows] = source
        both = jnp.dot(
            info[j, :, :slabs], source, precision=HIGHEST, preferred_element_type=jnp.float32
        )
        firsts.append(both[0:1])
        lasts.append(both[1:2])

    scalars = [block_scalars(info[j], slabs, (1, wells)) for j in range(blocks)]
    zero = jnp.zeros((1, wells), jnp.float32)
    couple = [zero]
    for j in range(1, blocks):
        couple.append(
            coupling(scalars[j][1], scalars[j - 1][0][1, 1], scalars[j][0][0, 0], slabs)
        )
    couple.append(zero)
    coefs, _ = chain([corner for corner, _ in scalars], couple)
    coef = lambda kind, j: coefs[j][kind]
    d = where_am_i[0]
    row = lax.broadcasted_iota(jnp.int32, (slabs, wells), 0)

    def with_ends(value, above, below):
        return value + jnp.where(row == 0, above, 0.0) + jnp.where(row == slabs - 1, below, 0.0)

    dot = functools.partial(
        jnp.dot, precision=HIGHEST, preferred_element_type=jnp.float32
    )
    above, below = backward(coef, firsts, forward(coef, firsts, lasts), zero)
    for j in range(blocks):
        pairs[j, 0, 0:1] = above[j]
        pairs[j, 1, 0:1] = below[j]
    own = force[pl.ds(pl.multiple_of(d * slabs, slabs), slabs)]
    wells_ref[...] = dot(inverse[...], with_ends(own, pairs[d, 0, 0:1], pairs[d, 1, 0:1]))

    tiles = flux.shape[2] // wells
    count = 2 * tiles
    firsts = [outside[j, :count] for j in range(blocks)]
    lasts = [outside[j, count : 2 * count] for j in range(blocks)]
    above, below = backward(coef, firsts, forward(coef, firsts, lasts), jnp.zeros_like(firsts[0]))
    for j in range(blocks):
        pairs[j, 0, :count] = above[j]
        pairs[j, 1, :count] = below[j]
    for n in range(2):
        for t in range(tiles):
            cols = slice(t * wells, (t + 1) * wells)
            at = n * tiles + t
            rows_ref[n, :, cols] = dot(
                inverse[...],
                with_ends(flux[n, :, cols], pairs[d, 0, at : at + 1], pairs[d, 1, at : at + 1]),
            )


def extras(table, depth_index, info, cells, outside, flux, inverse, well, holders):
    blocks, _, _, wells = cells.shape
    _, slabs, span = flux.shape
    smem = pl.BlockSpec(memory_space=pltpu.SMEM)
    vmem = pl.BlockSpec(memory_space=pltpu.VMEM)
    column = pltpu.VMEM((blocks * slabs, wells), jnp.float32)
    count = -(-2 * (span // wells) // ROWS) * ROWS
    return pl.pallas_call(
        extras_kernel,
        in_specs=[smem, smem] + [vmem] * 7,
        out_specs=[vmem] * 3,
        out_shape=[
            jax.ShapeDtypeStruct((slabs, wells), jnp.float32),
            jax.ShapeDtypeStruct((2, slabs, span), jnp.float32),
            jax.ShapeDtypeStruct((1, holders.shape[1]), jnp.float32),
        ],
        scratch_shapes=[column] * 5 + [pltpu.VMEM((blocks, 2, count, wells), jnp.float32)],
        compiler_params=pltpu.CompilerParams(vmem_limit_bytes=SMALL_VMEM),
        cost_estimate=pl.CostEstimate(flops=10**7, bytes_accessed=8 * cells.size, transcendentals=0),
        name="extras",
    )(table, depth_index.reshape(1), info, cells, outside, flux, inverse, well, holders)


def solve_kernel(right, uv, inverse, place_row, place_column, solved_wells, outer, out, factor, pick):
    together, slabs, rows, span = right.shape
    wells = place_row.shape[1]
    step = pl.program_id(0)
    size = slabs * rows

    @pl.when(step == 0)
    def _():
        spread = (
            lax.broadcasted_iota(jnp.int32, (size, slabs), 0) // rows
            == lax.broadcasted_iota(jnp.int32, (size, slabs), 1)
        ).astype(jnp.float32).astype(jnp.bfloat16)
        spread_t = (
            lax.broadcasted_iota(jnp.int32, (slabs, size), 1) // rows
            == lax.broadcasted_iota(jnp.int32, (slabs, size), 0)
        ).astype(jnp.float32).astype(jnp.bfloat16)
        same = (
            lax.broadcasted_iota(jnp.int32, (size, size), 0) % rows
            == lax.broadcasted_iota(jnp.int32, (size, size), 1) % rows
        )
        for n, part in enumerate(split_bf16(inverse[...], 2)):
            tall = jnp.dot(spread, part, preferred_element_type=jnp.float32).astype(jnp.bfloat16)
            wide = jnp.dot(tall, spread_t, preferred_element_type=jnp.float32)
            wide = jnp.where(same, wide, 0.0).astype(jnp.bfloat16)
            if n == 0:
                factor[:, :size] = wide
                factor[:, size : 2 * size] = wide
            else:
                factor[:, 2 * size : 3 * size] = wide
        column = lax.broadcasted_iota(jnp.int32, (wells, span), 1)
        chosen = (column == place_column[...] % span).astype(jnp.float32).astype(jnp.bfloat16)
        pick[:wells] = chosen
        pick[wells:] = chosen

    tile = min(span, 256)
    for n in range(together):
        line = lax.broadcasted_iota(jnp.int32, (slabs, rows, wells), 1) + (step * together + n) * rows
        at_wells = jnp.where(line == (place_row[...] // span)[None], solved_wells[...][:, None, :], 0.0)
        at_wells = jnp.concatenate(split_bf16(at_wells.reshape(size, wells), 2), axis=1)
        factor[:, 3 * size :] = at_wells
        lines = slice(n * rows, (n + 1) * rows)
        above = jnp.concatenate([uv[d, 0, lines] for d in range(uv.shape[0])], axis=1)
        below = jnp.concatenate([uv[d, 1, lines] for d in range(uv.shape[0])], axis=1)
        for t in range(span // tile):
            cols = slice(t * tile, (t + 1) * tile)
            value = jnp.concatenate(
                [
                    right[n, 0:1, :, cols] + above[None, :, cols],
                    right[n, 1 : slabs - 1, :, cols],
                    right[n, slabs - 1 :, :, cols] + below[None, :, cols],
                ],
                axis=0,
            ).reshape(size, tile)
            upper, lower = split_bf16(value, 2)
            result = jnp.dot(
                factor[...],
                jnp.concatenate([upper, lower, upper, pick[:, cols]], axis=0),
                preferred_element_type=jnp.float32,
            )
            out[:, lines, cols] = result.reshape(slabs, rows, tile)

    for n, (when, line) in enumerate(((0, 0), (pl.num_programs(0) - 1, together * rows - 1))):

        @pl.when(step == when)
        def _():
            for z in range(slabs):
                out[z, line : line + 1, :] += outer[n, z : z + 1, :]


def solve(right, uv, inverse, place_row, solved_wells, outer):
    groups, slabs, _, span = right.shape
    wells = place_row.shape[1]
    together = 2
    lines = together * ROWS
    shares, _, _, share = uv.shape
    whole = lambda *shape: pl.BlockSpec(shape, lambda g: (0,) * len(shape))
    size = slabs * ROWS
    return pl.pallas_call(
        solve_kernel,
        grid=(groups // together,),
        in_specs=[
            pl.BlockSpec((together, slabs, ROWS, span), lambda g: (g, 0, 0, 0)),
            pl.BlockSpec((shares, 2, lines, share), lambda g: (0, 0, g, 0)),
            whole(slabs, slabs),
            whole(1, wells),
            whole(wells, 1),
            whole(slabs, wells),
            whole(*outer.shape),
        ],
        out_specs=pl.BlockSpec((slabs, lines, span), lambda g: (0, g, 0)),
        out_shape=jax.ShapeDtypeStruct((slabs, groups * ROWS, span), jnp.float32),
        scratch_shapes=[
            pltpu.VMEM((size, 3 * size + 2 * wells), jnp.bfloat16),
            pltpu.VMEM((2 * wells, span), jnp.bfloat16),
        ],
        compiler_params=pltpu.CompilerParams(vmem_limit_bytes=SOLVE_VMEM),
        cost_estimate=pl.CostEstimate(
            flops=8 * size * right.size, bytes_accessed=8 * right.size, transcendentals=0
        ),
        name="depth_solve",
    )(right, uv, inverse, place_row, place_row.reshape(wells, 1), solved_wells, outer)


def body(
    warmth_before,
    stratum_category,
    conductance_catalogue,
    pivot_matrix_reciprocal,
    linkage_factor,
    well_position_inside,
    well_holder_sequence,
    well_reach,
    entering_warmth,
    well_transfer_speed,
):
    slabs, lines, span = warmth_before.shape
    depth_index = lax.axis_index("depth")
    depth_count = lax.axis_size("depth")
    wells = well_position_inside.shape[0]
    owned = wells // depth_count
    table = conductance_catalogue

    parts = depth_count // 2
    halves = [list(range(h * parts, (h + 1) * parts)) for h in range(2)]
    half = (depth_index // parts).astype(jnp.int32).reshape(1)

    place_row = well_position_inside.reshape(1, wells)
    right, fl, first, last, cells = stencil(
        warmth_before,
        stratum_category,
        table,
        pivot_matrix_reciprocal,
        linkage_factor,
        place_row,
        parts,
    )
    exchange = functools.partial(
        lax.all_to_all, axis_name="depth", split_axis=0, concat_axis=0, tiled=True
    )
    fl_all = exchange(fl, axis_index_groups=halves)

    count = lax.axis_size("strip")
    up = [(i, i + 1) for i in range(count - 1)]
    down = [(j, i) for i, j in up]
    before = lax.ppermute(last, "strip", up)
    after = lax.ppermute(first, "strip", down)
    cells = exchange(cells)
    flux, outside = outer_flux(first, last, before, after, pivot_matrix_reciprocal, depth_count)
    fl_all, cells, outside = lax.optimization_barrier((fl_all, cells, outside))

    mine = first_half(half, fl_all, slabs)
    mine, outside = lax.optimization_barrier((mine, outside))
    other = lax.ppermute(
        mine, "depth", [(i, (i + parts) % depth_count) for i in range(depth_count)]
    )
    outside = exchange(outside)
    uv, info_all = second_half(half, fl_all, mine, other, slabs)
    uv_own = exchange(uv, axis_index_groups=halves)

    well = jnp.stack([well_transfer_speed, entering_warmth, well_reach.astype(jnp.float32)])
    well = jnp.pad(well, ((0, ROWS - 3), (0, 0)))
    holders = lax.dynamic_slice_in_dim(well_holder_sequence, depth_index * owned, owned)
    solved_wells, outer, leaving = extras(
        table,
        depth_index,
        info_all,
        cells,
        outside,
        flux,
        pivot_matrix_reciprocal,
        well,
        holders.reshape(1, owned),
    )
    solved = solve(right, uv_own, pivot_matrix_reciprocal, place_row, solved_wells, outer)
    return solved, leaving.reshape(owned)


def solution(mesh):
    in_specs = (
        P("depth", "strip", None),
        P("depth", "strip", None),
        P(),
        P("depth", None),
        P("depth"),
        P("strip"),
        P("strip"),
        P("strip"),
        P("strip"),
        P("strip"),
    )
    out_specs = (P("depth", "strip", None), P(("strip", "depth")))
    return jax.shard_map(body, mesh=mesh, in_specs=in_specs, out_specs=out_specs, check_vma=False)
```

```python
import functools

import jax
import jax.numpy as jnp
from jax import lax
from jax.experimental import pallas as pl
from jax.experimental.pallas import tpu as pltpu
from jax.sharding import PartitionSpec as P

backward_euler_advance = 0.2
storage_volume = 2.0
flux_scale = 0.5 * backward_euler_advance
LANES = 128
ROWS = 8
VMEM_LIMIT = 48 * 1024 * 1024
SOLVE_VMEM = 32 * 1024 * 1024
SMALL_VMEM = 12 * 1024 * 1024
HIGHEST = lax.Precision.HIGHEST


def select_tree(category, entries):
    values = list(entries)
    bit = 1
    while len(values) > 1:
        odd = (category & bit) != 0
        values = [
            jnp.where(odd, values[k + 1], values[k]) if k + 1 < len(values) else values[k]
            for k in range(0, len(values), 2)
        ]
        bit *= 2
    return values[0]


def split_bf16(value, pieces):
    out = []
    for k in range(pieces):
        part = value.astype(jnp.bfloat16)
        out.append(part)
        if k + 1 < pieces:
            value = value - part.astype(jnp.float32)
    return out


def stencil_kernel(
    table,
    ends,
    w_ref,
    cat_ref,
    place,
    right_ref,
    acc,
    first_ref,
    last_ref,
    cells_ref,
    ws,
    cs,
    fs,
    pieces,
    shift,
    pick,
    edges,
):
    step = pl.program_id(0)
    planes, lines, span = w_ref.shape
    tiles = span // LANES
    groups = lines // ROWS
    wells = place.shape[1]
    entries = [flux_scale * table[k] for k in range(table.shape[0])]
    lane = lax.broadcasted_iota(jnp.int32, (lines, LANES), 1)
    top, end = ROWS, ROWS + lines

    @pl.when(step == 0)
    def _():
        acc[...] = jnp.zeros_like(acc)
        source = lax.broadcasted_iota(jnp.int32, shift.shape, 0) % (2 * LANES)
        target = lax.broadcasted_iota(jnp.int32, shift.shape, 1)
        shift[...] = (source == target + 1).astype(jnp.float32).astype(jnp.bfloat16)
        column = lax.broadcasted_iota(jnp.int32, (span, wells), 0)
        pick[...] = (column == place[...] % span).astype(jnp.float32).astype(jnp.bfloat16)

    def keep_face(k, t, face):
        rows = pl.ds(pl.multiple_of(k * lines, lines), lines)
        for n, part in enumerate(split_bf16(face, 2)):
            pieces[n, rows, t * LANES : (t + 1) * LANES] = part

    def plane(k, carry):
        left_w = left_c = jnp.zeros((lines, LANES), jnp.float32)
        for t in range(tiles):
            cols = slice(t * LANES, (t + 1) * LANES)
            w = w_ref[k, :, cols]
            c = select_tree(cat_ref[k, :, cols], entries)
            for n, (ref, value) in enumerate(((ws, w), (cs, c))):
                ref[t, top:end] = value
                edge_first, edge_last = value[0:1], value[lines - 1 : lines]
                ref[t, top - 1 : top] = edge_first
                ref[t, end : end + 1] = edge_last
                edges[k, n : n + 1, cols] = edge_first
                edges[k, n + 2 : n + 3, cols] = edge_last
            roll_w, roll_c = pltpu.roll(w, 1, 1), pltpu.roll(c, 1, 1)
            west_w = jnp.where(lane == 0, left_w, roll_w)
            west_c = jnp.where(lane == 0, left_c, roll_c)
            left_w, left_c = roll_w, roll_c
            face = (c + west_c) * (w - west_w)
            keep_face(k, t, face)
            if t == tiles - 1:
                keep_face(k, tiles, pltpu.roll(-c * w, 1, 1))
            north = (c + cs[t, top - 1 : end - 1]) * (w - ws[t, top - 1 : end - 1])
            fs[t, top:end] = north
            fs[t, end : end + 1] = jnp.zeros((1, LANES), jnp.float32)
            base = w - face - north + fs[t, top + 1 : end + 1]
            right_ref[:, k, :, cols] = base.reshape(groups, ROWS, LANES)
        return carry

    lax.fori_loop(0, planes, plane, 0)

    for t in range(tiles):
        cols = slice(t * LANES, (t + 1) * LANES)
        both = slice(t * LANES, (t + 2) * LANES)
        east = jnp.dot(
            jnp.concatenate([pieces[0, :, both], pieces[1, :, both]], axis=1),
            shift[...],
            preferred_element_type=jnp.float32,
        )
        first, final = acc[0, :, cols], acc[1, :, cols]
        for k in range(planes):
            z = step * planes + k
            value = right_ref[:, k, :, cols].reshape(lines, LANES) + east[k * lines : (k + 1) * lines]
            right_ref[:, k, :, cols] = value.reshape(groups, ROWS, LANES)
            first = first + ends[0, z] * value
            final = final + ends[ends.shape[0] - 1, z] * value
        acc[0, :, cols] = first
        acc[1, :, cols] = final

    for k in range(planes):
        for n in range(2):
            first_ref[n, k : k + 1, :] = edges[k, n : n + 1, :]
            last_ref[n, k : k + 1, :] = edges[k, n + 2 : n + 3, :]

    dot = functools.partial(jnp.dot, preferred_element_type=jnp.float32)
    own_line = lax.broadcasted_iota(jnp.int32, (lines, wells), 0) == place[...] // span
    upper, lower = split_bf16(w_ref[...].reshape(planes * lines, span), 2)
    kinds = cat_ref[...].astype(jnp.float32).reshape(planes * lines, span).astype(jnp.bfloat16)
    sums = [dot(upper, pick[...]) + dot(lower, pick[...]), dot(kinds, pick[...])]
    for n in range(2):
        for k in range(planes):
            mine = jnp.where(own_line, sums[n][k * lines : (k + 1) * lines], 0.0)
            cells_ref[n, k : k + 1, :] = jnp.sum(mine, axis=0, keepdims=True)


def stencil(w, cat, table, inverse, place_row):
    slabs, lines, span = w.shape
    planes, groups = 8, lines // ROWS
    wells = place_row.shape[1]
    block = pl.BlockSpec((planes, lines, span), lambda i: (i, 0, 0))
    edge = pl.BlockSpec((2, planes, span), lambda i: (0, i, 0))
    smem = pl.BlockSpec(memory_space=pltpu.SMEM)
    shifted = pltpu.VMEM((span // LANES, lines + 2 * ROWS, LANES), jnp.float32)
    return pl.pallas_call(
        stencil_kernel,
        grid=(slabs // planes,),
        in_specs=[smem, smem, block, block, pl.BlockSpec((1, wells), lambda i: (0, 0))],
        out_specs=[
            pl.BlockSpec((groups, planes, ROWS, span), lambda i: (0, i, 0, 0)),
            pl.BlockSpec((2, lines, span), lambda i: (0, 0, 0)),
            edge,
            edge,
            pl.BlockSpec((2, planes, wells), lambda i: (0, i, 0)),
        ],
        out_shape=[
            jax.ShapeDtypeStruct((groups, slabs, ROWS, span), jnp.float32),
            jax.ShapeDtypeStruct((2, lines, span), jnp.float32),
            jax.ShapeDtypeStruct((2, slabs, span), jnp.float32),
            jax.ShapeDtypeStruct((2, slabs, span), jnp.float32),
            jax.ShapeDtypeStruct((2, slabs, wells), jnp.float32),
        ],
        scratch_shapes=[
            shifted,
            shifted,
            shifted,
            pltpu.VMEM((2, planes * lines, span + LANES), jnp.bfloat16),
            pltpu.VMEM((4 * LANES, LANES), jnp.bfloat16),
            pltpu.VMEM((span, wells), jnp.bfloat16),
            pltpu.VMEM((planes, 4, span), jnp.float32),
        ],
        compiler_params=pltpu.CompilerParams(vmem_limit_bytes=VMEM_LIMIT),
        cost_estimate=pl.CostEstimate(flops=40 * w.size, bytes_accessed=12 * w.size, transcendentals=0),
        name="stencil",
    )(table, inverse, w, cat, place_row)


def cell_rows(slabs, wells, share):
    if share >= 2 * wells:
        return ((0, 0), (0, wells)), slabs
    return ((0, 0), (slabs, 0)), 2 * slabs


def payload_kernel(ratio, sums, first, last, before, after, inverse, cells, out_ref, flux_ref):
    copies, _, share = out_ref.shape
    _, lines, span = sums.shape
    slabs, wells = cells.shape[1:]
    ends = jnp.concatenate([inverse[0:1], inverse[slabs - 1 : slabs]], axis=0)
    info, start = 2 * lines, 2 * lines + ROWS
    places, _ = cell_rows(slabs, wells, share)
    for d in range(copies):
        cols = slice(d * share, (d + 1) * share)
        for q in range(2):
            out_ref[d, q * lines : (q + 1) * lines] = sums[q, :, cols]
        out_ref[d, info : info + ROWS] = jnp.zeros((ROWS, share), jnp.float32)
        out_ref[d, info : info + 2, :slabs] = ends
        out_ref[d, info : info + 1, slabs : slabs + 1] = jnp.full((1, 1), ratio[0])
        for n, (row, at) in enumerate(places):
            out_ref[d, start + row : start + row + slabs, at : at + wells] = cells[n]
    for own, other, line, n in ((first, before, 0, 0), (last, after, lines - 1, 1)):
        flux = (own[1] + other[1]) * (other[0] - own[0])
        flux_ref[n] = flux
        extra = jnp.dot(ends, flux, precision=HIGHEST, preferred_element_type=jnp.float32)
        for d in range(copies):
            for q in range(2):
                at = q * lines + line
                out_ref[d, at : at + 1] += extra[q : q + 1, d * share : (d + 1) * share]


def payload(ratio, sums, first, last, before, after, inverse, cells, copies):
    _, lines, span = sums.shape
    slabs, wells = cells.shape[1:]
    share = span // copies
    rows = 2 * lines + ROWS + cell_rows(slabs, wells, share)[1]
    vmem = pl.BlockSpec(memory_space=pltpu.VMEM)
    return pl.pallas_call(
        payload_kernel,
        in_specs=[pl.BlockSpec(memory_space=pltpu.SMEM)] + [vmem] * 7,
        out_specs=[vmem] * 2,
        out_shape=[
            jax.ShapeDtypeStruct((copies, rows, share), jnp.float32),
            jax.ShapeDtypeStruct((2, slabs, span), jnp.float32),
        ],
        compiler_params=pltpu.CompilerParams(vmem_limit_bytes=SMALL_VMEM),
        cost_estimate=pl.CostEstimate(flops=10**6, bytes_accessed=10**6, transcendentals=0),
        name="payload",
    )(ratio, sums, first, last, before, after, inverse, cells)


CORNERS = ((0, 0), (0, 1), (1, 0), (1, 1))


def block_scalars(tile, slabs, shape, flipped=None):
    at = lambda row, lane: jnp.broadcast_to(tile[row : row + 1, lane : lane + 1], shape)
    corner = {(r, c): at(r, c * (slabs - 1)) for r, c in CORNERS}
    if flipped is not None:
        corner = {(r, c): jnp.where(flipped, corner[1 - r, 1 - c], corner[r, c]) for r, c in CORNERS}
    return corner, at(0, slabs)


def coupling(ratio, one, other, slabs):
    return ratio * (slabs / (slabs + 1.0)) / jnp.sqrt(one * other)


def chain(corners, couple, q=None):
    out = []
    q = jnp.zeros_like(couple[0])
    for k, corner in enumerate(corners):
        vf, vl = couple[k] * corner[0, 0], couple[k] * corner[1, 0]
        wf, wl = couple[k + 1] * corner[0, 1], couple[k + 1] * corner[1, 1]
        inverse = 1.0 / (1.0 - vf * q)
        out.append(
            dict(
                p_first=vl * q * inverse,
                p_before=vl * inverse,
                a_first=inverse,
                a_before=vf * inverse,
                a_after=wf * inverse,
                couple=couple[k],
                couple_after=couple[k + 1],
                q=q,
            )
        )
        q = wl + vl * q * wf * inverse
    return out, q


KINDS = ("p_first", "p_before", "a_first", "a_before", "a_after", "couple", "couple_after", "q")


def forward(coef, firsts, lasts):
    before = [jnp.zeros_like(firsts[0])]
    for j in range(len(firsts)):
        before.append(
            lasts[j] + coef("p_first", j) * firsts[j] + coef("p_before", j) * before[j]
        )
    return before


def backward(coef, firsts, before, after):
    blocks = len(firsts)
    above, below = [None] * blocks, [None] * blocks
    for j in reversed(range(blocks)):
        below[j] = coef("couple_after", j) * after
        here = (
            coef("a_first", j) * firsts[j]
            + coef("a_before", j) * before[j]
            + coef("a_after", j) * after
        )
        above[j] = coef("couple", j) * (before[j] + coef("q", j) * here)
        after = here
    return above, below


def half_chain(tiles, slabs, flipped, middle):
    shape = (ROWS, LANES)
    scalars = [block_scalars(tile, slabs, shape, flipped) for tile in tiles]
    couple = [jnp.zeros(shape, jnp.float32)]
    for k in range(1, len(tiles)):
        ratio = jnp.where(flipped, scalars[k - 1][1], scalars[k][1])
        couple.append(coupling(ratio, scalars[k - 1][0][1, 1], scalars[k][0][0, 0], slabs))
    couple.append(middle)
    return chain([corner for corner, _ in scalars], couple)


def first_kernel(slabs, half, fl_ref, out_ref, cells_ref, table):
    blocks, _, share = fl_ref.shape
    wells = cells_ref.shape[-1]
    lines = out_ref.shape[0] - -(-2 * blocks // ROWS) * ROWS
    info, start = 2 * lines, 2 * lines + ROWS
    flip = half[0]
    flipped = flip == 1
    block = [k + flip * (blocks - 1 - 2 * k) for k in range(blocks)]
    entries, _ = half_chain(
        [fl_ref[block[k], info : info + ROWS, :LANES] for k in range(blocks)],
        slabs,
        flipped,
        jnp.zeros((ROWS, LANES), jnp.float32),
    )
    for k, entry in enumerate(entries):
        for n, kind in enumerate(KINDS[:2]):
            table[k, n] = entry[kind]
    coef = lambda kind, k: table[k, KINDS.index(kind)]

    def group(g, carry):
        rows = pl.ds(pl.multiple_of(g * ROWS, ROWS), ROWS)
        outer = pl.ds(pl.multiple_of(flip * lines + g * ROWS, ROWS), ROWS)
        inner = pl.ds(pl.multiple_of((1 - flip) * lines + g * ROWS, ROWS), ROWS)
        for t in range(share // LANES):
            cols = slice(t * LANES, (t + 1) * LANES)
            before = forward(
                coef,
                [fl_ref[block[k], outer, cols] for k in range(blocks)],
                [fl_ref[block[k], inner, cols] for k in range(blocks)],
            )
            out_ref[rows, cols] = before[blocks]
        return carry

    lax.fori_loop(0, lines // ROWS, group, 0)
    out_ref[lines:, :] = jnp.zeros((out_ref.shape[0] - lines, share), jnp.float32)
    places, _ = cell_rows(slabs, wells, share)
    for j in range(blocks):
        out_ref[lines + 2 * j : lines + 2 * j + 2, :] = fl_ref[j, info : info + 2, :]
        for n, (row, at) in enumerate(places):
            cells_ref[j, n] = fl_ref[j, start + row : start + row + slabs, at : at + wells]


def first_half(half, fl, slabs, lines, wells):
    parts, _, share = fl.shape
    vmem = pl.BlockSpec(memory_space=pltpu.VMEM)
    rows = lines + -(-2 * parts // ROWS) * ROWS
    return pl.pallas_call(
        functools.partial(first_kernel, slabs),
        in_specs=[pl.BlockSpec(memory_space=pltpu.SMEM), vmem],
        out_specs=[vmem, vmem],
        out_shape=[
            jax.ShapeDtypeStruct((rows, share), jnp.float32),
            jax.ShapeDtypeStruct((parts, 2, slabs, wells), jnp.float32),
        ],
        scratch_shapes=[pltpu.VMEM((parts, 2, ROWS, LANES), jnp.float32)],
        compiler_params=pltpu.CompilerParams(vmem_limit_bytes=SMALL_VMEM),
        cost_estimate=pl.CostEstimate(flops=4 * fl.size, bytes_accessed=5 * fl.size, transcendentals=0),
        name="reduced_in",
    )(half, fl)


def second_kernel(slabs, half, fl_ref, mine, other, uv_ref, info_ref, table):
    blocks, _, lines, share = uv_ref.shape
    flip = half[0]
    flipped = flip == 1
    block = [k + flip * (blocks - 1 - 2 * k) for k in range(blocks)]
    for j in range(blocks):
        info_ref[flip * blocks + j] = fl_ref[j, 2 * lines : 2 * lines + ROWS, :LANES]
        info_ref[(1 - flip) * blocks + j] = jnp.zeros((ROWS, LANES), jnp.float32)
        info_ref[(1 - flip) * blocks + j, 0:2] = other[lines + 2 * j : lines + 2 * j + 2, :LANES]
    shape = (ROWS, LANES)
    above, above_ratio = block_scalars(info_ref[blocks - 1], slabs, shape)
    below, below_ratio = block_scalars(info_ref[blocks], slabs, shape)
    middle = coupling(below_ratio, above[1, 1], below[0, 0], slabs)
    tiles = lambda flip: [
        info_ref[flip * blocks + k + flip * (blocks - 1 - 2 * k)] for k in range(blocks)
    ]
    entries, q_own = half_chain(tiles(flip), slabs, flipped, middle)
    _, q_other = half_chain(tiles(1 - flip), slabs, jnp.logical_not(flipped), middle)
    for k, entry in enumerate(entries):
        for n, kind in enumerate(KINDS):
            table[k, n] = entry[kind]
    table[blocks, 0] = 1.0 / (1.0 - q_own * q_other)
    table[blocks, 1] = q_other
    coef = lambda kind, k: table[k, KINDS.index(kind)]

    def group(g, carry):
        rows = pl.ds(pl.multiple_of(g * ROWS, ROWS), ROWS)
        outside = pl.ds(pl.multiple_of(flip * lines + g * ROWS, ROWS), ROWS)
        inside = pl.ds(pl.multiple_of((1 - flip) * lines + g * ROWS, ROWS), ROWS)
        for t in range(share // LANES):
            cols = slice(t * LANES, (t + 1) * LANES)
            firsts = [fl_ref[block[k], outside, cols] for k in range(blocks)]
            lasts = [fl_ref[block[k], inside, cols] for k in range(blocks - 1)]
            before = forward(coef, firsts[:-1], lasts)
            across = table[blocks, 0] * (other[rows, cols] + table[blocks, 1] * mine[rows, cols])
            outer, inner = backward(coef, firsts, before, across)
            for k in range(blocks):
                uv_ref[block[k], flip, rows, cols] = outer[k]
                uv_ref[block[k], 1 - flip, rows, cols] = inner[k]
        return carry

    lax.fori_loop(0, lines // ROWS, group, 0)


def second_half(half, fl, mine, other, slabs, lines):
    parts, _, share = fl.shape
    vmem = pl.BlockSpec(memory_space=pltpu.VMEM)
    return pl.pallas_call(
        functools.partial(second_kernel, slabs),
        in_specs=[pl.BlockSpec(memory_space=pltpu.SMEM), vmem, vmem, vmem],
        out_specs=[vmem, vmem],
        out_shape=[
            jax.ShapeDtypeStruct((parts, 2, lines, share), jnp.float32),
            jax.ShapeDtypeStruct((2 * parts, ROWS, LANES), jnp.float32),
        ],
        scratch_shapes=[pltpu.VMEM((parts + 1, len(KINDS), ROWS, LANES), jnp.float32)],
        compiler_params=pltpu.CompilerParams(vmem_limit_bytes=SMALL_VMEM),
        cost_estimate=pl.CostEstimate(flops=10 * fl.size, bytes_accessed=9 * fl.size, transcendentals=0),
        name="reduced_out",
    )(half, fl, mine, other)


def extras_kernel(
    table,
    where_am_i,
    info,
    cells_own,
    cells_other,
    flux,
    inverse,
    well,
    holders,
    wells_ref,
    rows_ref,
    leaving,
    keep,
    force,
    rate,
    down,
    rise,
    pairs,
):
    blocks = info.shape[0]
    slabs, wells = wells_ref.shape
    d = where_am_i[0]
    half = d // (blocks // 2)
    held_cells = [
        (ref, k, pl.multiple_of((side * (blocks // 2) + k) * slabs, slabs))
        for ref, side in ((cells_own, half), (cells_other, 1 - half))
        for k in range(blocks // 2)
    ]
    speed, inlet, reach = well[0:1], well[1:2], well[2:3]
    entries = [table[k] for k in range(table.shape[0])]
    level = lax.broadcasted_iota(jnp.int32, (slabs, wells), 0)
    for ref, k, start in held_cells:
        cond = select_tree(ref[k, 1].astype(jnp.int32), entries)
        inside = (level + start).astype(jnp.float32) < reach
        here = jnp.where(inside, speed * cond / (1.0 + cond), 0.0)
        rows = pl.ds(start, slabs)
        rate[rows] = here
        keep[rows] = 1.0 - here
        force[rows] = here * ref[k, 0]

    chunks = blocks * slabs // ROWS

    def descend(i, value):
        rows = pl.ds(pl.multiple_of(i * ROWS, ROWS), ROWS)
        a, b = keep[rows], force[rows]
        seen = []
        for r in range(ROWS):
            seen.append(value)
            value = a[r : r + 1] * value + b[r : r + 1]
        down[rows] = jnp.concatenate(seen, axis=0)
        return value

    def ascend(i, value):
        rows = pl.ds(pl.multiple_of((chunks - 1 - i) * ROWS, ROWS), ROWS)
        a, b = keep[rows], force[rows]
        seen = []
        for r in reversed(range(ROWS)):
            seen.append(value)
            value = a[r : r + 1] * value + b[r : r + 1]
        rise[rows] = jnp.concatenate(seen[::-1], axis=0)
        return value

    bottom = lax.fori_loop(0, chunks, descend, inlet)
    surface = lax.fori_loop(0, chunks, ascend, bottom)
    held = holders[...] == lax.broadcasted_iota(jnp.int32, (wells, holders.shape[1]), 0)
    leaving[...] = jnp.dot(
        jnp.broadcast_to(surface, (ROWS, wells)),
        held.astype(jnp.float32),
        precision=HIGHEST,
        preferred_element_type=jnp.float32,
    )[0:1]

    for ref, k, start in held_cells:
        rows = pl.ds(start, slabs)
        taken = rate[rows] * (2.0 * ref[k, 0] - down[rows] - rise[rows])
        force[rows] = -storage_volume * taken
    firsts, lasts = [], []
    for j in range(blocks):
        both = jnp.dot(
            info[j, :, :slabs],
            force[j * slabs : (j + 1) * slabs],
            precision=HIGHEST,
            preferred_element_type=jnp.float32,
        )
        firsts.append(both[0:1])
        lasts.append(both[1:2])

    scalars = [block_scalars(info[j], slabs, (1, wells)) for j in range(blocks)]
    zero = jnp.zeros((1, wells), jnp.float32)
    couple = [zero]
    for j in range(1, blocks):
        couple.append(
            coupling(scalars[j][1], scalars[j - 1][0][1, 1], scalars[j][0][0, 0], slabs)
        )
    couple.append(zero)
    coefs, _ = chain([corner for corner, _ in scalars], couple)
    coef = lambda kind, j: coefs[j][kind]
    above, below = backward(coef, firsts, forward(coef, firsts, lasts), zero)
    for j in range(blocks):
        pairs[j, 0:1] = above[j]
        pairs[j, 1:2] = below[j]
    pair = pairs[d]
    row = lax.broadcasted_iota(jnp.int32, (slabs, wells), 0)
    own = force[pl.ds(pl.multiple_of(d * slabs, slabs), slabs)]
    own = own + jnp.where(row == 0, pair[0:1], 0.0) + jnp.where(row == slabs - 1, pair[1:2], 0.0)
    dot = functools.partial(jnp.dot, precision=HIGHEST, preferred_element_type=jnp.float32)
    wells_ref[...] = dot(inverse[...], own)
    for n in range(2):
        rows_ref[n] = dot(inverse[...], flux[n])


def extras(table, depth_index, info, cells_own, cells_other, flux, inverse, well, holders):
    blocks = info.shape[0]
    _, slabs, span = flux.shape
    wells = cells_own.shape[-1]
    smem = pl.BlockSpec(memory_space=pltpu.SMEM)
    vmem = pl.BlockSpec(memory_space=pltpu.VMEM)
    column = pltpu.VMEM((blocks * slabs, wells), jnp.float32)
    return pl.pallas_call(
        extras_kernel,
        in_specs=[smem, smem] + [vmem] * 7,
        out_specs=[vmem] * 3,
        out_shape=[
            jax.ShapeDtypeStruct((slabs, wells), jnp.float32),
            jax.ShapeDtypeStruct((2, slabs, span), jnp.float32),
            jax.ShapeDtypeStruct((1, holders.shape[1]), jnp.float32),
        ],
        scratch_shapes=[column] * 5 + [pltpu.VMEM((blocks, ROWS, wells), jnp.float32)],
        compiler_params=pltpu.CompilerParams(vmem_limit_bytes=SMALL_VMEM),
        cost_estimate=pl.CostEstimate(flops=10**7, bytes_accessed=10**6, transcendentals=0),
        name="extras",
    )(table, depth_index.reshape(1), info, cells_own, cells_other, flux, inverse, well, holders)


def solve_kernel(right, uv, inverse, place_row, place_column, solved_wells, outer, out, factor, pick):
    together, slabs, rows, span = right.shape
    wells = place_row.shape[1]
    step = pl.program_id(0)
    size = slabs * rows

    @pl.when(step == 0)
    def _():
        spread = (
            lax.broadcasted_iota(jnp.int32, (size, slabs), 0) // rows
            == lax.broadcasted_iota(jnp.int32, (size, slabs), 1)
        ).astype(jnp.float32).astype(jnp.bfloat16)
        spread_t = (
            lax.broadcasted_iota(jnp.int32, (slabs, size), 1) // rows
            == lax.broadcasted_iota(jnp.int32, (slabs, size), 0)
        ).astype(jnp.float32).astype(jnp.bfloat16)
        same = (
            lax.broadcasted_iota(jnp.int32, (size, size), 0) % rows
            == lax.broadcasted_iota(jnp.int32, (size, size), 1) % rows
        )
        for n, part in enumerate(split_bf16(inverse[...], 2)):
            tall = jnp.dot(spread, part, preferred_element_type=jnp.float32).astype(jnp.bfloat16)
            wide = jnp.dot(tall, spread_t, preferred_element_type=jnp.float32)
            wide = jnp.where(same, wide, 0.0).astype(jnp.bfloat16)
            if n == 0:
                factor[:, :size] = wide
                factor[:, size : 2 * size] = wide
            else:
                factor[:, 2 * size : 3 * size] = wide
        column = lax.broadcasted_iota(jnp.int32, (wells, span), 1)
        chosen = (column == place_column[...] % span).astype(jnp.float32).astype(jnp.bfloat16)
        pick[:wells] = chosen
        pick[wells:] = chosen

    tile = min(span, 256)
    for n in range(together):
        line = lax.broadcasted_iota(jnp.int32, (slabs, rows, wells), 1) + (step * together + n) * rows
        at_wells = jnp.where(line == (place_row[...] // span)[None], solved_wells[...][:, None, :], 0.0)
        at_wells = jnp.concatenate(split_bf16(at_wells.reshape(size, wells), 2), axis=1)
        factor[:, 3 * size :] = at_wells
        lines = slice(n * rows, (n + 1) * rows)
        above = jnp.concatenate([uv[d, 0, lines] for d in range(uv.shape[0])], axis=1)
        below = jnp.concatenate([uv[d, 1, lines] for d in range(uv.shape[0])], axis=1)
        for t in range(span // tile):
            cols = slice(t * tile, (t + 1) * tile)
            value = jnp.concatenate(
                [
                    right[n, 0:1, :, cols] + above[None, :, cols],
                    right[n, 1 : slabs - 1, :, cols],
                    right[n, slabs - 1 :, :, cols] + below[None, :, cols],
                ],
                axis=0,
            ).reshape(size, tile)
            upper, lower = split_bf16(value, 2)
            result = jnp.dot(
                factor[...],
                jnp.concatenate([upper, lower, upper, pick[:, cols]], axis=0),
                preferred_element_type=jnp.float32,
            )
            out[:, lines, cols] = result.reshape(slabs, rows, tile)

    for n, (when, line) in enumerate(((0, 0), (pl.num_programs(0) - 1, together * rows - 1))):

        @pl.when(step == when)
        def _():
            for z in range(slabs):
                out[z, line : line + 1, :] += outer[n, z : z + 1, :]


def solve(right, uv, inverse, place_row, solved_wells, outer):
    groups, slabs, _, span = right.shape
    wells = place_row.shape[1]
    together = 2
    lines = together * ROWS
    shares, _, _, share = uv.shape
    whole = lambda *shape: pl.BlockSpec(shape, lambda g: (0,) * len(shape))
    size = slabs * ROWS
    return pl.pallas_call(
        solve_kernel,
        grid=(groups // together,),
        in_specs=[
            pl.BlockSpec((together, slabs, ROWS, span), lambda g: (g, 0, 0, 0)),
            pl.BlockSpec((shares, 2, lines, share), lambda g: (0, 0, g, 0)),
            whole(slabs, slabs),
            whole(1, wells),
            whole(wells, 1),
            whole(slabs, wells),
            whole(*outer.shape),
        ],
        out_specs=pl.BlockSpec((slabs, lines, span), lambda g: (0, g, 0)),
        out_shape=jax.ShapeDtypeStruct((slabs, groups * ROWS, span), jnp.float32),
        scratch_shapes=[
            pltpu.VMEM((size, 3 * size + 2 * wells), jnp.bfloat16),
            pltpu.VMEM((2 * wells, span), jnp.bfloat16),
        ],
        compiler_params=pltpu.CompilerParams(vmem_limit_bytes=SOLVE_VMEM),
        cost_estimate=pl.CostEstimate(
            flops=8 * size * right.size, bytes_accessed=8 * right.size, transcendentals=0
        ),
        name="depth_solve",
    )(right, uv, inverse, place_row, place_row.reshape(wells, 1), solved_wells, outer)


def body(
    warmth_before,
    stratum_category,
    conductance_catalogue,
    pivot_matrix_reciprocal,
    linkage_factor,
    well_position_inside,
    well_holder_sequence,
    well_reach,
    entering_warmth,
    well_transfer_speed,
):
    slabs, lines, span = warmth_before.shape
    depth_index = lax.axis_index("depth")
    depth_count = lax.axis_size("depth")
    wells = well_position_inside.shape[0]
    owned = wells // depth_count
    table = conductance_catalogue

    parts = depth_count // 2
    halves = [list(range(h * parts, (h + 1) * parts)) for h in range(2)]
    half = (depth_index // parts).astype(jnp.int32).reshape(1)

    place_row = well_position_inside.reshape(1, wells)
    right, sums, first, last, cells = stencil(
        warmth_before, stratum_category, table, pivot_matrix_reciprocal, place_row
    )
    count = lax.axis_size("strip")
    up = [(i, i + 1) for i in range(count - 1)]
    down = [(j, i) for i, j in up]
    before = lax.ppermute(last, "strip", up)
    after = lax.ppermute(first, "strip", down)
    fl, flux = payload(
        linkage_factor, sums, first, last, before, after, pivot_matrix_reciprocal, cells, parts
    )
    exchange = functools.partial(
        lax.all_to_all,
        axis_name="depth",
        split_axis=0,
        concat_axis=0,
        tiled=True,
        axis_index_groups=halves,
    )
    fl_all = exchange(fl)

    across = functools.partial(
        lax.ppermute,
        axis_name="depth",
        perm=[(i, (i + parts) % depth_count) for i in range(depth_count)],
    )
    mine, cells_own = first_half(half, fl_all, slabs, lines, wells)
    other = across(mine)
    uv, info_all = second_half(half, fl_all, mine, other, slabs, lines)
    uv, cells_own = lax.optimization_barrier((uv, cells_own))
    cells_other = across(cells_own)
    uv_own = exchange(uv)

    well = jnp.stack([well_transfer_speed, entering_warmth, well_reach.astype(jnp.float32)])
    well = jnp.pad(well, ((0, ROWS - 3), (0, 0)))
    holders = lax.dynamic_slice_in_dim(well_holder_sequence, depth_index * owned, owned)
    solved_wells, outer, leaving = extras(
        table,
        depth_index,
        info_all,
        cells_own,
        cells_other,
        flux,
        pivot_matrix_reciprocal,
        well,
        holders.reshape(1, owned),
    )
    solved = solve(right, uv_own, pivot_matrix_reciprocal, place_row, solved_wells, outer)
    return solved, leaving.reshape(owned)


def solution(mesh):
    in_specs = (
        P("depth", "strip", None),
        P("depth", "strip", None),
        P(),
        P("depth", None),
        P("depth"),
        P("strip"),
        P("strip"),
        P("strip"),
        P("strip"),
        P("strip"),
    )
    out_specs = (P("depth", "strip", None), P(("strip", "depth")))
    return jax.shard_map(body, mesh=mesh, in_specs=in_specs, out_specs=out_specs, check_vma=False)
```

```python
import functools

import jax
import jax.numpy as jnp
from jax import lax
from jax.experimental import pallas as pl
from jax.experimental.pallas import tpu as pltpu
from jax.sharding import PartitionSpec as P

backward_euler_advance = 0.2
storage_volume = 2.0
flux_scale = 0.5 * backward_euler_advance
LANES = 128
ROWS = 8
EDGE_VMEM = 56 * 1024 * 1024
VMEM_LIMIT = 40 * 1024 * 1024
SOLVE_VMEM = 24 * 1024 * 1024
SMALL_VMEM = 12 * 1024 * 1024
HIGHEST = lax.Precision.HIGHEST


def select_tree(category, entries):
    values = list(entries)
    bit = 1
    while len(values) > 1:
        odd = (category & bit) != 0
        values = [
            jnp.where(odd, values[k + 1], values[k]) if k + 1 < len(values) else values[k]
            for k in range(0, len(values), 2)
        ]
        bit *= 2
    return values[0]


def split_bf16(value, pieces):
    out = []
    for k in range(pieces):
        part = value.astype(jnp.bfloat16)
        out.append(part)
        if k + 1 < pieces:
            value = value - part.astype(jnp.float32)
    return out


def edge_kernel(table, w_first, cat_first, w_last, cat_last, first, last):
    slabs, rows, span = w_first.shape
    entries = [flux_scale * table[k] for k in range(table.shape[0])]
    sub = lax.broadcasted_iota(jnp.int32, (ROWS, span), 0)

    def gathered(ref, start, row):
        value = jnp.broadcast_to(ref[start, row : row + 1, :], (ROWS, span))
        for k in range(1, ROWS):
            value = jnp.where(sub == k, ref[start + k, row : row + 1, :], value)
        return value

    for w_ref, cat_ref, row, out in ((w_first, cat_first, 0, first), (w_last, cat_last, rows - 1, last)):
        for start in range(0, slabs, ROWS):
            out[0, start : start + ROWS] = gathered(w_ref, start, row)
            out[1, start : start + ROWS] = select_tree(gathered(cat_ref, start, row), entries)


def edge_rows(w, cat, table):
    slabs, lines, span = w.shape
    top = pl.BlockSpec((slabs, ROWS, span), lambda i: (0, 0, 0))
    end = pl.BlockSpec((slabs, ROWS, span), lambda i: (0, lines // ROWS - 1, 0))
    out = pl.BlockSpec((2, slabs, span), lambda i: (0, 0, 0))
    return pl.pallas_call(
        edge_kernel,
        grid=(1,),
        in_specs=[pl.BlockSpec(memory_space=pltpu.SMEM), top, top, end, end],
        out_specs=[out, out],
        out_shape=[jax.ShapeDtypeStruct((2, slabs, span), jnp.float32)] * 2,
        compiler_params=pltpu.CompilerParams(vmem_limit_bytes=EDGE_VMEM),
        cost_estimate=pl.CostEstimate(flops=10**6, bytes_accessed=w.size, transcendentals=0),
        name="edge_rows",
    )(table, w, cat, w, cat)


def stencil_kernel(
    table,
    ends,
    w_ref,
    cat_ref,
    place,
    right_ref,
    acc,
    cells_ref,
    ws,
    cs,
    fs,
    pieces,
    shift,
    pick,
):
    step = pl.program_id(0)
    planes, lines, span = w_ref.shape
    tiles = span // LANES
    groups = lines // ROWS
    wells = place.shape[1]
    entries = [flux_scale * table[k] for k in range(table.shape[0])]
    lane = lax.broadcasted_iota(jnp.int32, (lines, LANES), 1)
    top, end = ROWS, ROWS + lines

    @pl.when(step == 0)
    def _():
        acc[...] = jnp.zeros_like(acc)
        source = lax.broadcasted_iota(jnp.int32, shift.shape, 0) % (2 * LANES)
        target = lax.broadcasted_iota(jnp.int32, shift.shape, 1)
        shift[...] = (source == target + 1).astype(jnp.float32).astype(jnp.bfloat16)
        column = lax.broadcasted_iota(jnp.int32, (span, wells), 0)
        pick[...] = (column == place[...] % span).astype(jnp.float32).astype(jnp.bfloat16)

    def keep_face(k, t, face):
        rows = pl.ds(pl.multiple_of(k * lines, lines), lines)
        for n, part in enumerate(split_bf16(face, 2)):
            pieces[n, rows, t * LANES : (t + 1) * LANES] = part

    def plane(k, carry):
        left_w = left_c = jnp.zeros((lines, LANES), jnp.float32)
        for t in range(tiles):
            cols = slice(t * LANES, (t + 1) * LANES)
            w = w_ref[k, :, cols]
            c = select_tree(cat_ref[k, :, cols], entries)
            for ref, value in ((ws, w), (cs, c)):
                ref[t, top:end] = value
                ref[t, top - 1 : top] = value[0:1]
            roll_w, roll_c = pltpu.roll(w, 1, 1), pltpu.roll(c, 1, 1)
            west_w = jnp.where(lane == 0, left_w, roll_w)
            west_c = jnp.where(lane == 0, left_c, roll_c)
            left_w, left_c = roll_w, roll_c
            face = (c + west_c) * (w - west_w)
            keep_face(k, t, face)
            if t == tiles - 1:
                keep_face(k, tiles, pltpu.roll(-c * w, 1, 1))
            north = (c + cs[t, top - 1 : end - 1]) * (w - ws[t, top - 1 : end - 1])
            fs[t, top:end] = north
            fs[t, end : end + 1] = jnp.zeros((1, LANES), jnp.float32)
            base = w - face - north + fs[t, top + 1 : end + 1]
            right_ref[:, k, :, cols] = base.reshape(groups, ROWS, LANES)
        return carry

    lax.fori_loop(0, planes, plane, 0)

    for t in range(tiles):
        cols = slice(t * LANES, (t + 1) * LANES)
        both = slice(t * LANES, (t + 2) * LANES)
        east = jnp.dot(
            jnp.concatenate([pieces[0, :, both], pieces[1, :, both]], axis=1),
            shift[...],
            preferred_element_type=jnp.float32,
        )
        first, final = acc[0, :, cols], acc[1, :, cols]
        for k in range(planes):
            z = step * planes + k
            value = right_ref[:, k, :, cols].reshape(lines, LANES) + east[k * lines : (k + 1) * lines]
            right_ref[:, k, :, cols] = value.reshape(groups, ROWS, LANES)
            first = first + ends[0, z] * value
            final = final + ends[ends.shape[0] - 1, z] * value
        acc[0, :, cols] = first
        acc[1, :, cols] = final

    dot = functools.partial(jnp.dot, preferred_element_type=jnp.float32)
    own_line = lax.broadcasted_iota(jnp.int32, (lines, wells), 0) == place[...] // span
    upper, lower = split_bf16(w_ref[...].reshape(planes * lines, span), 2)
    kinds = cat_ref[...].astype(jnp.float32).reshape(planes * lines, span).astype(jnp.bfloat16)
    sums = [dot(upper, pick[...]) + dot(lower, pick[...]), dot(kinds, pick[...])]
    for n in range(2):
        for k in range(planes):
            mine = jnp.where(own_line, sums[n][k * lines : (k + 1) * lines], 0.0)
            cells_ref[n, k : k + 1, :] = jnp.sum(mine, axis=0, keepdims=True)


def stencil(w, cat, table, inverse, place_row):
    slabs, lines, span = w.shape
    planes, groups = 8, lines // ROWS
    wells = place_row.shape[1]
    block = pl.BlockSpec((planes, lines, span), lambda i: (i, 0, 0))
    smem = pl.BlockSpec(memory_space=pltpu.SMEM)
    shifted = pltpu.VMEM((span // LANES, lines + 2 * ROWS, LANES), jnp.float32)
    return pl.pallas_call(
        stencil_kernel,
        grid=(slabs // planes,),
        in_specs=[smem, smem, block, block, pl.BlockSpec((1, wells), lambda i: (0, 0))],
        out_specs=[
            pl.BlockSpec((groups, planes, ROWS, span), lambda i: (0, i, 0, 0)),
            pl.BlockSpec((2, lines, span), lambda i: (0, 0, 0)),
            pl.BlockSpec((2, planes, wells), lambda i: (0, i, 0)),
        ],
        out_shape=[
            jax.ShapeDtypeStruct((groups, slabs, ROWS, span), jnp.float32),
            jax.ShapeDtypeStruct((2, lines, span), jnp.float32),
            jax.ShapeDtypeStruct((2, slabs, wells), jnp.float32),
        ],
        scratch_shapes=[
            shifted,
            shifted,
            shifted,
            pltpu.VMEM((2, planes * lines, span + LANES), jnp.bfloat16),
            pltpu.VMEM((4 * LANES, LANES), jnp.bfloat16),
            pltpu.VMEM((span, wells), jnp.bfloat16),
        ],
        compiler_params=pltpu.CompilerParams(vmem_limit_bytes=VMEM_LIMIT),
        cost_estimate=pl.CostEstimate(flops=40 * w.size, bytes_accessed=12 * w.size, transcendentals=0),
        name="stencil",
    )(table, inverse, w, cat, place_row)


def cell_rows(slabs, wells, share):
    if share >= 2 * wells:
        return ((0, 0), (0, wells)), slabs
    return ((0, 0), (slabs, 0)), 2 * slabs


def payload_kernel(ratio, sums, first, last, before, after, inverse, cells, out_ref, flux_ref):
    copies, _, share = out_ref.shape
    _, lines, span = sums.shape
    slabs, wells = cells.shape[1:]
    ends = jnp.concatenate([inverse[0:1], inverse[slabs - 1 : slabs]], axis=0)
    info, start = 2 * lines, 2 * lines + ROWS
    places, _ = cell_rows(slabs, wells, share)
    for d in range(copies):
        cols = slice(d * share, (d + 1) * share)
        for q in range(2):
            out_ref[d, q * lines : (q + 1) * lines] = sums[q, :, cols]
        out_ref[d, info : info + ROWS] = jnp.zeros((ROWS, share), jnp.float32)
        out_ref[d, info : info + 2, :slabs] = ends
        out_ref[d, info : info + 1, slabs : slabs + 1] = jnp.full((1, 1), ratio[0])
        for n, (row, at) in enumerate(places):
            out_ref[d, start + row : start + row + slabs, at : at + wells] = cells[n]
    for own, other, line, n in ((first, before, 0, 0), (last, after, lines - 1, 1)):
        flux = (own[1] + other[1]) * (other[0] - own[0])
        flux_ref[n] = flux
        extra = jnp.dot(ends, flux, precision=HIGHEST, preferred_element_type=jnp.float32)
        for d in range(copies):
            for q in range(2):
                at = q * lines + line
                out_ref[d, at : at + 1] += extra[q : q + 1, d * share : (d + 1) * share]


def payload(ratio, sums, first, last, before, after, inverse, cells, copies):
    _, lines, span = sums.shape
    slabs, wells = cells.shape[1:]
    share = span // copies
    rows = 2 * lines + ROWS + cell_rows(slabs, wells, share)[1]
    vmem = pl.BlockSpec(memory_space=pltpu.VMEM)
    return pl.pallas_call(
        payload_kernel,
        in_specs=[pl.BlockSpec(memory_space=pltpu.SMEM)] + [vmem] * 7,
        out_specs=[vmem] * 2,
        out_shape=[
            jax.ShapeDtypeStruct((copies, rows, share), jnp.float32),
            jax.ShapeDtypeStruct((2, slabs, span), jnp.float32),
        ],
        compiler_params=pltpu.CompilerParams(vmem_limit_bytes=SMALL_VMEM),
        cost_estimate=pl.CostEstimate(flops=10**6, bytes_accessed=10**6, transcendentals=0),
        name="payload",
    )(ratio, sums, first, last, before, after, inverse, cells)


CORNERS = ((0, 0), (0, 1), (1, 0), (1, 1))


def block_scalars(tile, slabs, shape, flipped=None):
    at = lambda row, lane: jnp.broadcast_to(tile[row : row + 1, lane : lane + 1], shape)
    corner = {(r, c): at(r, c * (slabs - 1)) for r, c in CORNERS}
    if flipped is not None:
        corner = {(r, c): jnp.where(flipped, corner[1 - r, 1 - c], corner[r, c]) for r, c in CORNERS}
    return corner, at(0, slabs)


def coupling(ratio, one, other, slabs):
    return ratio * (slabs / (slabs + 1.0)) / jnp.sqrt(one * other)


def chain(corners, couple, q=None):
    out = []
    q = jnp.zeros_like(couple[0])
    for k, corner in enumerate(corners):
        vf, vl = couple[k] * corner[0, 0], couple[k] * corner[1, 0]
        wf, wl = couple[k + 1] * corner[0, 1], couple[k + 1] * corner[1, 1]
        inverse = 1.0 / (1.0 - vf * q)
        out.append(
            dict(
                p_first=vl * q * inverse,
                p_before=vl * inverse,
                a_first=inverse,
                a_before=vf * inverse,
                a_after=wf * inverse,
                couple=couple[k],
                couple_after=couple[k + 1],
                q=q,
            )
        )
        q = wl + vl * q * wf * inverse
    return out, q


KINDS = ("p_first", "p_before", "a_first", "a_before", "a_after", "couple", "couple_after", "q")


def forward(coef, firsts, lasts):
    before = [jnp.zeros_like(firsts[0])]
    for j in range(len(firsts)):
        before.append(
            lasts[j] + coef("p_first", j) * firsts[j] + coef("p_before", j) * before[j]
        )
    return before


def backward(coef, firsts, before, after):
    blocks = len(firsts)
    above, below = [None] * blocks, [None] * blocks
    for j in reversed(range(blocks)):
        below[j] = coef("couple_after", j) * after
        here = (
            coef("a_first", j) * firsts[j]
            + coef("a_before", j) * before[j]
            + coef("a_after", j) * after
        )
        above[j] = coef("couple", j) * (before[j] + coef("q", j) * here)
        after = here
    return above, below


def half_chain(tiles, slabs, flipped, middle):
    shape = (ROWS, LANES)
    scalars = [block_scalars(tile, slabs, shape, flipped) for tile in tiles]
    couple = [jnp.zeros(shape, jnp.float32)]
    for k in range(1, len(tiles)):
        ratio = jnp.where(flipped, scalars[k - 1][1], scalars[k][1])
        couple.append(coupling(ratio, scalars[k - 1][0][1, 1], scalars[k][0][0, 0], slabs))
    couple.append(middle)
    return chain([corner for corner, _ in scalars], couple)


def first_kernel(slabs, half, fl_ref, out_ref, cells_ref, table):
    blocks, _, share = fl_ref.shape
    wells = cells_ref.shape[-1]
    lines = out_ref.shape[0] - -(-2 * blocks // ROWS) * ROWS
    info, start = 2 * lines, 2 * lines + ROWS
    flip = half[0]
    flipped = flip == 1
    block = [k + flip * (blocks - 1 - 2 * k) for k in range(blocks)]
    entries, _ = half_chain(
        [fl_ref[block[k], info : info + ROWS, :LANES] for k in range(blocks)],
        slabs,
        flipped,
        jnp.zeros((ROWS, LANES), jnp.float32),
    )
    for k, entry in enumerate(entries):
        for n, kind in enumerate(KINDS[:2]):
            table[k, n] = entry[kind]
    coef = lambda kind, k: table[k, KINDS.index(kind)]

    def group(g, carry):
        rows = pl.ds(pl.multiple_of(g * ROWS, ROWS), ROWS)
        outer = pl.ds(pl.multiple_of(flip * lines + g * ROWS, ROWS), ROWS)
        inner = pl.ds(pl.multiple_of((1 - flip) * lines + g * ROWS, ROWS), ROWS)
        for t in range(share // LANES):
            cols = slice(t * LANES, (t + 1) * LANES)
            before = forward(
                coef,
                [fl_ref[block[k], outer, cols] for k in range(blocks)],
                [fl_ref[block[k], inner, cols] for k in range(blocks)],
            )
            out_ref[rows, cols] = before[blocks]
        return carry

    lax.fori_loop(0, lines // ROWS, group, 0)
    out_ref[lines:, :] = jnp.zeros((out_ref.shape[0] - lines, share), jnp.float32)
    places, _ = cell_rows(slabs, wells, share)
    for j in range(blocks):
        out_ref[lines + 2 * j : lines + 2 * j + 2, :] = fl_ref[j, info : info + 2, :]
        for n, (row, at) in enumerate(places):
            cells_ref[j, n] = fl_ref[j, start + row : start + row + slabs, at : at + wells]


def first_half(half, fl, slabs, lines, wells):
    parts, _, share = fl.shape
    vmem = pl.BlockSpec(memory_space=pltpu.VMEM)
    rows = lines + -(-2 * parts // ROWS) * ROWS
    return pl.pallas_call(
        functools.partial(first_kernel, slabs),
        in_specs=[pl.BlockSpec(memory_space=pltpu.SMEM), vmem],
        out_specs=[vmem, vmem],
        out_shape=[
            jax.ShapeDtypeStruct((rows, share), jnp.float32),
            jax.ShapeDtypeStruct((parts, 2, slabs, wells), jnp.float32),
        ],
        scratch_shapes=[pltpu.VMEM((parts, 2, ROWS, LANES), jnp.float32)],
        compiler_params=pltpu.CompilerParams(vmem_limit_bytes=SMALL_VMEM),
        cost_estimate=pl.CostEstimate(flops=4 * fl.size, bytes_accessed=5 * fl.size, transcendentals=0),
        name="reduced_in",
    )(half, fl)


def second_kernel(slabs, half, fl_ref, mine, other, uv_ref, info_ref, table):
    blocks, _, lines, share = uv_ref.shape
    flip = half[0]
    flipped = flip == 1
    block = [k + flip * (blocks - 1 - 2 * k) for k in range(blocks)]
    for j in range(blocks):
        info_ref[flip * blocks + j] = fl_ref[j, 2 * lines : 2 * lines + ROWS, :LANES]
        info_ref[(1 - flip) * blocks + j] = jnp.zeros((ROWS, LANES), jnp.float32)
        info_ref[(1 - flip) * blocks + j, 0:2] = other[lines + 2 * j : lines + 2 * j + 2, :LANES]
    shape = (ROWS, LANES)
    above, above_ratio = block_scalars(info_ref[blocks - 1], slabs, shape)
    below, below_ratio = block_scalars(info_ref[blocks], slabs, shape)
    middle = coupling(below_ratio, above[1, 1], below[0, 0], slabs)
    tiles = lambda flip: [
        info_ref[flip * blocks + k + flip * (blocks - 1 - 2 * k)] for k in range(blocks)
    ]
    entries, q_own = half_chain(tiles(flip), slabs, flipped, middle)
    _, q_other = half_chain(tiles(1 - flip), slabs, jnp.logical_not(flipped), middle)
    for k, entry in enumerate(entries):
        for n, kind in enumerate(KINDS):
            table[k, n] = entry[kind]
    table[blocks, 0] = 1.0 / (1.0 - q_own * q_other)
    table[blocks, 1] = q_other
    coef = lambda kind, k: table[k, KINDS.index(kind)]

    def group(g, carry):
        rows = pl.ds(pl.multiple_of(g * ROWS, ROWS), ROWS)
        outside = pl.ds(pl.multiple_of(flip * lines + g * ROWS, ROWS), ROWS)
        inside = pl.ds(pl.multiple_of((1 - flip) * lines + g * ROWS, ROWS), ROWS)
        for t in range(share // LANES):
            cols = slice(t * LANES, (t + 1) * LANES)
            firsts = [fl_ref[block[k], outside, cols] for k in range(blocks)]
            lasts = [fl_ref[block[k], inside, cols] for k in range(blocks - 1)]
            before = forward(coef, firsts[:-1], lasts)
            across = table[blocks, 0] * (other[rows, cols] + table[blocks, 1] * mine[rows, cols])
            outer, inner = backward(coef, firsts, before, across)
            for k in range(blocks):
                uv_ref[block[k], flip, rows, cols] = outer[k]
                uv_ref[block[k], 1 - flip, rows, cols] = inner[k]
        return carry

    lax.fori_loop(0, lines // ROWS, group, 0)


def second_half(half, fl, mine, other, slabs, lines):
    parts, _, share = fl.shape
    vmem = pl.BlockSpec(memory_space=pltpu.VMEM)
    return pl.pallas_call(
        functools.partial(second_kernel, slabs),
        in_specs=[pl.BlockSpec(memory_space=pltpu.SMEM), vmem, vmem, vmem],
        out_specs=[vmem, vmem],
        out_shape=[
            jax.ShapeDtypeStruct((parts, 2, lines, share), jnp.float32),
            jax.ShapeDtypeStruct((2 * parts, ROWS, LANES), jnp.float32),
        ],
        scratch_shapes=[pltpu.VMEM((parts + 1, len(KINDS), ROWS, LANES), jnp.float32)],
        compiler_params=pltpu.CompilerParams(vmem_limit_bytes=SMALL_VMEM),
        cost_estimate=pl.CostEstimate(flops=10 * fl.size, bytes_accessed=9 * fl.size, transcendentals=0),
        name="reduced_out",
    )(half, fl, mine, other)


def extras_kernel(
    table,
    where_am_i,
    info,
    cells_own,
    cells_other,
    flux,
    inverse,
    well,
    holders,
    wells_ref,
    rows_ref,
    leaving,
    keep,
    force,
    rate,
    down,
    rise,
    pairs,
):
    blocks = info.shape[0]
    slabs, wells = wells_ref.shape
    d = where_am_i[0]
    half = d // (blocks // 2)
    held_cells = [
        (ref, k, pl.multiple_of((side * (blocks // 2) + k) * slabs, slabs))
        for ref, side in ((cells_own, half), (cells_other, 1 - half))
        for k in range(blocks // 2)
    ]
    speed, inlet, reach = well[0:1], well[1:2], well[2:3]
    entries = [table[k] for k in range(table.shape[0])]
    level = lax.broadcasted_iota(jnp.int32, (slabs, wells), 0)
    for ref, k, start in held_cells:
        cond = select_tree(ref[k, 1].astype(jnp.int32), entries)
        inside = (level + start).astype(jnp.float32) < reach
        here = jnp.where(inside, speed * cond / (1.0 + cond), 0.0)
        rows = pl.ds(start, slabs)
        rate[rows] = here
        keep[rows] = 1.0 - here
        force[rows] = here * ref[k, 0]

    chunks = blocks * slabs // ROWS

    def descend(i, value):
        rows = pl.ds(pl.multiple_of(i * ROWS, ROWS), ROWS)
        a, b = keep[rows], force[rows]
        seen = []
        for r in range(ROWS):
            seen.append(value)
            value = a[r : r + 1] * value + b[r : r + 1]
        down[rows] = jnp.concatenate(seen, axis=0)
        return value

    def ascend(i, value):
        rows = pl.ds(pl.multiple_of((chunks - 1 - i) * ROWS, ROWS), ROWS)
        a, b = keep[rows], force[rows]
        seen = []
        for r in reversed(range(ROWS)):
            seen.append(value)
            value = a[r : r + 1] * value + b[r : r + 1]
        rise[rows] = jnp.concatenate(seen[::-1], axis=0)
        return value

    bottom = lax.fori_loop(0, chunks, descend, inlet)
    surface = lax.fori_loop(0, chunks, ascend, bottom)
    held = holders[...] == lax.broadcasted_iota(jnp.int32, (wells, holders.shape[1]), 0)
    leaving[...] = jnp.dot(
        jnp.broadcast_to(surface, (ROWS, wells)),
        held.astype(jnp.float32),
        precision=HIGHEST,
        preferred_element_type=jnp.float32,
    )[0:1]

    for ref, k, start in held_cells:
        rows = pl.ds(start, slabs)
        taken = rate[rows] * (2.0 * ref[k, 0] - down[rows] - rise[rows])
        force[rows] = -storage_volume * taken
    firsts, lasts = [], []
    for j in range(blocks):
        both = jnp.dot(
            info[j, :, :slabs],
            force[j * slabs : (j + 1) * slabs],
            precision=HIGHEST,
            preferred_element_type=jnp.float32,
        )
        firsts.append(both[0:1])
        lasts.append(both[1:2])

    scalars = [block_scalars(info[j], slabs, (1, wells)) for j in range(blocks)]
    zero = jnp.zeros((1, wells), jnp.float32)
    couple = [zero]
    for j in range(1, blocks):
        couple.append(
            coupling(scalars[j][1], scalars[j - 1][0][1, 1], scalars[j][0][0, 0], slabs)
        )
    couple.append(zero)
    coefs, _ = chain([corner for corner, _ in scalars], couple)
    coef = lambda kind, j: coefs[j][kind]
    above, below = backward(coef, firsts, forward(coef, firsts, lasts), zero)
    for j in range(blocks):
        pairs[j, 0:1] = above[j]
        pairs[j, 1:2] = below[j]
    pair = pairs[d]
    row = lax.broadcasted_iota(jnp.int32, (slabs, wells), 0)
    own = force[pl.ds(pl.multiple_of(d * slabs, slabs), slabs)]
    own = own + jnp.where(row == 0, pair[0:1], 0.0) + jnp.where(row == slabs - 1, pair[1:2], 0.0)
    dot = functools.partial(jnp.dot, precision=HIGHEST, preferred_element_type=jnp.float32)
    wells_ref[...] = dot(inverse[...], own)
    for n in range(2):
        rows_ref[n] = dot(inverse[...], flux[n])


def extras(table, depth_index, info, cells_own, cells_other, flux, inverse, well, holders):
    blocks = info.shape[0]
    _, slabs, span = flux.shape
    wells = cells_own.shape[-1]
    smem = pl.BlockSpec(memory_space=pltpu.SMEM)
    vmem = pl.BlockSpec(memory_space=pltpu.VMEM)
    column = pltpu.VMEM((blocks * slabs, wells), jnp.float32)
    return pl.pallas_call(
        extras_kernel,
        in_specs=[smem, smem] + [vmem] * 7,
        out_specs=[vmem] * 3,
        out_shape=[
            jax.ShapeDtypeStruct((slabs, wells), jnp.float32),
            jax.ShapeDtypeStruct((2, slabs, span), jnp.float32),
            jax.ShapeDtypeStruct((1, holders.shape[1]), jnp.float32),
        ],
        scratch_shapes=[column] * 5 + [pltpu.VMEM((blocks, ROWS, wells), jnp.float32)],
        compiler_params=pltpu.CompilerParams(vmem_limit_bytes=SMALL_VMEM),
        cost_estimate=pl.CostEstimate(flops=10**7, bytes_accessed=10**6, transcendentals=0),
        name="extras",
    )(table, depth_index.reshape(1), info, cells_own, cells_other, flux, inverse, well, holders)


def solve_kernel(right, uv, inverse, place_row, place_column, solved_wells, outer, out, factor, pick):
    together, slabs, rows, span = right.shape
    wells = place_row.shape[1]
    step = pl.program_id(0)
    size = slabs * rows

    @pl.when(step == 0)
    def _():
        spread = (
            lax.broadcasted_iota(jnp.int32, (size, slabs), 0) // rows
            == lax.broadcasted_iota(jnp.int32, (size, slabs), 1)
        ).astype(jnp.float32).astype(jnp.bfloat16)
        spread_t = (
            lax.broadcasted_iota(jnp.int32, (slabs, size), 1) // rows
            == lax.broadcasted_iota(jnp.int32, (slabs, size), 0)
        ).astype(jnp.float32).astype(jnp.bfloat16)
        same = (
            lax.broadcasted_iota(jnp.int32, (size, size), 0) % rows
            == lax.broadcasted_iota(jnp.int32, (size, size), 1) % rows
        )
        for n, part in enumerate(split_bf16(inverse[...], 2)):
            tall = jnp.dot(spread, part, preferred_element_type=jnp.float32).astype(jnp.bfloat16)
            wide = jnp.dot(tall, spread_t, preferred_element_type=jnp.float32)
            wide = jnp.where(same, wide, 0.0).astype(jnp.bfloat16)
            if n == 0:
                factor[:, :size] = wide
                factor[:, size : 2 * size] = wide
            else:
                factor[:, 2 * size : 3 * size] = wide
        column = lax.broadcasted_iota(jnp.int32, (wells, span), 1)
        chosen = (column == place_column[...] % span).astype(jnp.float32).astype(jnp.bfloat16)
        pick[:wells] = chosen
        pick[wells:] = chosen

    tile = min(span, 256)
    for n in range(together):
        line = lax.broadcasted_iota(jnp.int32, (slabs, rows, wells), 1) + (step * together + n) * rows
        at_wells = jnp.where(line == (place_row[...] // span)[None], solved_wells[...][:, None, :], 0.0)
        at_wells = jnp.concatenate(split_bf16(at_wells.reshape(size, wells), 2), axis=1)
        factor[:, 3 * size :] = at_wells
        lines = slice(n * rows, (n + 1) * rows)
        above = jnp.concatenate([uv[d, 0, lines] for d in range(uv.shape[0])], axis=1)
        below = jnp.concatenate([uv[d, 1, lines] for d in range(uv.shape[0])], axis=1)
        for t in range(span // tile):
            cols = slice(t * tile, (t + 1) * tile)
            value = jnp.concatenate(
                [
                    right[n, 0:1, :, cols] + above[None, :, cols],
                    right[n, 1 : slabs - 1, :, cols],
                    right[n, slabs - 1 :, :, cols] + below[None, :, cols],
                ],
                axis=0,
            ).reshape(size, tile)
            upper, lower = split_bf16(value, 2)
            result = jnp.dot(
                factor[...],
                jnp.concatenate([upper, lower, upper, pick[:, cols]], axis=0),
                preferred_element_type=jnp.float32,
            )
            out[:, lines, cols] = result.reshape(slabs, rows, tile)

    for n, (when, line) in enumerate(((0, 0), (pl.num_programs(0) - 1, together * rows - 1))):

        @pl.when(step == when)
        def _():
            for z in range(slabs):
                out[z, line : line + 1, :] += outer[n, z : z + 1, :]


def solve(right, uv, inverse, place_row, solved_wells, outer):
    groups, slabs, _, span = right.shape
    wells = place_row.shape[1]
    together = 2
    lines = together * ROWS
    shares, _, _, share = uv.shape
    whole = lambda *shape: pl.BlockSpec(shape, lambda g: (0,) * len(shape))
    size = slabs * ROWS
    return pl.pallas_call(
        solve_kernel,
        grid=(groups // together,),
        in_specs=[
            pl.BlockSpec((together, slabs, ROWS, span), lambda g: (g, 0, 0, 0)),
            pl.BlockSpec((shares, 2, lines, share), lambda g: (0, 0, g, 0)),
            whole(slabs, slabs),
            whole(1, wells),
            whole(wells, 1),
            whole(slabs, wells),
            whole(*outer.shape),
        ],
        out_specs=pl.BlockSpec((slabs, lines, span), lambda g: (0, g, 0)),
        out_shape=jax.ShapeDtypeStruct((slabs, groups * ROWS, span), jnp.float32),
        scratch_shapes=[
            pltpu.VMEM((size, 3 * size + 2 * wells), jnp.bfloat16),
            pltpu.VMEM((2 * wells, span), jnp.bfloat16),
        ],
        compiler_params=pltpu.CompilerParams(vmem_limit_bytes=SOLVE_VMEM),
        cost_estimate=pl.CostEstimate(
            flops=8 * size * right.size, bytes_accessed=8 * right.size, transcendentals=0
        ),
        name="depth_solve",
    )(right, uv, inverse, place_row, place_row.reshape(wells, 1), solved_wells, outer)


def body(
    warmth_before,
    stratum_category,
    conductance_catalogue,
    pivot_matrix_reciprocal,
    linkage_factor,
    well_position_inside,
    well_holder_sequence,
    well_reach,
    entering_warmth,
    well_transfer_speed,
):
    slabs, lines, span = warmth_before.shape
    depth_index = lax.axis_index("depth")
    depth_count = lax.axis_size("depth")
    wells = well_position_inside.shape[0]
    owned = wells // depth_count
    table = conductance_catalogue

    parts = depth_count // 2
    halves = [list(range(h * parts, (h + 1) * parts)) for h in range(2)]
    half = (depth_index // parts).astype(jnp.int32).reshape(1)

    place_row = well_position_inside.reshape(1, wells)
    first, last = edge_rows(warmth_before, stratum_category, table)
    count = lax.axis_size("strip")
    up = [(i, i + 1) for i in range(count - 1)]
    down = [(j, i) for i, j in up]
    before = lax.ppermute(last, "strip", up)
    after = lax.ppermute(first, "strip", down)
    right, sums, cells = stencil(
        warmth_before, stratum_category, table, pivot_matrix_reciprocal, place_row
    )
    fl, flux = payload(
        linkage_factor, sums, first, last, before, after, pivot_matrix_reciprocal, cells, parts
    )
    exchange = functools.partial(
        lax.all_to_all,
        axis_name="depth",
        split_axis=0,
        concat_axis=0,
        tiled=True,
        axis_index_groups=halves,
    )
    fl_all = exchange(fl)

    across = functools.partial(
        lax.ppermute,
        axis_name="depth",
        perm=[(i, (i + parts) % depth_count) for i in range(depth_count)],
    )
    mine, cells_own = first_half(half, fl_all, slabs, lines, wells)
    other = across(mine)
    other, cells_own = lax.optimization_barrier((other, cells_own))
    cells_other = across(cells_own)
    uv, info_all = second_half(half, fl_all, mine, other, slabs, lines)
    uv_own = exchange(uv)

    well = jnp.stack([well_transfer_speed, entering_warmth, well_reach.astype(jnp.float32)])
    well = jnp.pad(well, ((0, ROWS - 3), (0, 0)))
    holders = lax.dynamic_slice_in_dim(well_holder_sequence, depth_index * owned, owned)
    solved_wells, outer, leaving = extras(
        table,
        depth_index,
        info_all,
        cells_own,
        cells_other,
        flux,
        pivot_matrix_reciprocal,
        well,
        holders.reshape(1, owned),
    )
    solved = solve(right, uv_own, pivot_matrix_reciprocal, place_row, solved_wells, outer)
    return solved, leaving.reshape(owned)


def solution(mesh):
    in_specs = (
        P("depth", "strip", None),
        P("depth", "strip", None),
        P(),
        P("depth", None),
        P("depth"),
        P("strip"),
        P("strip"),
        P("strip"),
        P("strip"),
        P("strip"),
    )
    out_specs = (P("depth", "strip", None), P(("strip", "depth")))
    return jax.shard_map(body, mesh=mesh, in_specs=in_specs, out_specs=out_specs, check_vma=False)
```

```python
import functools

import jax
import jax.numpy as jnp
from jax import lax
from jax.experimental import pallas as pl
from jax.experimental.pallas import tpu as pltpu
from jax.sharding import PartitionSpec as P

backward_euler_advance = 0.2
storage_volume = 2.0
flux_scale = 0.5 * backward_euler_advance
LANES = 128
ROWS = 8
EDGE_VMEM = 56 * 1024 * 1024
VMEM_LIMIT = 48 * 1024 * 1024
SOLVE_VMEM = 48 * 1024 * 1024
SMALL_VMEM = 12 * 1024 * 1024
HIGHEST = lax.Precision.HIGHEST


def select_tree(category, entries):
    values = list(entries)
    bit = 1
    while len(values) > 1:
        odd = (category & bit) != 0
        values = [
            jnp.where(odd, values[k + 1], values[k]) if k + 1 < len(values) else values[k]
            for k in range(0, len(values), 2)
        ]
        bit *= 2
    return values[0]


def split_bf16(value, pieces):
    out = []
    for k in range(pieces):
        part = value.astype(jnp.bfloat16)
        out.append(part)
        if k + 1 < pieces:
            value = value - part.astype(jnp.float32)
    return out


def edge_kernel(table, w_first, cat_first, w_last, cat_last, first, last):
    slabs, rows, span = w_first.shape
    entries = [flux_scale * table[k] for k in range(table.shape[0])]
    sub = lax.broadcasted_iota(jnp.int32, (ROWS, span), 0)

    def gathered(ref, start, row):
        value = jnp.broadcast_to(ref[start, row : row + 1, :], (ROWS, span))
        for k in range(1, ROWS):
            value = jnp.where(sub == k, ref[start + k, row : row + 1, :], value)
        return value

    for w_ref, cat_ref, row, out in ((w_first, cat_first, 0, first), (w_last, cat_last, rows - 1, last)):
        for start in range(0, slabs, ROWS):
            out[0, start : start + ROWS] = gathered(w_ref, start, row)
            out[1, start : start + ROWS] = select_tree(gathered(cat_ref, start, row), entries)


def edge_rows(w, cat, table):
    slabs, lines, span = w.shape
    top = pl.BlockSpec((slabs, ROWS, span), lambda i: (0, 0, 0))
    end = pl.BlockSpec((slabs, ROWS, span), lambda i: (0, lines // ROWS - 1, 0))
    out = pl.BlockSpec((2, slabs, span), lambda i: (0, 0, 0))
    return pl.pallas_call(
        edge_kernel,
        grid=(1,),
        in_specs=[pl.BlockSpec(memory_space=pltpu.SMEM), top, top, end, end],
        out_specs=[out, out],
        out_shape=[jax.ShapeDtypeStruct((2, slabs, span), jnp.float32)] * 2,
        compiler_params=pltpu.CompilerParams(vmem_limit_bytes=EDGE_VMEM),
        cost_estimate=pl.CostEstimate(flops=10**6, bytes_accessed=w.size, transcendentals=0),
        name="edge_rows",
    )(table, w, cat, w, cat)


def stencil_kernel(
    table,
    ends,
    w_ref,
    cat_ref,
    place,
    right_ref,
    acc,
    cells_ref,
    ws,
    cs,
    fs,
    pieces,
    shift,
    pick,
):
    step = pl.program_id(0)
    planes, lines, span = w_ref.shape
    tiles = span // LANES
    groups = lines // ROWS
    wells = place.shape[1]
    entries = [flux_scale * table[k] for k in range(table.shape[0])]
    lane = lax.broadcasted_iota(jnp.int32, (lines, LANES), 1)
    top, end = ROWS, ROWS + lines

    @pl.when(step == 0)
    def _():
        acc[...] = jnp.zeros_like(acc)
        source = lax.broadcasted_iota(jnp.int32, shift.shape, 0) % (2 * LANES)
        target = lax.broadcasted_iota(jnp.int32, shift.shape, 1)
        shift[...] = (source == target + 1).astype(jnp.float32).astype(jnp.bfloat16)
        column = lax.broadcasted_iota(jnp.int32, (span, wells), 0)
        pick[...] = (column == place[...] % span).astype(jnp.float32).astype(jnp.bfloat16)

    def keep_face(k, t, face):
        rows = pl.ds(pl.multiple_of(k * lines, lines), lines)
        for n, part in enumerate(split_bf16(face, 2)):
            pieces[n, rows, t * LANES : (t + 1) * LANES] = part

    def plane(k, carry):
        left_w = left_c = jnp.zeros((lines, LANES), jnp.float32)
        for t in range(tiles):
            cols = slice(t * LANES, (t + 1) * LANES)
            w = w_ref[k, :, cols]
            c = select_tree(cat_ref[k, :, cols], entries)
            for ref, value in ((ws, w), (cs, c)):
                ref[t, top:end] = value
                ref[t, top - 1 : top] = value[0:1]
            roll_w, roll_c = pltpu.roll(w, 1, 1), pltpu.roll(c, 1, 1)
            west_w = jnp.where(lane == 0, left_w, roll_w)
            west_c = jnp.where(lane == 0, left_c, roll_c)
            left_w, left_c = roll_w, roll_c
            face = (c + west_c) * (w - west_w)
            keep_face(k, t, face)
            if t == tiles - 1:
                keep_face(k, tiles, pltpu.roll(-c * w, 1, 1))
            north = (c + cs[t, top - 1 : end - 1]) * (w - ws[t, top - 1 : end - 1])
            fs[t, top:end] = north
            fs[t, end : end + 1] = jnp.zeros((1, LANES), jnp.float32)
            base = w - face - north + fs[t, top + 1 : end + 1]
            right_ref[:, k, :, cols] = base.reshape(groups, ROWS, LANES)
        return carry

    lax.fori_loop(0, planes, plane, 0)

    for t in range(tiles):
        cols = slice(t * LANES, (t + 1) * LANES)
        both = slice(t * LANES, (t + 2) * LANES)
        east = jnp.dot(
            jnp.concatenate([pieces[0, :, both], pieces[1, :, both]], axis=1),
            shift[...],
            preferred_element_type=jnp.float32,
        )
        first, final = acc[0, :, cols], acc[1, :, cols]
        for k in range(planes):
            z = step * planes + k
            value = right_ref[:, k, :, cols].reshape(lines, LANES) + east[k * lines : (k + 1) * lines]
            right_ref[:, k, :, cols] = value.reshape(groups, ROWS, LANES)
            first = first + ends[0, z] * value
            final = final + ends[ends.shape[0] - 1, z] * value
        acc[0, :, cols] = first
        acc[1, :, cols] = final

    dot = functools.partial(jnp.dot, preferred_element_type=jnp.float32)
    own_line = lax.broadcasted_iota(jnp.int32, (lines, wells), 0) == place[...] // span
    upper, lower = split_bf16(w_ref[...].reshape(planes * lines, span), 2)
    kinds = cat_ref[...].astype(jnp.float32).reshape(planes * lines, span).astype(jnp.bfloat16)
    sums = [dot(upper, pick[...]) + dot(lower, pick[...]), dot(kinds, pick[...])]
    for n in range(2):
        for k in range(planes):
            mine = jnp.where(own_line, sums[n][k * lines : (k + 1) * lines], 0.0)
            cells_ref[n, k : k + 1, :] = jnp.sum(mine, axis=0, keepdims=True)


def stencil(w, cat, table, inverse, place_row):
    slabs, lines, span = w.shape
    planes, groups = 8, lines // ROWS
    wells = place_row.shape[1]
    block = pl.BlockSpec((planes, lines, span), lambda i: (i, 0, 0))
    smem = pl.BlockSpec(memory_space=pltpu.SMEM)
    shifted = pltpu.VMEM((span // LANES, lines + 2 * ROWS, LANES), jnp.float32)
    return pl.pallas_call(
        stencil_kernel,
        grid=(slabs // planes,),
        in_specs=[smem, smem, block, block, pl.BlockSpec((1, wells), lambda i: (0, 0))],
        out_specs=[
            pl.BlockSpec((groups, planes, ROWS, span), lambda i: (0, i, 0, 0)),
            pl.BlockSpec((2, lines, span), lambda i: (0, 0, 0)),
            pl.BlockSpec((2, planes, wells), lambda i: (0, i, 0)),
        ],
        out_shape=[
            jax.ShapeDtypeStruct((groups, slabs, ROWS, span), jnp.float32),
            jax.ShapeDtypeStruct((2, lines, span), jnp.float32),
            jax.ShapeDtypeStruct((2, slabs, wells), jnp.float32),
        ],
        scratch_shapes=[
            shifted,
            shifted,
            shifted,
            pltpu.VMEM((2, planes * lines, span + LANES), jnp.bfloat16),
            pltpu.VMEM((4 * LANES, LANES), jnp.bfloat16),
            pltpu.VMEM((span, wells), jnp.bfloat16),
        ],
        compiler_params=pltpu.CompilerParams(vmem_limit_bytes=VMEM_LIMIT),
        cost_estimate=pl.CostEstimate(flops=40 * w.size, bytes_accessed=12 * w.size, transcendentals=0),
        name="stencil",
    )(table, inverse, w, cat, place_row)


def payload_kernel(ratio, sums, first, last, before, after, inverse, out_ref, flux_ref):
    copies, _, share = out_ref.shape
    _, lines, span = sums.shape
    slabs = inverse.shape[0]
    ends = jnp.concatenate([inverse[0:1], inverse[slabs - 1 : slabs]], axis=0)
    info = 2 * lines
    for d in range(copies):
        cols = slice(d * share, (d + 1) * share)
        for q in range(2):
            out_ref[d, q * lines : (q + 1) * lines] = sums[q, :, cols]
        out_ref[d, info : info + ROWS] = jnp.zeros((ROWS, share), jnp.float32)
        out_ref[d, info : info + 2, :slabs] = ends
        out_ref[d, info : info + 1, slabs : slabs + 1] = jnp.full((1, 1), ratio[0])
    for own, other, line, n in ((first, before, 0, 0), (last, after, lines - 1, 1)):
        flux = (own[1] + other[1]) * (other[0] - own[0])
        flux_ref[n] = flux
        extra = jnp.dot(ends, flux, precision=HIGHEST, preferred_element_type=jnp.float32)
        for d in range(copies):
            for q in range(2):
                at = q * lines + line
                out_ref[d, at : at + 1] += extra[q : q + 1, d * share : (d + 1) * share]


def payload(ratio, sums, first, last, before, after, inverse, copies):
    _, lines, span = sums.shape
    slabs = inverse.shape[0]
    share = span // copies
    rows = 2 * lines + ROWS
    vmem = pl.BlockSpec(memory_space=pltpu.VMEM)
    return pl.pallas_call(
        payload_kernel,
        in_specs=[pl.BlockSpec(memory_space=pltpu.SMEM)] + [vmem] * 6,
        out_specs=[vmem] * 2,
        out_shape=[
            jax.ShapeDtypeStruct((copies, rows, share), jnp.float32),
            jax.ShapeDtypeStruct((2, slabs, span), jnp.float32),
        ],
        compiler_params=pltpu.CompilerParams(vmem_limit_bytes=SMALL_VMEM),
        cost_estimate=pl.CostEstimate(flops=10**6, bytes_accessed=10**6, transcendentals=0),
        name="payload",
    )(ratio, sums, first, last, before, after, inverse)


CORNERS = ((0, 0), (0, 1), (1, 0), (1, 1))


def block_scalars(tile, slabs, shape, flipped=None):
    at = lambda row, lane: jnp.broadcast_to(tile[row : row + 1, lane : lane + 1], shape)
    corner = {(r, c): at(r, c * (slabs - 1)) for r, c in CORNERS}
    if flipped is not None:
        corner = {(r, c): jnp.where(flipped, corner[1 - r, 1 - c], corner[r, c]) for r, c in CORNERS}
    return corner, at(0, slabs)


def coupling(ratio, one, other, slabs):
    return ratio * (slabs / (slabs + 1.0)) / jnp.sqrt(one * other)


def chain(corners, couple, q=None):
    out = []
    q = jnp.zeros_like(couple[0])
    for k, corner in enumerate(corners):
        vf, vl = couple[k] * corner[0, 0], couple[k] * corner[1, 0]
        wf, wl = couple[k + 1] * corner[0, 1], couple[k + 1] * corner[1, 1]
        inverse = 1.0 / (1.0 - vf * q)
        out.append(
            dict(
                p_first=vl * q * inverse,
                p_before=vl * inverse,
                a_first=inverse,
                a_before=vf * inverse,
                a_after=wf * inverse,
                couple=couple[k],
                couple_after=couple[k + 1],
                q=q,
            )
        )
        q = wl + vl * q * wf * inverse
    return out, q


KINDS = ("p_first", "p_before", "a_first", "a_before", "a_after", "couple", "couple_after", "q")


def forward(coef, firsts, lasts):
    before = [jnp.zeros_like(firsts[0])]
    for j in range(len(firsts)):
        before.append(
            lasts[j] + coef("p_first", j) * firsts[j] + coef("p_before", j) * before[j]
        )
    return before


def backward(coef, firsts, before, after):
    blocks = len(firsts)
    above, below = [None] * blocks, [None] * blocks
    for j in reversed(range(blocks)):
        below[j] = coef("couple_after", j) * after
        here = (
            coef("a_first", j) * firsts[j]
            + coef("a_before", j) * before[j]
            + coef("a_after", j) * after
        )
        above[j] = coef("couple", j) * (before[j] + coef("q", j) * here)
        after = here
    return above, below


def half_chain(tiles, slabs, flipped, middle):
    shape = (ROWS, LANES)
    scalars = [block_scalars(tile, slabs, shape, flipped) for tile in tiles]
    couple = [jnp.zeros(shape, jnp.float32)]
    for k in range(1, len(tiles)):
        ratio = jnp.where(flipped, scalars[k - 1][1], scalars[k][1])
        couple.append(coupling(ratio, scalars[k - 1][0][1, 1], scalars[k][0][0, 0], slabs))
    couple.append(middle)
    return chain([corner for corner, _ in scalars], couple)


def first_kernel(slabs, half, fl_ref, out_ref, table):
    blocks, rows, share = fl_ref.shape
    lines = (rows - ROWS) // 2
    info = 2 * lines
    flip = half[0]
    flipped = flip == 1
    block = [k + flip * (blocks - 1 - 2 * k) for k in range(blocks)]
    entries, _ = half_chain(
        [fl_ref[block[k], info : info + ROWS, :LANES] for k in range(blocks)],
        slabs,
        flipped,
        jnp.zeros((ROWS, LANES), jnp.float32),
    )
    for k, entry in enumerate(entries):
        for n, kind in enumerate(KINDS[:2]):
            table[k, n] = entry[kind]
    coef = lambda kind, k: table[k, KINDS.index(kind)]

    def group(g, carry):
        rows = pl.ds(pl.multiple_of(g * ROWS, ROWS), ROWS)
        outer = pl.ds(pl.multiple_of(flip * lines + g * ROWS, ROWS), ROWS)
        inner = pl.ds(pl.multiple_of((1 - flip) * lines + g * ROWS, ROWS), ROWS)
        for t in range(share // LANES):
            cols = slice(t * LANES, (t + 1) * LANES)
            before = forward(
                coef,
                [fl_ref[block[k], outer, cols] for k in range(blocks)],
                [fl_ref[block[k], inner, cols] for k in range(blocks)],
            )
            out_ref[rows, cols] = before[blocks]
        return carry

    lax.fori_loop(0, lines // ROWS, group, 0)
    out_ref[lines:, :] = jnp.zeros((out_ref.shape[0] - lines, share), jnp.float32)
    for j in range(blocks):
        out_ref[lines + 2 * j : lines + 2 * j + 2, :] = fl_ref[j, info : info + 2, :]


def first_half(half, fl, slabs):
    parts, rows, share = fl.shape
    vmem = pl.BlockSpec(memory_space=pltpu.VMEM)
    rows = (rows - ROWS) // 2 + -(-2 * parts // ROWS) * ROWS
    return pl.pallas_call(
        functools.partial(first_kernel, slabs),
        in_specs=[pl.BlockSpec(memory_space=pltpu.SMEM), vmem],
        out_specs=vmem,
        out_shape=jax.ShapeDtypeStruct((rows, share), jnp.float32),
        scratch_shapes=[pltpu.VMEM((parts, 2, ROWS, LANES), jnp.float32)],
        compiler_params=pltpu.CompilerParams(vmem_limit_bytes=SMALL_VMEM),
        cost_estimate=pl.CostEstimate(flops=4 * fl.size, bytes_accessed=5 * fl.size, transcendentals=0),
        name="reduced_in",
    )(half, fl)


def second_kernel(slabs, half, fl_ref, mine, other, uv_ref, info_ref, table):
    blocks, _, lines, share = uv_ref.shape
    flip = half[0]
    flipped = flip == 1
    block = [k + flip * (blocks - 1 - 2 * k) for k in range(blocks)]
    for j in range(blocks):
        info_ref[flip * blocks + j] = fl_ref[j, 2 * lines : 2 * lines + ROWS, :LANES]
        info_ref[(1 - flip) * blocks + j] = jnp.zeros((ROWS, LANES), jnp.float32)
        info_ref[(1 - flip) * blocks + j, 0:2] = other[lines + 2 * j : lines + 2 * j + 2, :LANES]
    shape = (ROWS, LANES)
    above, above_ratio = block_scalars(info_ref[blocks - 1], slabs, shape)
    below, below_ratio = block_scalars(info_ref[blocks], slabs, shape)
    middle = coupling(below_ratio, above[1, 1], below[0, 0], slabs)
    tiles = lambda flip: [
        info_ref[flip * blocks + k + flip * (blocks - 1 - 2 * k)] for k in range(blocks)
    ]
    entries, q_own = half_chain(tiles(flip), slabs, flipped, middle)
    _, q_other = half_chain(tiles(1 - flip), slabs, jnp.logical_not(flipped), middle)
    for k, entry in enumerate(entries):
        for n, kind in enumerate(KINDS):
            table[k, n] = entry[kind]
    table[blocks, 0] = 1.0 / (1.0 - q_own * q_other)
    table[blocks, 1] = q_other
    coef = lambda kind, k: table[k, KINDS.index(kind)]

    def group(g, carry):
        rows = pl.ds(pl.multiple_of(g * ROWS, ROWS), ROWS)
        outside = pl.ds(pl.multiple_of(flip * lines + g * ROWS, ROWS), ROWS)
        inside = pl.ds(pl.multiple_of((1 - flip) * lines + g * ROWS, ROWS), ROWS)
        for t in range(share // LANES):
            cols = slice(t * LANES, (t + 1) * LANES)
            firsts = [fl_ref[block[k], outside, cols] for k in range(blocks)]
            lasts = [fl_ref[block[k], inside, cols] for k in range(blocks - 1)]
            before = forward(coef, firsts[:-1], lasts)
            across = table[blocks, 0] * (other[rows, cols] + table[blocks, 1] * mine[rows, cols])
            outer, inner = backward(coef, firsts, before, across)
            for k in range(blocks):
                uv_ref[block[k], flip, rows, cols] = outer[k]
                uv_ref[block[k], 1 - flip, rows, cols] = inner[k]
        return carry

    lax.fori_loop(0, lines // ROWS, group, 0)


def second_half(half, fl, mine, other, slabs):
    parts, rows, share = fl.shape
    lines = (rows - ROWS) // 2
    vmem = pl.BlockSpec(memory_space=pltpu.VMEM)
    return pl.pallas_call(
        functools.partial(second_kernel, slabs),
        in_specs=[pl.BlockSpec(memory_space=pltpu.SMEM), vmem, vmem, vmem],
        out_specs=[vmem, vmem],
        out_shape=[
            jax.ShapeDtypeStruct((parts, 2, lines, share), jnp.float32),
            jax.ShapeDtypeStruct((2 * parts, ROWS, LANES), jnp.float32),
        ],
        scratch_shapes=[pltpu.VMEM((parts + 1, len(KINDS), ROWS, LANES), jnp.float32)],
        compiler_params=pltpu.CompilerParams(vmem_limit_bytes=SMALL_VMEM),
        cost_estimate=pl.CostEstimate(flops=10 * fl.size, bytes_accessed=9 * fl.size, transcendentals=0),
        name="reduced_out",
    )(half, fl, mine, other)


def extras_kernel(
    table,
    where_am_i,
    info,
    cells,
    flux,
    inverse,
    well,
    holders,
    wells_ref,
    rows_ref,
    leaving,
    keep,
    force,
    rate,
    down,
    rise,
    pairs,
):
    blocks = info.shape[0]
    slabs, wells = wells_ref.shape
    d = where_am_i[0]
    place = []
    for j in range(blocks):
        apart = d ^ j
        place.append(2 * (apart & (blocks // 2 - 1)) + apart // (blocks // 2))
    speed, inlet, reach = well[0:1], well[1:2], well[2:3]
    entries = [table[k] for k in range(table.shape[0])]
    level = lax.broadcasted_iota(jnp.int32, (slabs, wells), 0)
    for j in range(blocks):
        cond = select_tree(cells[place[j], 1].astype(jnp.int32), entries)
        inside = (level + j * slabs).astype(jnp.float32) < reach
        here = jnp.where(inside, speed * cond / (1.0 + cond), 0.0)
        rows = slice(j * slabs, (j + 1) * slabs)
        rate[rows] = here
        keep[rows] = 1.0 - here
        force[rows] = here * cells[place[j], 0]

    chunks = blocks * slabs // ROWS

    def descend(i, value):
        rows = pl.ds(pl.multiple_of(i * ROWS, ROWS), ROWS)
        a, b = keep[rows], force[rows]
        seen = []
        for r in range(ROWS):
            seen.append(value)
            value = a[r : r + 1] * value + b[r : r + 1]
        down[rows] = jnp.concatenate(seen, axis=0)
        return value

    def ascend(i, value):
        rows = pl.ds(pl.multiple_of((chunks - 1 - i) * ROWS, ROWS), ROWS)
        a, b = keep[rows], force[rows]
        seen = []
        for r in reversed(range(ROWS)):
            seen.append(value)
            value = a[r : r + 1] * value + b[r : r + 1]
        rise[rows] = jnp.concatenate(seen[::-1], axis=0)
        return value

    bottom = lax.fori_loop(0, chunks, descend, inlet)
    surface = lax.fori_loop(0, chunks, ascend, bottom)
    held = holders[...] == lax.broadcasted_iota(jnp.int32, (wells, holders.shape[1]), 0)
    leaving[...] = jnp.dot(
        jnp.broadcast_to(surface, (ROWS, wells)),
        held.astype(jnp.float32),
        precision=HIGHEST,
        preferred_element_type=jnp.float32,
    )[0:1]

    for j in range(blocks):
        rows = slice(j * slabs, (j + 1) * slabs)
        taken = rate[rows] * (2.0 * cells[place[j], 0] - down[rows] - rise[rows])
        force[rows] = -storage_volume * taken
    firsts, lasts = [], []
    for j in range(blocks):
        both = jnp.dot(
            info[j, :, :slabs],
            force[j * slabs : (j + 1) * slabs],
            precision=HIGHEST,
            preferred_element_type=jnp.float32,
        )
        firsts.append(both[0:1])
        lasts.append(both[1:2])

    scalars = [block_scalars(info[j], slabs, (1, wells)) for j in range(blocks)]
    zero = jnp.zeros((1, wells), jnp.float32)
    couple = [zero]
    for j in range(1, blocks):
        couple.append(
            coupling(scalars[j][1], scalars[j - 1][0][1, 1], scalars[j][0][0, 0], slabs)
        )
    couple.append(zero)
    coefs, _ = chain([corner for corner, _ in scalars], couple)
    coef = lambda kind, j: coefs[j][kind]
    above, below = backward(coef, firsts, forward(coef, firsts, lasts), zero)
    for j in range(blocks):
        pairs[j, 0:1] = above[j]
        pairs[j, 1:2] = below[j]
    pair = pairs[d]
    row = lax.broadcasted_iota(jnp.int32, (slabs, wells), 0)
    own = force[pl.ds(pl.multiple_of(d * slabs, slabs), slabs)]
    own = own + jnp.where(row == 0, pair[0:1], 0.0) + jnp.where(row == slabs - 1, pair[1:2], 0.0)
    dot = functools.partial(jnp.dot, precision=HIGHEST, preferred_element_type=jnp.float32)
    wells_ref[...] = dot(inverse[...], own)
    for n in range(2):
        rows_ref[n] = dot(inverse[...], flux[n])


def extras(table, depth_index, info, cells, flux, inverse, well, holders):
    blocks = info.shape[0]
    _, slabs, span = flux.shape
    wells = cells.shape[-1]
    smem = pl.BlockSpec(memory_space=pltpu.SMEM)
    vmem = pl.BlockSpec(memory_space=pltpu.VMEM)
    column = pltpu.VMEM((blocks * slabs, wells), jnp.float32)
    return pl.pallas_call(
        extras_kernel,
        in_specs=[smem, smem] + [vmem] * 6,
        out_specs=[vmem] * 3,
        out_shape=[
            jax.ShapeDtypeStruct((slabs, wells), jnp.float32),
            jax.ShapeDtypeStruct((2, slabs, span), jnp.float32),
            jax.ShapeDtypeStruct((1, holders.shape[1]), jnp.float32),
        ],
        scratch_shapes=[column] * 5 + [pltpu.VMEM((blocks, ROWS, wells), jnp.float32)],
        compiler_params=pltpu.CompilerParams(vmem_limit_bytes=SMALL_VMEM),
        cost_estimate=pl.CostEstimate(flops=10**7, bytes_accessed=10**6, transcendentals=0),
        name="extras",
    )(table, depth_index.reshape(1), info, cells, flux, inverse, well, holders)


def solve_kernel(right, uv, inverse, place_row, place_column, solved_wells, outer, out, factor, pick):
    together, slabs, rows, span = right.shape
    wells = place_row.shape[1]
    step = pl.program_id(0)
    size = slabs * rows

    @pl.when(step == 0)
    def _():
        spread = (
            lax.broadcasted_iota(jnp.int32, (size, slabs), 0) // rows
            == lax.broadcasted_iota(jnp.int32, (size, slabs), 1)
        ).astype(jnp.float32).astype(jnp.bfloat16)
        spread_t = (
            lax.broadcasted_iota(jnp.int32, (slabs, size), 1) // rows
            == lax.broadcasted_iota(jnp.int32, (slabs, size), 0)
        ).astype(jnp.float32).astype(jnp.bfloat16)
        same = (
            lax.broadcasted_iota(jnp.int32, (size, size), 0) % rows
            == lax.broadcasted_iota(jnp.int32, (size, size), 1) % rows
        )
        for n, part in enumerate(split_bf16(inverse[...], 2)):
            tall = jnp.dot(spread, part, preferred_element_type=jnp.float32).astype(jnp.bfloat16)
            wide = jnp.dot(tall, spread_t, preferred_element_type=jnp.float32)
            wide = jnp.where(same, wide, 0.0).astype(jnp.bfloat16)
            if n == 0:
                factor[:, :size] = wide
                factor[:, size : 2 * size] = wide
            else:
                factor[:, 2 * size : 3 * size] = wide
        column = lax.broadcasted_iota(jnp.int32, (wells, span), 1)
        chosen = (column == place_column[...] % span).astype(jnp.float32).astype(jnp.bfloat16)
        pick[:wells] = chosen
        pick[wells:] = chosen

    tile = min(span, 256)
    for n in range(together):
        line = lax.broadcasted_iota(jnp.int32, (slabs, rows, wells), 1) + (step * together + n) * rows
        at_wells = jnp.where(line == (place_row[...] // span)[None], solved_wells[...][:, None, :], 0.0)
        at_wells = jnp.concatenate(split_bf16(at_wells.reshape(size, wells), 2), axis=1)
        factor[:, 3 * size :] = at_wells
        lines = slice(n * rows, (n + 1) * rows)
        above = jnp.concatenate([uv[d, 0, lines] for d in range(uv.shape[0])], axis=1)
        below = jnp.concatenate([uv[d, 1, lines] for d in range(uv.shape[0])], axis=1)
        for t in range(span // tile):
            cols = slice(t * tile, (t + 1) * tile)
            value = jnp.concatenate(
                [
                    right[n, 0:1, :, cols] + above[None, :, cols],
                    right[n, 1 : slabs - 1, :, cols],
                    right[n, slabs - 1 :, :, cols] + below[None, :, cols],
                ],
                axis=0,
            ).reshape(size, tile)
            upper, lower = split_bf16(value, 2)
            result = jnp.dot(
                factor[...],
                jnp.concatenate([upper, lower, upper, pick[:, cols]], axis=0),
                preferred_element_type=jnp.float32,
            )
            out[:, lines, cols] = result.reshape(slabs, rows, tile)

    for n, (when, line) in enumerate(((0, 0), (pl.num_programs(0) - 1, together * rows - 1))):

        @pl.when(step == when)
        def _():
            for z in range(slabs):
                out[z, line : line + 1, :] += outer[n, z : z + 1, :]


def solve(right, uv, inverse, place_row, solved_wells, outer):
    groups, slabs, _, span = right.shape
    wells = place_row.shape[1]
    together = 1
    lines = together * ROWS
    shares, _, _, share = uv.shape
    whole = lambda *shape: pl.BlockSpec(shape, lambda g: (0,) * len(shape))
    size = slabs * ROWS
    return pl.pallas_call(
        solve_kernel,
        grid=(groups // together,),
        in_specs=[
            pl.BlockSpec((together, slabs, ROWS, span), lambda g: (g, 0, 0, 0)),
            pl.BlockSpec((shares, 2, lines, share), lambda g: (0, 0, g, 0)),
            whole(slabs, slabs),
            whole(1, wells),
            whole(wells, 1),
            whole(slabs, wells),
            whole(*outer.shape),
        ],
        out_specs=pl.BlockSpec((slabs, lines, span), lambda g: (0, g, 0)),
        out_shape=jax.ShapeDtypeStruct((slabs, groups * ROWS, span), jnp.float32),
        scratch_shapes=[
            pltpu.VMEM((size, 3 * size + 2 * wells), jnp.bfloat16),
            pltpu.VMEM((2 * wells, span), jnp.bfloat16),
        ],
        compiler_params=pltpu.CompilerParams(vmem_limit_bytes=SOLVE_VMEM),
        cost_estimate=pl.CostEstimate(
            flops=8 * size * right.size, bytes_accessed=8 * right.size, transcendentals=0
        ),
        name="depth_solve",
    )(right, uv, inverse, place_row, place_row.reshape(wells, 1), solved_wells, outer)


def body(
    warmth_before,
    stratum_category,
    conductance_catalogue,
    pivot_matrix_reciprocal,
    linkage_factor,
    well_position_inside,
    well_holder_sequence,
    well_reach,
    entering_warmth,
    well_transfer_speed,
):
    slabs, lines, span = warmth_before.shape
    depth_index = lax.axis_index("depth")
    depth_count = lax.axis_size("depth")
    wells = well_position_inside.shape[0]
    owned = wells // depth_count
    table = conductance_catalogue

    parts = depth_count // 2
    halves = [list(range(h * parts, (h + 1) * parts)) for h in range(2)]
    half = (depth_index // parts).astype(jnp.int32).reshape(1)

    place_row = well_position_inside.reshape(1, wells)
    first, last = edge_rows(warmth_before, stratum_category, table)
    first, last, place_row = lax.optimization_barrier((first, last, place_row))
    count = lax.axis_size("strip")
    up = [(i, i + 1) for i in range(count - 1)]
    down = [(j, i) for i, j in up]
    before = lax.ppermute(last, "strip", up)
    after = lax.ppermute(first, "strip", down)
    right, sums, cells = stencil(
        warmth_before, stratum_category, table, pivot_matrix_reciprocal, place_row
    )
    fl, flux = payload(
        linkage_factor, sums, first, last, before, after, pivot_matrix_reciprocal, parts
    )
    exchange = functools.partial(
        lax.all_to_all,
        axis_name="depth",
        split_axis=0,
        concat_axis=0,
        tiled=True,
        axis_index_groups=halves,
    )
    fl, cells = lax.optimization_barrier((fl, cells))
    fl_all = exchange(fl)

    def swapped(value, mask):
        return lax.ppermute(value, "depth", [(i, i ^ mask) for i in range(depth_count)])

    cells = cells[None]
    for mask in [parts] + [2**k for k in range(parts.bit_length() - 1)]:
        cells = jnp.concatenate([cells, swapped(cells, mask)])

    mine = first_half(half, fl_all, slabs)
    other = swapped(mine, parts)
    uv, info_all = second_half(half, fl_all, mine, other, slabs)
    uv, cells = lax.optimization_barrier((uv, cells))
    uv_own = exchange(uv)

    well = jnp.stack([well_transfer_speed, entering_warmth, well_reach.astype(jnp.float32)])
    well = jnp.pad(well, ((0, ROWS - 3), (0, 0)))
    holders = lax.dynamic_slice_in_dim(well_holder_sequence, depth_index * owned, owned)
    solved_wells, outer, leaving = extras(
        table,
        depth_index,
        info_all,
        cells,
        flux,
        pivot_matrix_reciprocal,
        well,
        holders.reshape(1, owned),
    )
    solved = solve(right, uv_own, pivot_matrix_reciprocal, place_row, solved_wells, outer)
    return solved, leaving.reshape(owned)


def solution(mesh):
    in_specs = (
        P("depth", "strip", None),
        P("depth", "strip", None),
        P(),
        P("depth", None),
        P("depth"),
        P("strip"),
        P("strip"),
        P("strip"),
        P("strip"),
        P("strip"),
    )
    out_specs = (P("depth", "strip", None), P(("strip", "depth")))
    return jax.shard_map(body, mesh=mesh, in_specs=in_specs, out_specs=out_specs, check_vma=False)
```

```python
import functools

import jax
import jax.numpy as jnp
from jax import lax
from jax.experimental import pallas as pl
from jax.experimental.pallas import tpu as pltpu
from jax.sharding import PartitionSpec as P

backward_euler_advance = 0.2
storage_volume = 2.0
flux_scale = 0.5 * backward_euler_advance
LANES = 128
ROWS = 8
EDGE_VMEM = 56 * 1024 * 1024
VMEM_LIMIT = 48 * 1024 * 1024
SOLVE_VMEM = 48 * 1024 * 1024
SMALL_VMEM = 12 * 1024 * 1024
HIGHEST = lax.Precision.HIGHEST


def select_tree(category, entries):
    values = list(entries)
    bit = 1
    while len(values) > 1:
        odd = (category & bit) != 0
        values = [
            jnp.where(odd, values[k + 1], values[k]) if k + 1 < len(values) else values[k]
            for k in range(0, len(values), 2)
        ]
        bit *= 2
    return values[0]


def split_bf16(value, pieces):
    out = []
    for k in range(pieces):
        part = value.astype(jnp.bfloat16)
        out.append(part)
        if k + 1 < pieces:
            value = value - part.astype(jnp.float32)
    return out


def edge_kernel(table, w_first, cat_first, w_last, cat_last, first, last):
    slabs, rows, span = w_first.shape
    entries = [flux_scale * table[k] for k in range(table.shape[0])]
    sub = lax.broadcasted_iota(jnp.int32, (ROWS, span), 0)

    def gathered(ref, start, row):
        value = jnp.broadcast_to(ref[start, row : row + 1, :], (ROWS, span))
        for k in range(1, ROWS):
            value = jnp.where(sub == k, ref[start + k, row : row + 1, :], value)
        return value

    for w_ref, cat_ref, row, out in ((w_first, cat_first, 0, first), (w_last, cat_last, rows - 1, last)):
        for start in range(0, slabs, ROWS):
            out[0, start : start + ROWS] = gathered(w_ref, start, row)
            out[1, start : start + ROWS] = select_tree(gathered(cat_ref, start, row), entries)


def edge_rows(w, cat, table):
    slabs, lines, span = w.shape
    top = pl.BlockSpec((slabs, ROWS, span), lambda i: (0, 0, 0))
    end = pl.BlockSpec((slabs, ROWS, span), lambda i: (0, lines // ROWS - 1, 0))
    out = pl.BlockSpec((2, slabs, span), lambda i: (0, 0, 0))
    return pl.pallas_call(
        edge_kernel,
        grid=(1,),
        in_specs=[pl.BlockSpec(memory_space=pltpu.SMEM), top, top, end, end],
        out_specs=[out, out],
        out_shape=[jax.ShapeDtypeStruct((2, slabs, span), jnp.float32)] * 2,
        compiler_params=pltpu.CompilerParams(vmem_limit_bytes=EDGE_VMEM),
        cost_estimate=pl.CostEstimate(flops=10**6, bytes_accessed=w.size, transcendentals=0),
        name="edge_rows",
    )(table, w, cat, w, cat)


def stencil_kernel(
    table,
    ends,
    w_ref,
    cat_ref,
    place,
    right_ref,
    acc,
    cells_ref,
    ws,
    cs,
    fs,
    pieces,
    shift,
    pick,
):
    step = pl.program_id(0)
    planes, lines, span = w_ref.shape
    tiles = span // LANES
    groups = lines // ROWS
    wells = place.shape[1]
    entries = [flux_scale * table[k] for k in range(table.shape[0])]
    lane = lax.broadcasted_iota(jnp.int32, (lines, LANES), 1)
    top, end = ROWS, ROWS + lines

    @pl.when(step == 0)
    def _():
        acc[...] = jnp.zeros_like(acc)
        source = lax.broadcasted_iota(jnp.int32, shift.shape, 0) % (2 * LANES)
        target = lax.broadcasted_iota(jnp.int32, shift.shape, 1)
        shift[...] = (source == target + 1).astype(jnp.float32).astype(jnp.bfloat16)
        column = lax.broadcasted_iota(jnp.int32, (span, wells), 0)
        pick[...] = (column == place[...] % span).astype(jnp.float32).astype(jnp.bfloat16)

    def keep_face(k, t, face):
        rows = pl.ds(pl.multiple_of(k * lines, lines), lines)
        for n, part in enumerate(split_bf16(face, 2)):
            pieces[n, rows, t * LANES : (t + 1) * LANES] = part

    def plane(k, carry):
        left_w = left_c = jnp.zeros((lines, LANES), jnp.float32)
        for t in range(tiles):
            cols = slice(t * LANES, (t + 1) * LANES)
            w = w_ref[k, :, cols]
            c = select_tree(cat_ref[k, :, cols], entries)
            for ref, value in ((ws, w), (cs, c)):
                ref[t, top:end] = value
                ref[t, top - 1 : top] = value[0:1]
            roll_w, roll_c = pltpu.roll(w, 1, 1), pltpu.roll(c, 1, 1)
            west_w = jnp.where(lane == 0, left_w, roll_w)
            west_c = jnp.where(lane == 0, left_c, roll_c)
            left_w, left_c = roll_w, roll_c
            face = (c + west_c) * (w - west_w)
            keep_face(k, t, face)
            if t == tiles - 1:
                keep_face(k, tiles, pltpu.roll(-c * w, 1, 1))
            north = (c + cs[t, top - 1 : end - 1]) * (w - ws[t, top - 1 : end - 1])
            fs[t, top:end] = north
            fs[t, end : end + 1] = jnp.zeros((1, LANES), jnp.float32)
            base = w - face - north + fs[t, top + 1 : end + 1]
            right_ref[:, k, :, cols] = base.reshape(groups, ROWS, LANES)
        return carry

    lax.fori_loop(0, planes, plane, 0)

    for t in range(tiles):
        cols = slice(t * LANES, (t + 1) * LANES)
        both = slice(t * LANES, (t + 2) * LANES)
        east = jnp.dot(
            jnp.concatenate([pieces[0, :, both], pieces[1, :, both]], axis=1),
            shift[...],
            preferred_element_type=jnp.float32,
        )
        first, final = acc[0, :, cols], acc[1, :, cols]
        for k in range(planes):
            z = step * planes + k
            value = right_ref[:, k, :, cols].reshape(lines, LANES) + east[k * lines : (k + 1) * lines]
            right_ref[:, k, :, cols] = value.reshape(groups, ROWS, LANES)
            first = first + ends[0, z] * value
            final = final + ends[ends.shape[0] - 1, z] * value
        acc[0, :, cols] = first
        acc[1, :, cols] = final

    dot = functools.partial(jnp.dot, preferred_element_type=jnp.float32)
    own_line = lax.broadcasted_iota(jnp.int32, (lines, wells), 0) == place[...] // span
    upper, lower = split_bf16(w_ref[...].reshape(planes * lines, span), 2)
    kinds = cat_ref[...].astype(jnp.float32).reshape(planes * lines, span).astype(jnp.bfloat16)
    sums = [dot(upper, pick[...]) + dot(lower, pick[...]), dot(kinds, pick[...])]
    for n in range(2):
        for k in range(planes):
            mine = jnp.where(own_line, sums[n][k * lines : (k + 1) * lines], 0.0)
            cells_ref[n, k : k + 1, :] = jnp.sum(mine, axis=0, keepdims=True)


def stencil(w, cat, table, inverse, place_row):
    slabs, lines, span = w.shape
    planes, groups = 8, lines // ROWS
    wells = place_row.shape[1]
    block = pl.BlockSpec((planes, lines, span), lambda i: (i, 0, 0))
    smem = pl.BlockSpec(memory_space=pltpu.SMEM)
    shifted = pltpu.VMEM((span // LANES, lines + 2 * ROWS, LANES), jnp.float32)
    return pl.pallas_call(
        stencil_kernel,
        grid=(slabs // planes,),
        in_specs=[smem, smem, block, block, pl.BlockSpec((1, wells), lambda i: (0, 0))],
        out_specs=[
            pl.BlockSpec((groups, planes, ROWS, span), lambda i: (0, i, 0, 0)),
            pl.BlockSpec((2, lines, span), lambda i: (0, 0, 0)),
            pl.BlockSpec((2, planes, wells), lambda i: (0, i, 0)),
        ],
        out_shape=[
            jax.ShapeDtypeStruct((groups, slabs, ROWS, span), jnp.float32),
            jax.ShapeDtypeStruct((2, lines, span), jnp.float32),
            jax.ShapeDtypeStruct((2, slabs, wells), jnp.float32),
        ],
        scratch_shapes=[
            shifted,
            shifted,
            shifted,
            pltpu.VMEM((2, planes * lines, span + LANES), jnp.bfloat16),
            pltpu.VMEM((4 * LANES, LANES), jnp.bfloat16),
            pltpu.VMEM((span, wells), jnp.bfloat16),
        ],
        compiler_params=pltpu.CompilerParams(vmem_limit_bytes=VMEM_LIMIT),
        cost_estimate=pl.CostEstimate(flops=40 * w.size, bytes_accessed=12 * w.size, transcendentals=0),
        name="stencil",
    )(table, inverse, w, cat, place_row)


def cell_rows(slabs, wells, share):
    if share >= 2 * wells:
        return ((0, 0), (0, wells)), slabs
    return ((0, 0), (slabs, 0)), 2 * slabs


def payload_kernel(ratio, sums, first, last, before, after, inverse, cells, out_ref, flux_ref):
    copies, _, share = out_ref.shape
    _, lines, span = sums.shape
    slabs, wells = cells.shape[1:]
    ends = jnp.concatenate([inverse[0:1], inverse[slabs - 1 : slabs]], axis=0)
    info, start = 2 * lines, 2 * lines + ROWS
    places, _ = cell_rows(slabs, wells, share)
    for d in range(copies):
        cols = slice(d * share, (d + 1) * share)
        for q in range(2):
            out_ref[d, q * lines : (q + 1) * lines] = sums[q, :, cols]
        out_ref[d, info : info + ROWS] = jnp.zeros((ROWS, share), jnp.float32)
        out_ref[d, info : info + 2, :slabs] = ends
        out_ref[d, info : info + 1, slabs : slabs + 1] = jnp.full((1, 1), ratio[0])
        for n, (row, at) in enumerate(places):
            out_ref[d, start + row : start + row + slabs, at : at + wells] = cells[n]
    for own, other, line, n in ((first, before, 0, 0), (last, after, lines - 1, 1)):
        flux = (own[1] + other[1]) * (other[0] - own[0])
        flux_ref[n] = flux
        extra = jnp.dot(ends, flux, precision=HIGHEST, preferred_element_type=jnp.float32)
        for d in range(copies):
            for q in range(2):
                at = q * lines + line
                out_ref[d, at : at + 1] += extra[q : q + 1, d * share : (d + 1) * share]


def payload(ratio, sums, first, last, before, after, inverse, cells, copies):
    _, lines, span = sums.shape
    slabs, wells = cells.shape[1:]
    share = span // copies
    rows = 2 * lines + ROWS + cell_rows(slabs, wells, share)[1]
    vmem = pl.BlockSpec(memory_space=pltpu.VMEM)
    return pl.pallas_call(
        payload_kernel,
        in_specs=[pl.BlockSpec(memory_space=pltpu.SMEM)] + [vmem] * 7,
        out_specs=[vmem] * 2,
        out_shape=[
            jax.ShapeDtypeStruct((copies, rows, share), jnp.float32),
            jax.ShapeDtypeStruct((2, slabs, span), jnp.float32),
        ],
        compiler_params=pltpu.CompilerParams(vmem_limit_bytes=SMALL_VMEM),
        cost_estimate=pl.CostEstimate(flops=10**6, bytes_accessed=10**6, transcendentals=0),
        name="payload",
    )(ratio, sums, first, last, before, after, inverse, cells)


CORNERS = ((0, 0), (0, 1), (1, 0), (1, 1))


def block_scalars(tile, slabs, shape, flipped=None):
    at = lambda row, lane: jnp.broadcast_to(tile[row : row + 1, lane : lane + 1], shape)
    corner = {(r, c): at(r, c * (slabs - 1)) for r, c in CORNERS}
    if flipped is not None:
        corner = {(r, c): jnp.where(flipped, corner[1 - r, 1 - c], corner[r, c]) for r, c in CORNERS}
    return corner, at(0, slabs)


def coupling(ratio, one, other, slabs):
    return ratio * (slabs / (slabs + 1.0)) / jnp.sqrt(one * other)


def chain(corners, couple, q=None):
    out = []
    q = jnp.zeros_like(couple[0])
    for k, corner in enumerate(corners):
        vf, vl = couple[k] * corner[0, 0], couple[k] * corner[1, 0]
        wf, wl = couple[k + 1] * corner[0, 1], couple[k + 1] * corner[1, 1]
        inverse = 1.0 / (1.0 - vf * q)
        out.append(
            dict(
                p_first=vl * q * inverse,
                p_before=vl * inverse,
                a_first=inverse,
                a_before=vf * inverse,
                a_after=wf * inverse,
                couple=couple[k],
                couple_after=couple[k + 1],
                q=q,
            )
        )
        q = wl + vl * q * wf * inverse
    return out, q


KINDS = ("p_first", "p_before", "a_first", "a_before", "a_after", "couple", "couple_after", "q")


def forward(coef, firsts, lasts):
    before = [jnp.zeros_like(firsts[0])]
    for j in range(len(firsts)):
        before.append(
            lasts[j] + coef("p_first", j) * firsts[j] + coef("p_before", j) * before[j]
        )
    return before


def backward(coef, firsts, before, after):
    blocks = len(firsts)
    above, below = [None] * blocks, [None] * blocks
    for j in reversed(range(blocks)):
        below[j] = coef("couple_after", j) * after
        here = (
            coef("a_first", j) * firsts[j]
            + coef("a_before", j) * before[j]
            + coef("a_after", j) * after
        )
        above[j] = coef("couple", j) * (before[j] + coef("q", j) * here)
        after = here
    return above, below


def half_chain(tiles, slabs, flipped, middle):
    shape = (ROWS, LANES)
    scalars = [block_scalars(tile, slabs, shape, flipped) for tile in tiles]
    couple = [jnp.zeros(shape, jnp.float32)]
    for k in range(1, len(tiles)):
        ratio = jnp.where(flipped, scalars[k - 1][1], scalars[k][1])
        couple.append(coupling(ratio, scalars[k - 1][0][1, 1], scalars[k][0][0, 0], slabs))
    couple.append(middle)
    return chain([corner for corner, _ in scalars], couple)


def first_kernel(slabs, half, fl_ref, out_ref, cells_ref, table):
    blocks, _, share = fl_ref.shape
    wells = cells_ref.shape[-1]
    lines = out_ref.shape[0] - -(-2 * blocks // ROWS) * ROWS
    info, start = 2 * lines, 2 * lines + ROWS
    flip = half[0]
    flipped = flip == 1
    block = [k + flip * (blocks - 1 - 2 * k) for k in range(blocks)]
    entries, _ = half_chain(
        [fl_ref[block[k], info : info + ROWS, :LANES] for k in range(blocks)],
        slabs,
        flipped,
        jnp.zeros((ROWS, LANES), jnp.float32),
    )
    for k, entry in enumerate(entries):
        for n, kind in enumerate(KINDS[:2]):
            table[k, n] = entry[kind]
    coef = lambda kind, k: table[k, KINDS.index(kind)]

    def group(g, carry):
        rows = pl.ds(pl.multiple_of(g * ROWS, ROWS), ROWS)
        outer = pl.ds(pl.multiple_of(flip * lines + g * ROWS, ROWS), ROWS)
        inner = pl.ds(pl.multiple_of((1 - flip) * lines + g * ROWS, ROWS), ROWS)
        for t in range(share // LANES):
            cols = slice(t * LANES, (t + 1) * LANES)
            before = forward(
                coef,
                [fl_ref[block[k], outer, cols] for k in range(blocks)],
                [fl_ref[block[k], inner, cols] for k in range(blocks)],
            )
            out_ref[rows, cols] = before[blocks]
        return carry

    lax.fori_loop(0, lines // ROWS, group, 0)
    out_ref[lines:, :] = jnp.zeros((out_ref.shape[0] - lines, share), jnp.float32)
    places, _ = cell_rows(slabs, wells, share)
    for j in range(blocks):
        out_ref[lines + 2 * j : lines + 2 * j + 2, :] = fl_ref[j, info : info + 2, :]
        for n, (row, at) in enumerate(places):
            cells_ref[j, n] = fl_ref[j, start + row : start + row + slabs, at : at + wells]


def first_half(half, fl, slabs, lines, wells):
    parts, _, share = fl.shape
    vmem = pl.BlockSpec(memory_space=pltpu.VMEM)
    rows = lines + -(-2 * parts // ROWS) * ROWS
    return pl.pallas_call(
        functools.partial(first_kernel, slabs),
        in_specs=[pl.BlockSpec(memory_space=pltpu.SMEM), vmem],
        out_specs=[vmem, vmem],
        out_shape=[
            jax.ShapeDtypeStruct((rows, share), jnp.float32),
            jax.ShapeDtypeStruct((parts, 2, slabs, wells), jnp.float32),
        ],
        scratch_shapes=[pltpu.VMEM((parts, 2, ROWS, LANES), jnp.float32)],
        compiler_params=pltpu.CompilerParams(vmem_limit_bytes=SMALL_VMEM),
        cost_estimate=pl.CostEstimate(flops=4 * fl.size, bytes_accessed=5 * fl.size, transcendentals=0),
        name="reduced_in",
    )(half, fl)


def second_in_line(first, value):
    def kernel(first_ref, value_ref, out_ref):
        out_ref[...] = value_ref[...]

    vmem = pl.BlockSpec(memory_space=pltpu.VMEM)
    return pl.pallas_call(
        kernel,
        in_specs=[vmem, vmem],
        out_specs=vmem,
        out_shape=jax.ShapeDtypeStruct(value.shape, value.dtype),
        compiler_params=pltpu.CompilerParams(vmem_limit_bytes=SMALL_VMEM),
        cost_estimate=pl.CostEstimate(flops=0, bytes_accessed=8 * value.size, transcendentals=0),
        name="second_in_line",
    )(first, value)


def second_kernel(slabs, half, fl_ref, mine, other, uv_ref, info_ref, table):
    blocks, _, lines, share = uv_ref.shape
    flip = half[0]
    flipped = flip == 1
    block = [k + flip * (blocks - 1 - 2 * k) for k in range(blocks)]
    for j in range(blocks):
        info_ref[flip * blocks + j] = fl_ref[j, 2 * lines : 2 * lines + ROWS, :LANES]
        info_ref[(1 - flip) * blocks + j] = jnp.zeros((ROWS, LANES), jnp.float32)
        info_ref[(1 - flip) * blocks + j, 0:2] = other[lines + 2 * j : lines + 2 * j + 2, :LANES]
    shape = (ROWS, LANES)
    above, above_ratio = block_scalars(info_ref[blocks - 1], slabs, shape)
    below, below_ratio = block_scalars(info_ref[blocks], slabs, shape)
    middle = coupling(below_ratio, above[1, 1], below[0, 0], slabs)
    tiles = lambda flip: [
        info_ref[flip * blocks + k + flip * (blocks - 1 - 2 * k)] for k in range(blocks)
    ]
    entries, q_own = half_chain(tiles(flip), slabs, flipped, middle)
    _, q_other = half_chain(tiles(1 - flip), slabs, jnp.logical_not(flipped), middle)
    for k, entry in enumerate(entries):
        for n, kind in enumerate(KINDS):
            table[k, n] = entry[kind]
    table[blocks, 0] = 1.0 / (1.0 - q_own * q_other)
    table[blocks, 1] = q_other
    coef = lambda kind, k: table[k, KINDS.index(kind)]

    def group(g, carry):
        rows = pl.ds(pl.multiple_of(g * ROWS, ROWS), ROWS)
        outside = pl.ds(pl.multiple_of(flip * lines + g * ROWS, ROWS), ROWS)
        inside = pl.ds(pl.multiple_of((1 - flip) * lines + g * ROWS, ROWS), ROWS)
        for t in range(share // LANES):
            cols = slice(t * LANES, (t + 1) * LANES)
            firsts = [fl_ref[block[k], outside, cols] for k in range(blocks)]
            lasts = [fl_ref[block[k], inside, cols] for k in range(blocks - 1)]
            before = forward(coef, firsts[:-1], lasts)
            across = table[blocks, 0] * (other[rows, cols] + table[blocks, 1] * mine[rows, cols])
            outer, inner = backward(coef, firsts, before, across)
            for k in range(blocks):
                uv_ref[block[k], flip, rows, cols] = outer[k]
                uv_ref[block[k], 1 - flip, rows, cols] = inner[k]
        return carry

    lax.fori_loop(0, lines // ROWS, group, 0)


def second_half(half, fl, mine, other, slabs, lines):
    parts, _, share = fl.shape
    vmem = pl.BlockSpec(memory_space=pltpu.VMEM)
    return pl.pallas_call(
        functools.partial(second_kernel, slabs),
        in_specs=[pl.BlockSpec(memory_space=pltpu.SMEM), vmem, vmem, vmem],
        out_specs=[vmem, vmem],
        out_shape=[
            jax.ShapeDtypeStruct((parts, 2, lines, share), jnp.float32),
            jax.ShapeDtypeStruct((2 * parts, ROWS, LANES), jnp.float32),
        ],
        scratch_shapes=[pltpu.VMEM((parts + 1, len(KINDS), ROWS, LANES), jnp.float32)],
        compiler_params=pltpu.CompilerParams(vmem_limit_bytes=SMALL_VMEM),
        cost_estimate=pl.CostEstimate(flops=10 * fl.size, bytes_accessed=9 * fl.size, transcendentals=0),
        name="reduced_out",
    )(half, fl, mine, other)


def extras_kernel(
    table,
    where_am_i,
    info,
    cells_own,
    cells_other,
    flux,
    inverse,
    well,
    holders,
    wells_ref,
    rows_ref,
    leaving,
    keep,
    force,
    rate,
    down,
    rise,
    pairs,
):
    blocks = info.shape[0]
    slabs, wells = wells_ref.shape
    d = where_am_i[0]
    half = d // (blocks // 2)
    held_cells = [
        (ref, k, pl.multiple_of((side * (blocks // 2) + k) * slabs, slabs))
        for ref, side in ((cells_own, half), (cells_other, 1 - half))
        for k in range(blocks // 2)
    ]
    speed, inlet, reach = well[0:1], well[1:2], well[2:3]
    entries = [table[k] for k in range(table.shape[0])]
    level = lax.broadcasted_iota(jnp.int32, (slabs, wells), 0)
    for ref, k, start in held_cells:
        cond = select_tree(ref[k, 1].astype(jnp.int32), entries)
        inside = (level + start).astype(jnp.float32) < reach
        here = jnp.where(inside, speed * cond / (1.0 + cond), 0.0)
        rows = pl.ds(start, slabs)
        rate[rows] = here
        keep[rows] = 1.0 - here
        force[rows] = here * ref[k, 0]

    chunks = blocks * slabs // ROWS

    def descend(i, value):
        rows = pl.ds(pl.multiple_of(i * ROWS, ROWS), ROWS)
        a, b = keep[rows], force[rows]
        seen = []
        for r in range(ROWS):
            seen.append(value)
            value = a[r : r + 1] * value + b[r : r + 1]
        down[rows] = jnp.concatenate(seen, axis=0)
        return value

    def ascend(i, value):
        rows = pl.ds(pl.multiple_of((chunks - 1 - i) * ROWS, ROWS), ROWS)
        a, b = keep[rows], force[rows]
        seen = []
        for r in reversed(range(ROWS)):
            seen.append(value)
            value = a[r : r + 1] * value + b[r : r + 1]
        rise[rows] = jnp.concatenate(seen[::-1], axis=0)
        return value

    bottom = lax.fori_loop(0, chunks, descend, inlet)
    surface = lax.fori_loop(0, chunks, ascend, bottom)
    held = holders[...] == lax.broadcasted_iota(jnp.int32, (wells, holders.shape[1]), 0)
    leaving[...] = jnp.dot(
        jnp.broadcast_to(surface, (ROWS, wells)),
        held.astype(jnp.float32),
        precision=HIGHEST,
        preferred_element_type=jnp.float32,
    )[0:1]

    for ref, k, start in held_cells:
        rows = pl.ds(start, slabs)
        taken = rate[rows] * (2.0 * ref[k, 0] - down[rows] - rise[rows])
        force[rows] = -storage_volume * taken
    firsts, lasts = [], []
    for j in range(blocks):
        both = jnp.dot(
            info[j, :, :slabs],
            force[j * slabs : (j + 1) * slabs],
            precision=HIGHEST,
            preferred_element_type=jnp.float32,
        )
        firsts.append(both[0:1])
        lasts.append(both[1:2])

    scalars = [block_scalars(info[j], slabs, (1, wells)) for j in range(blocks)]
    zero = jnp.zeros((1, wells), jnp.float32)
    couple = [zero]
    for j in range(1, blocks):
        couple.append(
            coupling(scalars[j][1], scalars[j - 1][0][1, 1], scalars[j][0][0, 0], slabs)
        )
    couple.append(zero)
    coefs, _ = chain([corner for corner, _ in scalars], couple)
    coef = lambda kind, j: coefs[j][kind]
    above, below = backward(coef, firsts, forward(coef, firsts, lasts), zero)
    for j in range(blocks):
        pairs[j, 0:1] = above[j]
        pairs[j, 1:2] = below[j]
    pair = pairs[d]
    row = lax.broadcasted_iota(jnp.int32, (slabs, wells), 0)
    own = force[pl.ds(pl.multiple_of(d * slabs, slabs), slabs)]
    own = own + jnp.where(row == 0, pair[0:1], 0.0) + jnp.where(row == slabs - 1, pair[1:2], 0.0)
    dot = functools.partial(jnp.dot, precision=HIGHEST, preferred_element_type=jnp.float32)
    wells_ref[...] = dot(inverse[...], own)
    for n in range(2):
        rows_ref[n] = dot(inverse[...], flux[n])


def extras(table, depth_index, info, cells_own, cells_other, flux, inverse, well, holders):
    blocks = info.shape[0]
    _, slabs, span = flux.shape
    wells = cells_own.shape[-1]
    smem = pl.BlockSpec(memory_space=pltpu.SMEM)
    vmem = pl.BlockSpec(memory_space=pltpu.VMEM)
    column = pltpu.VMEM((blocks * slabs, wells), jnp.float32)
    return pl.pallas_call(
        extras_kernel,
        in_specs=[smem, smem] + [vmem] * 7,
        out_specs=[vmem] * 3,
        out_shape=[
            jax.ShapeDtypeStruct((slabs, wells), jnp.float32),
            jax.ShapeDtypeStruct((2, slabs, span), jnp.float32),
            jax.ShapeDtypeStruct((1, holders.shape[1]), jnp.float32),
        ],
        scratch_shapes=[column] * 5 + [pltpu.VMEM((blocks, ROWS, wells), jnp.float32)],
        compiler_params=pltpu.CompilerParams(vmem_limit_bytes=SMALL_VMEM),
        cost_estimate=pl.CostEstimate(flops=10**7, bytes_accessed=10**6, transcendentals=0),
        name="extras",
    )(table, depth_index.reshape(1), info, cells_own, cells_other, flux, inverse, well, holders)


def solve_kernel(right, uv, inverse, place_row, place_column, solved_wells, outer, out, factor, pick):
    together, slabs, rows, span = right.shape
    wells = place_row.shape[1]
    step = pl.program_id(0)
    size = slabs * rows

    @pl.when(step == 0)
    def _():
        spread = (
            lax.broadcasted_iota(jnp.int32, (size, slabs), 0) // rows
            == lax.broadcasted_iota(jnp.int32, (size, slabs), 1)
        ).astype(jnp.float32).astype(jnp.bfloat16)
        spread_t = (
            lax.broadcasted_iota(jnp.int32, (slabs, size), 1) // rows
            == lax.broadcasted_iota(jnp.int32, (slabs, size), 0)
        ).astype(jnp.float32).astype(jnp.bfloat16)
        same = (
            lax.broadcasted_iota(jnp.int32, (size, size), 0) % rows
            == lax.broadcasted_iota(jnp.int32, (size, size), 1) % rows
        )
        for n, part in enumerate(split_bf16(inverse[...], 2)):
            tall = jnp.dot(spread, part, preferred_element_type=jnp.float32).astype(jnp.bfloat16)
            wide = jnp.dot(tall, spread_t, preferred_element_type=jnp.float32)
            wide = jnp.where(same, wide, 0.0).astype(jnp.bfloat16)
            if n == 0:
                factor[:, :size] = wide
                factor[:, size : 2 * size] = wide
            else:
                factor[:, 2 * size : 3 * size] = wide
        column = lax.broadcasted_iota(jnp.int32, (wells, span), 1)
        chosen = (column == place_column[...] % span).astype(jnp.float32).astype(jnp.bfloat16)
        pick[:wells] = chosen
        pick[wells:] = chosen

    tile = min(span, 256)
    for n in range(together):
        line = lax.broadcasted_iota(jnp.int32, (slabs, rows, wells), 1) + (step * together + n) * rows
        at_wells = jnp.where(line == (place_row[...] // span)[None], solved_wells[...][:, None, :], 0.0)
        at_wells = jnp.concatenate(split_bf16(at_wells.reshape(size, wells), 2), axis=1)
        factor[:, 3 * size :] = at_wells
        lines = slice(n * rows, (n + 1) * rows)
        above = jnp.concatenate([uv[d, 0, lines] for d in range(uv.shape[0])], axis=1)
        below = jnp.concatenate([uv[d, 1, lines] for d in range(uv.shape[0])], axis=1)
        for t in range(span // tile):
            cols = slice(t * tile, (t + 1) * tile)
            value = jnp.concatenate(
                [
                    right[n, 0:1, :, cols] + above[None, :, cols],
                    right[n, 1 : slabs - 1, :, cols],
                    right[n, slabs - 1 :, :, cols] + below[None, :, cols],
                ],
                axis=0,
            ).reshape(size, tile)
            upper, lower = split_bf16(value, 2)
            result = jnp.dot(
                factor[...],
                jnp.concatenate([upper, lower, upper, pick[:, cols]], axis=0),
                preferred_element_type=jnp.float32,
            )
            out[:, lines, cols] = result.reshape(slabs, rows, tile)

    for n, (when, line) in enumerate(((0, 0), (pl.num_programs(0) - 1, together * rows - 1))):

        @pl.when(step == when)
        def _():
            for z in range(slabs):
                out[z, line : line + 1, :] += outer[n, z : z + 1, :]


def solve(right, uv, inverse, place_row, solved_wells, outer):
    groups, slabs, _, span = right.shape
    wells = place_row.shape[1]
    together = 2
    lines = together * ROWS
    shares, _, _, share = uv.shape
    whole = lambda *shape: pl.BlockSpec(shape, lambda g: (0,) * len(shape))
    size = slabs * ROWS
    return pl.pallas_call(
        solve_kernel,
        grid=(groups // together,),
        in_specs=[
            pl.BlockSpec((together, slabs, ROWS, span), lambda g: (g, 0, 0, 0)),
            pl.BlockSpec((shares, 2, lines, share), lambda g: (0, 0, g, 0)),
            whole(slabs, slabs),
            whole(1, wells),
            whole(wells, 1),
            whole(slabs, wells),
            whole(*outer.shape),
        ],
        out_specs=pl.BlockSpec((slabs, lines, span), lambda g: (0, g, 0)),
        out_shape=jax.ShapeDtypeStruct((slabs, groups * ROWS, span), jnp.float32),
        scratch_shapes=[
            pltpu.VMEM((size, 3 * size + 2 * wells), jnp.bfloat16),
            pltpu.VMEM((2 * wells, span), jnp.bfloat16),
        ],
        compiler_params=pltpu.CompilerParams(vmem_limit_bytes=SOLVE_VMEM),
        cost_estimate=pl.CostEstimate(
            flops=8 * size * right.size, bytes_accessed=8 * right.size, transcendentals=0
        ),
        name="depth_solve",
    )(right, uv, inverse, place_row, place_row.reshape(wells, 1), solved_wells, outer)


def body(
    warmth_before,
    stratum_category,
    conductance_catalogue,
    pivot_matrix_reciprocal,
    linkage_factor,
    well_position_inside,
    well_holder_sequence,
    well_reach,
    entering_warmth,
    well_transfer_speed,
):
    slabs, lines, span = warmth_before.shape
    depth_index = lax.axis_index("depth")
    depth_count = lax.axis_size("depth")
    wells = well_position_inside.shape[0]
    owned = wells // depth_count
    table = conductance_catalogue

    parts = depth_count // 2
    halves = [list(range(h * parts, (h + 1) * parts)) for h in range(2)]
    half = (depth_index // parts).astype(jnp.int32).reshape(1)

    place_row = well_position_inside.reshape(1, wells)
    first, last = edge_rows(warmth_before, stratum_category, table)
    first, last, place_row = lax.optimization_barrier((first, last, place_row))
    count = lax.axis_size("strip")
    up = [(i, i + 1) for i in range(count - 1)]
    down = [(j, i) for i, j in up]
    before = lax.ppermute(last, "strip", up)
    after = lax.ppermute(first, "strip", down)
    right, sums, cells = stencil(
        warmth_before, stratum_category, table, pivot_matrix_reciprocal, place_row
    )
    fl, flux = payload(
        linkage_factor, sums, first, last, before, after, pivot_matrix_reciprocal, cells, parts
    )
    exchange = functools.partial(
        lax.all_to_all,
        axis_name="depth",
        split_axis=0,
        concat_axis=0,
        tiled=True,
        axis_index_groups=halves,
    )
    fl_all = exchange(fl)

    across = functools.partial(
        lax.ppermute,
        axis_name="depth",
        perm=[(i, (i + parts) % depth_count) for i in range(depth_count)],
    )
    mine, cells_own = first_half(half, fl_all, slabs, lines, wells)
    other = across(mine)
    cells_other = across(second_in_line(mine, cells_own))
    uv, info_all = second_half(half, fl_all, mine, other, slabs, lines)
    uv_own = exchange(uv)

    well = jnp.stack([well_transfer_speed, entering_warmth, well_reach.astype(jnp.float32)])
    well = jnp.pad(well, ((0, ROWS - 3), (0, 0)))
    holders = lax.dynamic_slice_in_dim(well_holder_sequence, depth_index * owned, owned)
    solved_wells, outer, leaving = extras(
        table,
        depth_index,
        info_all,
        cells_own,
        cells_other,
        flux,
        pivot_matrix_reciprocal,
        well,
        holders.reshape(1, owned),
    )
    solved = solve(right, uv_own, pivot_matrix_reciprocal, place_row, solved_wells, outer)
    return solved, leaving.reshape(owned)


def solution(mesh):
    in_specs = (
        P("depth", "strip", None),
        P("depth", "strip", None),
        P(),
        P("depth", None),
        P("depth"),
        P("strip"),
        P("strip"),
        P("strip"),
        P("strip"),
        P("strip"),
    )
    out_specs = (P("depth", "strip", None), P(("strip", "depth")))
    return jax.shard_map(body, mesh=mesh, in_specs=in_specs, out_specs=out_specs, check_vma=False)
```

```python
import functools

import jax
import jax.numpy as jnp
from jax import lax
from jax.experimental import pallas as pl
from jax.experimental.pallas import tpu as pltpu
from jax.sharding import PartitionSpec as P

backward_euler_advance = 0.2
storage_volume = 2.0
flux_scale = 0.5 * backward_euler_advance
LANES = 128
ROWS = 8
EDGE_VMEM = 56 * 1024 * 1024
VMEM_LIMIT = 48 * 1024 * 1024
SOLVE_VMEM = 48 * 1024 * 1024
SMALL_VMEM = 12 * 1024 * 1024
HIGHEST = lax.Precision.HIGHEST


def select_tree(category, entries):
    values = list(entries)
    bit = 1
    while len(values) > 1:
        odd = (category & bit) != 0
        values = [
            jnp.where(odd, values[k + 1], values[k]) if k + 1 < len(values) else values[k]
            for k in range(0, len(values), 2)
        ]
        bit *= 2
    return values[0]


def split_bf16(value, pieces):
    out = []
    for k in range(pieces):
        part = value.astype(jnp.bfloat16)
        out.append(part)
        if k + 1 < pieces:
            value = value - part.astype(jnp.float32)
    return out


def edge_kernel(table, w_first, cat_first, w_last, cat_last, first, last):
    slabs, rows, span = w_first.shape
    entries = [flux_scale * table[k] for k in range(table.shape[0])]
    sub = lax.broadcasted_iota(jnp.int32, (ROWS, span), 0)

    def gathered(ref, start, row):
        value = jnp.broadcast_to(ref[start, row : row + 1, :], (ROWS, span))
        for k in range(1, ROWS):
            value = jnp.where(sub == k, ref[start + k, row : row + 1, :], value)
        return value

    for w_ref, cat_ref, row, out in ((w_first, cat_first, 0, first), (w_last, cat_last, rows - 1, last)):
        for start in range(0, slabs, ROWS):
            out[0, start : start + ROWS] = gathered(w_ref, start, row)
            out[1, start : start + ROWS] = select_tree(gathered(cat_ref, start, row), entries)


def edge_rows(w, cat, table):
    slabs, lines, span = w.shape
    top = pl.BlockSpec((slabs, ROWS, span), lambda i: (0, 0, 0))
    end = pl.BlockSpec((slabs, ROWS, span), lambda i: (0, lines // ROWS - 1, 0))
    out = pl.BlockSpec((2, slabs, span), lambda i: (0, 0, 0))
    return pl.pallas_call(
        edge_kernel,
        grid=(1,),
        in_specs=[pl.BlockSpec(memory_space=pltpu.SMEM), top, top, end, end],
        out_specs=[out, out],
        out_shape=[jax.ShapeDtypeStruct((2, slabs, span), jnp.float32)] * 2,
        compiler_params=pltpu.CompilerParams(vmem_limit_bytes=EDGE_VMEM),
        cost_estimate=pl.CostEstimate(flops=10**6, bytes_accessed=w.size, transcendentals=0),
        name="edge_rows",
    )(table, w, cat, w, cat)


def stencil_kernel(
    table,
    ends,
    w_ref,
    cat_ref,
    place,
    right_ref,
    acc,
    cells_ref,
    ws,
    cs,
    fs,
    pieces,
    shift,
    pick,
):
    step = pl.program_id(0)
    planes, lines, span = w_ref.shape
    tiles = span // LANES
    groups = lines // ROWS
    wells = place.shape[1]
    entries = [flux_scale * table[k] for k in range(table.shape[0])]
    lane = lax.broadcasted_iota(jnp.int32, (lines, LANES), 1)
    top, end = ROWS, ROWS + lines

    @pl.when(step == 0)
    def _():
        acc[...] = jnp.zeros_like(acc)
        source = lax.broadcasted_iota(jnp.int32, shift.shape, 0) % (2 * LANES)
        target = lax.broadcasted_iota(jnp.int32, shift.shape, 1)
        shift[...] = (source == target + 1).astype(jnp.float32).astype(jnp.bfloat16)
        column = lax.broadcasted_iota(jnp.int32, (span, wells), 0)
        pick[...] = (column == place[...] % span).astype(jnp.float32).astype(jnp.bfloat16)

    def keep_face(k, t, face):
        rows = pl.ds(pl.multiple_of(k * lines, lines), lines)
        for n, part in enumerate(split_bf16(face, 2)):
            pieces[n, rows, t * LANES : (t + 1) * LANES] = part

    def plane(k, carry):
        left_w = left_c = jnp.zeros((lines, LANES), jnp.float32)
        for t in range(tiles):
            cols = slice(t * LANES, (t + 1) * LANES)
            w = w_ref[k, :, cols]
            c = select_tree(cat_ref[k, :, cols], entries)
            for ref, value in ((ws, w), (cs, c)):
                ref[t, top:end] = value
                ref[t, top - 1 : top] = value[0:1]
            roll_w, roll_c = pltpu.roll(w, 1, 1), pltpu.roll(c, 1, 1)
            west_w = jnp.where(lane == 0, left_w, roll_w)
            west_c = jnp.where(lane == 0, left_c, roll_c)
            left_w, left_c = roll_w, roll_c
            face = (c + west_c) * (w - west_w)
            keep_face(k, t, face)
            if t == tiles - 1:
                keep_face(k, tiles, pltpu.roll(-c * w, 1, 1))
            north = (c + cs[t, top - 1 : end - 1]) * (w - ws[t, top - 1 : end - 1])
            fs[t, top:end] = north
            fs[t, end : end + 1] = jnp.zeros((1, LANES), jnp.float32)
            base = w - face - north + fs[t, top + 1 : end + 1]
            right_ref[:, k, :, cols] = base.reshape(groups, ROWS, LANES)
        return carry

    lax.fori_loop(0, planes, plane, 0)

    for t in range(tiles):
        cols = slice(t * LANES, (t + 1) * LANES)
        both = slice(t * LANES, (t + 2) * LANES)
        east = jnp.dot(
            jnp.concatenate([pieces[0, :, both], pieces[1, :, both]], axis=1),
            shift[...],
            preferred_element_type=jnp.float32,
        )
        first, final = acc[0, :, cols], acc[1, :, cols]
        for k in range(planes):
            z = step * planes + k
            value = right_ref[:, k, :, cols].reshape(lines, LANES) + east[k * lines : (k + 1) * lines]
            right_ref[:, k, :, cols] = value.reshape(groups, ROWS, LANES)
            first = first + ends[0, z] * value
            final = final + ends[ends.shape[0] - 1, z] * value
        acc[0, :, cols] = first
        acc[1, :, cols] = final

    dot = functools.partial(jnp.dot, preferred_element_type=jnp.float32)
    own_line = lax.broadcasted_iota(jnp.int32, (lines, wells), 0) == place[...] // span
    upper, lower = split_bf16(w_ref[...].reshape(planes * lines, span), 2)
    kinds = cat_ref[...].astype(jnp.float32).reshape(planes * lines, span).astype(jnp.bfloat16)
    sums = [dot(upper, pick[...]) + dot(lower, pick[...]), dot(kinds, pick[...])]
    for n in range(2):
        for k in range(planes):
            mine = jnp.where(own_line, sums[n][k * lines : (k + 1) * lines], 0.0)
            cells_ref[n, k : k + 1, :] = jnp.sum(mine, axis=0, keepdims=True)


def stencil(w, cat, table, inverse, place_row):
    slabs, lines, span = w.shape
    planes, groups = 8, lines // ROWS
    wells = place_row.shape[1]
    block = pl.BlockSpec((planes, lines, span), lambda i: (i, 0, 0))
    smem = pl.BlockSpec(memory_space=pltpu.SMEM)
    shifted = pltpu.VMEM((span // LANES, lines + 2 * ROWS, LANES), jnp.float32)
    return pl.pallas_call(
        stencil_kernel,
        grid=(slabs // planes,),
        in_specs=[smem, smem, block, block, pl.BlockSpec((1, wells), lambda i: (0, 0))],
        out_specs=[
            pl.BlockSpec((groups, planes, ROWS, span), lambda i: (0, i, 0, 0)),
            pl.BlockSpec((2, lines, span), lambda i: (0, 0, 0)),
            pl.BlockSpec((2, planes, wells), lambda i: (0, i, 0)),
        ],
        out_shape=[
            jax.ShapeDtypeStruct((groups, slabs, ROWS, span), jnp.float32),
            jax.ShapeDtypeStruct((2, lines, span), jnp.float32),
            jax.ShapeDtypeStruct((2, slabs, wells), jnp.float32),
        ],
        scratch_shapes=[
            shifted,
            shifted,
            shifted,
            pltpu.VMEM((2, planes * lines, span + LANES), jnp.bfloat16),
            pltpu.VMEM((4 * LANES, LANES), jnp.bfloat16),
            pltpu.VMEM((span, wells), jnp.bfloat16),
        ],
        compiler_params=pltpu.CompilerParams(vmem_limit_bytes=VMEM_LIMIT),
        cost_estimate=pl.CostEstimate(flops=40 * w.size, bytes_accessed=12 * w.size, transcendentals=0),
        name="stencil",
    )(table, inverse, w, cat, place_row)


META = 11
META_ROWS = 16


def payload_kernel(
    ratio,
    table,
    where_am_i,
    sums,
    first,
    last,
    before,
    after,
    inverse,
    cells,
    speed,
    reach,
    out_ref,
    flux_ref,
    source_ref,
    keep,
    force,
    paths,
):
    copies, _, share = out_ref.shape
    _, lines, span = sums.shape
    _, slabs, wells = cells.shape
    dot = functools.partial(jnp.dot, precision=HIGHEST, preferred_element_type=jnp.float32)
    ends = jnp.concatenate([inverse[0:1], inverse[slabs - 1 : slabs]], axis=0)
    meta = 2 * lines

    entries = [table[k] for k in range(table.shape[0])]
    level = lax.broadcasted_iota(jnp.int32, (slabs, wells), 0) + where_am_i[0] * slabs
    rock = cells[0]
    cond = select_tree(cells[1].astype(jnp.int32), entries)
    rate = jnp.where(level < reach[...], speed[...] * cond / (1.0 + cond), 0.0)
    keep[...] = 1.0 - rate
    force[...] = rate * rock
    ones, zeros = jnp.ones((1, wells), jnp.float32), jnp.zeros((1, wells), jnp.float32)
    ways = []
    for n, order in enumerate((range(slabs), reversed(range(slabs)))):
        scale, shift = ones, zeros
        for z in order:
            paths[n, 0, z : z + 1] = scale
            paths[n, 1, z : z + 1] = shift
            scale, shift = keep[z : z + 1] * scale, keep[z : z + 1] * shift + force[z : z + 1]
        ways.append((scale, shift))
    source_ref[0] = -storage_volume * rate * (2.0 * rock - paths[0, 1] - paths[1, 1])
    source_ref[1] = storage_volume * rate * paths[0, 0]
    source_ref[2] = storage_volume * rate * paths[1, 0]
    own_sums = [dot(ends, source_ref[n]) for n in range(3)]

    for d in range(copies):
        cols = slice(d * share, (d + 1) * share)
        for q in range(2):
            out_ref[d, q * lines : (q + 1) * lines] = sums[q, :, cols]
        out_ref[d, meta : meta + META_ROWS] = jnp.zeros((META_ROWS, share), jnp.float32)
        out_ref[d, meta : meta + 2, :slabs] = ends
        out_ref[d, meta : meta + 1, slabs : slabs + 1] = jnp.full((1, 1), ratio[0])
        rows = [ways[0][0], ways[0][1], ways[1][1]]
        rows += [own_sums[n][q : q + 1] for q in range(2) for n in range(3)]
        for n, row in enumerate(rows):
            out_ref[d, meta + 2 + n : meta + 3 + n, :wells] = row
    for own, other, line, n in ((first, before, 0, 0), (last, after, lines - 1, 1)):
        flux = (own[1] + other[1]) * (other[0] - own[0])
        flux_ref[n] = flux
        extra = dot(ends, flux)
        for d in range(copies):
            for q in range(2):
                at = q * lines + line
                out_ref[d, at : at + 1] += extra[q : q + 1, d * share : (d + 1) * share]


def payload(ratio, table, depth_index, sums, edges, inverse, cells, speed, reach, copies):
    _, lines, span = sums.shape
    _, slabs, wells = cells.shape
    share = span // copies
    smem = pl.BlockSpec(memory_space=pltpu.SMEM)
    vmem = pl.BlockSpec(memory_space=pltpu.VMEM)
    column = pltpu.VMEM((slabs, wells), jnp.float32)
    return pl.pallas_call(
        payload_kernel,
        in_specs=[smem] * 3 + [vmem] * 9,
        out_specs=[vmem] * 3,
        out_shape=[
            jax.ShapeDtypeStruct((copies, 2 * lines + META_ROWS, share), jnp.float32),
            jax.ShapeDtypeStruct((2, slabs, span), jnp.float32),
            jax.ShapeDtypeStruct((3, slabs, wells), jnp.float32),
        ],
        scratch_shapes=[column, column, pltpu.VMEM((2, 2, slabs, wells), jnp.float32)],
        compiler_params=pltpu.CompilerParams(vmem_limit_bytes=SMALL_VMEM),
        cost_estimate=pl.CostEstimate(flops=10**6, bytes_accessed=10**6, transcendentals=0),
        name="payload",
    )(ratio, table, depth_index.reshape(1), sums, *edges, inverse, cells, speed, reach)


CORNERS = ((0, 0), (0, 1), (1, 0), (1, 1))


def block_scalars(tile, slabs, shape, flipped=None):
    at = lambda row, lane: jnp.broadcast_to(tile[row : row + 1, lane : lane + 1], shape)
    corner = {(r, c): at(r, c * (slabs - 1)) for r, c in CORNERS}
    if flipped is not None:
        corner = {(r, c): jnp.where(flipped, corner[1 - r, 1 - c], corner[r, c]) for r, c in CORNERS}
    return corner, at(0, slabs)


def coupling(ratio, one, other, slabs):
    return ratio * (slabs / (slabs + 1.0)) / jnp.sqrt(one * other)


def chain(corners, couple, q=None):
    out = []
    q = jnp.zeros_like(couple[0])
    for k, corner in enumerate(corners):
        vf, vl = couple[k] * corner[0, 0], couple[k] * corner[1, 0]
        wf, wl = couple[k + 1] * corner[0, 1], couple[k + 1] * corner[1, 1]
        inverse = 1.0 / (1.0 - vf * q)
        out.append(
            dict(
                p_first=vl * q * inverse,
                p_before=vl * inverse,
                a_first=inverse,
                a_before=vf * inverse,
                a_after=wf * inverse,
                couple=couple[k],
                couple_after=couple[k + 1],
                q=q,
            )
        )
        q = wl + vl * q * wf * inverse
    return out, q


KINDS = ("p_first", "p_before", "a_first", "a_before", "a_after", "couple", "couple_after", "q")


def forward(coef, firsts, lasts):
    before = [jnp.zeros_like(firsts[0])]
    for j in range(len(firsts)):
        before.append(
            lasts[j] + coef("p_first", j) * firsts[j] + coef("p_before", j) * before[j]
        )
    return before


def backward(coef, firsts, before, after):
    blocks = len(firsts)
    above, below = [None] * blocks, [None] * blocks
    for j in reversed(range(blocks)):
        below[j] = coef("couple_after", j) * after
        here = (
            coef("a_first", j) * firsts[j]
            + coef("a_before", j) * before[j]
            + coef("a_after", j) * after
        )
        above[j] = coef("couple", j) * (before[j] + coef("q", j) * here)
        after = here
    return above, below


def half_chain(tiles, slabs, flipped, middle):
    shape = (ROWS, LANES)
    scalars = [block_scalars(tile, slabs, shape, flipped) for tile in tiles]
    couple = [jnp.zeros(shape, jnp.float32)]
    for k in range(1, len(tiles)):
        ratio = jnp.where(flipped, scalars[k - 1][1], scalars[k][1])
        couple.append(coupling(ratio, scalars[k - 1][0][1, 1], scalars[k][0][0, 0], slabs))
    couple.append(middle)
    return chain([corner for corner, _ in scalars], couple)


def meta_place(j, lines, share):
    side = share // LANES
    row = lines + j // side * META
    return slice(row, row + META), slice(j % side * LANES, (j % side + 1) * LANES)


def first_kernel(slabs, half, fl_ref, out_ref, table):
    blocks, rows, share = fl_ref.shape
    lines = (rows - META_ROWS) // 2
    flip = half[0]
    flipped = flip == 1
    block = [k + flip * (blocks - 1 - 2 * k) for k in range(blocks)]
    entries, _ = half_chain(
        [fl_ref[block[k], 2 * lines : 2 * lines + ROWS, :LANES] for k in range(blocks)],
        slabs,
        flipped,
        jnp.zeros((ROWS, LANES), jnp.float32),
    )
    for k, entry in enumerate(entries):
        for n, kind in enumerate(KINDS[:2]):
            table[k, n] = entry[kind]
    coef = lambda kind, k: table[k, KINDS.index(kind)]

    def group(g, carry):
        rows = pl.ds(pl.multiple_of(g * ROWS, ROWS), ROWS)
        outer = pl.ds(pl.multiple_of(flip * lines + g * ROWS, ROWS), ROWS)
        inner = pl.ds(pl.multiple_of((1 - flip) * lines + g * ROWS, ROWS), ROWS)
        for t in range(share // LANES):
            cols = slice(t * LANES, (t + 1) * LANES)
            before = forward(
                coef,
                [fl_ref[block[k], outer, cols] for k in range(blocks)],
                [fl_ref[block[k], inner, cols] for k in range(blocks)],
            )
            out_ref[rows, cols] = before[blocks]
        return carry

    lax.fori_loop(0, lines // ROWS, group, 0)
    out_ref[lines:, :] = jnp.zeros((out_ref.shape[0] - lines, share), jnp.float32)
    for j in range(blocks):
        rows, cols = meta_place(j, lines, share)
        out_ref[rows, cols] = fl_ref[j, 2 * lines : 2 * lines + META, :LANES]


def first_half(half, fl, slabs):
    parts, rows, share = fl.shape
    lines = (rows - META_ROWS) // 2
    vmem = pl.BlockSpec(memory_space=pltpu.VMEM)
    rows = -(-meta_place(parts - 1, lines, share)[0].stop // ROWS) * ROWS
    return pl.pallas_call(
        functools.partial(first_kernel, slabs),
        in_specs=[pl.BlockSpec(memory_space=pltpu.SMEM), vmem],
        out_specs=vmem,
        out_shape=jax.ShapeDtypeStruct((rows, share), jnp.float32),
        scratch_shapes=[pltpu.VMEM((parts, 2, ROWS, LANES), jnp.float32)],
        compiler_params=pltpu.CompilerParams(vmem_limit_bytes=SMALL_VMEM),
        cost_estimate=pl.CostEstimate(flops=4 * fl.size, bytes_accessed=5 * fl.size, transcendentals=0),
        name="reduced_in",
    )(half, fl)


def second_kernel(slabs, half, fl_ref, mine, other, uv_ref, info_ref, table):
    blocks, _, lines, share = uv_ref.shape
    flip = half[0]
    flipped = flip == 1
    block = [k + flip * (blocks - 1 - 2 * k) for k in range(blocks)]
    for j in range(blocks):
        rows, cols = meta_place(j, lines, share)
        info_ref[flip * blocks + j] = fl_ref[j, 2 * lines :, :LANES]
        info_ref[(1 - flip) * blocks + j] = jnp.zeros((META_ROWS, LANES), jnp.float32)
        info_ref[(1 - flip) * blocks + j, :META] = other[rows, cols]
    shape = (ROWS, LANES)
    above, above_ratio = block_scalars(info_ref[blocks - 1], slabs, shape)
    below, below_ratio = block_scalars(info_ref[blocks], slabs, shape)
    middle = coupling(below_ratio, above[1, 1], below[0, 0], slabs)
    tiles = lambda flip: [
        info_ref[flip * blocks + k + flip * (blocks - 1 - 2 * k)] for k in range(blocks)
    ]
    entries, q_own = half_chain(tiles(flip), slabs, flipped, middle)
    _, q_other = half_chain(tiles(1 - flip), slabs, jnp.logical_not(flipped), middle)
    for k, entry in enumerate(entries):
        for n, kind in enumerate(KINDS):
            table[k, n] = entry[kind]
    table[blocks, 0] = 1.0 / (1.0 - q_own * q_other)
    table[blocks, 1] = q_other
    coef = lambda kind, k: table[k, KINDS.index(kind)]

    def group(g, carry):
        rows = pl.ds(pl.multiple_of(g * ROWS, ROWS), ROWS)
        outside = pl.ds(pl.multiple_of(flip * lines + g * ROWS, ROWS), ROWS)
        inside = pl.ds(pl.multiple_of((1 - flip) * lines + g * ROWS, ROWS), ROWS)
        for t in range(share // LANES):
            cols = slice(t * LANES, (t + 1) * LANES)
            firsts = [fl_ref[block[k], outside, cols] for k in range(blocks)]
            lasts = [fl_ref[block[k], inside, cols] for k in range(blocks - 1)]
            before = forward(coef, firsts[:-1], lasts)
            across = table[blocks, 0] * (other[rows, cols] + table[blocks, 1] * mine[rows, cols])
            outer, inner = backward(coef, firsts, before, across)
            for k in range(blocks):
                uv_ref[block[k], flip, rows, cols] = outer[k]
                uv_ref[block[k], 1 - flip, rows, cols] = inner[k]
        return carry

    lax.fori_loop(0, lines // ROWS, group, 0)


def second_half(half, fl, mine, other, slabs):
    parts, rows, share = fl.shape
    lines = (rows - META_ROWS) // 2
    vmem = pl.BlockSpec(memory_space=pltpu.VMEM)
    return pl.pallas_call(
        functools.partial(second_kernel, slabs),
        in_specs=[pl.BlockSpec(memory_space=pltpu.SMEM), vmem, vmem, vmem],
        out_specs=[vmem, vmem],
        out_shape=[
            jax.ShapeDtypeStruct((parts, 2, lines, share), jnp.float32),
            jax.ShapeDtypeStruct((2 * parts, META_ROWS, LANES), jnp.float32),
        ],
        scratch_shapes=[pltpu.VMEM((parts + 1, len(KINDS), ROWS, LANES), jnp.float32)],
        compiler_params=pltpu.CompilerParams(vmem_limit_bytes=SMALL_VMEM),
        cost_estimate=pl.CostEstimate(flops=10 * fl.size, bytes_accessed=9 * fl.size, transcendentals=0),
        name="reduced_out",
    )(half, fl, mine, other)


def extras_kernel(where_am_i, info, source, flux, inverse, inlet, holders, wells_ref, rows_ref, leaving, found):
    blocks = info.shape[0]
    slabs, wells = wells_ref.shape
    d = where_am_i[0]
    dot = functools.partial(jnp.dot, precision=HIGHEST, preferred_element_type=jnp.float32)
    row_of = lambda j, n: info[j, 2 + n : 3 + n, :wells]
    down, rise = [None] * blocks, [None] * blocks
    value = inlet[...]
    for j in range(blocks):
        down[j] = value
        value = row_of(j, 0) * value + row_of(j, 1)
    for j in reversed(range(blocks)):
        rise[j] = value
        value = row_of(j, 0) * value + row_of(j, 2)
    held = holders[...] == lax.broadcasted_iota(jnp.int32, (wells, holders.shape[1]), 0)
    leaving[...] = dot(jnp.broadcast_to(value, (ROWS, wells)), held.astype(jnp.float32))[0:1]

    ends = [
        [row_of(j, n) + row_of(j, n + 1) * down[j] + row_of(j, n + 2) * rise[j] for j in range(blocks)]
        for n in (3, 6)
    ]
    scalars = [block_scalars(info[j], slabs, (1, wells)) for j in range(blocks)]
    zero = jnp.zeros((1, wells), jnp.float32)
    couple = [zero]
    for j in range(1, blocks):
        couple.append(
            coupling(scalars[j][1], scalars[j - 1][0][1, 1], scalars[j][0][0, 0], slabs)
        )
    couple.append(zero)
    coefs, _ = chain([corner for corner, _ in scalars], couple)
    coef = lambda kind, j: coefs[j][kind]
    above, below = backward(coef, ends[0], forward(coef, *ends), zero)
    for j in range(blocks):
        for n, value in enumerate((down[j], rise[j], above[j], below[j])):
            found[j, n : n + 1] = value
    mine = found[d]
    row = lax.broadcasted_iota(jnp.int32, (slabs, wells), 0)
    own = source[0] + source[1] * mine[0:1] + source[2] * mine[1:2]
    own = own + jnp.where(row == 0, mine[2:3], 0.0) + jnp.where(row == slabs - 1, mine[3:4], 0.0)
    wells_ref[...] = dot(inverse[...], own)
    for n in range(2):
        rows_ref[n] = dot(inverse[...], flux[n])


def extras(depth_index, info, source, flux, inverse, inlet, holders):
    blocks = info.shape[0]
    _, slabs, span = flux.shape
    wells = source.shape[-1]
    vmem = pl.BlockSpec(memory_space=pltpu.VMEM)
    return pl.pallas_call(
        extras_kernel,
        in_specs=[pl.BlockSpec(memory_space=pltpu.SMEM)] + [vmem] * 6,
        out_specs=[vmem] * 3,
        out_shape=[
            jax.ShapeDtypeStruct((slabs, wells), jnp.float32),
            jax.ShapeDtypeStruct((2, slabs, span), jnp.float32),
            jax.ShapeDtypeStruct((1, holders.shape[1]), jnp.float32),
        ],
        scratch_shapes=[pltpu.VMEM((blocks, ROWS, wells), jnp.float32)],
        compiler_params=pltpu.CompilerParams(vmem_limit_bytes=SMALL_VMEM),
        cost_estimate=pl.CostEstimate(flops=10**7, bytes_accessed=10**6, transcendentals=0),
        name="extras",
    )(depth_index.reshape(1), info, source, flux, inverse, inlet, holders)


def solve_kernel(right, uv, inverse, place_row, place_column, solved_wells, outer, out, factor, pick):
    together, slabs, rows, span = right.shape
    wells = place_row.shape[1]
    step = pl.program_id(0)
    size = slabs * rows

    @pl.when(step == 0)
    def _():
        spread = (
            lax.broadcasted_iota(jnp.int32, (size, slabs), 0) // rows
            == lax.broadcasted_iota(jnp.int32, (size, slabs), 1)
        ).astype(jnp.float32).astype(jnp.bfloat16)
        spread_t = (
            lax.broadcasted_iota(jnp.int32, (slabs, size), 1) // rows
            == lax.broadcasted_iota(jnp.int32, (slabs, size), 0)
        ).astype(jnp.float32).astype(jnp.bfloat16)
        same = (
            lax.broadcasted_iota(jnp.int32, (size, size), 0) % rows
            == lax.broadcasted_iota(jnp.int32, (size, size), 1) % rows
        )
        for n, part in enumerate(split_bf16(inverse[...], 2)):
            tall = jnp.dot(spread, part, preferred_element_type=jnp.float32).astype(jnp.bfloat16)
            wide = jnp.dot(tall, spread_t, preferred_element_type=jnp.float32)
            wide = jnp.where(same, wide, 0.0).astype(jnp.bfloat16)
            if n == 0:
                factor[:, :size] = wide
                factor[:, size : 2 * size] = wide
            else:
                factor[:, 2 * size : 3 * size] = wide
        column = lax.broadcasted_iota(jnp.int32, (wells, span), 1)
        chosen = (column == place_column[...] % span).astype(jnp.float32).astype(jnp.bfloat16)
        pick[:wells] = chosen
        pick[wells:] = chosen

    tile = min(span, 256)
    for n in range(together):
        line = lax.broadcasted_iota(jnp.int32, (slabs, rows, wells), 1) + (step * together + n) * rows
        at_wells = jnp.where(line == (place_row[...] // span)[None], solved_wells[...][:, None, :], 0.0)
        at_wells = jnp.concatenate(split_bf16(at_wells.reshape(size, wells), 2), axis=1)
        factor[:, 3 * size :] = at_wells
        lines = slice(n * rows, (n + 1) * rows)
        above = jnp.concatenate([uv[d, 0, lines] for d in range(uv.shape[0])], axis=1)
        below = jnp.concatenate([uv[d, 1, lines] for d in range(uv.shape[0])], axis=1)
        for t in range(span // tile):
            cols = slice(t * tile, (t + 1) * tile)
            value = jnp.concatenate(
                [
                    right[n, 0:1, :, cols] + above[None, :, cols],
                    right[n, 1 : slabs - 1, :, cols],
                    right[n, slabs - 1 :, :, cols] + below[None, :, cols],
                ],
                axis=0,
            ).reshape(size, tile)
            upper, lower = split_bf16(value, 2)
            result = jnp.dot(
                factor[...],
                jnp.concatenate([upper, lower, upper, pick[:, cols]], axis=0),
                preferred_element_type=jnp.float32,
            )
            out[:, lines, cols] = result.reshape(slabs, rows, tile)

    for n, (when, line) in enumerate(((0, 0), (pl.num_programs(0) - 1, together * rows - 1))):

        @pl.when(step == when)
        def _():
            for z in range(slabs):
                out[z, line : line + 1, :] += outer[n, z : z + 1, :]


def solve(right, uv, inverse, place_row, solved_wells, outer):
    groups, slabs, _, span = right.shape
    wells = place_row.shape[1]
    together = 2
    lines = together * ROWS
    shares, _, _, share = uv.shape
    whole = lambda *shape: pl.BlockSpec(shape, lambda g: (0,) * len(shape))
    size = slabs * ROWS
    return pl.pallas_call(
        solve_kernel,
        grid=(groups // together,),
        in_specs=[
            pl.BlockSpec((together, slabs, ROWS, span), lambda g: (g, 0, 0, 0)),
            pl.BlockSpec((shares, 2, lines, share), lambda g: (0, 0, g, 0)),
            whole(slabs, slabs),
            whole(1, wells),
            whole(wells, 1),
            whole(slabs, wells),
            whole(*outer.shape),
        ],
        out_specs=pl.BlockSpec((slabs, lines, span), lambda g: (0, g, 0)),
        out_shape=jax.ShapeDtypeStruct((slabs, groups * ROWS, span), jnp.float32),
        scratch_shapes=[
            pltpu.VMEM((size, 3 * size + 2 * wells), jnp.bfloat16),
            pltpu.VMEM((2 * wells, span), jnp.bfloat16),
        ],
        compiler_params=pltpu.CompilerParams(vmem_limit_bytes=SOLVE_VMEM),
        cost_estimate=pl.CostEstimate(
            flops=8 * size * right.size, bytes_accessed=8 * right.size, transcendentals=0
        ),
        name="depth_solve",
    )(right, uv, inverse, place_row, place_row.reshape(wells, 1), solved_wells, outer)


def body(
    warmth_before,
    stratum_category,
    conductance_catalogue,
    pivot_matrix_reciprocal,
    linkage_factor,
    well_position_inside,
    well_holder_sequence,
    well_reach,
    entering_warmth,
    well_transfer_speed,
):
    slabs, lines, span = warmth_before.shape
    depth_index = lax.axis_index("depth")
    depth_count = lax.axis_size("depth")
    wells = well_position_inside.shape[0]
    owned = wells // depth_count
    table = conductance_catalogue

    parts = depth_count // 2
    halves = [list(range(h * parts, (h + 1) * parts)) for h in range(2)]
    half = (depth_index // parts).astype(jnp.int32).reshape(1)

    place_row = well_position_inside.reshape(1, wells)
    first, last = edge_rows(warmth_before, stratum_category, table)
    first, last, place_row = lax.optimization_barrier((first, last, place_row))
    count = lax.axis_size("strip")
    up = [(i, i + 1) for i in range(count - 1)]
    down = [(j, i) for i, j in up]
    before = lax.ppermute(last, "strip", up)
    after = lax.ppermute(first, "strip", down)
    right, sums, cells = stencil(
        warmth_before, stratum_category, table, pivot_matrix_reciprocal, place_row
    )
    fl, flux, source = payload(
        linkage_factor,
        table,
        depth_index,
        sums,
        (first, last, before, after),
        pivot_matrix_reciprocal,
        cells,
        well_transfer_speed.reshape(1, wells),
        well_reach.reshape(1, wells),
        parts,
    )
    exchange = functools.partial(
        lax.all_to_all,
        axis_name="depth",
        split_axis=0,
        concat_axis=0,
        tiled=True,
        axis_index_groups=halves,
    )
    fl_all = exchange(fl)

    mine = first_half(half, fl_all, slabs)
    other = lax.ppermute(
        mine, "depth", [(i, (i + parts) % depth_count) for i in range(depth_count)]
    )
    uv, info_all = second_half(half, fl_all, mine, other, slabs)
    uv_own = exchange(uv)

    holders = lax.dynamic_slice_in_dim(well_holder_sequence, depth_index * owned, owned)
    solved_wells, outer, leaving = extras(
        depth_index,
        info_all,
        source,
        flux,
        pivot_matrix_reciprocal,
        entering_warmth.reshape(1, wells),
        holders.reshape(1, owned),
    )
    solved = solve(right, uv_own, pivot_matrix_reciprocal, place_row, solved_wells, outer)
    return solved, leaving.reshape(owned)


def solution(mesh):
    in_specs = (
        P("depth", "strip", None),
        P("depth", "strip", None),
        P(),
        P("depth", None),
        P("depth"),
        P("strip"),
        P("strip"),
        P("strip"),
        P("strip"),
        P("strip"),
    )
    out_specs = (P("depth", "strip", None), P(("strip", "depth")))
    return jax.shard_map(body, mesh=mesh, in_specs=in_specs, out_specs=out_specs, check_vma=False)
```

```python
import functools

import jax
import jax.numpy as jnp
from jax import lax
from jax.experimental import pallas as pl
from jax.experimental.pallas import tpu as pltpu
from jax.sharding import PartitionSpec as P

backward_euler_advance = 0.2
storage_volume = 2.0
flux_scale = 0.5 * backward_euler_advance
LANES = 128
ROWS = 8
EDGE_VMEM = 56 * 1024 * 1024
VMEM_LIMIT = 48 * 1024 * 1024
SOLVE_VMEM = 48 * 1024 * 1024
SMALL_VMEM = 12 * 1024 * 1024
HIGHEST = lax.Precision.HIGHEST


def select_tree(category, entries):
    values = list(entries)
    bit = 1
    while len(values) > 1:
        odd = (category & bit) != 0
        values = [
            jnp.where(odd, values[k + 1], values[k]) if k + 1 < len(values) else values[k]
            for k in range(0, len(values), 2)
        ]
        bit *= 2
    return values[0]


def split_bf16(value, pieces):
    out = []
    for k in range(pieces):
        part = value.astype(jnp.bfloat16)
        out.append(part)
        if k + 1 < pieces:
            value = value - part.astype(jnp.float32)
    return out


def edge_kernel(table, w_first, cat_first, w_last, cat_last, first, last):
    slabs, rows, span = w_first.shape
    entries = [flux_scale * table[k] for k in range(table.shape[0])]
    sub = lax.broadcasted_iota(jnp.int32, (ROWS, span), 0)

    def gathered(ref, start, row):
        value = jnp.broadcast_to(ref[start, row : row + 1, :], (ROWS, span))
        for k in range(1, ROWS):
            value = jnp.where(sub == k, ref[start + k, row : row + 1, :], value)
        return value

    for w_ref, cat_ref, row, out in ((w_first, cat_first, 0, first), (w_last, cat_last, rows - 1, last)):
        for start in range(0, slabs, ROWS):
            out[0, start : start + ROWS] = gathered(w_ref, start, row)
            out[1, start : start + ROWS] = select_tree(gathered(cat_ref, start, row), entries)


def edge_rows(w, cat, table):
    slabs, lines, span = w.shape
    top = pl.BlockSpec((slabs, ROWS, span), lambda i: (0, 0, 0))
    end = pl.BlockSpec((slabs, ROWS, span), lambda i: (0, lines // ROWS - 1, 0))
    out = pl.BlockSpec((2, slabs, span), lambda i: (0, 0, 0))
    return pl.pallas_call(
        edge_kernel,
        grid=(1,),
        in_specs=[pl.BlockSpec(memory_space=pltpu.SMEM), top, top, end, end],
        out_specs=[out, out],
        out_shape=[jax.ShapeDtypeStruct((2, slabs, span), jnp.float32)] * 2,
        compiler_params=pltpu.CompilerParams(vmem_limit_bytes=EDGE_VMEM),
        cost_estimate=pl.CostEstimate(flops=10**6, bytes_accessed=w.size, transcendentals=0),
        name="edge_rows",
    )(table, w, cat, w, cat)


def stencil_kernel(
    table,
    ends,
    w_ref,
    cat_ref,
    place,
    right_ref,
    acc,
    cells_ref,
    ws,
    cs,
    fs,
    base,
    pieces,
    shift,
    pick,
    found,
):
    step = pl.program_id(0)
    planes, lines, span = w_ref.shape
    tiles = span // LANES
    groups = lines // ROWS
    wells = place.shape[1]
    entries = [flux_scale * table[k] for k in range(table.shape[0])]
    lane = lax.broadcasted_iota(jnp.int32, (lines, LANES), 1)
    own_line = lax.broadcasted_iota(jnp.int32, (lines, wells), 0) == place[...] // span
    top, end = ROWS, ROWS + lines
    dot = functools.partial(jnp.dot, preferred_element_type=jnp.float32)

    @pl.when(step == 0)
    def _():
        acc[...] = jnp.zeros_like(acc)
        base[...] = jnp.zeros_like(base)
        pieces[...] = jnp.zeros_like(pieces)
        source = lax.broadcasted_iota(jnp.int32, shift.shape, 0) % (2 * LANES)
        target = lax.broadcasted_iota(jnp.int32, shift.shape, 1)
        shift[...] = (source == target + 1).astype(jnp.float32).astype(jnp.bfloat16)
        column = lax.broadcasted_iota(jnp.int32, (span, wells), 0)
        pick[...] = (column == place[...] % span).astype(jnp.float32).astype(jnp.bfloat16)

    def keep_face(slot, t, face):
        for n, part in enumerate(split_bf16(face, 2)):
            pieces[slot, n, t] = part

    def faces(k, slot):
        left_w = left_c = jnp.zeros((lines, LANES), jnp.float32)
        for t in range(tiles):
            cols = slice(t * LANES, (t + 1) * LANES)
            w = w_ref[k, :, cols]
            c = select_tree(cat_ref[k, :, cols], entries)
            for ref, value in ((ws, w), (cs, c)):
                ref[t, top:end] = value
                ref[t, top - 1 : top] = value[0:1]
            roll_w, roll_c = pltpu.roll(w, 1, 1), pltpu.roll(c, 1, 1)
            west_w = jnp.where(lane == 0, left_w, roll_w)
            west_c = jnp.where(lane == 0, left_c, roll_c)
            left_w, left_c = roll_w, roll_c
            face = (c + west_c) * (w - west_w)
            keep_face(slot, t, face)
            if t == tiles - 1:
                keep_face(slot, tiles, pltpu.roll(-c * w, 1, 1))
            north = (c + cs[t, top - 1 : end - 1]) * (w - ws[t, top - 1 : end - 1])
            fs[t, top:end] = north
            fs[t, end : end + 1] = jnp.zeros((1, LANES), jnp.float32)
            base[slot, t] = w - face - north + fs[t, top + 1 : end + 1]

    def well_cells(k):
        upper, lower = split_bf16(w_ref[k], 2)
        kinds = cat_ref[k].astype(jnp.float32).astype(jnp.bfloat16)
        sums = dot(jnp.concatenate([upper, lower, kinds], axis=0), pick[...])
        for n, value in enumerate((sums[:lines] + sums[lines : 2 * lines], sums[2 * lines :])):
            mine = jnp.where(own_line, value, 0.0)
            found[k, n : n + 1, :] = jnp.sum(mine, axis=0, keepdims=True)

    def finish(k, slot, on):
        z = step * planes + k
        end_first = jnp.where(on, ends[0, z], 0.0)
        end_last = jnp.where(on, ends[ends.shape[0] - 1, z], 0.0)
        parts = [
            pieces[slot, n, d : d + tiles].reshape(tiles * lines, LANES)
            for n in range(2)
            for d in range(2)
        ]
        east = dot(jnp.concatenate(parts, axis=1), shift[...])
        for t in range(tiles):
            cols = slice(t * LANES, (t + 1) * LANES)
            value = base[slot, t] + east[t * lines : (t + 1) * lines]
            right_ref[:, k, :, cols] = value.reshape(groups, ROWS, LANES)
            acc[0, :, cols] += end_first * value
            acc[1, :, cols] += end_last * value

    def two_planes(m, carry):
        k = 2 * m
        finish(jnp.maximum(k - 1, 0), 1, m > 0)
        faces(k, 0)
        well_cells(k)
        finish(k, 0, True)
        faces(k + 1, 1)
        well_cells(k + 1)
        return carry

    lax.fori_loop(0, planes // 2, two_planes, 0)
    finish(planes - 1, 1, True)
    for k in range(planes):
        for n in range(2):
            cells_ref[n, k : k + 1, :] = found[k, n : n + 1, :]


def stencil(w, cat, table, inverse, place_row):
    slabs, lines, span = w.shape
    planes, groups = 8, lines // ROWS
    wells = place_row.shape[1]
    block = pl.BlockSpec((planes, lines, span), lambda i: (i, 0, 0))
    smem = pl.BlockSpec(memory_space=pltpu.SMEM)
    shifted = pltpu.VMEM((span // LANES, lines + 2 * ROWS, LANES), jnp.float32)
    return pl.pallas_call(
        stencil_kernel,
        grid=(slabs // planes,),
        in_specs=[smem, smem, block, block, pl.BlockSpec((1, wells), lambda i: (0, 0))],
        out_specs=[
            pl.BlockSpec((groups, planes, ROWS, span), lambda i: (0, i, 0, 0)),
            pl.BlockSpec((2, lines, span), lambda i: (0, 0, 0)),
            pl.BlockSpec((2, planes, wells), lambda i: (0, i, 0)),
        ],
        out_shape=[
            jax.ShapeDtypeStruct((groups, slabs, ROWS, span), jnp.float32),
            jax.ShapeDtypeStruct((2, lines, span), jnp.float32),
            jax.ShapeDtypeStruct((2, slabs, wells), jnp.float32),
        ],
        scratch_shapes=[
            shifted,
            shifted,
            shifted,
            pltpu.VMEM((2, span // LANES, lines, LANES), jnp.float32),
            pltpu.VMEM((2, 2, span // LANES + 1, lines, LANES), jnp.bfloat16),
            pltpu.VMEM((4 * LANES, LANES), jnp.bfloat16),
            pltpu.VMEM((span, wells), jnp.bfloat16),
            pltpu.VMEM((planes, 2, wells), jnp.float32),
        ],
        compiler_params=pltpu.CompilerParams(vmem_limit_bytes=VMEM_LIMIT),
        cost_estimate=pl.CostEstimate(flops=40 * w.size, bytes_accessed=12 * w.size, transcendentals=0),
        name="stencil",
    )(table, inverse, w, cat, place_row)


META = 11
META_ROWS = 16


def payload_kernel(
    ratio,
    table,
    where_am_i,
    sums,
    first,
    last,
    before,
    after,
    inverse,
    cells,
    speed,
    reach,
    out_ref,
    flux_ref,
    source_ref,
    keep,
    force,
    paths,
):
    copies, _, share = out_ref.shape
    _, lines, span = sums.shape
    _, slabs, wells = cells.shape
    dot = functools.partial(jnp.dot, precision=HIGHEST, preferred_element_type=jnp.float32)
    ends = jnp.concatenate([inverse[0:1], inverse[slabs - 1 : slabs]], axis=0)
    meta = 2 * lines

    entries = [table[k] for k in range(table.shape[0])]
    level = lax.broadcasted_iota(jnp.int32, (slabs, wells), 0) + where_am_i[0] * slabs
    rock = cells[0]
    cond = select_tree(cells[1].astype(jnp.int32), entries)
    rate = jnp.where(level < reach[...], speed[...] * cond / (1.0 + cond), 0.0)
    keep[...] = 1.0 - rate
    force[...] = rate * rock
    ones, zeros = jnp.ones((1, wells), jnp.float32), jnp.zeros((1, wells), jnp.float32)
    ways = []
    for n, order in enumerate((range(slabs), reversed(range(slabs)))):
        scale, shift = ones, zeros
        for z in order:
            paths[n, 0, z : z + 1] = scale
            paths[n, 1, z : z + 1] = shift
            scale, shift = keep[z : z + 1] * scale, keep[z : z + 1] * shift + force[z : z + 1]
        ways.append((scale, shift))
    source_ref[0] = -storage_volume * rate * (2.0 * rock - paths[0, 1] - paths[1, 1])
    source_ref[1] = storage_volume * rate * paths[0, 0]
    source_ref[2] = storage_volume * rate * paths[1, 0]
    own_sums = [dot(ends, source_ref[n]) for n in range(3)]

    for d in range(copies):
        cols = slice(d * share, (d + 1) * share)
        for q in range(2):
            out_ref[d, q * lines : (q + 1) * lines] = sums[q, :, cols]
        out_ref[d, meta : meta + META_ROWS] = jnp.zeros((META_ROWS, share), jnp.float32)
        out_ref[d, meta : meta + 2, :slabs] = ends
        out_ref[d, meta : meta + 1, slabs : slabs + 1] = jnp.full((1, 1), ratio[0])
        rows = [ways[0][0], ways[0][1], ways[1][1]]
        rows += [own_sums[n][q : q + 1] for q in range(2) for n in range(3)]
        for n, row in enumerate(rows):
            out_ref[d, meta + 2 + n : meta + 3 + n, :wells] = row
    for own, other, line, n in ((first, before, 0, 0), (last, after, lines - 1, 1)):
        flux = (own[1] + other[1]) * (other[0] - own[0])
        flux_ref[n] = flux
        extra = dot(ends, flux)
        for d in range(copies):
            for q in range(2):
                at = q * lines + line
                out_ref[d, at : at + 1] += extra[q : q + 1, d * share : (d + 1) * share]


def payload(ratio, table, depth_index, sums, edges, inverse, cells, speed, reach, copies):
    _, lines, span = sums.shape
    _, slabs, wells = cells.shape
    share = span // copies
    smem = pl.BlockSpec(memory_space=pltpu.SMEM)
    vmem = pl.BlockSpec(memory_space=pltpu.VMEM)
    column = pltpu.VMEM((slabs, wells), jnp.float32)
    return pl.pallas_call(
        payload_kernel,
        in_specs=[smem] * 3 + [vmem] * 9,
        out_specs=[vmem] * 3,
        out_shape=[
            jax.ShapeDtypeStruct((copies, 2 * lines + META_ROWS, share), jnp.float32),
            jax.ShapeDtypeStruct((2, slabs, span), jnp.float32),
            jax.ShapeDtypeStruct((3, slabs, wells), jnp.float32),
        ],
        scratch_shapes=[column, column, pltpu.VMEM((2, 2, slabs, wells), jnp.float32)],
        compiler_params=pltpu.CompilerParams(vmem_limit_bytes=SMALL_VMEM),
        cost_estimate=pl.CostEstimate(flops=10**6, bytes_accessed=10**6, transcendentals=0),
        name="payload",
    )(ratio, table, depth_index.reshape(1), sums, *edges, inverse, cells, speed, reach)


CORNERS = ((0, 0), (0, 1), (1, 0), (1, 1))


def block_scalars(tile, slabs, shape, flipped=None):
    at = lambda row, lane: jnp.broadcast_to(tile[row : row + 1, lane : lane + 1], shape)
    corner = {(r, c): at(r, c * (slabs - 1)) for r, c in CORNERS}
    if flipped is not None:
        corner = {(r, c): jnp.where(flipped, corner[1 - r, 1 - c], corner[r, c]) for r, c in CORNERS}
    return corner, at(0, slabs)


def coupling(ratio, one, other, slabs):
    return ratio * (slabs / (slabs + 1.0)) / jnp.sqrt(one * other)


def chain(corners, couple, q=None):
    out = []
    q = jnp.zeros_like(couple[0])
    for k, corner in enumerate(corners):
        vf, vl = couple[k] * corner[0, 0], couple[k] * corner[1, 0]
        wf, wl = couple[k + 1] * corner[0, 1], couple[k + 1] * corner[1, 1]
        inverse = 1.0 / (1.0 - vf * q)
        out.append(
            dict(
                p_first=vl * q * inverse,
                p_before=vl * inverse,
                a_first=inverse,
                a_before=vf * inverse,
                a_after=wf * inverse,
                couple=couple[k],
                couple_after=couple[k + 1],
                q=q,
            )
        )
        q = wl + vl * q * wf * inverse
    return out, q


KINDS = ("p_first", "p_before", "a_first", "a_before", "a_after", "couple", "couple_after", "q")


def forward(coef, firsts, lasts):
    before = [jnp.zeros_like(firsts[0])]
    for j in range(len(firsts)):
        before.append(
            lasts[j] + coef("p_first", j) * firsts[j] + coef("p_before", j) * before[j]
        )
    return before


def backward(coef, firsts, before, after):
    blocks = len(firsts)
    above, below = [None] * blocks, [None] * blocks
    for j in reversed(range(blocks)):
        below[j] = coef("couple_after", j) * after
        here = (
            coef("a_first", j) * firsts[j]
            + coef("a_before", j) * before[j]
            + coef("a_after", j) * after
        )
        above[j] = coef("couple", j) * (before[j] + coef("q", j) * here)
        after = here
    return above, below


def half_chain(tiles, slabs, flipped, middle):
    shape = (ROWS, LANES)
    scalars = [block_scalars(tile, slabs, shape, flipped) for tile in tiles]
    couple = [jnp.zeros(shape, jnp.float32)]
    for k in range(1, len(tiles)):
        ratio = jnp.where(flipped, scalars[k - 1][1], scalars[k][1])
        couple.append(coupling(ratio, scalars[k - 1][0][1, 1], scalars[k][0][0, 0], slabs))
    couple.append(middle)
    return chain([corner for corner, _ in scalars], couple)


def meta_place(j, lines, share):
    side = share // LANES
    row = lines + j // side * META
    return slice(row, row + META), slice(j % side * LANES, (j % side + 1) * LANES)


def first_kernel(slabs, half, fl_ref, out_ref, table):
    blocks, rows, share = fl_ref.shape
    lines = (rows - META_ROWS) // 2
    flip = half[0]
    flipped = flip == 1
    block = [k + flip * (blocks - 1 - 2 * k) for k in range(blocks)]
    entries, _ = half_chain(
        [fl_ref[block[k], 2 * lines : 2 * lines + ROWS, :LANES] for k in range(blocks)],
        slabs,
        flipped,
        jnp.zeros((ROWS, LANES), jnp.float32),
    )
    for k, entry in enumerate(entries):
        for n, kind in enumerate(KINDS[:2]):
            table[k, n] = entry[kind]
    coef = lambda kind, k: table[k, KINDS.index(kind)]

    def group(g, carry):
        rows = pl.ds(pl.multiple_of(g * ROWS, ROWS), ROWS)
        outer = pl.ds(pl.multiple_of(flip * lines + g * ROWS, ROWS), ROWS)
        inner = pl.ds(pl.multiple_of((1 - flip) * lines + g * ROWS, ROWS), ROWS)
        for t in range(share // LANES):
            cols = slice(t * LANES, (t + 1) * LANES)
            before = forward(
                coef,
                [fl_ref[block[k], outer, cols] for k in range(blocks)],
                [fl_ref[block[k], inner, cols] for k in range(blocks)],
            )
            out_ref[rows, cols] = before[blocks]
        return carry

    lax.fori_loop(0, lines // ROWS, group, 0)
    out_ref[lines:, :] = jnp.zeros((out_ref.shape[0] - lines, share), jnp.float32)
    for j in range(blocks):
        rows, cols = meta_place(j, lines, share)
        out_ref[rows, cols] = fl_ref[j, 2 * lines : 2 * lines + META, :LANES]


def first_half(half, fl, slabs):
    parts, rows, share = fl.shape
    lines = (rows - META_ROWS) // 2
    vmem = pl.BlockSpec(memory_space=pltpu.VMEM)
    rows = -(-meta_place(parts - 1, lines, share)[0].stop // ROWS) * ROWS
    return pl.pallas_call(
        functools.partial(first_kernel, slabs),
        in_specs=[pl.BlockSpec(memory_space=pltpu.SMEM), vmem],
        out_specs=vmem,
        out_shape=jax.ShapeDtypeStruct((rows, share), jnp.float32),
        scratch_shapes=[pltpu.VMEM((parts, 2, ROWS, LANES), jnp.float32)],
        compiler_params=pltpu.CompilerParams(vmem_limit_bytes=SMALL_VMEM),
        cost_estimate=pl.CostEstimate(flops=4 * fl.size, bytes_accessed=5 * fl.size, transcendentals=0),
        name="reduced_in",
    )(half, fl)


def second_kernel(slabs, half, fl_ref, mine, other, uv_ref, info_ref, table):
    blocks, _, lines, share = uv_ref.shape
    flip = half[0]
    flipped = flip == 1
    block = [k + flip * (blocks - 1 - 2 * k) for k in range(blocks)]
    for j in range(blocks):
        rows, cols = meta_place(j, lines, share)
        info_ref[flip * blocks + j] = fl_ref[j, 2 * lines :, :LANES]
        info_ref[(1 - flip) * blocks + j] = jnp.zeros((META_ROWS, LANES), jnp.float32)
        info_ref[(1 - flip) * blocks + j, :META] = other[rows, cols]
    shape = (ROWS, LANES)
    above, above_ratio = block_scalars(info_ref[blocks - 1], slabs, shape)
    below, below_ratio = block_scalars(info_ref[blocks], slabs, shape)
    middle = coupling(below_ratio, above[1, 1], below[0, 0], slabs)
    tiles = lambda flip: [
        info_ref[flip * blocks + k + flip * (blocks - 1 - 2 * k)] for k in range(blocks)
    ]
    entries, q_own = half_chain(tiles(flip), slabs, flipped, middle)
    _, q_other = half_chain(tiles(1 - flip), slabs, jnp.logical_not(flipped), middle)
    for k, entry in enumerate(entries):
        for n, kind in enumerate(KINDS):
            table[k, n] = entry[kind]
    table[blocks, 0] = 1.0 / (1.0 - q_own * q_other)
    table[blocks, 1] = q_other
    coef = lambda kind, k: table[k, KINDS.index(kind)]

    def group(g, carry):
        rows = pl.ds(pl.multiple_of(g * ROWS, ROWS), ROWS)
        outside = pl.ds(pl.multiple_of(flip * lines + g * ROWS, ROWS), ROWS)
        inside = pl.ds(pl.multiple_of((1 - flip) * lines + g * ROWS, ROWS), ROWS)
        for t in range(share // LANES):
            cols = slice(t * LANES, (t + 1) * LANES)
            firsts = [fl_ref[block[k], outside, cols] for k in range(blocks)]
            lasts = [fl_ref[block[k], inside, cols] for k in range(blocks - 1)]
            before = forward(coef, firsts[:-1], lasts)
            across = table[blocks, 0] * (other[rows, cols] + table[blocks, 1] * mine[rows, cols])
            outer, inner = backward(coef, firsts, before, across)
            for k in range(blocks):
                uv_ref[block[k], flip, rows, cols] = outer[k]
                uv_ref[block[k], 1 - flip, rows, cols] = inner[k]
        return carry

    lax.fori_loop(0, lines // ROWS, group, 0)


def second_half(half, fl, mine, other, slabs):
    parts, rows, share = fl.shape
    lines = (rows - META_ROWS) // 2
    vmem = pl.BlockSpec(memory_space=pltpu.VMEM)
    return pl.pallas_call(
        functools.partial(second_kernel, slabs),
        in_specs=[pl.BlockSpec(memory_space=pltpu.SMEM), vmem, vmem, vmem],
        out_specs=[vmem, vmem],
        out_shape=[
            jax.ShapeDtypeStruct((parts, 2, lines, share), jnp.float32),
            jax.ShapeDtypeStruct((2 * parts, META_ROWS, LANES), jnp.float32),
        ],
        scratch_shapes=[pltpu.VMEM((parts + 1, len(KINDS), ROWS, LANES), jnp.float32)],
        compiler_params=pltpu.CompilerParams(vmem_limit_bytes=SMALL_VMEM),
        cost_estimate=pl.CostEstimate(flops=10 * fl.size, bytes_accessed=9 * fl.size, transcendentals=0),
        name="reduced_out",
    )(half, fl, mine, other)


def extras_kernel(where_am_i, info, source, flux, inverse, inlet, holders, wells_ref, rows_ref, leaving, found):
    blocks = info.shape[0]
    slabs, wells = wells_ref.shape
    d = where_am_i[0]
    dot = functools.partial(jnp.dot, precision=HIGHEST, preferred_element_type=jnp.float32)
    row_of = lambda j, n: info[j, 2 + n : 3 + n, :wells]
    down, rise = [None] * blocks, [None] * blocks
    value = inlet[...]
    for j in range(blocks):
        down[j] = value
        value = row_of(j, 0) * value + row_of(j, 1)
    for j in reversed(range(blocks)):
        rise[j] = value
        value = row_of(j, 0) * value + row_of(j, 2)
    held = holders[...] == lax.broadcasted_iota(jnp.int32, (wells, holders.shape[1]), 0)
    leaving[...] = dot(jnp.broadcast_to(value, (ROWS, wells)), held.astype(jnp.float32))[0:1]

    ends = [
        [row_of(j, n) + row_of(j, n + 1) * down[j] + row_of(j, n + 2) * rise[j] for j in range(blocks)]
        for n in (3, 6)
    ]
    scalars = [block_scalars(info[j], slabs, (1, wells)) for j in range(blocks)]
    zero = jnp.zeros((1, wells), jnp.float32)
    couple = [zero]
    for j in range(1, blocks):
        couple.append(
            coupling(scalars[j][1], scalars[j - 1][0][1, 1], scalars[j][0][0, 0], slabs)
        )
    couple.append(zero)
    coefs, _ = chain([corner for corner, _ in scalars], couple)
    coef = lambda kind, j: coefs[j][kind]
    above, below = backward(coef, ends[0], forward(coef, *ends), zero)
    for j in range(blocks):
        for n, value in enumerate((down[j], rise[j], above[j], below[j])):
            found[j, n : n + 1] = value
    mine = found[d]
    row = lax.broadcasted_iota(jnp.int32, (slabs, wells), 0)
    own = source[0] + source[1] * mine[0:1] + source[2] * mine[1:2]
    own = own + jnp.where(row == 0, mine[2:3], 0.0) + jnp.where(row == slabs - 1, mine[3:4], 0.0)
    wells_ref[...] = dot(inverse[...], own)
    for n in range(2):
        rows_ref[n] = dot(inverse[...], flux[n])


def extras(depth_index, info, source, flux, inverse, inlet, holders):
    blocks = info.shape[0]
    _, slabs, span = flux.shape
    wells = source.shape[-1]
    vmem = pl.BlockSpec(memory_space=pltpu.VMEM)
    return pl.pallas_call(
        extras_kernel,
        in_specs=[pl.BlockSpec(memory_space=pltpu.SMEM)] + [vmem] * 6,
        out_specs=[vmem] * 3,
        out_shape=[
            jax.ShapeDtypeStruct((slabs, wells), jnp.float32),
            jax.ShapeDtypeStruct((2, slabs, span), jnp.float32),
            jax.ShapeDtypeStruct((1, holders.shape[1]), jnp.float32),
        ],
        scratch_shapes=[pltpu.VMEM((blocks, ROWS, wells), jnp.float32)],
        compiler_params=pltpu.CompilerParams(vmem_limit_bytes=SMALL_VMEM),
        cost_estimate=pl.CostEstimate(flops=10**7, bytes_accessed=10**6, transcendentals=0),
        name="extras",
    )(depth_index.reshape(1), info, source, flux, inverse, inlet, holders)


def solve_kernel(right, uv, inverse, place_row, place_column, solved_wells, outer, out, factor, pick):
    together, slabs, rows, span = right.shape
    wells = place_row.shape[1]
    step = pl.program_id(0)
    size = slabs * rows

    @pl.when(step == 0)
    def _():
        spread = (
            lax.broadcasted_iota(jnp.int32, (size, slabs), 0) // rows
            == lax.broadcasted_iota(jnp.int32, (size, slabs), 1)
        ).astype(jnp.float32).astype(jnp.bfloat16)
        spread_t = (
            lax.broadcasted_iota(jnp.int32, (slabs, size), 1) // rows
            == lax.broadcasted_iota(jnp.int32, (slabs, size), 0)
        ).astype(jnp.float32).astype(jnp.bfloat16)
        same = (
            lax.broadcasted_iota(jnp.int32, (size, size), 0) % rows
            == lax.broadcasted_iota(jnp.int32, (size, size), 1) % rows
        )
        for n, part in enumerate(split_bf16(inverse[...], 2)):
            tall = jnp.dot(spread, part, preferred_element_type=jnp.float32).astype(jnp.bfloat16)
            wide = jnp.dot(tall, spread_t, preferred_element_type=jnp.float32)
            wide = jnp.where(same, wide, 0.0).astype(jnp.bfloat16)
            if n == 0:
                factor[:, :size] = wide
                factor[:, size : 2 * size] = wide
            else:
                factor[:, 2 * size : 3 * size] = wide
        column = lax.broadcasted_iota(jnp.int32, (wells, span), 1)
        chosen = (column == place_column[...] % span).astype(jnp.float32).astype(jnp.bfloat16)
        pick[:wells] = chosen
        pick[wells:] = chosen

    tile = min(span, 256)
    for n in range(together):
        line = lax.broadcasted_iota(jnp.int32, (slabs, rows, wells), 1) + (step * together + n) * rows
        at_wells = jnp.where(line == (place_row[...] // span)[None], solved_wells[...][:, None, :], 0.0)
        at_wells = jnp.concatenate(split_bf16(at_wells.reshape(size, wells), 2), axis=1)
        factor[:, 3 * size :] = at_wells
        lines = slice(n * rows, (n + 1) * rows)
        above = jnp.concatenate([uv[d, 0, lines] for d in range(uv.shape[0])], axis=1)
        below = jnp.concatenate([uv[d, 1, lines] for d in range(uv.shape[0])], axis=1)
        for t in range(span // tile):
            cols = slice(t * tile, (t + 1) * tile)
            value = jnp.concatenate(
                [
                    right[n, 0:1, :, cols] + above[None, :, cols],
                    right[n, 1 : slabs - 1, :, cols],
                    right[n, slabs - 1 :, :, cols] + below[None, :, cols],
                ],
                axis=0,
            ).reshape(size, tile)
            upper, lower = split_bf16(value, 2)
            result = jnp.dot(
                factor[...],
                jnp.concatenate([upper, lower, upper, pick[:, cols]], axis=0),
                preferred_element_type=jnp.float32,
            )
            out[:, lines, cols] = result.reshape(slabs, rows, tile)

    for n, (when, line) in enumerate(((0, 0), (pl.num_programs(0) - 1, together * rows - 1))):

        @pl.when(step == when)
        def _():
            for z in range(slabs):
                out[z, line : line + 1, :] += outer[n, z : z + 1, :]


def solve(right, uv, inverse, place_row, solved_wells, outer):
    groups, slabs, _, span = right.shape
    wells = place_row.shape[1]
    together = 2
    lines = together * ROWS
    shares, _, _, share = uv.shape
    whole = lambda *shape: pl.BlockSpec(shape, lambda g: (0,) * len(shape))
    size = slabs * ROWS
    return pl.pallas_call(
        solve_kernel,
        grid=(groups // together,),
        in_specs=[
            pl.BlockSpec((together, slabs, ROWS, span), lambda g: (g, 0, 0, 0)),
            pl.BlockSpec((shares, 2, lines, share), lambda g: (0, 0, g, 0)),
            whole(slabs, slabs),
            whole(1, wells),
            whole(wells, 1),
            whole(slabs, wells),
            whole(*outer.shape),
        ],
        out_specs=pl.BlockSpec((slabs, lines, span), lambda g: (0, g, 0)),
        out_shape=jax.ShapeDtypeStruct((slabs, groups * ROWS, span), jnp.float32),
        scratch_shapes=[
            pltpu.VMEM((size, 3 * size + 2 * wells), jnp.bfloat16),
            pltpu.VMEM((2 * wells, span), jnp.bfloat16),
        ],
        compiler_params=pltpu.CompilerParams(vmem_limit_bytes=SOLVE_VMEM),
        cost_estimate=pl.CostEstimate(
            flops=8 * size * right.size, bytes_accessed=8 * right.size, transcendentals=0
        ),
        name="depth_solve",
    )(right, uv, inverse, place_row, place_row.reshape(wells, 1), solved_wells, outer)


def body(
    warmth_before,
    stratum_category,
    conductance_catalogue,
    pivot_matrix_reciprocal,
    linkage_factor,
    well_position_inside,
    well_holder_sequence,
    well_reach,
    entering_warmth,
    well_transfer_speed,
):
    slabs, lines, span = warmth_before.shape
    depth_index = lax.axis_index("depth")
    depth_count = lax.axis_size("depth")
    wells = well_position_inside.shape[0]
    owned = wells // depth_count
    table = conductance_catalogue

    parts = depth_count // 2
    halves = [list(range(h * parts, (h + 1) * parts)) for h in range(2)]
    half = (depth_index // parts).astype(jnp.int32).reshape(1)

    place_row = well_position_inside.reshape(1, wells)
    first, last = edge_rows(warmth_before, stratum_category, table)
    first, last, place_row = lax.optimization_barrier((first, last, place_row))
    count = lax.axis_size("strip")
    up = [(i, i + 1) for i in range(count - 1)]
    down = [(j, i) for i, j in up]
    before = lax.ppermute(last, "strip", up)
    after = lax.ppermute(first, "strip", down)
    right, sums, cells = stencil(
        warmth_before, stratum_category, table, pivot_matrix_reciprocal, place_row
    )
    fl, flux, source = payload(
        linkage_factor,
        table,
        depth_index,
        sums,
        (first, last, before, after),
        pivot_matrix_reciprocal,
        cells,
        well_transfer_speed.reshape(1, wells),
        well_reach.reshape(1, wells),
        parts,
    )
    exchange = functools.partial(
        lax.all_to_all,
        axis_name="depth",
        split_axis=0,
        concat_axis=0,
        tiled=True,
        axis_index_groups=halves,
    )
    fl_all = exchange(fl)

    mine = first_half(half, fl_all, slabs)
    other = lax.ppermute(
        mine, "depth", [(i, (i + parts) % depth_count) for i in range(depth_count)]
    )
    uv, info_all = second_half(half, fl_all, mine, other, slabs)
    uv_own = exchange(uv)

    holders = lax.dynamic_slice_in_dim(well_holder_sequence, depth_index * owned, owned)
    solved_wells, outer, leaving = extras(
        depth_index,
        info_all,
        source,
        flux,
        pivot_matrix_reciprocal,
        entering_warmth.reshape(1, wells),
        holders.reshape(1, owned),
    )
    solved = solve(right, uv_own, pivot_matrix_reciprocal, place_row, solved_wells, outer)
    return solved, leaving.reshape(owned)


def solution(mesh):
    in_specs = (
        P("depth", "strip", None),
        P("depth", "strip", None),
        P(),
        P("depth", None),
        P("depth"),
        P("strip"),
        P("strip"),
        P("strip"),
        P("strip"),
        P("strip"),
    )
    out_specs = (P("depth", "strip", None), P(("strip", "depth")))
    return jax.shard_map(body, mesh=mesh, in_specs=in_specs, out_specs=out_specs, check_vma=False)
```

```python
import functools

import jax
import jax.numpy as jnp
from jax import lax
from jax.experimental import pallas as pl
from jax.experimental.pallas import tpu as pltpu
from jax.sharding import PartitionSpec as P

backward_euler_advance = 0.2
storage_volume = 2.0
flux_scale = 0.5 * backward_euler_advance
LANES = 128
ROWS = 8
EDGE_VMEM = 56 * 1024 * 1024
VMEM_LIMIT = 48 * 1024 * 1024
SOLVE_VMEM = 48 * 1024 * 1024
SMALL_VMEM = 12 * 1024 * 1024
HIGHEST = lax.Precision.HIGHEST
TREE_TILES = (1, 4, 6)


def select_tree(category, entries):
    values = list(entries)
    half = 1
    while 2 * half < len(values):
        half *= 2
    highest = True
    while len(values) > 1:
        upper = category >= half if highest else (category & half) != 0
        values = [
            jnp.where(upper, values[k + half], values[k]) if k + half < len(values) else values[k]
            for k in range(min(half, len(values)))
        ]
        half //= 2
        highest = False
    return values[0]


def lane_lookup(category, row):
    return jnp.concatenate(
        [
            jnp.take_along_axis(row, category[k : k + ROWS], axis=1, mode="promise_in_bounds")
            for k in range(0, category.shape[0], ROWS)
        ],
        axis=0,
    )


def split_bf16(value, pieces):
    out = []
    for k in range(pieces):
        part = value.astype(jnp.bfloat16)
        out.append(part)
        if k + 1 < pieces:
            value = value - part.astype(jnp.float32)
    return out


def edge_kernel(table, w_first, cat_first, w_last, cat_last, first, last):
    slabs, rows, span = w_first.shape
    entries = [flux_scale * table[k] for k in range(table.shape[0])]
    sub = lax.broadcasted_iota(jnp.int32, (ROWS, span), 0)

    def gathered(ref, start, row):
        value = jnp.broadcast_to(ref[start, row : row + 1, :], (ROWS, span))
        for k in range(1, ROWS):
            value = jnp.where(sub == k, ref[start + k, row : row + 1, :], value)
        return value

    for w_ref, cat_ref, row, out in ((w_first, cat_first, 0, first), (w_last, cat_last, rows - 1, last)):
        for start in range(0, slabs, ROWS):
            out[0, start : start + ROWS] = gathered(w_ref, start, row)
            out[1, start : start + ROWS] = select_tree(gathered(cat_ref, start, row), entries)


def edge_rows(w, cat, table):
    slabs, lines, span = w.shape
    top = pl.BlockSpec((slabs, ROWS, span), lambda i: (0, 0, 0))
    end = pl.BlockSpec((slabs, ROWS, span), lambda i: (0, lines // ROWS - 1, 0))
    out = pl.BlockSpec((2, slabs, span), lambda i: (0, 0, 0))
    return pl.pallas_call(
        edge_kernel,
        grid=(1,),
        in_specs=[pl.BlockSpec(memory_space=pltpu.SMEM), top, top, end, end],
        out_specs=[out, out],
        out_shape=[jax.ShapeDtypeStruct((2, slabs, span), jnp.float32)] * 2,
        compiler_params=pltpu.CompilerParams(vmem_limit_bytes=EDGE_VMEM),
        cost_estimate=pl.CostEstimate(flops=10**6, bytes_accessed=w.size, transcendentals=0),
        name="edge_rows",
    )(table, w, cat, w, cat)


def stencil_kernel(
    table,
    ends,
    w_ref,
    cat_ref,
    place,
    right_ref,
    acc,
    cells_ref,
    ws,
    cs,
    fs,
    base,
    pieces,
    shift,
    pick,
    found,
):
    step = pl.program_id(0)
    planes, lines, span = w_ref.shape
    tiles = span // LANES
    groups = lines // ROWS
    wells = place.shape[1]
    entries = [flux_scale * table[k] for k in range(table.shape[0])]
    lane = lax.broadcasted_iota(jnp.int32, (lines, LANES), 1)
    table_row = jnp.zeros((ROWS, LANES), jnp.float32)
    for n, entry in enumerate(entries):
        table_row = jnp.where(lane[:ROWS] == n, entry, table_row)
    own_line = lax.broadcasted_iota(jnp.int32, (lines, wells), 0) == place[...] // span
    top, end = ROWS, ROWS + lines
    dot = functools.partial(jnp.dot, preferred_element_type=jnp.float32)

    @pl.when(step == 0)
    def _():
        acc[...] = jnp.zeros_like(acc)
        base[...] = jnp.zeros_like(base)
        pieces[...] = jnp.zeros_like(pieces)
        source = lax.broadcasted_iota(jnp.int32, shift.shape, 0) % (2 * LANES)
        target = lax.broadcasted_iota(jnp.int32, shift.shape, 1)
        shift[...] = (source == target + 1).astype(jnp.float32).astype(jnp.bfloat16)
        column = lax.broadcasted_iota(jnp.int32, (span, wells), 0)
        pick[...] = (column == place[...] % span).astype(jnp.float32).astype(jnp.bfloat16)

    def keep_face(slot, t, face):
        for n, part in enumerate(split_bf16(face, 2)):
            pieces[slot, n, t] = part

    def faces(k, slot):
        left_w = left_c = jnp.zeros((lines, LANES), jnp.float32)
        for t in range(tiles):
            cols = slice(t * LANES, (t + 1) * LANES)
            w = w_ref[k, :, cols]
            kinds = cat_ref[k, :, cols]
            c = select_tree(kinds, entries) if t % 8 in TREE_TILES else lane_lookup(kinds, table_row)
            for ref, value in ((ws, w), (cs, c)):
                ref[t, top:end] = value
                ref[t, top - 1 : top] = value[0:1]
            roll_w, roll_c = pltpu.roll(w, 1, 1), pltpu.roll(c, 1, 1)
            west_w = jnp.where(lane == 0, left_w, roll_w)
            west_c = jnp.where(lane == 0, left_c, roll_c)
            left_w, left_c = roll_w, roll_c
            face = (c + west_c) * (w - west_w)
            keep_face(slot, t, face)
            if t == tiles - 1:
                keep_face(slot, tiles, pltpu.roll(-c * w, 1, 1))
            north = (c + cs[t, top - 1 : end - 1]) * (w - ws[t, top - 1 : end - 1])
            fs[t, top:end] = north
            fs[t, end : end + 1] = jnp.zeros((1, LANES), jnp.float32)
            base[slot, t] = w - face - north + fs[t, top + 1 : end + 1]

    def well_cells(k):
        upper, lower = split_bf16(w_ref[k], 2)
        kinds = cat_ref[k].astype(jnp.float32).astype(jnp.bfloat16)
        sums = dot(jnp.concatenate([upper, lower, kinds], axis=0), pick[...])
        for n, value in enumerate((sums[:lines] + sums[lines : 2 * lines], sums[2 * lines :])):
            mine = jnp.where(own_line, value, 0.0)
            found[k, n : n + 1, :] = jnp.sum(mine, axis=0, keepdims=True)

    def finish(k, slot, on):
        z = step * planes + k
        end_first = jnp.where(on, ends[0, z], 0.0)
        end_last = jnp.where(on, ends[ends.shape[0] - 1, z], 0.0)
        parts = [
            pieces[slot, n, d : d + tiles].reshape(tiles * lines, LANES)
            for n in range(2)
            for d in range(2)
        ]
        east = dot(jnp.concatenate(parts, axis=1), shift[...])
        for t in range(tiles):
            cols = slice(t * LANES, (t + 1) * LANES)
            value = base[slot, t] + east[t * lines : (t + 1) * lines]
            right_ref[:, k, :, cols] = value.reshape(groups, ROWS, LANES)
            acc[0, :, cols] += end_first * value
            acc[1, :, cols] += end_last * value

    def two_planes(m, carry):
        k = 2 * m
        finish(jnp.maximum(k - 1, 0), 1, m > 0)
        faces(k, 0)
        well_cells(k)
        finish(k, 0, True)
        faces(k + 1, 1)
        well_cells(k + 1)
        return carry

    lax.fori_loop(0, planes // 2, two_planes, 0)
    finish(planes - 1, 1, True)
    for k in range(planes):
        for n in range(2):
            cells_ref[n, k : k + 1, :] = found[k, n : n + 1, :]


def stencil(w, cat, table, inverse, place_row):
    slabs, lines, span = w.shape
    planes, groups = 8, lines // ROWS
    wells = place_row.shape[1]
    block = pl.BlockSpec((planes, lines, span), lambda i: (i, 0, 0))
    smem = pl.BlockSpec(memory_space=pltpu.SMEM)
    shifted = pltpu.VMEM((span // LANES, lines + 2 * ROWS, LANES), jnp.float32)
    return pl.pallas_call(
        stencil_kernel,
        grid=(slabs // planes,),
        in_specs=[smem, smem, block, block, pl.BlockSpec((1, wells), lambda i: (0, 0))],
        out_specs=[
            pl.BlockSpec((groups, planes, ROWS, span), lambda i: (0, i, 0, 0)),
            pl.BlockSpec((2, lines, span), lambda i: (0, 0, 0)),
            pl.BlockSpec((2, planes, wells), lambda i: (0, i, 0)),
        ],
        out_shape=[
            jax.ShapeDtypeStruct((groups, slabs, ROWS, span), jnp.float32),
            jax.ShapeDtypeStruct((2, lines, span), jnp.float32),
            jax.ShapeDtypeStruct((2, slabs, wells), jnp.float32),
        ],
        scratch_shapes=[
            shifted,
            shifted,
            shifted,
            pltpu.VMEM((2, span // LANES, lines, LANES), jnp.float32),
            pltpu.VMEM((2, 2, span // LANES + 1, lines, LANES), jnp.bfloat16),
            pltpu.VMEM((4 * LANES, LANES), jnp.bfloat16),
            pltpu.VMEM((span, wells), jnp.bfloat16),
            pltpu.VMEM((planes, 2, wells), jnp.float32),
        ],
        compiler_params=pltpu.CompilerParams(vmem_limit_bytes=VMEM_LIMIT),
        cost_estimate=pl.CostEstimate(flops=40 * w.size, bytes_accessed=12 * w.size, transcendentals=0),
        name="stencil",
    )(table, inverse, w, cat, place_row)


META = 11
META_ROWS = 16


def payload_kernel(
    ratio,
    table,
    where_am_i,
    sums,
    first,
    last,
    before,
    after,
    inverse,
    cells,
    speed,
    reach,
    out_ref,
    flux_ref,
    source_ref,
    keep,
    force,
    paths,
):
    copies, _, share = out_ref.shape
    _, lines, span = sums.shape
    _, slabs, wells = cells.shape
    dot = functools.partial(jnp.dot, precision=HIGHEST, preferred_element_type=jnp.float32)
    ends = jnp.concatenate([inverse[0:1], inverse[slabs - 1 : slabs]], axis=0)
    meta = 2 * lines

    entries = [table[k] for k in range(table.shape[0])]
    level = lax.broadcasted_iota(jnp.int32, (slabs, wells), 0) + where_am_i[0] * slabs
    rock = cells[0]
    cond = select_tree(cells[1].astype(jnp.int32), entries)
    rate = jnp.where(level < reach[...], speed[...] * cond / (1.0 + cond), 0.0)
    keep[...] = 1.0 - rate
    force[...] = rate * rock
    ones, zeros = jnp.ones((1, wells), jnp.float32), jnp.zeros((1, wells), jnp.float32)
    ways = []
    for n, order in enumerate((range(slabs), reversed(range(slabs)))):
        scale, shift = ones, zeros
        for z in order:
            paths[n, 0, z : z + 1] = scale
            paths[n, 1, z : z + 1] = shift
            scale, shift = keep[z : z + 1] * scale, keep[z : z + 1] * shift + force[z : z + 1]
        ways.append((scale, shift))
    source_ref[0] = -storage_volume * rate * (2.0 * rock - paths[0, 1] - paths[1, 1])
    source_ref[1] = storage_volume * rate * paths[0, 0]
    source_ref[2] = storage_volume * rate * paths[1, 0]
    own_sums = [dot(ends, source_ref[n]) for n in range(3)]

    for d in range(copies):
        cols = slice(d * share, (d + 1) * share)
        for q in range(2):
            out_ref[d, q * lines : (q + 1) * lines] = sums[q, :, cols]
        out_ref[d, meta : meta + META_ROWS] = jnp.zeros((META_ROWS, share), jnp.float32)
        out_ref[d, meta : meta + 2, :slabs] = ends
        out_ref[d, meta : meta + 1, slabs : slabs + 1] = jnp.full((1, 1), ratio[0])
        rows = [ways[0][0], ways[0][1], ways[1][1]]
        rows += [own_sums[n][q : q + 1] for q in range(2) for n in range(3)]
        for n, row in enumerate(rows):
            out_ref[d, meta + 2 + n : meta + 3 + n, :wells] = row
    for own, other, line, n in ((first, before, 0, 0), (last, after, lines - 1, 1)):
        flux = (own[1] + other[1]) * (other[0] - own[0])
        flux_ref[n] = flux
        extra = dot(ends, flux)
        for d in range(copies):
            for q in range(2):
                at = q * lines + line
                out_ref[d, at : at + 1] += extra[q : q + 1, d * share : (d + 1) * share]


def payload(ratio, table, depth_index, sums, edges, inverse, cells, speed, reach, copies):
    _, lines, span = sums.shape
    _, slabs, wells = cells.shape
    share = span // copies
    smem = pl.BlockSpec(memory_space=pltpu.SMEM)
    vmem = pl.BlockSpec(memory_space=pltpu.VMEM)
    column = pltpu.VMEM((slabs, wells), jnp.float32)
    return pl.pallas_call(
        payload_kernel,
        in_specs=[smem] * 3 + [vmem] * 9,
        out_specs=[vmem] * 3,
        out_shape=[
            jax.ShapeDtypeStruct((copies, 2 * lines + META_ROWS, share), jnp.float32),
            jax.ShapeDtypeStruct((2, slabs, span), jnp.float32),
            jax.ShapeDtypeStruct((3, slabs, wells), jnp.float32),
        ],
        scratch_shapes=[column, column, pltpu.VMEM((2, 2, slabs, wells), jnp.float32)],
        compiler_params=pltpu.CompilerParams(vmem_limit_bytes=SMALL_VMEM),
        cost_estimate=pl.CostEstimate(flops=10**6, bytes_accessed=10**6, transcendentals=0),
        name="payload",
    )(ratio, table, depth_index.reshape(1), sums, *edges, inverse, cells, speed, reach)


CORNERS = ((0, 0), (0, 1), (1, 0), (1, 1))


def block_scalars(tile, slabs, shape, flipped=None):
    at = lambda row, lane: jnp.broadcast_to(tile[row : row + 1, lane : lane + 1], shape)
    corner = {(r, c): at(r, c * (slabs - 1)) for r, c in CORNERS}
    if flipped is not None:
        corner = {(r, c): jnp.where(flipped, corner[1 - r, 1 - c], corner[r, c]) for r, c in CORNERS}
    return corner, at(0, slabs)


def coupling(ratio, one, other, slabs):
    return ratio * (slabs / (slabs + 1.0)) / jnp.sqrt(one * other)


def chain(corners, couple, q=None):
    out = []
    q = jnp.zeros_like(couple[0])
    for k, corner in enumerate(corners):
        vf, vl = couple[k] * corner[0, 0], couple[k] * corner[1, 0]
        wf, wl = couple[k + 1] * corner[0, 1], couple[k + 1] * corner[1, 1]
        inverse = 1.0 / (1.0 - vf * q)
        out.append(
            dict(
                p_first=vl * q * inverse,
                p_before=vl * inverse,
                a_first=inverse,
                a_before=vf * inverse,
                a_after=wf * inverse,
                couple=couple[k],
                couple_after=couple[k + 1],
                q=q,
            )
        )
        q = wl + vl * q * wf * inverse
    return out, q


KINDS = ("p_first", "p_before", "a_first", "a_before", "a_after", "couple", "couple_after", "q")


def forward(coef, firsts, lasts):
    before = [jnp.zeros_like(firsts[0])]
    for j in range(len(firsts)):
        before.append(
            lasts[j] + coef("p_first", j) * firsts[j] + coef("p_before", j) * before[j]
        )
    return before


def backward(coef, firsts, before, after):
    blocks = len(firsts)
    above, below = [None] * blocks, [None] * blocks
    for j in reversed(range(blocks)):
        below[j] = coef("couple_after", j) * after
        here = (
            coef("a_first", j) * firsts[j]
            + coef("a_before", j) * before[j]
            + coef("a_after", j) * after
        )
        above[j] = coef("couple", j) * (before[j] + coef("q", j) * here)
        after = here
    return above, below


def half_chain(tiles, slabs, flipped, middle):
    shape = (ROWS, LANES)
    scalars = [block_scalars(tile, slabs, shape, flipped) for tile in tiles]
    couple = [jnp.zeros(shape, jnp.float32)]
    for k in range(1, len(tiles)):
        ratio = jnp.where(flipped, scalars[k - 1][1], scalars[k][1])
        couple.append(coupling(ratio, scalars[k - 1][0][1, 1], scalars[k][0][0, 0], slabs))
    couple.append(middle)
    return chain([corner for corner, _ in scalars], couple)


def meta_place(j, lines, share):
    side = share // LANES
    row = lines + j // side * META
    return slice(row, row + META), slice(j % side * LANES, (j % side + 1) * LANES)


def first_kernel(slabs, half, fl_ref, out_ref, table):
    blocks, rows, share = fl_ref.shape
    lines = (rows - META_ROWS) // 2
    flip = half[0]
    flipped = flip == 1
    block = [k + flip * (blocks - 1 - 2 * k) for k in range(blocks)]
    entries, _ = half_chain(
        [fl_ref[block[k], 2 * lines : 2 * lines + ROWS, :LANES] for k in range(blocks)],
        slabs,
        flipped,
        jnp.zeros((ROWS, LANES), jnp.float32),
    )
    for k, entry in enumerate(entries):
        for n, kind in enumerate(KINDS[:2]):
            table[k, n] = entry[kind]
    coef = lambda kind, k: table[k, KINDS.index(kind)]

    def group(g, carry):
        rows = pl.ds(pl.multiple_of(g * ROWS, ROWS), ROWS)
        outer = pl.ds(pl.multiple_of(flip * lines + g * ROWS, ROWS), ROWS)
        inner = pl.ds(pl.multiple_of((1 - flip) * lines + g * ROWS, ROWS), ROWS)
        for t in range(share // LANES):
            cols = slice(t * LANES, (t + 1) * LANES)
            before = forward(
                coef,
                [fl_ref[block[k], outer, cols] for k in range(blocks)],
                [fl_ref[block[k], inner, cols] for k in range(blocks)],
            )
            out_ref[rows, cols] = before[blocks]
        return carry

    lax.fori_loop(0, lines // ROWS, group, 0)
    out_ref[lines:, :] = jnp.zeros((out_ref.shape[0] - lines, share), jnp.float32)
    for j in range(blocks):
        rows, cols = meta_place(j, lines, share)
        out_ref[rows, cols] = fl_ref[j, 2 * lines : 2 * lines + META, :LANES]


def first_half(half, fl, slabs):
    parts, rows, share = fl.shape
    lines = (rows - META_ROWS) // 2
    vmem = pl.BlockSpec(memory_space=pltpu.VMEM)
    rows = -(-meta_place(parts - 1, lines, share)[0].stop // ROWS) * ROWS
    return pl.pallas_call(
        functools.partial(first_kernel, slabs),
        in_specs=[pl.BlockSpec(memory_space=pltpu.SMEM), vmem],
        out_specs=vmem,
        out_shape=jax.ShapeDtypeStruct((rows, share), jnp.float32),
        scratch_shapes=[pltpu.VMEM((parts, 2, ROWS, LANES), jnp.float32)],
        compiler_params=pltpu.CompilerParams(vmem_limit_bytes=SMALL_VMEM),
        cost_estimate=pl.CostEstimate(flops=4 * fl.size, bytes_accessed=5 * fl.size, transcendentals=0),
        name="reduced_in",
    )(half, fl)


def second_kernel(slabs, half, fl_ref, mine, other, uv_ref, info_ref, table):
    blocks, _, lines, share = uv_ref.shape
    flip = half[0]
    flipped = flip == 1
    block = [k + flip * (blocks - 1 - 2 * k) for k in range(blocks)]
    for j in range(blocks):
        rows, cols = meta_place(j, lines, share)
        info_ref[flip * blocks + j] = fl_ref[j, 2 * lines :, :LANES]
        info_ref[(1 - flip) * blocks + j] = jnp.zeros((META_ROWS, LANES), jnp.float32)
        info_ref[(1 - flip) * blocks + j, :META] = other[rows, cols]
    shape = (ROWS, LANES)
    above, above_ratio = block_scalars(info_ref[blocks - 1], slabs, shape)
    below, below_ratio = block_scalars(info_ref[blocks], slabs, shape)
    middle = coupling(below_ratio, above[1, 1], below[0, 0], slabs)
    tiles = lambda flip: [
        info_ref[flip * blocks + k + flip * (blocks - 1 - 2 * k)] for k in range(blocks)
    ]
    entries, q_own = half_chain(tiles(flip), slabs, flipped, middle)
    _, q_other = half_chain(tiles(1 - flip), slabs, jnp.logical_not(flipped), middle)
    for k, entry in enumerate(entries):
        for n, kind in enumerate(KINDS):
            table[k, n] = entry[kind]
    table[blocks, 0] = 1.0 / (1.0 - q_own * q_other)
    table[blocks, 1] = q_other
    coef = lambda kind, k: table[k, KINDS.index(kind)]

    def group(g, carry):
        rows = pl.ds(pl.multiple_of(g * ROWS, ROWS), ROWS)
        outside = pl.ds(pl.multiple_of(flip * lines + g * ROWS, ROWS), ROWS)
        inside = pl.ds(pl.multiple_of((1 - flip) * lines + g * ROWS, ROWS), ROWS)
        for t in range(share // LANES):
            cols = slice(t * LANES, (t + 1) * LANES)
            firsts = [fl_ref[block[k], outside, cols] for k in range(blocks)]
            lasts = [fl_ref[block[k], inside, cols] for k in range(blocks - 1)]
            before = forward(coef, firsts[:-1], lasts)
            across = table[blocks, 0] * (other[rows, cols] + table[blocks, 1] * mine[rows, cols])
            outer, inner = backward(coef, firsts, before, across)
            for k in range(blocks):
                uv_ref[block[k], flip, rows, cols] = outer[k]
                uv_ref[block[k], 1 - flip, rows, cols] = inner[k]
        return carry

    lax.fori_loop(0, lines // ROWS, group, 0)


def second_half(half, fl, mine, other, slabs):
    parts, rows, share = fl.shape
    lines = (rows - META_ROWS) // 2
    vmem = pl.BlockSpec(memory_space=pltpu.VMEM)
    return pl.pallas_call(
        functools.partial(second_kernel, slabs),
        in_specs=[pl.BlockSpec(memory_space=pltpu.SMEM), vmem, vmem, vmem],
        out_specs=[vmem, vmem],
        out_shape=[
            jax.ShapeDtypeStruct((parts, 2, lines, share), jnp.float32),
            jax.ShapeDtypeStruct((2 * parts, META_ROWS, LANES), jnp.float32),
        ],
        scratch_shapes=[pltpu.VMEM((parts + 1, len(KINDS), ROWS, LANES), jnp.float32)],
        compiler_params=pltpu.CompilerParams(vmem_limit_bytes=SMALL_VMEM),
        cost_estimate=pl.CostEstimate(flops=10 * fl.size, bytes_accessed=9 * fl.size, transcendentals=0),
        name="reduced_out",
    )(half, fl, mine, other)


def extras_kernel(where_am_i, info, source, flux, inverse, inlet, holders, wells_ref, rows_ref, leaving, found):
    blocks = info.shape[0]
    slabs, wells = wells_ref.shape
    d = where_am_i[0]
    dot = functools.partial(jnp.dot, precision=HIGHEST, preferred_element_type=jnp.float32)
    row_of = lambda j, n: info[j, 2 + n : 3 + n, :wells]
    down, rise = [None] * blocks, [None] * blocks
    value = inlet[...]
    for j in range(blocks):
        down[j] = value
        value = row_of(j, 0) * value + row_of(j, 1)
    for j in reversed(range(blocks)):
        rise[j] = value
        value = row_of(j, 0) * value + row_of(j, 2)
    held = holders[...] == lax.broadcasted_iota(jnp.int32, (wells, holders.shape[1]), 0)
    leaving[...] = dot(jnp.broadcast_to(value, (ROWS, wells)), held.astype(jnp.float32))[0:1]

    ends = [
        [row_of(j, n) + row_of(j, n + 1) * down[j] + row_of(j, n + 2) * rise[j] for j in range(blocks)]
        for n in (3, 6)
    ]
    scalars = [block_scalars(info[j], slabs, (1, wells)) for j in range(blocks)]
    zero = jnp.zeros((1, wells), jnp.float32)
    couple = [zero]
    for j in range(1, blocks):
        couple.append(
            coupling(scalars[j][1], scalars[j - 1][0][1, 1], scalars[j][0][0, 0], slabs)
        )
    couple.append(zero)
    coefs, _ = chain([corner for corner, _ in scalars], couple)
    coef = lambda kind, j: coefs[j][kind]
    above, below = backward(coef, ends[0], forward(coef, *ends), zero)
    for j in range(blocks):
        for n, value in enumerate((down[j], rise[j], above[j], below[j])):
            found[j, n : n + 1] = value
    mine = found[d]
    row = lax.broadcasted_iota(jnp.int32, (slabs, wells), 0)
    own = source[0] + source[1] * mine[0:1] + source[2] * mine[1:2]
    own = own + jnp.where(row == 0, mine[2:3], 0.0) + jnp.where(row == slabs - 1, mine[3:4], 0.0)
    wells_ref[...] = dot(inverse[...], own)
    for n in range(2):
        rows_ref[n] = dot(inverse[...], flux[n])


def extras(depth_index, info, source, flux, inverse, inlet, holders):
    blocks = info.shape[0]
    _, slabs, span = flux.shape
    wells = source.shape[-1]
    vmem = pl.BlockSpec(memory_space=pltpu.VMEM)
    return pl.pallas_call(
        extras_kernel,
        in_specs=[pl.BlockSpec(memory_space=pltpu.SMEM)] + [vmem] * 6,
        out_specs=[vmem] * 3,
        out_shape=[
            jax.ShapeDtypeStruct((slabs, wells), jnp.float32),
            jax.ShapeDtypeStruct((2, slabs, span), jnp.float32),
            jax.ShapeDtypeStruct((1, holders.shape[1]), jnp.float32),
        ],
        scratch_shapes=[pltpu.VMEM((blocks, ROWS, wells), jnp.float32)],
        compiler_params=pltpu.CompilerParams(vmem_limit_bytes=SMALL_VMEM),
        cost_estimate=pl.CostEstimate(flops=10**7, bytes_accessed=10**6, transcendentals=0),
        name="extras",
    )(depth_index.reshape(1), info, source, flux, inverse, inlet, holders)


def solve_kernel(right, uv, inverse, place_row, place_column, solved_wells, outer, out, factor, pick):
    together, slabs, rows, span = right.shape
    wells = place_row.shape[1]
    step = pl.program_id(0)
    size = slabs * rows

    @pl.when(step == 0)
    def _():
        spread = (
            lax.broadcasted_iota(jnp.int32, (size, slabs), 0) // rows
            == lax.broadcasted_iota(jnp.int32, (size, slabs), 1)
        ).astype(jnp.float32).astype(jnp.bfloat16)
        spread_t = (
            lax.broadcasted_iota(jnp.int32, (slabs, size), 1) // rows
            == lax.broadcasted_iota(jnp.int32, (slabs, size), 0)
        ).astype(jnp.float32).astype(jnp.bfloat16)
        same = (
            lax.broadcasted_iota(jnp.int32, (size, size), 0) % rows
            == lax.broadcasted_iota(jnp.int32, (size, size), 1) % rows
        )
        for n, part in enumerate(split_bf16(inverse[...], 2)):
            tall = jnp.dot(spread, part, preferred_element_type=jnp.float32).astype(jnp.bfloat16)
            wide = jnp.dot(tall, spread_t, preferred_element_type=jnp.float32)
            wide = jnp.where(same, wide, 0.0).astype(jnp.bfloat16)
            if n == 0:
                factor[:, :size] = wide
                factor[:, size : 2 * size] = wide
            else:
                factor[:, 2 * size : 3 * size] = wide
        column = lax.broadcasted_iota(jnp.int32, (wells, span), 1)
        chosen = (column == place_column[...] % span).astype(jnp.float32).astype(jnp.bfloat16)
        pick[:wells] = chosen
        pick[wells:] = chosen

    tile = min(span, 256)
    for n in range(together):
        line = lax.broadcasted_iota(jnp.int32, (slabs, rows, wells), 1) + (step * together + n) * rows
        at_wells = jnp.where(line == (place_row[...] // span)[None], solved_wells[...][:, None, :], 0.0)
        at_wells = jnp.concatenate(split_bf16(at_wells.reshape(size, wells), 2), axis=1)
        factor[:, 3 * size :] = at_wells
        lines = slice(n * rows, (n + 1) * rows)
        above = jnp.concatenate([uv[d, 0, lines] for d in range(uv.shape[0])], axis=1)
        below = jnp.concatenate([uv[d, 1, lines] for d in range(uv.shape[0])], axis=1)
        for t in range(span // tile):
            cols = slice(t * tile, (t + 1) * tile)
            value = jnp.concatenate(
                [
                    right[n, 0:1, :, cols] + above[None, :, cols],
                    right[n, 1 : slabs - 1, :, cols],
                    right[n, slabs - 1 :, :, cols] + below[None, :, cols],
                ],
                axis=0,
            ).reshape(size, tile)
            upper, lower = split_bf16(value, 2)
            result = jnp.dot(
                factor[...],
                jnp.concatenate([upper, lower, upper, pick[:, cols]], axis=0),
                preferred_element_type=jnp.float32,
            )
            out[:, lines, cols] = result.reshape(slabs, rows, tile)

    for n, (when, line) in enumerate(((0, 0), (pl.num_programs(0) - 1, together * rows - 1))):

        @pl.when(step == when)
        def _():
            for z in range(slabs):
                out[z, line : line + 1, :] += outer[n, z : z + 1, :]


def solve(right, uv, inverse, place_row, solved_wells, outer):
    groups, slabs, _, span = right.shape
    wells = place_row.shape[1]
    together = 2
    lines = together * ROWS
    shares, _, _, share = uv.shape
    whole = lambda *shape: pl.BlockSpec(shape, lambda g: (0,) * len(shape))
    size = slabs * ROWS
    return pl.pallas_call(
        solve_kernel,
        grid=(groups // together,),
        in_specs=[
            pl.BlockSpec((together, slabs, ROWS, span), lambda g: (g, 0, 0, 0)),
            pl.BlockSpec((shares, 2, lines, share), lambda g: (0, 0, g, 0)),
            whole(slabs, slabs),
            whole(1, wells),
            whole(wells, 1),
            whole(slabs, wells),
            whole(*outer.shape),
        ],
        out_specs=pl.BlockSpec((slabs, lines, span), lambda g: (0, g, 0)),
        out_shape=jax.ShapeDtypeStruct((slabs, groups * ROWS, span), jnp.float32),
        scratch_shapes=[
            pltpu.VMEM((size, 3 * size + 2 * wells), jnp.bfloat16),
            pltpu.VMEM((2 * wells, span), jnp.bfloat16),
        ],
        compiler_params=pltpu.CompilerParams(vmem_limit_bytes=SOLVE_VMEM),
        cost_estimate=pl.CostEstimate(
            flops=8 * size * right.size, bytes_accessed=8 * right.size, transcendentals=0
        ),
        name="depth_solve",
    )(right, uv, inverse, place_row, place_row.reshape(wells, 1), solved_wells, outer)


def body(
    warmth_before,
    stratum_category,
    conductance_catalogue,
    pivot_matrix_reciprocal,
    linkage_factor,
    well_position_inside,
    well_holder_sequence,
    well_reach,
    entering_warmth,
    well_transfer_speed,
):
    slabs, lines, span = warmth_before.shape
    depth_index = lax.axis_index("depth")
    depth_count = lax.axis_size("depth")
    wells = well_position_inside.shape[0]
    owned = wells // depth_count
    table = conductance_catalogue

    parts = depth_count // 2
    halves = [list(range(h * parts, (h + 1) * parts)) for h in range(2)]
    half = (depth_index // parts).astype(jnp.int32).reshape(1)

    place_row = well_position_inside.reshape(1, wells)
    first, last = edge_rows(warmth_before, stratum_category, table)
    first, last, place_row = lax.optimization_barrier((first, last, place_row))
    count = lax.axis_size("strip")
    up = [(i, i + 1) for i in range(count - 1)]
    down = [(j, i) for i, j in up]
    before = lax.ppermute(last, "strip", up)
    after = lax.ppermute(first, "strip", down)
    right, sums, cells = stencil(
        warmth_before, stratum_category, table, pivot_matrix_reciprocal, place_row
    )
    fl, flux, source = payload(
        linkage_factor,
        table,
        depth_index,
        sums,
        (first, last, before, after),
        pivot_matrix_reciprocal,
        cells,
        well_transfer_speed.reshape(1, wells),
        well_reach.reshape(1, wells),
        parts,
    )
    exchange = functools.partial(
        lax.all_to_all,
        axis_name="depth",
        split_axis=0,
        concat_axis=0,
        tiled=True,
        axis_index_groups=halves,
    )
    fl_all = exchange(fl)

    mine = first_half(half, fl_all, slabs)
    other = lax.ppermute(
        mine, "depth", [(i, (i + parts) % depth_count) for i in range(depth_count)]
    )
    uv, info_all = second_half(half, fl_all, mine, other, slabs)
    uv_own = exchange(uv)

    holders = lax.dynamic_slice_in_dim(well_holder_sequence, depth_index * owned, owned)
    solved_wells, outer, leaving = extras(
        depth_index,
        info_all,
        source,
        flux,
        pivot_matrix_reciprocal,
        entering_warmth.reshape(1, wells),
        holders.reshape(1, owned),
    )
    solved = solve(right, uv_own, pivot_matrix_reciprocal, place_row, solved_wells, outer)
    return solved, leaving.reshape(owned)


def solution(mesh):
    in_specs = (
        P("depth", "strip", None),
        P("depth", "strip", None),
        P(),
        P("depth", None),
        P("depth"),
        P("strip"),
        P("strip"),
        P("strip"),
        P("strip"),
        P("strip"),
    )
    out_specs = (P("depth", "strip", None), P(("strip", "depth")))
    return jax.shard_map(body, mesh=mesh, in_specs=in_specs, out_specs=out_specs, check_vma=False)
```

```python
import functools

import jax
import jax.numpy as jnp
from jax import lax
from jax.experimental import pallas as pl
from jax.experimental.pallas import tpu as pltpu
from jax.sharding import PartitionSpec as P

backward_euler_advance = 0.2
storage_volume = 2.0
flux_scale = 0.5 * backward_euler_advance
LANES = 128
ROWS = 8
EDGE_VMEM = 56 * 1024 * 1024
VMEM_LIMIT = 48 * 1024 * 1024
SOLVE_VMEM = 48 * 1024 * 1024
SMALL_VMEM = 12 * 1024 * 1024
HIGHEST = lax.Precision.HIGHEST


def select_tree(category, entries):
    values = list(entries)
    half = 1
    while 2 * half < len(values):
        half *= 2
    highest = True
    while len(values) > 1:
        upper = category >= half if highest else (category & half) != 0
        values = [
            jnp.where(upper, values[k + half], values[k]) if k + half < len(values) else values[k]
            for k in range(min(half, len(values)))
        ]
        half //= 2
        highest = False
    return values[0]


def split_bf16(value, pieces):
    out = []
    for k in range(pieces):
        part = value.astype(jnp.bfloat16)
        out.append(part)
        if k + 1 < pieces:
            value = value - part.astype(jnp.float32)
    return out


def edge_kernel(table, w_first, cat_first, w_last, cat_last, first, last):
    slabs, rows, span = w_first.shape
    entries = [flux_scale * table[k] for k in range(table.shape[0])]
    sub = lax.broadcasted_iota(jnp.int32, (ROWS, span), 0)

    def gathered(ref, start, row):
        value = jnp.broadcast_to(ref[start, row : row + 1, :], (ROWS, span))
        for k in range(1, ROWS):
            value = jnp.where(sub == k, ref[start + k, row : row + 1, :], value)
        return value

    for w_ref, cat_ref, row, out in ((w_first, cat_first, 0, first), (w_last, cat_last, rows - 1, last)):
        for start in range(0, slabs, ROWS):
            out[0, start : start + ROWS] = gathered(w_ref, start, row)
            out[1, start : start + ROWS] = select_tree(gathered(cat_ref, start, row), entries)


def edge_rows(w, cat, table):
    slabs, lines, span = w.shape
    top = pl.BlockSpec((slabs, ROWS, span), lambda i: (0, 0, 0))
    end = pl.BlockSpec((slabs, ROWS, span), lambda i: (0, lines // ROWS - 1, 0))
    out = pl.BlockSpec((2, slabs, span), lambda i: (0, 0, 0))
    return pl.pallas_call(
        edge_kernel,
        grid=(1,),
        in_specs=[pl.BlockSpec(memory_space=pltpu.SMEM), top, top, end, end],
        out_specs=[out, out],
        out_shape=[jax.ShapeDtypeStruct((2, slabs, span), jnp.float32)] * 2,
        compiler_params=pltpu.CompilerParams(vmem_limit_bytes=EDGE_VMEM),
        cost_estimate=pl.CostEstimate(flops=10**6, bytes_accessed=w.size, transcendentals=0),
        name="edge_rows",
    )(table, w, cat, w, cat)


def stencil_kernel(
    table,
    ends,
    w_ref,
    cat_ref,
    place,
    right_ref,
    acc,
    cells_ref,
    ws,
    cs,
    fs,
    base,
    pieces,
    shift,
    pick,
    found,
):
    step = pl.program_id(0)
    planes, lines, span = w_ref.shape
    tiles = span // LANES
    groups = lines // ROWS
    wells = place.shape[1]
    entries = [flux_scale * table[k] for k in range(table.shape[0])]
    part = lines // 2
    lane = lax.broadcasted_iota(jnp.int32, (part, LANES), 1)
    own_line = lax.broadcasted_iota(jnp.int32, (lines, wells), 0) == place[...] // span
    top, end = ROWS, ROWS + lines
    dot = functools.partial(jnp.dot, preferred_element_type=jnp.float32)

    @pl.when(step == 0)
    def _():
        acc[...] = jnp.zeros_like(acc)
        base[...] = jnp.zeros_like(base)
        pieces[...] = jnp.zeros_like(pieces)
        fs[...] = jnp.zeros_like(fs)
        source = lax.broadcasted_iota(jnp.int32, shift.shape, 0) % (2 * LANES)
        target = lax.broadcasted_iota(jnp.int32, shift.shape, 1)
        shift[...] = (source == target + 1).astype(jnp.float32).astype(jnp.bfloat16)
        column = lax.broadcasted_iota(jnp.int32, (span, wells), 0)
        pick[...] = (column == place[...] % span).astype(jnp.float32).astype(jnp.bfloat16)

    def keep_face(slot, t, start, face):
        for n, piece in enumerate(split_bf16(face, 2)):
            pieces[slot, n, t, start : start + part] = piece

    def faces(k, slot):
        for start in range(0, lines, part):
            left_w = left_c = jnp.zeros((part, LANES), jnp.float32)
            here = slice(top + start, top + start + part)
            above = slice(top + start - 1, top + start + part - 1)
            for t in range(tiles):
                cols = slice(t * LANES, (t + 1) * LANES)
                w = w_ref[k, start : start + part, cols]
                c = select_tree(cat_ref[k, start : start + part, cols], entries)
                for ref, value in ((ws, w), (cs, c)):
                    ref[t, here] = value
                    if start == 0:
                        ref[t, top - 1 : top] = value[0:1]
                roll_w, roll_c = pltpu.roll(w, 1, 1), pltpu.roll(c, 1, 1)
                west_w = jnp.where(lane == 0, left_w, roll_w)
                west_c = jnp.where(lane == 0, left_c, roll_c)
                left_w, left_c = roll_w, roll_c
                face = (c + west_c) * (w - west_w)
                keep_face(slot, t, start, face)
                if t == tiles - 1:
                    keep_face(slot, tiles, start, pltpu.roll(-c * w, 1, 1))
                north = (c + cs[t, above]) * (w - ws[t, above])
                fs[slot, t, here] = north
                base[slot, t, start : start + part] = w - face - north

    def well_cells(k):
        width = min(span, 2 * LANES)
        sums = jnp.zeros((3 * lines, wells), jnp.float32)
        for start in range(0, span, width):
            cols = slice(start, start + width)
            upper, lower = split_bf16(w_ref[k, :, cols], 2)
            kinds = cat_ref[k, :, cols].astype(jnp.float32).astype(jnp.bfloat16)
            sums = sums + dot(jnp.concatenate([upper, lower, kinds], axis=0), pick[cols])
        for n, value in enumerate((sums[:lines] + sums[lines : 2 * lines], sums[2 * lines :])):
            mine = jnp.where(own_line, value, 0.0)
            found[k, n : n + 1, :] = jnp.sum(mine, axis=0, keepdims=True)

    def finish(k, slot, on):
        z = step * planes + k
        end_first = jnp.where(on, ends[0, z], 0.0)
        end_last = jnp.where(on, ends[ends.shape[0] - 1, z], 0.0)
        some = tiles // 2
        for from_tile in range(0, tiles, some):
            parts = [
                pieces[slot, n, from_tile + d : from_tile + d + some].reshape(some * lines, LANES)
                for n in range(2)
                for d in range(2)
            ]
            east = dot(jnp.concatenate(parts, axis=1), shift[...])
            for t in range(from_tile, from_tile + some):
                cols = slice(t * LANES, (t + 1) * LANES)
                for start in range(0, lines, part):
                    rows = slice(start, start + part)
                    at = (t - from_tile) * lines + start
                    south = fs[slot, t, top + start + 1 : top + start + part + 1]
                    value = base[slot, t, rows] + south + east[at : at + part]
                    right_ref[start // ROWS : (start + part) // ROWS, k, :, cols] = value.reshape(
                        part // ROWS, ROWS, LANES
                    )
                    acc[0, rows, cols] += end_first * value
                    acc[1, rows, cols] += end_last * value

    def two_planes(m, carry):
        k = 2 * m
        finish(jnp.maximum(k - 1, 0), 1, m > 0)
        faces(k, 0)
        well_cells(k)
        finish(k, 0, True)
        faces(k + 1, 1)
        well_cells(k + 1)
        return carry

    lax.fori_loop(0, planes // 2, two_planes, 0)
    finish(planes - 1, 1, True)
    for k in range(planes):
        for n in range(2):
            cells_ref[n, k : k + 1, :] = found[k, n : n + 1, :]


def stencil(w, cat, table, inverse, place_row):
    slabs, lines, span = w.shape
    planes, groups = 8, lines // ROWS
    wells = place_row.shape[1]
    block = pl.BlockSpec((planes, lines, span), lambda i: (i, 0, 0))
    smem = pl.BlockSpec(memory_space=pltpu.SMEM)
    shifted = pltpu.VMEM((span // LANES, lines + 2 * ROWS, LANES), jnp.float32)
    return pl.pallas_call(
        stencil_kernel,
        grid=(slabs // planes,),
        in_specs=[smem, smem, block, block, pl.BlockSpec((1, wells), lambda i: (0, 0))],
        out_specs=[
            pl.BlockSpec((groups, planes, ROWS, span), lambda i: (0, i, 0, 0)),
            pl.BlockSpec((2, lines, span), lambda i: (0, 0, 0)),
            pl.BlockSpec((2, planes, wells), lambda i: (0, i, 0)),
        ],
        out_shape=[
            jax.ShapeDtypeStruct((groups, slabs, ROWS, span), jnp.float32),
            jax.ShapeDtypeStruct((2, lines, span), jnp.float32),
            jax.ShapeDtypeStruct((2, slabs, wells), jnp.float32),
        ],
        scratch_shapes=[
            shifted,
            shifted,
            pltpu.VMEM((2, span // LANES, lines + 2 * ROWS, LANES), jnp.float32),
            pltpu.VMEM((2, span // LANES, lines, LANES), jnp.float32),
            pltpu.VMEM((2, 2, span // LANES + 1, lines, LANES), jnp.bfloat16),
            pltpu.VMEM((4 * LANES, LANES), jnp.bfloat16),
            pltpu.VMEM((span, wells), jnp.bfloat16),
            pltpu.VMEM((planes, 2, wells), jnp.float32),
        ],
        compiler_params=pltpu.CompilerParams(vmem_limit_bytes=VMEM_LIMIT),
        cost_estimate=pl.CostEstimate(flops=40 * w.size, bytes_accessed=12 * w.size, transcendentals=0),
        name="stencil",
    )(table, inverse, w, cat, place_row)


META = 11
META_ROWS = 16


def payload_kernel(
    ratio,
    table,
    where_am_i,
    sums,
    first,
    last,
    before,
    after,
    inverse,
    cells,
    speed,
    reach,
    out_ref,
    flux_ref,
    source_ref,
    keep,
    force,
    paths,
):
    copies, _, share = out_ref.shape
    _, lines, span = sums.shape
    _, slabs, wells = cells.shape
    dot = functools.partial(jnp.dot, precision=HIGHEST, preferred_element_type=jnp.float32)
    ends = jnp.concatenate([inverse[0:1], inverse[slabs - 1 : slabs]], axis=0)
    meta = 2 * lines

    entries = [table[k] for k in range(table.shape[0])]
    level = lax.broadcasted_iota(jnp.int32, (slabs, wells), 0) + where_am_i[0] * slabs
    rock = cells[0]
    cond = select_tree(cells[1].astype(jnp.int32), entries)
    rate = jnp.where(level < reach[...], speed[...] * cond / (1.0 + cond), 0.0)
    keep[...] = 1.0 - rate
    force[...] = rate * rock
    ones, zeros = jnp.ones((1, wells), jnp.float32), jnp.zeros((1, wells), jnp.float32)
    ways = []
    for n, order in enumerate((range(slabs), reversed(range(slabs)))):
        scale, shift = ones, zeros
        for z in order:
            paths[n, 0, z : z + 1] = scale
            paths[n, 1, z : z + 1] = shift
            scale, shift = keep[z : z + 1] * scale, keep[z : z + 1] * shift + force[z : z + 1]
        ways.append((scale, shift))
    source_ref[0] = -storage_volume * rate * (2.0 * rock - paths[0, 1] - paths[1, 1])
    source_ref[1] = storage_volume * rate * paths[0, 0]
    source_ref[2] = storage_volume * rate * paths[1, 0]
    own_sums = [dot(ends, source_ref[n]) for n in range(3)]

    for d in range(copies):
        cols = slice(d * share, (d + 1) * share)
        for q in range(2):
            out_ref[d, q * lines : (q + 1) * lines] = sums[q, :, cols]
        out_ref[d, meta : meta + META_ROWS] = jnp.zeros((META_ROWS, share), jnp.float32)
        out_ref[d, meta : meta + 2, :slabs] = ends
        out_ref[d, meta : meta + 1, slabs : slabs + 1] = jnp.full((1, 1), ratio[0])
        rows = [ways[0][0], ways[0][1], ways[1][1]]
        rows += [own_sums[n][q : q + 1] for q in range(2) for n in range(3)]
        for n, row in enumerate(rows):
            out_ref[d, meta + 2 + n : meta + 3 + n, :wells] = row
    for own, other, line, n in ((first, before, 0, 0), (last, after, lines - 1, 1)):
        flux = (own[1] + other[1]) * (other[0] - own[0])
        flux_ref[n] = flux
        extra = dot(ends, flux)
        for d in range(copies):
            for q in range(2):
                at = q * lines + line
                out_ref[d, at : at + 1] += extra[q : q + 1, d * share : (d + 1) * share]


def payload(ratio, table, depth_index, sums, edges, inverse, cells, speed, reach, copies):
    _, lines, span = sums.shape
    _, slabs, wells = cells.shape
    share = span // copies
    smem = pl.BlockSpec(memory_space=pltpu.SMEM)
    vmem = pl.BlockSpec(memory_space=pltpu.VMEM)
    column = pltpu.VMEM((slabs, wells), jnp.float32)
    return pl.pallas_call(
        payload_kernel,
        in_specs=[smem] * 3 + [vmem] * 9,
        out_specs=[vmem] * 3,
        out_shape=[
            jax.ShapeDtypeStruct((copies, 2 * lines + META_ROWS, share), jnp.float32),
            jax.ShapeDtypeStruct((2, slabs, span), jnp.float32),
            jax.ShapeDtypeStruct((3, slabs, wells), jnp.float32),
        ],
        scratch_shapes=[column, column, pltpu.VMEM((2, 2, slabs, wells), jnp.float32)],
        compiler_params=pltpu.CompilerParams(vmem_limit_bytes=SMALL_VMEM),
        cost_estimate=pl.CostEstimate(flops=10**6, bytes_accessed=10**6, transcendentals=0),
        name="payload",
    )(ratio, table, depth_index.reshape(1), sums, *edges, inverse, cells, speed, reach)


CORNERS = ((0, 0), (0, 1), (1, 0), (1, 1))


def block_scalars(tile, slabs, shape, flipped=None):
    at = lambda row, lane: jnp.broadcast_to(tile[row : row + 1, lane : lane + 1], shape)
    corner = {(r, c): at(r, c * (slabs - 1)) for r, c in CORNERS}
    if flipped is not None:
        corner = {(r, c): jnp.where(flipped, corner[1 - r, 1 - c], corner[r, c]) for r, c in CORNERS}
    return corner, at(0, slabs)


def coupling(ratio, one, other, slabs):
    return ratio * (slabs / (slabs + 1.0)) / jnp.sqrt(one * other)


def chain(corners, couple, q=None):
    out = []
    q = jnp.zeros_like(couple[0])
    for k, corner in enumerate(corners):
        vf, vl = couple[k] * corner[0, 0], couple[k] * corner[1, 0]
        wf, wl = couple[k + 1] * corner[0, 1], couple[k + 1] * corner[1, 1]
        inverse = 1.0 / (1.0 - vf * q)
        out.append(
            dict(
                p_first=vl * q * inverse,
                p_before=vl * inverse,
                a_first=inverse,
                a_before=vf * inverse,
                a_after=wf * inverse,
                couple=couple[k],
                couple_after=couple[k + 1],
                q=q,
            )
        )
        q = wl + vl * q * wf * inverse
    return out, q


KINDS = ("p_first", "p_before", "a_first", "a_before", "a_after", "couple", "couple_after", "q")


def forward(coef, firsts, lasts):
    before = [jnp.zeros_like(firsts[0])]
    for j in range(len(firsts)):
        before.append(
            lasts[j] + coef("p_first", j) * firsts[j] + coef("p_before", j) * before[j]
        )
    return before


def backward(coef, firsts, before, after):
    blocks = len(firsts)
    above, below = [None] * blocks, [None] * blocks
    for j in reversed(range(blocks)):
        below[j] = coef("couple_after", j) * after
        here = (
            coef("a_first", j) * firsts[j]
            + coef("a_before", j) * before[j]
            + coef("a_after", j) * after
        )
        above[j] = coef("couple", j) * (before[j] + coef("q", j) * here)
        after = here
    return above, below


def half_chain(tiles, slabs, flipped, middle):
    shape = (ROWS, LANES)
    scalars = [block_scalars(tile, slabs, shape, flipped) for tile in tiles]
    couple = [jnp.zeros(shape, jnp.float32)]
    for k in range(1, len(tiles)):
        ratio = jnp.where(flipped, scalars[k - 1][1], scalars[k][1])
        couple.append(coupling(ratio, scalars[k - 1][0][1, 1], scalars[k][0][0, 0], slabs))
    couple.append(middle)
    return chain([corner for corner, _ in scalars], couple)


def meta_place(j, lines, share):
    side = share // LANES
    row = lines + j // side * META
    return slice(row, row + META), slice(j % side * LANES, (j % side + 1) * LANES)


def first_kernel(slabs, half, fl_ref, out_ref, table):
    blocks, rows, share = fl_ref.shape
    lines = (rows - META_ROWS) // 2
    flip = half[0]
    flipped = flip == 1
    block = [k + flip * (blocks - 1 - 2 * k) for k in range(blocks)]
    entries, _ = half_chain(
        [fl_ref[block[k], 2 * lines : 2 * lines + ROWS, :LANES] for k in range(blocks)],
        slabs,
        flipped,
        jnp.zeros((ROWS, LANES), jnp.float32),
    )
    for k, entry in enumerate(entries):
        for n, kind in enumerate(KINDS[:2]):
            table[k, n] = entry[kind]
    coef = lambda kind, k: table[k, KINDS.index(kind)]

    def group(g, carry):
        rows = pl.ds(pl.multiple_of(g * ROWS, ROWS), ROWS)
        outer = pl.ds(pl.multiple_of(flip * lines + g * ROWS, ROWS), ROWS)
        inner = pl.ds(pl.multiple_of((1 - flip) * lines + g * ROWS, ROWS), ROWS)
        for t in range(share // LANES):
            cols = slice(t * LANES, (t + 1) * LANES)
            before = forward(
                coef,
                [fl_ref[block[k], outer, cols] for k in range(blocks)],
                [fl_ref[block[k], inner, cols] for k in range(blocks)],
            )
            out_ref[rows, cols] = before[blocks]
        return carry

    lax.fori_loop(0, lines // ROWS, group, 0)
    out_ref[lines:, :] = jnp.zeros((out_ref.shape[0] - lines, share), jnp.float32)
    for j in range(blocks):
        rows, cols = meta_place(j, lines, share)
        out_ref[rows, cols] = fl_ref[j, 2 * lines : 2 * lines + META, :LANES]


def first_half(half, fl, slabs):
    parts, rows, share = fl.shape
    lines = (rows - META_ROWS) // 2
    vmem = pl.BlockSpec(memory_space=pltpu.VMEM)
    rows = -(-meta_place(parts - 1, lines, share)[0].stop // ROWS) * ROWS
    return pl.pallas_call(
        functools.partial(first_kernel, slabs),
        in_specs=[pl.BlockSpec(memory_space=pltpu.SMEM), vmem],
        out_specs=vmem,
        out_shape=jax.ShapeDtypeStruct((rows, share), jnp.float32),
        scratch_shapes=[pltpu.VMEM((parts, 2, ROWS, LANES), jnp.float32)],
        compiler_params=pltpu.CompilerParams(vmem_limit_bytes=SMALL_VMEM),
        cost_estimate=pl.CostEstimate(flops=4 * fl.size, bytes_accessed=5 * fl.size, transcendentals=0),
        name="reduced_in",
    )(half, fl)


def second_kernel(slabs, half, fl_ref, mine, other, uv_ref, info_ref, table):
    blocks, _, lines, share = uv_ref.shape
    flip = half[0]
    flipped = flip == 1
    block = [k + flip * (blocks - 1 - 2 * k) for k in range(blocks)]
    for j in range(blocks):
        rows, cols = meta_place(j, lines, share)
        info_ref[flip * blocks + j] = fl_ref[j, 2 * lines :, :LANES]
        info_ref[(1 - flip) * blocks + j] = jnp.zeros((META_ROWS, LANES), jnp.float32)
        info_ref[(1 - flip) * blocks + j, :META] = other[rows, cols]
    shape = (ROWS, LANES)
    above, above_ratio = block_scalars(info_ref[blocks - 1], slabs, shape)
    below, below_ratio = block_scalars(info_ref[blocks], slabs, shape)
    middle = coupling(below_ratio, above[1, 1], below[0, 0], slabs)
    tiles = lambda flip: [
        info_ref[flip * blocks + k + flip * (blocks - 1 - 2 * k)] for k in range(blocks)
    ]
    entries, q_own = half_chain(tiles(flip), slabs, flipped, middle)
    _, q_other = half_chain(tiles(1 - flip), slabs, jnp.logical_not(flipped), middle)
    for k, entry in enumerate(entries):
        for n, kind in enumerate(KINDS):
            table[k, n] = entry[kind]
    table[blocks, 0] = 1.0 / (1.0 - q_own * q_other)
    table[blocks, 1] = q_other
    coef = lambda kind, k: table[k, KINDS.index(kind)]

    def group(g, carry):
        rows = pl.ds(pl.multiple_of(g * ROWS, ROWS), ROWS)
        outside = pl.ds(pl.multiple_of(flip * lines + g * ROWS, ROWS), ROWS)
        inside = pl.ds(pl.multiple_of((1 - flip) * lines + g * ROWS, ROWS), ROWS)
        for t in range(share // LANES):
            cols = slice(t * LANES, (t + 1) * LANES)
            firsts = [fl_ref[block[k], outside, cols] for k in range(blocks)]
            lasts = [fl_ref[block[k], inside, cols] for k in range(blocks - 1)]
            before = forward(coef, firsts[:-1], lasts)
            across = table[blocks, 0] * (other[rows, cols] + table[blocks, 1] * mine[rows, cols])
            outer, inner = backward(coef, firsts, before, across)
            for k in range(blocks):
                uv_ref[block[k], flip, rows, cols] = outer[k]
                uv_ref[block[k], 1 - flip, rows, cols] = inner[k]
        return carry

    lax.fori_loop(0, lines // ROWS, group, 0)


def second_half(half, fl, mine, other, slabs):
    parts, rows, share = fl.shape
    lines = (rows - META_ROWS) // 2
    vmem = pl.BlockSpec(memory_space=pltpu.VMEM)
    return pl.pallas_call(
        functools.partial(second_kernel, slabs),
        in_specs=[pl.BlockSpec(memory_space=pltpu.SMEM), vmem, vmem, vmem],
        out_specs=[vmem, vmem],
        out_shape=[
            jax.ShapeDtypeStruct((parts, 2, lines, share), jnp.float32),
            jax.ShapeDtypeStruct((2 * parts, META_ROWS, LANES), jnp.float32),
        ],
        scratch_shapes=[pltpu.VMEM((parts + 1, len(KINDS), ROWS, LANES), jnp.float32)],
        compiler_params=pltpu.CompilerParams(vmem_limit_bytes=SMALL_VMEM),
        cost_estimate=pl.CostEstimate(flops=10 * fl.size, bytes_accessed=9 * fl.size, transcendentals=0),
        name="reduced_out",
    )(half, fl, mine, other)


def extras_kernel(where_am_i, info, source, flux, inverse, inlet, holders, wells_ref, rows_ref, leaving, found):
    blocks = info.shape[0]
    slabs, wells = wells_ref.shape
    d = where_am_i[0]
    dot = functools.partial(jnp.dot, precision=HIGHEST, preferred_element_type=jnp.float32)
    row_of = lambda j, n: info[j, 2 + n : 3 + n, :wells]
    down, rise = [None] * blocks, [None] * blocks
    value = inlet[...]
    for j in range(blocks):
        down[j] = value
        value = row_of(j, 0) * value + row_of(j, 1)
    for j in reversed(range(blocks)):
        rise[j] = value
        value = row_of(j, 0) * value + row_of(j, 2)
    held = holders[...] == lax.broadcasted_iota(jnp.int32, (wells, holders.shape[1]), 0)
    leaving[...] = dot(jnp.broadcast_to(value, (ROWS, wells)), held.astype(jnp.float32))[0:1]

    ends = [
        [row_of(j, n) + row_of(j, n + 1) * down[j] + row_of(j, n + 2) * rise[j] for j in range(blocks)]
        for n in (3, 6)
    ]
    scalars = [block_scalars(info[j], slabs, (1, wells)) for j in range(blocks)]
    zero = jnp.zeros((1, wells), jnp.float32)
    couple = [zero]
    for j in range(1, blocks):
        couple.append(
            coupling(scalars[j][1], scalars[j - 1][0][1, 1], scalars[j][0][0, 0], slabs)
        )
    couple.append(zero)
    coefs, _ = chain([corner for corner, _ in scalars], couple)
    coef = lambda kind, j: coefs[j][kind]
    above, below = backward(coef, ends[0], forward(coef, *ends), zero)
    for j in range(blocks):
        for n, value in enumerate((down[j], rise[j], above[j], below[j])):
            found[j, n : n + 1] = value
    mine = found[d]
    row = lax.broadcasted_iota(jnp.int32, (slabs, wells), 0)
    own = source[0] + source[1] * mine[0:1] + source[2] * mine[1:2]
    own = own + jnp.where(row == 0, mine[2:3], 0.0) + jnp.where(row == slabs - 1, mine[3:4], 0.0)
    wells_ref[...] = dot(inverse[...], own)
    for n in range(2):
        rows_ref[n] = dot(inverse[...], flux[n])


def extras(depth_index, info, source, flux, inverse, inlet, holders):
    blocks = info.shape[0]
    _, slabs, span = flux.shape
    wells = source.shape[-1]
    vmem = pl.BlockSpec(memory_space=pltpu.VMEM)
    return pl.pallas_call(
        extras_kernel,
        in_specs=[pl.BlockSpec(memory_space=pltpu.SMEM)] + [vmem] * 6,
        out_specs=[vmem] * 3,
        out_shape=[
            jax.ShapeDtypeStruct((slabs, wells), jnp.float32),
            jax.ShapeDtypeStruct((2, slabs, span), jnp.float32),
            jax.ShapeDtypeStruct((1, holders.shape[1]), jnp.float32),
        ],
        scratch_shapes=[pltpu.VMEM((blocks, ROWS, wells), jnp.float32)],
        compiler_params=pltpu.CompilerParams(vmem_limit_bytes=SMALL_VMEM),
        cost_estimate=pl.CostEstimate(flops=10**7, bytes_accessed=10**6, transcendentals=0),
        name="extras",
    )(depth_index.reshape(1), info, source, flux, inverse, inlet, holders)


def solve_kernel(right, uv, inverse, place_row, place_column, solved_wells, outer, out, factor, pick):
    together, slabs, rows, span = right.shape
    wells = place_row.shape[1]
    step = pl.program_id(0)
    size = slabs * rows

    @pl.when(step == 0)
    def _():
        spread = (
            lax.broadcasted_iota(jnp.int32, (size, slabs), 0) // rows
            == lax.broadcasted_iota(jnp.int32, (size, slabs), 1)
        ).astype(jnp.float32).astype(jnp.bfloat16)
        spread_t = (
            lax.broadcasted_iota(jnp.int32, (slabs, size), 1) // rows
            == lax.broadcasted_iota(jnp.int32, (slabs, size), 0)
        ).astype(jnp.float32).astype(jnp.bfloat16)
        same = (
            lax.broadcasted_iota(jnp.int32, (size, size), 0) % rows
            == lax.broadcasted_iota(jnp.int32, (size, size), 1) % rows
        )
        for n, part in enumerate(split_bf16(inverse[...], 2)):
            tall = jnp.dot(spread, part, preferred_element_type=jnp.float32).astype(jnp.bfloat16)
            wide = jnp.dot(tall, spread_t, preferred_element_type=jnp.float32)
            wide = jnp.where(same, wide, 0.0).astype(jnp.bfloat16)
            if n == 0:
                factor[:, :size] = wide
                factor[:, size : 2 * size] = wide
            else:
                factor[:, 2 * size : 3 * size] = wide
        column = lax.broadcasted_iota(jnp.int32, (wells, span), 1)
        chosen = (column == place_column[...] % span).astype(jnp.float32).astype(jnp.bfloat16)
        pick[:wells] = chosen
        pick[wells:] = chosen

    tile = min(span, 256)
    for n in range(together):
        line = lax.broadcasted_iota(jnp.int32, (slabs, rows, wells), 1) + (step * together + n) * rows
        at_wells = jnp.where(line == (place_row[...] // span)[None], solved_wells[...][:, None, :], 0.0)
        at_wells = jnp.concatenate(split_bf16(at_wells.reshape(size, wells), 2), axis=1)
        factor[:, 3 * size :] = at_wells
        lines = slice(n * rows, (n + 1) * rows)
        above = jnp.concatenate([uv[d, 0, lines] for d in range(uv.shape[0])], axis=1)
        below = jnp.concatenate([uv[d, 1, lines] for d in range(uv.shape[0])], axis=1)
        for t in range(span // tile):
            cols = slice(t * tile, (t + 1) * tile)
            value = jnp.concatenate(
                [
                    right[n, 0:1, :, cols] + above[None, :, cols],
                    right[n, 1 : slabs - 1, :, cols],
                    right[n, slabs - 1 :, :, cols] + below[None, :, cols],
                ],
                axis=0,
            ).reshape(size, tile)
            upper, lower = split_bf16(value, 2)
            result = jnp.dot(
                factor[...],
                jnp.concatenate([upper, lower, upper, pick[:, cols]], axis=0),
                preferred_element_type=jnp.float32,
            )
            out[:, lines, cols] = result.reshape(slabs, rows, tile)

    for n, (when, line) in enumerate(((0, 0), (pl.num_programs(0) - 1, together * rows - 1))):

        @pl.when(step == when)
        def _():
            for z in range(slabs):
                out[z, line : line + 1, :] += outer[n, z : z + 1, :]


def solve(right, uv, inverse, place_row, solved_wells, outer):
    groups, slabs, _, span = right.shape
    wells = place_row.shape[1]
    together = 2
    lines = together * ROWS
    shares, _, _, share = uv.shape
    whole = lambda *shape: pl.BlockSpec(shape, lambda g: (0,) * len(shape))
    size = slabs * ROWS
    return pl.pallas_call(
        solve_kernel,
        grid=(groups // together,),
        in_specs=[
            pl.BlockSpec((together, slabs, ROWS, span), lambda g: (g, 0, 0, 0)),
            pl.BlockSpec((shares, 2, lines, share), lambda g: (0, 0, g, 0)),
            whole(slabs, slabs),
            whole(1, wells),
            whole(wells, 1),
            whole(slabs, wells),
            whole(*outer.shape),
        ],
        out_specs=pl.BlockSpec((slabs, lines, span), lambda g: (0, g, 0)),
        out_shape=jax.ShapeDtypeStruct((slabs, groups * ROWS, span), jnp.float32),
        scratch_shapes=[
            pltpu.VMEM((size, 3 * size + 2 * wells), jnp.bfloat16),
            pltpu.VMEM((2 * wells, span), jnp.bfloat16),
        ],
        compiler_params=pltpu.CompilerParams(vmem_limit_bytes=SOLVE_VMEM),
        cost_estimate=pl.CostEstimate(
            flops=8 * size * right.size, bytes_accessed=8 * right.size, transcendentals=0
        ),
        name="depth_solve",
    )(right, uv, inverse, place_row, place_row.reshape(wells, 1), solved_wells, outer)


def body(
    warmth_before,
    stratum_category,
    conductance_catalogue,
    pivot_matrix_reciprocal,
    linkage_factor,
    well_position_inside,
    well_holder_sequence,
    well_reach,
    entering_warmth,
    well_transfer_speed,
):
    slabs, lines, span = warmth_before.shape
    depth_index = lax.axis_index("depth")
    depth_count = lax.axis_size("depth")
    wells = well_position_inside.shape[0]
    owned = wells // depth_count
    table = conductance_catalogue

    parts = depth_count // 2
    halves = [list(range(h * parts, (h + 1) * parts)) for h in range(2)]
    half = (depth_index // parts).astype(jnp.int32).reshape(1)

    place_row = well_position_inside.reshape(1, wells)
    first, last = edge_rows(warmth_before, stratum_category, table)
    first, last, place_row = lax.optimization_barrier((first, last, place_row))
    count = lax.axis_size("strip")
    up = [(i, i + 1) for i in range(count - 1)]
    down = [(j, i) for i, j in up]
    before = lax.ppermute(last, "strip", up)
    after = lax.ppermute(first, "strip", down)
    right, sums, cells = stencil(
        warmth_before, stratum_category, table, pivot_matrix_reciprocal, place_row
    )
    fl, flux, source = payload(
        linkage_factor,
        table,
        depth_index,
        sums,
        (first, last, before, after),
        pivot_matrix_reciprocal,
        cells,
        well_transfer_speed.reshape(1, wells),
        well_reach.reshape(1, wells),
        parts,
    )
    exchange = functools.partial(
        lax.all_to_all,
        axis_name="depth",
        split_axis=0,
        concat_axis=0,
        tiled=True,
        axis_index_groups=halves,
    )
    fl_all = exchange(fl)

    mine = first_half(half, fl_all, slabs)
    other = lax.ppermute(
        mine, "depth", [(i, (i + parts) % depth_count) for i in range(depth_count)]
    )
    uv, info_all = second_half(half, fl_all, mine, other, slabs)
    uv_own = exchange(uv)

    holders = lax.dynamic_slice_in_dim(well_holder_sequence, depth_index * owned, owned)
    solved_wells, outer, leaving = extras(
        depth_index,
        info_all,
        source,
        flux,
        pivot_matrix_reciprocal,
        entering_warmth.reshape(1, wells),
        holders.reshape(1, owned),
    )
    solved = solve(right, uv_own, pivot_matrix_reciprocal, place_row, solved_wells, outer)
    return solved, leaving.reshape(owned)


def solution(mesh):
    in_specs = (
        P("depth", "strip", None),
        P("depth", "strip", None),
        P(),
        P("depth", None),
        P("depth"),
        P("strip"),
        P("strip"),
        P("strip"),
        P("strip"),
        P("strip"),
    )
    out_specs = (P("depth", "strip", None), P(("strip", "depth")))
    return jax.shard_map(body, mesh=mesh, in_specs=in_specs, out_specs=out_specs, check_vma=False)
```

```python
import functools

import jax
import jax.numpy as jnp
from jax import lax
from jax.experimental import pallas as pl
from jax.experimental.pallas import tpu as pltpu
from jax.sharding import PartitionSpec as P

backward_euler_advance = 0.2
storage_volume = 2.0
flux_scale = 0.5 * backward_euler_advance
LANES = 128
ROWS = 8
EDGE_VMEM = 56 * 1024 * 1024
VMEM_LIMIT = 40 * 1024 * 1024
SOLVE_VMEM = 24 * 1024 * 1024
SMALL_VMEM = 12 * 1024 * 1024
HIGHEST = lax.Precision.HIGHEST


def select_tree(category, entries):
    values = list(entries)
    bit = 1
    while len(values) > 1:
        odd = (category & bit) != 0
        values = [
            jnp.where(odd, values[k + 1], values[k]) if k + 1 < len(values) else values[k]
            for k in range(0, len(values), 2)
        ]
        bit *= 2
    return values[0]


def split_bf16(value, pieces):
    out = []
    for k in range(pieces):
        part = value.astype(jnp.bfloat16)
        out.append(part)
        if k + 1 < pieces:
            value = value - part.astype(jnp.float32)
    return out


def edge_kernel(table, w_first, cat_first, w_last, cat_last, first, last):
    slabs, rows, span = w_first.shape
    entries = [flux_scale * table[k] for k in range(table.shape[0])]
    sub = lax.broadcasted_iota(jnp.int32, (ROWS, span), 0)

    def gathered(ref, start, row):
        value = jnp.broadcast_to(ref[start, row : row + 1, :], (ROWS, span))
        for k in range(1, ROWS):
            value = jnp.where(sub == k, ref[start + k, row : row + 1, :], value)
        return value

    for w_ref, cat_ref, row, out in ((w_first, cat_first, 0, first), (w_last, cat_last, rows - 1, last)):
        for start in range(0, slabs, ROWS):
            out[0, start : start + ROWS] = gathered(w_ref, start, row)
            out[1, start : start + ROWS] = select_tree(gathered(cat_ref, start, row), entries)


def edge_rows(w, cat, table):
    slabs, lines, span = w.shape
    top = pl.BlockSpec((slabs, ROWS, span), lambda i: (0, 0, 0))
    end = pl.BlockSpec((slabs, ROWS, span), lambda i: (0, lines // ROWS - 1, 0))
    out = pl.BlockSpec((2, slabs, span), lambda i: (0, 0, 0))
    return pl.pallas_call(
        edge_kernel,
        grid=(1,),
        in_specs=[pl.BlockSpec(memory_space=pltpu.SMEM), top, top, end, end],
        out_specs=[out, out],
        out_shape=[jax.ShapeDtypeStruct((2, slabs, span), jnp.float32)] * 2,
        compiler_params=pltpu.CompilerParams(vmem_limit_bytes=EDGE_VMEM),
        cost_estimate=pl.CostEstimate(flops=10**6, bytes_accessed=w.size, transcendentals=0),
        name="edge_rows",
    )(table, w, cat, w, cat)


def stencil_kernel(
    table,
    ends,
    w_ref,
    cat_ref,
    place,
    right_ref,
    acc,
    cells_ref,
    ws,
    cs,
    fs,
    base,
    pieces,
    shift,
    pick,
    found,
):
    step = pl.program_id(0)
    planes, lines, span = w_ref.shape
    tiles = span // LANES
    groups = lines // ROWS
    wells = place.shape[1]
    entries = [flux_scale * table[k] for k in range(table.shape[0])]
    lane = lax.broadcasted_iota(jnp.int32, (lines, LANES), 1)
    own_line = lax.broadcasted_iota(jnp.int32, (lines, wells), 0) == place[...] // span
    top, end = ROWS, ROWS + lines
    dot = functools.partial(jnp.dot, preferred_element_type=jnp.float32)

    @pl.when(step == 0)
    def _():
        acc[...] = jnp.zeros_like(acc)
        base[...] = jnp.zeros_like(base)
        pieces[...] = jnp.zeros_like(pieces)
        source = lax.broadcasted_iota(jnp.int32, shift.shape, 0) % (2 * LANES)
        target = lax.broadcasted_iota(jnp.int32, shift.shape, 1)
        shift[...] = (source == target + 1).astype(jnp.float32).astype(jnp.bfloat16)
        column = lax.broadcasted_iota(jnp.int32, (span, wells), 0)
        pick[...] = (column == place[...] % span).astype(jnp.float32).astype(jnp.bfloat16)

    def keep_face(slot, t, face):
        for n, part in enumerate(split_bf16(face, 2)):
            pieces[slot, n, t] = part

    def faces(k, slot):
        left_w = left_c = jnp.zeros((lines, LANES), jnp.float32)
        for t in range(tiles):
            cols = slice(t * LANES, (t + 1) * LANES)
            w = w_ref[k, :, cols]
            c = select_tree(cat_ref[k, :, cols], entries)
            for ref, value in ((ws, w), (cs, c)):
                ref[t, top:end] = value
                ref[t, top - 1 : top] = value[0:1]
            roll_w, roll_c = pltpu.roll(w, 1, 1), pltpu.roll(c, 1, 1)
            west_w = jnp.where(lane == 0, left_w, roll_w)
            west_c = jnp.where(lane == 0, left_c, roll_c)
            left_w, left_c = roll_w, roll_c
            face = (c + west_c) * (w - west_w)
            keep_face(slot, t, face)
            if t == tiles - 1:
                keep_face(slot, tiles, pltpu.roll(-c * w, 1, 1))
            north = (c + cs[t, top - 1 : end - 1]) * (w - ws[t, top - 1 : end - 1])
            fs[t, top:end] = north
            fs[t, end : end + 1] = jnp.zeros((1, LANES), jnp.float32)
            base[slot, t] = w - face - north + fs[t, top + 1 : end + 1]

    def well_cells(k):
        upper, lower = split_bf16(w_ref[k], 2)
        kinds = cat_ref[k].astype(jnp.float32).astype(jnp.bfloat16)
        sums = dot(jnp.concatenate([upper, lower, kinds], axis=0), pick[...])
        for n, value in enumerate((sums[:lines] + sums[lines : 2 * lines], sums[2 * lines :])):
            mine = jnp.where(own_line, value, 0.0)
            found[k, n : n + 1, :] = jnp.sum(mine, axis=0, keepdims=True)

    def finish(k, slot, on):
        z = step * planes + k
        end_first = jnp.where(on, ends[0, z], 0.0)
        end_last = jnp.where(on, ends[ends.shape[0] - 1, z], 0.0)
        parts = [
            pieces[slot, n, d : d + tiles].reshape(tiles * lines, LANES)
            for n in range(2)
            for d in range(2)
        ]
        east = dot(jnp.concatenate(parts, axis=1), shift[...])
        for t in range(tiles):
            cols = slice(t * LANES, (t + 1) * LANES)
            value = base[slot, t] + east[t * lines : (t + 1) * lines]
            right_ref[:, k, :, cols] = value.reshape(groups, ROWS, LANES)
            acc[0, :, cols] += end_first * value
            acc[1, :, cols] += end_last * value

    def two_planes(m, carry):
        k = 2 * m
        finish(jnp.maximum(k - 1, 0), 1, m > 0)
        faces(k, 0)
        well_cells(k)
        finish(k, 0, True)
        faces(k + 1, 1)
        well_cells(k + 1)
        return carry

    lax.fori_loop(0, planes // 2, two_planes, 0)
    finish(planes - 1, 1, True)
    for k in range(planes):
        for n in range(2):
            cells_ref[n, k : k + 1, :] = found[k, n : n + 1, :]


def stencil(w, cat, table, inverse, place_row):
    slabs, lines, span = w.shape
    planes, groups = 8, lines // ROWS
    wells = place_row.shape[1]
    block = pl.BlockSpec((planes, lines, span), lambda i: (i, 0, 0))
    smem = pl.BlockSpec(memory_space=pltpu.SMEM)
    shifted = pltpu.VMEM((span // LANES, lines + 2 * ROWS, LANES), jnp.float32)
    return pl.pallas_call(
        stencil_kernel,
        grid=(slabs // planes,),
        in_specs=[smem, smem, block, block, pl.BlockSpec((1, wells), lambda i: (0, 0))],
        out_specs=[
            pl.BlockSpec((groups, planes, ROWS, span), lambda i: (0, i, 0, 0)),
            pl.BlockSpec((2, lines, span), lambda i: (0, 0, 0)),
            pl.BlockSpec((2, planes, wells), lambda i: (0, i, 0)),
        ],
        out_shape=[
            jax.ShapeDtypeStruct((groups, slabs, ROWS, span), jnp.float32),
            jax.ShapeDtypeStruct((2, lines, span), jnp.float32),
            jax.ShapeDtypeStruct((2, slabs, wells), jnp.float32),
        ],
        scratch_shapes=[
            shifted,
            shifted,
            shifted,
            pltpu.VMEM((2, span // LANES, lines, LANES), jnp.float32),
            pltpu.VMEM((2, 2, span // LANES + 1, lines, LANES), jnp.bfloat16),
            pltpu.VMEM((4 * LANES, LANES), jnp.bfloat16),
            pltpu.VMEM((span, wells), jnp.bfloat16),
            pltpu.VMEM((planes, 2, wells), jnp.float32),
        ],
        compiler_params=pltpu.CompilerParams(vmem_limit_bytes=VMEM_LIMIT),
        cost_estimate=pl.CostEstimate(flops=40 * w.size, bytes_accessed=12 * w.size, transcendentals=0),
        name="stencil",
    )(table, inverse, w, cat, place_row)


META = 11
META_ROWS = 16


def payload_kernel(
    ratio,
    table,
    where_am_i,
    sums,
    first,
    last,
    before,
    after,
    inverse,
    cells,
    speed,
    reach,
    *refs,
):
    out_refs, (flux_ref, source_ref, keep, force, paths, totals) = refs[:-6], refs[-6:]
    copies = len(out_refs)
    share = out_refs[0].shape[1]
    mine = where_am_i[0] & (copies - 1)
    _, lines, span = sums.shape
    _, slabs, wells = cells.shape
    dot = functools.partial(jnp.dot, precision=HIGHEST, preferred_element_type=jnp.float32)
    ends = jnp.concatenate([inverse[0:1], inverse[slabs - 1 : slabs]], axis=0)
    meta = 2 * lines

    entries = [table[k] for k in range(table.shape[0])]
    level = lax.broadcasted_iota(jnp.int32, (slabs, wells), 0) + where_am_i[0] * slabs
    rock = cells[0]
    cond = select_tree(cells[1].astype(jnp.int32), entries)
    rate = jnp.where(level < reach[...], speed[...] * cond / (1.0 + cond), 0.0)
    keep[...] = 1.0 - rate
    force[...] = rate * rock
    ones, zeros = jnp.ones((1, wells), jnp.float32), jnp.zeros((1, wells), jnp.float32)
    ways = []
    for n, order in enumerate((range(slabs), reversed(range(slabs)))):
        scale, shift = ones, zeros
        for z in order:
            paths[n, 0, z : z + 1] = scale
            paths[n, 1, z : z + 1] = shift
            scale, shift = keep[z : z + 1] * scale, keep[z : z + 1] * shift + force[z : z + 1]
        ways.append((scale, shift))
    source_ref[0] = -storage_volume * rate * (2.0 * rock - paths[0, 1] - paths[1, 1])
    source_ref[1] = storage_volume * rate * paths[0, 0]
    source_ref[2] = storage_volume * rate * paths[1, 0]
    own_sums = [dot(ends, source_ref[n]) for n in range(3)]

    rows = [ways[0][0], ways[0][1], ways[1][1]]
    rows += [own_sums[n][q : q + 1] for q in range(2) for n in range(3)]
    extras = []
    for own, other, line, n in ((first, before, 0, 0), (last, after, lines - 1, 1)):
        flux = (own[1] + other[1]) * (other[0] - own[0])
        flux_ref[n] = flux
        extras.append((line, dot(ends, flux)))
    totals[...] = sums[...]
    for line, extra in extras:
        for q in range(2):
            totals[q, line : line + 1, :] += extra[q : q + 1]
    for m, out_ref in enumerate(out_refs):
        cols = pl.ds(pl.multiple_of((mine ^ m) * share, share), share)
        for q in range(2):
            out_ref[q * lines : (q + 1) * lines] = totals[q, :, cols]
        out_ref[meta : meta + META_ROWS] = jnp.zeros((META_ROWS, share), jnp.float32)
        out_ref[meta : meta + 2, :slabs] = ends
        out_ref[meta : meta + 1, slabs : slabs + 1] = jnp.full((1, 1), ratio[0])
        for n, row in enumerate(rows):
            out_ref[meta + 2 + n : meta + 3 + n, :wells] = row


def payload(ratio, table, where, sums, edges, inverse, cells, speed, reach, copies):
    _, lines, span = sums.shape
    _, slabs, wells = cells.shape
    share = span // copies
    smem = pl.BlockSpec(memory_space=pltpu.SMEM)
    vmem = pl.BlockSpec(memory_space=pltpu.VMEM)
    column = pltpu.VMEM((slabs, wells), jnp.float32)
    return pl.pallas_call(
        payload_kernel,
        in_specs=[smem] * 3 + [vmem] * 9,
        out_specs=[vmem] * (copies + 2),
        out_shape=[jax.ShapeDtypeStruct((2 * lines + META_ROWS, share), jnp.float32)] * copies
        + [
            jax.ShapeDtypeStruct((2, slabs, span), jnp.float32),
            jax.ShapeDtypeStruct((3, slabs, wells), jnp.float32),
        ],
        scratch_shapes=[
            column,
            column,
            pltpu.VMEM((2, 2, slabs, wells), jnp.float32),
            pltpu.VMEM((2, lines, span), jnp.float32),
        ],
        compiler_params=pltpu.CompilerParams(vmem_limit_bytes=SMALL_VMEM),
        cost_estimate=pl.CostEstimate(flops=10**6, bytes_accessed=10**6, transcendentals=0),
        name="payload",
    )(ratio, table, where, sums, *edges, inverse, cells, speed, reach)


CORNERS = ((0, 0), (0, 1), (1, 0), (1, 1))


def block_scalars(tile, slabs, shape, flipped=None):
    at = lambda row, lane: jnp.broadcast_to(tile[row : row + 1, lane : lane + 1], shape)
    corner = {(r, c): at(r, c * (slabs - 1)) for r, c in CORNERS}
    if flipped is not None:
        corner = {(r, c): jnp.where(flipped, corner[1 - r, 1 - c], corner[r, c]) for r, c in CORNERS}
    return corner, at(0, slabs)


def coupling(ratio, one, other, slabs):
    return ratio * (slabs / (slabs + 1.0)) / jnp.sqrt(one * other)


def chain(corners, couple, q=None):
    out = []
    q = jnp.zeros_like(couple[0])
    for k, corner in enumerate(corners):
        vf, vl = couple[k] * corner[0, 0], couple[k] * corner[1, 0]
        wf, wl = couple[k + 1] * corner[0, 1], couple[k + 1] * corner[1, 1]
        inverse = 1.0 / (1.0 - vf * q)
        out.append(
            dict(
                p_first=vl * q * inverse,
                p_before=vl * inverse,
                a_first=inverse,
                a_before=vf * inverse,
                a_after=wf * inverse,
                couple=couple[k],
                couple_after=couple[k + 1],
                q=q,
            )
        )
        q = wl + vl * q * wf * inverse
    return out, q


KINDS = ("p_first", "p_before", "a_first", "a_before", "a_after", "couple", "couple_after", "q")


def forward(coef, firsts, lasts):
    before = [jnp.zeros_like(firsts[0])]
    for j in range(len(firsts)):
        before.append(
            lasts[j] + coef("p_first", j) * firsts[j] + coef("p_before", j) * before[j]
        )
    return before


def backward(coef, firsts, before, after):
    blocks = len(firsts)
    above, below = [None] * blocks, [None] * blocks
    for j in reversed(range(blocks)):
        below[j] = coef("couple_after", j) * after
        here = (
            coef("a_first", j) * firsts[j]
            + coef("a_before", j) * before[j]
            + coef("a_after", j) * after
        )
        above[j] = coef("couple", j) * (before[j] + coef("q", j) * here)
        after = here
    return above, below


def half_chain(tiles, slabs, flipped, middle):
    shape = (ROWS, LANES)
    scalars = [block_scalars(tile, slabs, shape, flipped) for tile in tiles]
    couple = [jnp.zeros(shape, jnp.float32)]
    for k in range(1, len(tiles)):
        ratio = jnp.where(flipped, scalars[k - 1][1], scalars[k][1])
        couple.append(coupling(ratio, scalars[k - 1][0][1, 1], scalars[k][0][0, 0], slabs))
    couple.append(middle)
    return chain([corner for corner, _ in scalars], couple)


def meta_place(j, lines, share):
    side = share // LANES
    row = lines + j // side * META
    return slice(row, row + META), slice(j % side * LANES, (j % side + 1) * LANES)


def first_kernel(slabs, where, *refs):
    piece_refs, (out_ref, fl_ref, table) = refs[:-3], refs[-3:]
    blocks, rows, share = fl_ref.shape
    lines = (rows - META_ROWS) // 2
    mine = where[0] & (blocks - 1)
    for m, piece in enumerate(piece_refs):
        fl_ref[mine ^ m] = piece[...]
    flip = where[0] // blocks
    flipped = flip == 1
    block = [k + flip * (blocks - 1 - 2 * k) for k in range(blocks)]
    entries, _ = half_chain(
        [fl_ref[block[k], 2 * lines : 2 * lines + ROWS, :LANES] for k in range(blocks)],
        slabs,
        flipped,
        jnp.zeros((ROWS, LANES), jnp.float32),
    )
    for k, entry in enumerate(entries):
        for n, kind in enumerate(KINDS[:2]):
            table[k, n] = entry[kind]
    coef = lambda kind, k: table[k, KINDS.index(kind)]

    def group(g, carry):
        rows = pl.ds(pl.multiple_of(g * ROWS, ROWS), ROWS)
        outer = pl.ds(pl.multiple_of(flip * lines + g * ROWS, ROWS), ROWS)
        inner = pl.ds(pl.multiple_of((1 - flip) * lines + g * ROWS, ROWS), ROWS)
        for t in range(share // LANES):
            cols = slice(t * LANES, (t + 1) * LANES)
            before = forward(
                coef,
                [fl_ref[block[k], outer, cols] for k in range(blocks)],
                [fl_ref[block[k], inner, cols] for k in range(blocks)],
            )
            out_ref[rows, cols] = before[blocks]
        return carry

    lax.fori_loop(0, lines // ROWS, group, 0)
    out_ref[lines:, :] = jnp.zeros((out_ref.shape[0] - lines, share), jnp.float32)
    for j in range(blocks):
        rows, cols = meta_place(j, lines, share)
        out_ref[rows, cols] = fl_ref[j, 2 * lines : 2 * lines + META, :LANES]


def first_half(where, pieces, slabs):
    parts = len(pieces)
    rows, share = pieces[0].shape
    lines = (rows - META_ROWS) // 2
    vmem = pl.BlockSpec(memory_space=pltpu.VMEM)
    crossing = -(-meta_place(parts - 1, lines, share)[0].stop // ROWS) * ROWS
    return pl.pallas_call(
        functools.partial(first_kernel, slabs),
        in_specs=[pl.BlockSpec(memory_space=pltpu.SMEM)] + [vmem] * parts,
        out_specs=[vmem, vmem],
        out_shape=[
            jax.ShapeDtypeStruct((crossing, share), jnp.float32),
            jax.ShapeDtypeStruct((parts, rows, share), jnp.float32),
        ],
        scratch_shapes=[pltpu.VMEM((parts, 2, ROWS, LANES), jnp.float32)],
        compiler_params=pltpu.CompilerParams(vmem_limit_bytes=SMALL_VMEM),
        cost_estimate=pl.CostEstimate(flops=10**6, bytes_accessed=10**6, transcendentals=0),
        name="reduced_in",
    )(where, *pieces)


def second_kernel(slabs, where, fl_ref, mine, other, *refs):
    out_refs, (info_ref, table, uv_ref) = refs[:-3], refs[-3:]
    blocks, _, lines, share = uv_ref.shape
    flip = where[0] // blocks
    flipped = flip == 1
    block = [k + flip * (blocks - 1 - 2 * k) for k in range(blocks)]
    for j in range(blocks):
        rows, cols = meta_place(j, lines, share)
        info_ref[flip * blocks + j] = fl_ref[j, 2 * lines :, :LANES]
        info_ref[(1 - flip) * blocks + j] = jnp.zeros((META_ROWS, LANES), jnp.float32)
        info_ref[(1 - flip) * blocks + j, :META] = other[rows, cols]
    shape = (ROWS, LANES)
    above, above_ratio = block_scalars(info_ref[blocks - 1], slabs, shape)
    below, below_ratio = block_scalars(info_ref[blocks], slabs, shape)
    middle = coupling(below_ratio, above[1, 1], below[0, 0], slabs)
    tiles = lambda flip: [
        info_ref[flip * blocks + k + flip * (blocks - 1 - 2 * k)] for k in range(blocks)
    ]
    entries, q_own = half_chain(tiles(flip), slabs, flipped, middle)
    _, q_other = half_chain(tiles(1 - flip), slabs, jnp.logical_not(flipped), middle)
    for k, entry in enumerate(entries):
        for n, kind in enumerate(KINDS):
            table[k, n] = entry[kind]
    table[blocks, 0] = 1.0 / (1.0 - q_own * q_other)
    table[blocks, 1] = q_other
    coef = lambda kind, k: table[k, KINDS.index(kind)]

    def group(g, carry):
        rows = pl.ds(pl.multiple_of(g * ROWS, ROWS), ROWS)
        outside = pl.ds(pl.multiple_of(flip * lines + g * ROWS, ROWS), ROWS)
        inside = pl.ds(pl.multiple_of((1 - flip) * lines + g * ROWS, ROWS), ROWS)
        for t in range(share // LANES):
            cols = slice(t * LANES, (t + 1) * LANES)
            firsts = [fl_ref[block[k], outside, cols] for k in range(blocks)]
            lasts = [fl_ref[block[k], inside, cols] for k in range(blocks - 1)]
            before = forward(coef, firsts[:-1], lasts)
            across = table[blocks, 0] * (other[rows, cols] + table[blocks, 1] * mine[rows, cols])
            outer, inner = backward(coef, firsts, before, across)
            for k in range(blocks):
                uv_ref[block[k], flip, rows, cols] = outer[k]
                uv_ref[block[k], 1 - flip, rows, cols] = inner[k]
        return carry

    lax.fori_loop(0, lines // ROWS, group, 0)
    for m, out_ref in enumerate(out_refs):
        out_ref[...] = uv_ref[(where[0] & (blocks - 1)) ^ m]


def second_half(where, fl, mine, other, slabs):
    parts, rows, share = fl.shape
    lines = (rows - META_ROWS) // 2
    vmem = pl.BlockSpec(memory_space=pltpu.VMEM)
    return pl.pallas_call(
        functools.partial(second_kernel, slabs),
        in_specs=[pl.BlockSpec(memory_space=pltpu.SMEM), vmem, vmem, vmem],
        out_specs=[vmem] * (parts + 1),
        out_shape=[jax.ShapeDtypeStruct((2, lines, share), jnp.float32)] * parts
        + [jax.ShapeDtypeStruct((2 * parts, META_ROWS, LANES), jnp.float32)],
        scratch_shapes=[
            pltpu.VMEM((parts + 1, len(KINDS), ROWS, LANES), jnp.float32),
            pltpu.VMEM((parts, 2, lines, share), jnp.float32),
        ],
        compiler_params=pltpu.CompilerParams(vmem_limit_bytes=SMALL_VMEM),
        cost_estimate=pl.CostEstimate(flops=10 * fl.size, bytes_accessed=9 * fl.size, transcendentals=0),
        name="reduced_out",
    )(where, fl, mine, other)


def extras_kernel(where_am_i, info, source, flux, inverse, inlet, holders, wells_ref, rows_ref, leaving, found):
    blocks = info.shape[0]
    slabs, wells = wells_ref.shape
    d = where_am_i[0]
    dot = functools.partial(jnp.dot, precision=HIGHEST, preferred_element_type=jnp.float32)
    row_of = lambda j, n: info[j, 2 + n : 3 + n, :wells]
    down, rise = [None] * blocks, [None] * blocks
    value = inlet[...]
    for j in range(blocks):
        down[j] = value
        value = row_of(j, 0) * value + row_of(j, 1)
    for j in reversed(range(blocks)):
        rise[j] = value
        value = row_of(j, 0) * value + row_of(j, 2)
    held = holders[...] == lax.broadcasted_iota(jnp.int32, (wells, holders.shape[1]), 0)
    leaving[...] = dot(jnp.broadcast_to(value, (ROWS, wells)), held.astype(jnp.float32))[0:1]

    ends = [
        [row_of(j, n) + row_of(j, n + 1) * down[j] + row_of(j, n + 2) * rise[j] for j in range(blocks)]
        for n in (3, 6)
    ]
    scalars = [block_scalars(info[j], slabs, (1, wells)) for j in range(blocks)]
    zero = jnp.zeros((1, wells), jnp.float32)
    couple = [zero]
    for j in range(1, blocks):
        couple.append(
            coupling(scalars[j][1], scalars[j - 1][0][1, 1], scalars[j][0][0, 0], slabs)
        )
    couple.append(zero)
    coefs, _ = chain([corner for corner, _ in scalars], couple)
    coef = lambda kind, j: coefs[j][kind]
    above, below = backward(coef, ends[0], forward(coef, *ends), zero)
    for j in range(blocks):
        for n, value in enumerate((down[j], rise[j], above[j], below[j])):
            found[j, n : n + 1] = value
    mine = found[d]
    row = lax.broadcasted_iota(jnp.int32, (slabs, wells), 0)
    own = source[0] + source[1] * mine[0:1] + source[2] * mine[1:2]
    own = own + jnp.where(row == 0, mine[2:3], 0.0) + jnp.where(row == slabs - 1, mine[3:4], 0.0)
    wells_ref[...] = dot(inverse[...], own)
    for n in range(2):
        rows_ref[n] = dot(inverse[...], flux[n])


def extras(where, info, source, flux, inverse, inlet, holders):
    blocks = info.shape[0]
    _, slabs, span = flux.shape
    wells = source.shape[-1]
    vmem = pl.BlockSpec(memory_space=pltpu.VMEM)
    return pl.pallas_call(
        extras_kernel,
        in_specs=[pl.BlockSpec(memory_space=pltpu.SMEM)] + [vmem] * 6,
        out_specs=[vmem] * 3,
        out_shape=[
            jax.ShapeDtypeStruct((slabs, wells), jnp.float32),
            jax.ShapeDtypeStruct((2, slabs, span), jnp.float32),
            jax.ShapeDtypeStruct((1, holders.shape[1]), jnp.float32),
        ],
        scratch_shapes=[pltpu.VMEM((blocks, ROWS, wells), jnp.float32)],
        compiler_params=pltpu.CompilerParams(vmem_limit_bytes=SMALL_VMEM),
        cost_estimate=pl.CostEstimate(flops=10**7, bytes_accessed=10**6, transcendentals=0),
        name="extras",
    )(where, info, source, flux, inverse, inlet, holders)


def solve_kernel(where, right, inverse, place_row, place_column, solved_wells, outer, *refs):
    uv_refs, (out, factor, pick, uv) = refs[:-4], refs[-4:]
    for m, piece in enumerate(uv_refs):
        uv[(where[0] & (len(uv_refs) - 1)) ^ m] = piece[...]
    together, slabs, rows, span = right.shape
    wells = place_row.shape[1]
    step = pl.program_id(0)
    size = slabs * rows

    @pl.when(step == 0)
    def _():
        spread = (
            lax.broadcasted_iota(jnp.int32, (size, slabs), 0) // rows
            == lax.broadcasted_iota(jnp.int32, (size, slabs), 1)
        ).astype(jnp.float32).astype(jnp.bfloat16)
        spread_t = (
            lax.broadcasted_iota(jnp.int32, (slabs, size), 1) // rows
            == lax.broadcasted_iota(jnp.int32, (slabs, size), 0)
        ).astype(jnp.float32).astype(jnp.bfloat16)
        same = (
            lax.broadcasted_iota(jnp.int32, (size, size), 0) % rows
            == lax.broadcasted_iota(jnp.int32, (size, size), 1) % rows
        )
        for n, part in enumerate(split_bf16(inverse[...], 2)):
            tall = jnp.dot(spread, part, preferred_element_type=jnp.float32).astype(jnp.bfloat16)
            wide = jnp.dot(tall, spread_t, preferred_element_type=jnp.float32)
            wide = jnp.where(same, wide, 0.0).astype(jnp.bfloat16)
            if n == 0:
                factor[:, :size] = wide
                factor[:, size : 2 * size] = wide
            else:
                factor[:, 2 * size : 3 * size] = wide
        column = lax.broadcasted_iota(jnp.int32, (wells, span), 1)
        chosen = (column == place_column[...] % span).astype(jnp.float32).astype(jnp.bfloat16)
        pick[:wells] = chosen
        pick[wells:] = chosen

    tile = min(span, 256)
    for n in range(together):
        line = lax.broadcasted_iota(jnp.int32, (slabs, rows, wells), 1) + (step * together + n) * rows
        at_wells = jnp.where(line == (place_row[...] // span)[None], solved_wells[...][:, None, :], 0.0)
        at_wells = jnp.concatenate(split_bf16(at_wells.reshape(size, wells), 2), axis=1)
        factor[:, 3 * size :] = at_wells
        lines = slice(n * rows, (n + 1) * rows)
        above = jnp.concatenate([uv[d, 0, lines] for d in range(uv.shape[0])], axis=1)
        below = jnp.concatenate([uv[d, 1, lines] for d in range(uv.shape[0])], axis=1)
        for t in range(span // tile):
            cols = slice(t * tile, (t + 1) * tile)
            value = jnp.concatenate(
                [
                    right[n, 0:1, :, cols] + above[None, :, cols],
                    right[n, 1 : slabs - 1, :, cols],
                    right[n, slabs - 1 :, :, cols] + below[None, :, cols],
                ],
                axis=0,
            ).reshape(size, tile)
            upper, lower = split_bf16(value, 2)
            result = jnp.dot(
                factor[...],
                jnp.concatenate([upper, lower, upper, pick[:, cols]], axis=0),
                preferred_element_type=jnp.float32,
            )
            out[:, lines, cols] = result.reshape(slabs, rows, tile)

    for n, (when, line) in enumerate(((0, 0), (pl.num_programs(0) - 1, together * rows - 1))):

        @pl.when(step == when)
        def _():
            for z in range(slabs):
                out[z, line : line + 1, :] += outer[n, z : z + 1, :]


def solve(where, right, uv, inverse, place_row, place_column, solved_wells, outer):
    groups, slabs, _, span = right.shape
    wells = place_row.shape[1]
    together = 2
    lines = together * ROWS
    _, _, share = uv[0].shape
    whole = lambda *shape: pl.BlockSpec(shape, lambda g: (0,) * len(shape))
    size = slabs * ROWS
    return pl.pallas_call(
        solve_kernel,
        grid=(groups // together,),
        in_specs=[
            pl.BlockSpec(memory_space=pltpu.SMEM),
            pl.BlockSpec((together, slabs, ROWS, span), lambda g: (g, 0, 0, 0)),
            whole(slabs, slabs),
            whole(1, wells),
            whole(wells, 1),
            whole(slabs, wells),
            whole(*outer.shape),
        ]
        + [pl.BlockSpec((2, lines, share), lambda g: (0, g, 0))] * len(uv),
        out_specs=pl.BlockSpec((slabs, lines, span), lambda g: (0, g, 0)),
        out_shape=jax.ShapeDtypeStruct((slabs, groups * ROWS, span), jnp.float32),
        scratch_shapes=[
            pltpu.VMEM((size, 3 * size + 2 * wells), jnp.bfloat16),
            pltpu.VMEM((2 * wells, span), jnp.bfloat16),
            pltpu.VMEM((len(uv), 2, lines, share), jnp.float32),
        ],
        compiler_params=pltpu.CompilerParams(vmem_limit_bytes=SOLVE_VMEM),
        cost_estimate=pl.CostEstimate(
            flops=8 * size * right.size, bytes_accessed=8 * right.size, transcendentals=0
        ),
        name="depth_solve",
    )(where, right, inverse, place_row, place_column, solved_wells, outer, *uv)


def body(
    warmth_before,
    stratum_category,
    conductance_catalogue,
    pivot_matrix_reciprocal,
    linkage_factor,
    well_position_inside,
    well_holder_sequence,
    well_reach,
    entering_warmth,
    well_transfer_speed,
):
    slabs, lines, span = warmth_before.shape
    depth_index = lax.axis_index("depth")
    depth_count = lax.axis_size("depth")
    wells = well_position_inside.shape[0]
    owned = wells // depth_count
    table = conductance_catalogue

    parts = depth_count // 2

    place_row = well_position_inside.reshape(1, wells)
    place_column = well_position_inside.reshape(wells, 1)
    where = depth_index.reshape(1)
    holders = lax.dynamic_slice_in_dim(well_holder_sequence, depth_index * owned, owned)
    holders = holders.reshape(1, owned)
    first, last = edge_rows(warmth_before, stratum_category, table)
    first, last, place_row, place_column, where, holders = lax.optimization_barrier(
        (first, last, place_row, place_column, where, holders)
    )
    count = lax.axis_size("strip")
    up = [(i, i + 1) for i in range(count - 1)]
    down = [(j, i) for i, j in up]
    before = lax.ppermute(last, "strip", up)
    after = lax.ppermute(first, "strip", down)
    right, sums, cells = stencil(
        warmth_before, stratum_category, table, pivot_matrix_reciprocal, place_row
    )
    *pieces, flux, source = payload(
        linkage_factor,
        table,
        where,
        sums,
        (first, last, before, after),
        pivot_matrix_reciprocal,
        cells,
        well_transfer_speed.reshape(1, wells),
        well_reach.reshape(1, wells),
        parts,
    )

    def swapped(value, mask):
        return lax.ppermute(value, "depth", [(i, i ^ mask) for i in range(depth_count)])

    pieces = [swapped(pieces[m], m) for m in reversed(range(1, parts))][::-1] + [pieces[0]]
    pieces = [pieces[-1]] + pieces[:-1]
    mine, fl_all = first_half(where, pieces, slabs)
    other = swapped(mine, parts)
    *uv, info_all = second_half(where, fl_all, mine, other, slabs)
    uv_own = [swapped(uv[m], m) for m in reversed(range(1, parts))][::-1]
    uv_own = [uv[0]] + uv_own

    solved_wells, outer, leaving = extras(
        where,
        info_all,
        source,
        flux,
        pivot_matrix_reciprocal,
        entering_warmth.reshape(1, wells),
        holders,
    )
    solved = solve(
        where, right, uv_own, pivot_matrix_reciprocal, place_row, place_column, solved_wells, outer
    )
    return solved, leaving.reshape(owned)


def solution(mesh):
    in_specs = (
        P("depth", "strip", None),
        P("depth", "strip", None),
        P(),
        P("depth", None),
        P("depth"),
        P("strip"),
        P("strip"),
        P("strip"),
        P("strip"),
        P("strip"),
    )
    out_specs = (P("depth", "strip", None), P(("strip", "depth")))
    return jax.shard_map(body, mesh=mesh, in_specs=in_specs, out_specs=out_specs, check_vma=False)
```

```python
import functools

import jax
import jax.numpy as jnp
from jax import lax
from jax.experimental import pallas as pl
from jax.experimental.pallas import tpu as pltpu
from jax.sharding import PartitionSpec as P

backward_euler_advance = 0.2
storage_volume = 2.0
flux_scale = 0.5 * backward_euler_advance
LANES = 128
ROWS = 8
EDGE_VMEM = 56 * 1024 * 1024
VMEM_LIMIT = 40 * 1024 * 1024
SOLVE_VMEM = 24 * 1024 * 1024
SMALL_VMEM = 12 * 1024 * 1024
HIGHEST = lax.Precision.HIGHEST


def select_tree(category, entries):
    values = list(entries)
    bit = 1
    while len(values) > 1:
        odd = (category & bit) != 0
        values = [
            jnp.where(odd, values[k + 1], values[k]) if k + 1 < len(values) else values[k]
            for k in range(0, len(values), 2)
        ]
        bit *= 2
    return values[0]


def split_bf16(value, pieces):
    out = []
    for k in range(pieces):
        part = value.astype(jnp.bfloat16)
        out.append(part)
        if k + 1 < pieces:
            value = value - part.astype(jnp.float32)
    return out


def edge_kernel(table, w_first, cat_first, w_last, cat_last, first, last):
    slabs, rows, span = w_first.shape
    entries = [flux_scale * table[k] for k in range(table.shape[0])]
    sub = lax.broadcasted_iota(jnp.int32, (ROWS, span), 0)

    def gathered(ref, start, row):
        value = jnp.broadcast_to(ref[start, row : row + 1, :], (ROWS, span))
        for k in range(1, ROWS):
            value = jnp.where(sub == k, ref[start + k, row : row + 1, :], value)
        return value

    for w_ref, cat_ref, row, out in ((w_first, cat_first, 0, first), (w_last, cat_last, rows - 1, last)):
        for start in range(0, slabs, ROWS):
            out[0, start : start + ROWS] = gathered(w_ref, start, row)
            out[1, start : start + ROWS] = select_tree(gathered(cat_ref, start, row), entries)


def edge_rows(w, cat, table):
    slabs, lines, span = w.shape
    top = pl.BlockSpec((slabs, ROWS, span), lambda i: (0, 0, 0))
    end = pl.BlockSpec((slabs, ROWS, span), lambda i: (0, lines // ROWS - 1, 0))
    out = pl.BlockSpec((2, slabs, span), lambda i: (0, 0, 0))
    return pl.pallas_call(
        edge_kernel,
        grid=(1,),
        in_specs=[pl.BlockSpec(memory_space=pltpu.SMEM), top, top, end, end],
        out_specs=[out, out],
        out_shape=[jax.ShapeDtypeStruct((2, slabs, span), jnp.float32)] * 2,
        compiler_params=pltpu.CompilerParams(vmem_limit_bytes=EDGE_VMEM),
        cost_estimate=pl.CostEstimate(flops=10**6, bytes_accessed=w.size, transcendentals=0),
        name="edge_rows",
    )(table, w, cat, w, cat)


def stencil_kernel(
    table,
    ends,
    w_ref,
    cat_ref,
    place,
    right_ref,
    acc,
    cells_ref,
    ws,
    cs,
    fs,
    base,
    pieces,
    shift,
    pick,
    found,
):
    step = pl.program_id(0)
    planes, lines, span = w_ref.shape
    tiles = span // LANES
    groups = lines // ROWS
    wells = place.shape[1]
    entries = [flux_scale * table[k] for k in range(table.shape[0])]
    lane = lax.broadcasted_iota(jnp.int32, (lines, LANES), 1)
    own_line = lax.broadcasted_iota(jnp.int32, (lines, wells), 0) == place[...] // span
    top, end = ROWS, ROWS + lines
    dot = functools.partial(jnp.dot, preferred_element_type=jnp.float32)

    @pl.when(step == 0)
    def _():
        acc[...] = jnp.zeros_like(acc)
        base[...] = jnp.zeros_like(base)
        pieces[...] = jnp.zeros_like(pieces)
        source = lax.broadcasted_iota(jnp.int32, shift.shape, 0) % (2 * LANES)
        target = lax.broadcasted_iota(jnp.int32, shift.shape, 1)
        shift[...] = (source == target + 1).astype(jnp.float32).astype(jnp.bfloat16)
        column = lax.broadcasted_iota(jnp.int32, (span, wells), 0)
        pick[...] = (column == place[...] % span).astype(jnp.float32).astype(jnp.bfloat16)

    def keep_face(slot, t, face):
        for n, part in enumerate(split_bf16(face, 2)):
            pieces[slot, n, t] = part

    def faces(k, slot):
        left_w = left_c = jnp.zeros((lines, LANES), jnp.float32)
        for t in range(tiles):
            cols = slice(t * LANES, (t + 1) * LANES)
            w = w_ref[k, :, cols]
            c = select_tree(cat_ref[k, :, cols], entries)
            for ref, value in ((ws, w), (cs, c)):
                ref[t, top:end] = value
                ref[t, top - 1 : top] = value[0:1]
            roll_w, roll_c = pltpu.roll(w, 1, 1), pltpu.roll(c, 1, 1)
            west_w = jnp.where(lane == 0, left_w, roll_w)
            west_c = jnp.where(lane == 0, left_c, roll_c)
            left_w, left_c = roll_w, roll_c
            face = (c + west_c) * (w - west_w)
            keep_face(slot, t, face)
            if t == tiles - 1:
                keep_face(slot, tiles, pltpu.roll(-c * w, 1, 1))
            north = (c + cs[t, top - 1 : end - 1]) * (w - ws[t, top - 1 : end - 1])
            fs[t, top:end] = north
            fs[t, end : end + 1] = jnp.zeros((1, LANES), jnp.float32)
            base[slot, t] = w - face - north + fs[t, top + 1 : end + 1]

    def well_cells(k):
        upper, lower = split_bf16(w_ref[k], 2)
        kinds = cat_ref[k].astype(jnp.float32).astype(jnp.bfloat16)
        sums = dot(jnp.concatenate([upper, lower, kinds], axis=0), pick[...])
        for n, value in enumerate((sums[:lines] + sums[lines : 2 * lines], sums[2 * lines :])):
            mine = jnp.where(own_line, value, 0.0)
            found[k, n : n + 1, :] = jnp.sum(mine, axis=0, keepdims=True)

    def finish(k, slot, on):
        z = step * planes + k
        end_first = jnp.where(on, ends[0, z], 0.0)
        end_last = jnp.where(on, ends[ends.shape[0] - 1, z], 0.0)
        parts = [
            pieces[slot, n, d : d + tiles].reshape(tiles * lines, LANES)
            for n in range(2)
            for d in range(2)
        ]
        east = dot(jnp.concatenate(parts, axis=1), shift[...])
        for t in range(tiles):
            cols = slice(t * LANES, (t + 1) * LANES)
            value = base[slot, t] + east[t * lines : (t + 1) * lines]
            right_ref[:, k, :, cols] = value.reshape(groups, ROWS, LANES)
            acc[0, :, cols] += end_first * value
            acc[1, :, cols] += end_last * value

    def two_planes(m, carry):
        k = 2 * m
        finish(jnp.maximum(k - 1, 0), 1, m > 0)
        faces(k, 0)
        well_cells(k)
        finish(k, 0, True)
        faces(k + 1, 1)
        well_cells(k + 1)
        return carry

    lax.fori_loop(0, planes // 2, two_planes, 0)
    finish(planes - 1, 1, True)
    for k in range(planes):
        for n in range(2):
            cells_ref[n, k : k + 1, :] = found[k, n : n + 1, :]


def stencil(w, cat, table, inverse, place_row):
    slabs, lines, span = w.shape
    planes, groups = 8, lines // ROWS
    wells = place_row.shape[1]
    block = pl.BlockSpec((planes, lines, span), lambda i: (i, 0, 0))
    smem = pl.BlockSpec(memory_space=pltpu.SMEM)
    shifted = pltpu.VMEM((span // LANES, lines + 2 * ROWS, LANES), jnp.float32)
    return pl.pallas_call(
        stencil_kernel,
        grid=(slabs // planes,),
        in_specs=[smem, smem, block, block, pl.BlockSpec((1, wells), lambda i: (0, 0))],
        out_specs=[
            pl.BlockSpec((groups, planes, ROWS, span), lambda i: (0, i, 0, 0)),
            pl.BlockSpec((2, lines, span), lambda i: (0, 0, 0)),
            pl.BlockSpec((2, planes, wells), lambda i: (0, i, 0)),
        ],
        out_shape=[
            jax.ShapeDtypeStruct((groups, slabs, ROWS, span), jnp.float32),
            jax.ShapeDtypeStruct((2, lines, span), jnp.float32),
            jax.ShapeDtypeStruct((2, slabs, wells), jnp.float32),
        ],
        scratch_shapes=[
            shifted,
            shifted,
            shifted,
            pltpu.VMEM((2, span // LANES, lines, LANES), jnp.float32),
            pltpu.VMEM((2, 2, span // LANES + 1, lines, LANES), jnp.bfloat16),
            pltpu.VMEM((4 * LANES, LANES), jnp.bfloat16),
            pltpu.VMEM((span, wells), jnp.bfloat16),
            pltpu.VMEM((planes, 2, wells), jnp.float32),
        ],
        compiler_params=pltpu.CompilerParams(vmem_limit_bytes=VMEM_LIMIT),
        cost_estimate=pl.CostEstimate(flops=40 * w.size, bytes_accessed=12 * w.size, transcendentals=0),
        name="stencil",
    )(table, inverse, w, cat, place_row)


META = 11
META_ROWS = 16


def payload_kernel(
    ratio,
    table,
    where_am_i,
    sums,
    first,
    last,
    before,
    after,
    inverse,
    cells,
    speed,
    reach,
    *refs,
):
    out_refs, (flux_ref, source_ref, keep, force, paths, totals) = refs[:-6], refs[-6:]
    copies = len(out_refs)
    share = out_refs[0].shape[1]
    mine = where_am_i[0] & (copies - 1)
    _, lines, span = sums.shape
    _, slabs, wells = cells.shape
    dot = functools.partial(jnp.dot, precision=HIGHEST, preferred_element_type=jnp.float32)
    ends = jnp.concatenate([inverse[0:1], inverse[slabs - 1 : slabs]], axis=0)
    meta = 2 * lines

    entries = [table[k] for k in range(table.shape[0])]
    level = lax.broadcasted_iota(jnp.int32, (slabs, wells), 0) + where_am_i[0] * slabs
    rock = cells[0]
    cond = select_tree(cells[1].astype(jnp.int32), entries)
    rate = jnp.where(level < reach[...], speed[...] * cond / (1.0 + cond), 0.0)
    keep[...] = 1.0 - rate
    force[...] = rate * rock
    ones, zeros = jnp.ones((1, wells), jnp.float32), jnp.zeros((1, wells), jnp.float32)
    ways = []
    for n, order in enumerate((range(slabs), reversed(range(slabs)))):
        scale, shift = ones, zeros
        for z in order:
            paths[n, 0, z : z + 1] = scale
            paths[n, 1, z : z + 1] = shift
            scale, shift = keep[z : z + 1] * scale, keep[z : z + 1] * shift + force[z : z + 1]
        ways.append((scale, shift))
    source_ref[0] = -storage_volume * rate * (2.0 * rock - paths[0, 1] - paths[1, 1])
    source_ref[1] = storage_volume * rate * paths[0, 0]
    source_ref[2] = storage_volume * rate * paths[1, 0]
    own_sums = [dot(ends, source_ref[n]) for n in range(3)]

    rows = [ways[0][0], ways[0][1], ways[1][1]]
    rows += [own_sums[n][q : q + 1] for q in range(2) for n in range(3)]
    extras = []
    for own, other, line, n in ((first, before, 0, 0), (last, after, lines - 1, 1)):
        flux = (own[1] + other[1]) * (other[0] - own[0])
        flux_ref[n] = flux
        extras.append((line, dot(ends, flux)))
    totals[...] = sums[...]
    for line, extra in extras:
        for q in range(2):
            totals[q, line : line + 1, :] += extra[q : q + 1]
    for m, out_ref in enumerate(out_refs):
        cols = pl.ds(pl.multiple_of((mine ^ m) * share, share), share)
        for q in range(2):
            out_ref[q * lines : (q + 1) * lines] = totals[q, :, cols]
        out_ref[meta : meta + META_ROWS] = jnp.zeros((META_ROWS, share), jnp.float32)
        out_ref[meta : meta + 2, :slabs] = ends
        out_ref[meta : meta + 1, slabs : slabs + 1] = jnp.full((1, 1), ratio[0])
        for n, row in enumerate(rows):
            out_ref[meta + 2 + n : meta + 3 + n, :wells] = row


def payload(ratio, table, where, sums, edges, inverse, cells, speed, reach, copies):
    _, lines, span = sums.shape
    _, slabs, wells = cells.shape
    share = span // copies
    smem = pl.BlockSpec(memory_space=pltpu.SMEM)
    vmem = pl.BlockSpec(memory_space=pltpu.VMEM)
    column = pltpu.VMEM((slabs, wells), jnp.float32)
    return pl.pallas_call(
        payload_kernel,
        in_specs=[smem] * 3 + [vmem] * 9,
        out_specs=[vmem] * (copies + 2),
        out_shape=[jax.ShapeDtypeStruct((2 * lines + META_ROWS, share), jnp.float32)] * copies
        + [
            jax.ShapeDtypeStruct((2, slabs, span), jnp.float32),
            jax.ShapeDtypeStruct((3, slabs, wells), jnp.float32),
        ],
        scratch_shapes=[
            column,
            column,
            pltpu.VMEM((2, 2, slabs, wells), jnp.float32),
            pltpu.VMEM((2, lines, span), jnp.float32),
        ],
        compiler_params=pltpu.CompilerParams(vmem_limit_bytes=SMALL_VMEM),
        cost_estimate=pl.CostEstimate(flops=10**6, bytes_accessed=10**6, transcendentals=0),
        name="payload",
    )(ratio, table, where, sums, *edges, inverse, cells, speed, reach)


CORNERS = ((0, 0), (0, 1), (1, 0), (1, 1))


def block_scalars(tile, slabs, shape, flipped=None):
    at = lambda row, lane: jnp.broadcast_to(tile[row : row + 1, lane : lane + 1], shape)
    corner = {(r, c): at(r, c * (slabs - 1)) for r, c in CORNERS}
    if flipped is not None:
        corner = {(r, c): jnp.where(flipped, corner[1 - r, 1 - c], corner[r, c]) for r, c in CORNERS}
    return corner, at(0, slabs)


def coupling(ratio, one, other, slabs):
    return ratio * (slabs / (slabs + 1.0)) / jnp.sqrt(one * other)


def chain(corners, couple, q=None):
    out = []
    q = jnp.zeros_like(couple[0])
    for k, corner in enumerate(corners):
        vf, vl = couple[k] * corner[0, 0], couple[k] * corner[1, 0]
        wf, wl = couple[k + 1] * corner[0, 1], couple[k + 1] * corner[1, 1]
        inverse = 1.0 / (1.0 - vf * q)
        out.append(
            dict(
                p_first=vl * q * inverse,
                p_before=vl * inverse,
                a_first=inverse,
                a_before=vf * inverse,
                a_after=wf * inverse,
                couple=couple[k],
                couple_after=couple[k + 1],
                q=q,
            )
        )
        q = wl + vl * q * wf * inverse
    return out, q


KINDS = ("p_first", "p_before", "a_first", "a_before", "a_after", "couple", "couple_after", "q")


def forward(coef, firsts, lasts):
    before = [jnp.zeros_like(firsts[0])]
    for j in range(len(firsts)):
        before.append(
            lasts[j] + coef("p_first", j) * firsts[j] + coef("p_before", j) * before[j]
        )
    return before


def backward(coef, firsts, before, after):
    blocks = len(firsts)
    above, below = [None] * blocks, [None] * blocks
    for j in reversed(range(blocks)):
        below[j] = coef("couple_after", j) * after
        here = (
            coef("a_first", j) * firsts[j]
            + coef("a_before", j) * before[j]
            + coef("a_after", j) * after
        )
        above[j] = coef("couple", j) * (before[j] + coef("q", j) * here)
        after = here
    return above, below


def half_chain(tiles, slabs, flipped, middle):
    shape = (ROWS, LANES)
    scalars = [block_scalars(tile, slabs, shape, flipped) for tile in tiles]
    couple = [jnp.zeros(shape, jnp.float32)]
    for k in range(1, len(tiles)):
        ratio = jnp.where(flipped, scalars[k - 1][1], scalars[k][1])
        couple.append(coupling(ratio, scalars[k - 1][0][1, 1], scalars[k][0][0, 0], slabs))
    couple.append(middle)
    return chain([corner for corner, _ in scalars], couple)


def meta_place(j, lines, share):
    side = share // LANES
    row = lines + j // side * META
    return slice(row, row + META), slice(j % side * LANES, (j % side + 1) * LANES)


def first_kernel(slabs, where, *refs):
    piece_refs, (out_ref, fl_ref, table) = refs[:-3], refs[-3:]
    blocks, rows, share = fl_ref.shape
    lines = (rows - META_ROWS) // 2
    mine = where[0] & (blocks - 1)
    for m, piece in enumerate(piece_refs):
        fl_ref[mine ^ m] = piece[...]
    flip = where[0] // blocks
    flipped = flip == 1
    block = [k + flip * (blocks - 1 - 2 * k) for k in range(blocks)]
    entries, _ = half_chain(
        [fl_ref[block[k], 2 * lines : 2 * lines + ROWS, :LANES] for k in range(blocks)],
        slabs,
        flipped,
        jnp.zeros((ROWS, LANES), jnp.float32),
    )
    for k, entry in enumerate(entries):
        for n, kind in enumerate(KINDS[:2]):
            table[k, n] = entry[kind]
    coef = lambda kind, k: table[k, KINDS.index(kind)]

    def group(g, carry):
        rows = pl.ds(pl.multiple_of(g * ROWS, ROWS), ROWS)
        outer = pl.ds(pl.multiple_of(flip * lines + g * ROWS, ROWS), ROWS)
        inner = pl.ds(pl.multiple_of((1 - flip) * lines + g * ROWS, ROWS), ROWS)
        for t in range(share // LANES):
            cols = slice(t * LANES, (t + 1) * LANES)
            before = forward(
                coef,
                [fl_ref[block[k], outer, cols] for k in range(blocks)],
                [fl_ref[block[k], inner, cols] for k in range(blocks)],
            )
            out_ref[rows, cols] = before[blocks]
        return carry

    lax.fori_loop(0, lines // ROWS, group, 0)
    out_ref[lines:, :] = jnp.zeros((out_ref.shape[0] - lines, share), jnp.float32)
    for j in range(blocks):
        rows, cols = meta_place(j, lines, share)
        out_ref[rows, cols] = fl_ref[j, 2 * lines : 2 * lines + META, :LANES]


def first_half(where, pieces, slabs):
    parts = len(pieces)
    rows, share = pieces[0].shape
    lines = (rows - META_ROWS) // 2
    vmem = pl.BlockSpec(memory_space=pltpu.VMEM)
    crossing = -(-meta_place(parts - 1, lines, share)[0].stop // ROWS) * ROWS
    return pl.pallas_call(
        functools.partial(first_kernel, slabs),
        in_specs=[pl.BlockSpec(memory_space=pltpu.SMEM)] + [vmem] * parts,
        out_specs=[vmem, vmem],
        out_shape=[
            jax.ShapeDtypeStruct((crossing, share), jnp.float32),
            jax.ShapeDtypeStruct((parts, rows, share), jnp.float32),
        ],
        scratch_shapes=[pltpu.VMEM((parts, 2, ROWS, LANES), jnp.float32)],
        compiler_params=pltpu.CompilerParams(vmem_limit_bytes=SMALL_VMEM),
        cost_estimate=pl.CostEstimate(flops=10**6, bytes_accessed=10**6, transcendentals=0),
        name="reduced_in",
    )(where, *pieces)


def second_kernel(slabs, where, fl_ref, mine, other, *refs):
    out_refs, (info_ref, table, uv_ref) = refs[:-3], refs[-3:]
    blocks, _, lines, share = uv_ref.shape
    flip = where[0] // blocks
    flipped = flip == 1
    block = [k + flip * (blocks - 1 - 2 * k) for k in range(blocks)]
    for j in range(blocks):
        rows, cols = meta_place(j, lines, share)
        info_ref[flip * blocks + j] = fl_ref[j, 2 * lines :, :LANES]
        info_ref[(1 - flip) * blocks + j] = jnp.zeros((META_ROWS, LANES), jnp.float32)
        info_ref[(1 - flip) * blocks + j, :META] = other[rows, cols]
    shape = (ROWS, LANES)
    above, above_ratio = block_scalars(info_ref[blocks - 1], slabs, shape)
    below, below_ratio = block_scalars(info_ref[blocks], slabs, shape)
    middle = coupling(below_ratio, above[1, 1], below[0, 0], slabs)
    tiles = lambda flip: [
        info_ref[flip * blocks + k + flip * (blocks - 1 - 2 * k)] for k in range(blocks)
    ]
    entries, q_own = half_chain(tiles(flip), slabs, flipped, middle)
    _, q_other = half_chain(tiles(1 - flip), slabs, jnp.logical_not(flipped), middle)
    for k, entry in enumerate(entries):
        for n, kind in enumerate(KINDS):
            table[k, n] = entry[kind]
    table[blocks, 0] = 1.0 / (1.0 - q_own * q_other)
    table[blocks, 1] = q_other
    coef = lambda kind, k: table[k, KINDS.index(kind)]

    def group(g, carry):
        rows = pl.ds(pl.multiple_of(g * ROWS, ROWS), ROWS)
        outside = pl.ds(pl.multiple_of(flip * lines + g * ROWS, ROWS), ROWS)
        inside = pl.ds(pl.multiple_of((1 - flip) * lines + g * ROWS, ROWS), ROWS)
        for t in range(share // LANES):
            cols = slice(t * LANES, (t + 1) * LANES)
            firsts = [fl_ref[block[k], outside, cols] for k in range(blocks)]
            lasts = [fl_ref[block[k], inside, cols] for k in range(blocks - 1)]
            before = forward(coef, firsts[:-1], lasts)
            across = table[blocks, 0] * (other[rows, cols] + table[blocks, 1] * mine[rows, cols])
            outer, inner = backward(coef, firsts, before, across)
            for k in range(blocks):
                uv_ref[block[k], flip, rows, cols] = outer[k]
                uv_ref[block[k], 1 - flip, rows, cols] = inner[k]
        return carry

    lax.fori_loop(0, lines // ROWS, group, 0)
    for m, out_ref in enumerate(out_refs):
        out_ref[...] = uv_ref[(where[0] & (blocks - 1)) ^ m]


def second_half(where, fl, mine, other, slabs):
    parts, rows, share = fl.shape
    lines = (rows - META_ROWS) // 2
    vmem = pl.BlockSpec(memory_space=pltpu.VMEM)
    return pl.pallas_call(
        functools.partial(second_kernel, slabs),
        in_specs=[pl.BlockSpec(memory_space=pltpu.SMEM), vmem, vmem, vmem],
        out_specs=[vmem] * (parts + 1),
        out_shape=[jax.ShapeDtypeStruct((2, lines, share), jnp.float32)] * parts
        + [jax.ShapeDtypeStruct((2 * parts, META_ROWS, LANES), jnp.float32)],
        scratch_shapes=[
            pltpu.VMEM((parts + 1, len(KINDS), ROWS, LANES), jnp.float32),
            pltpu.VMEM((parts, 2, lines, share), jnp.float32),
        ],
        compiler_params=pltpu.CompilerParams(vmem_limit_bytes=SMALL_VMEM),
        cost_estimate=pl.CostEstimate(flops=10 * fl.size, bytes_accessed=9 * fl.size, transcendentals=0),
        name="reduced_out",
    )(where, fl, mine, other)


def extras_kernel(where_am_i, info, source, flux, inverse, inlet, holders, wells_ref, rows_ref, leaving, found):
    blocks = info.shape[0]
    slabs, wells = wells_ref.shape
    d = where_am_i[0]
    dot = functools.partial(jnp.dot, precision=HIGHEST, preferred_element_type=jnp.float32)
    row_of = lambda j, n: info[j, 2 + n : 3 + n, :wells]
    down, rise = [None] * blocks, [None] * blocks
    value = inlet[...]
    for j in range(blocks):
        down[j] = value
        value = row_of(j, 0) * value + row_of(j, 1)
    for j in reversed(range(blocks)):
        rise[j] = value
        value = row_of(j, 0) * value + row_of(j, 2)
    held = holders[...] == lax.broadcasted_iota(jnp.int32, (wells, wells), 0)
    ordered = dot(jnp.broadcast_to(value, (ROWS, wells)), held.astype(jnp.float32))
    owned = leaving.shape[1]
    source_lane = lax.broadcasted_iota(jnp.int32, (wells, owned), 0)
    mine = source_lane == d * owned + lax.broadcasted_iota(jnp.int32, (wells, owned), 1)
    leaving[...] = dot(ordered, mine.astype(jnp.float32))[0:1]

    ends = [
        [row_of(j, n) + row_of(j, n + 1) * down[j] + row_of(j, n + 2) * rise[j] for j in range(blocks)]
        for n in (3, 6)
    ]
    scalars = [block_scalars(info[j], slabs, (1, wells)) for j in range(blocks)]
    zero = jnp.zeros((1, wells), jnp.float32)
    couple = [zero]
    for j in range(1, blocks):
        couple.append(
            coupling(scalars[j][1], scalars[j - 1][0][1, 1], scalars[j][0][0, 0], slabs)
        )
    couple.append(zero)
    coefs, _ = chain([corner for corner, _ in scalars], couple)
    coef = lambda kind, j: coefs[j][kind]
    above, below = backward(coef, ends[0], forward(coef, *ends), zero)
    for j in range(blocks):
        for n, value in enumerate((down[j], rise[j], above[j], below[j])):
            found[j, n : n + 1] = value
    mine = found[d]
    row = lax.broadcasted_iota(jnp.int32, (slabs, wells), 0)
    own = source[0] + source[1] * mine[0:1] + source[2] * mine[1:2]
    own = own + jnp.where(row == 0, mine[2:3], 0.0) + jnp.where(row == slabs - 1, mine[3:4], 0.0)
    wells_ref[...] = dot(inverse[...], own)
    for n in range(2):
        rows_ref[n] = dot(inverse[...], flux[n])


def extras(where, info, source, flux, inverse, inlet, holders):
    blocks = info.shape[0]
    _, slabs, span = flux.shape
    wells = source.shape[-1]
    vmem = pl.BlockSpec(memory_space=pltpu.VMEM)
    return pl.pallas_call(
        extras_kernel,
        in_specs=[pl.BlockSpec(memory_space=pltpu.SMEM)] + [vmem] * 6,
        out_specs=[vmem] * 3,
        out_shape=[
            jax.ShapeDtypeStruct((slabs, wells), jnp.float32),
            jax.ShapeDtypeStruct((2, slabs, span), jnp.float32),
            jax.ShapeDtypeStruct((1, wells // blocks), jnp.float32),
        ],
        scratch_shapes=[pltpu.VMEM((blocks, ROWS, wells), jnp.float32)],
        compiler_params=pltpu.CompilerParams(vmem_limit_bytes=SMALL_VMEM),
        cost_estimate=pl.CostEstimate(flops=10**7, bytes_accessed=10**6, transcendentals=0),
        name="extras",
    )(where, info, source, flux, inverse, inlet, holders)


def solve_kernel(where, right, inverse, place_row, solved_wells, outer, *refs):
    uv_refs, (out, factor, pick, uv) = refs[:-4], refs[-4:]
    for m, piece in enumerate(uv_refs):
        uv[(where[0] & (len(uv_refs) - 1)) ^ m] = piece[...]
    together, slabs, rows, span = right.shape
    wells = place_row.shape[1]
    step = pl.program_id(0)
    size = slabs * rows

    @pl.when(step == 0)
    def _():
        spread = (
            lax.broadcasted_iota(jnp.int32, (size, slabs), 0) // rows
            == lax.broadcasted_iota(jnp.int32, (size, slabs), 1)
        ).astype(jnp.float32).astype(jnp.bfloat16)
        spread_t = (
            lax.broadcasted_iota(jnp.int32, (slabs, size), 1) // rows
            == lax.broadcasted_iota(jnp.int32, (slabs, size), 0)
        ).astype(jnp.float32).astype(jnp.bfloat16)
        same = (
            lax.broadcasted_iota(jnp.int32, (size, size), 0) % rows
            == lax.broadcasted_iota(jnp.int32, (size, size), 1) % rows
        )
        for n, part in enumerate(split_bf16(inverse[...], 2)):
            tall = jnp.dot(spread, part, preferred_element_type=jnp.float32).astype(jnp.bfloat16)
            wide = jnp.dot(tall, spread_t, preferred_element_type=jnp.float32)
            wide = jnp.where(same, wide, 0.0).astype(jnp.bfloat16)
            if n == 0:
                factor[:, :size] = wide
                factor[:, size : 2 * size] = wide
            else:
                factor[:, 2 * size : 3 * size] = wide
        across = lax.broadcasted_iota(jnp.int32, (wells, wells), 1)
        diagonal = lax.broadcasted_iota(jnp.int32, (wells, wells), 0) == across
        place = jnp.where(diagonal, (place_row[...] % span).astype(jnp.float32), 0.0)
        place = jnp.sum(place, axis=1, keepdims=True)
        column = lax.broadcasted_iota(jnp.int32, (wells, span), 1).astype(jnp.float32)
        chosen = (column == place).astype(jnp.float32).astype(jnp.bfloat16)
        pick[:wells] = chosen
        pick[wells:] = chosen

    tile = min(span, 256)
    for n in range(together):
        line = lax.broadcasted_iota(jnp.int32, (slabs, rows, wells), 1) + (step * together + n) * rows
        at_wells = jnp.where(line == (place_row[...] // span)[None], solved_wells[...][:, None, :], 0.0)
        at_wells = jnp.concatenate(split_bf16(at_wells.reshape(size, wells), 2), axis=1)
        factor[:, 3 * size :] = at_wells
        lines = slice(n * rows, (n + 1) * rows)
        above = jnp.concatenate([uv[d, 0, lines] for d in range(uv.shape[0])], axis=1)
        below = jnp.concatenate([uv[d, 1, lines] for d in range(uv.shape[0])], axis=1)
        for t in range(span // tile):
            cols = slice(t * tile, (t + 1) * tile)
            value = jnp.concatenate(
                [
                    right[n, 0:1, :, cols] + above[None, :, cols],
                    right[n, 1 : slabs - 1, :, cols],
                    right[n, slabs - 1 :, :, cols] + below[None, :, cols],
                ],
                axis=0,
            ).reshape(size, tile)
            upper, lower = split_bf16(value, 2)
            result = jnp.dot(
                factor[...],
                jnp.concatenate([upper, lower, upper, pick[:, cols]], axis=0),
                preferred_element_type=jnp.float32,
            )
            out[:, lines, cols] = result.reshape(slabs, rows, tile)

    for n, (when, line) in enumerate(((0, 0), (pl.num_programs(0) - 1, together * rows - 1))):

        @pl.when(step == when)
        def _():
            for z in range(slabs):
                out[z, line : line + 1, :] += outer[n, z : z + 1, :]


def solve(where, right, uv, inverse, place_row, solved_wells, outer):
    groups, slabs, _, span = right.shape
    wells = place_row.shape[1]
    together = 2
    lines = together * ROWS
    _, _, share = uv[0].shape
    whole = lambda *shape: pl.BlockSpec(shape, lambda g: (0,) * len(shape))
    size = slabs * ROWS
    return pl.pallas_call(
        solve_kernel,
        grid=(groups // together,),
        in_specs=[
            pl.BlockSpec(memory_space=pltpu.SMEM),
            pl.BlockSpec((together, slabs, ROWS, span), lambda g: (g, 0, 0, 0)),
            whole(slabs, slabs),
            whole(1, wells),
            whole(slabs, wells),
            whole(*outer.shape),
        ]
        + [pl.BlockSpec((2, lines, share), lambda g: (0, g, 0))] * len(uv),
        out_specs=pl.BlockSpec((slabs, lines, span), lambda g: (0, g, 0)),
        out_shape=jax.ShapeDtypeStruct((slabs, groups * ROWS, span), jnp.float32),
        scratch_shapes=[
            pltpu.VMEM((size, 3 * size + 2 * wells), jnp.bfloat16),
            pltpu.VMEM((2 * wells, span), jnp.bfloat16),
            pltpu.VMEM((len(uv), 2, lines, share), jnp.float32),
        ],
        compiler_params=pltpu.CompilerParams(vmem_limit_bytes=SOLVE_VMEM),
        cost_estimate=pl.CostEstimate(
            flops=8 * size * right.size, bytes_accessed=8 * right.size, transcendentals=0
        ),
        name="depth_solve",
    )(where, right, inverse, place_row, solved_wells, outer, *uv)


def body(
    warmth_before,
    stratum_category,
    conductance_catalogue,
    pivot_matrix_reciprocal,
    linkage_factor,
    well_position_inside,
    well_holder_sequence,
    well_reach,
    entering_warmth,
    well_transfer_speed,
):
    slabs, lines, span = warmth_before.shape
    depth_index = lax.axis_index("depth")
    depth_count = lax.axis_size("depth")
    wells = well_position_inside.shape[0]
    owned = wells // depth_count
    table = conductance_catalogue

    parts = depth_count // 2

    place_row = well_position_inside.reshape(1, wells)
    where = depth_index.reshape(1)
    first, last = edge_rows(warmth_before, stratum_category, table)
    first, last, place_row, where = lax.optimization_barrier((first, last, place_row, where))
    count = lax.axis_size("strip")
    up = [(i, i + 1) for i in range(count - 1)]
    down = [(j, i) for i, j in up]
    before = lax.ppermute(last, "strip", up)
    after = lax.ppermute(first, "strip", down)
    right, sums, cells = stencil(
        warmth_before, stratum_category, table, pivot_matrix_reciprocal, place_row
    )
    *pieces, flux, source = payload(
        linkage_factor,
        table,
        where,
        sums,
        (first, last, before, after),
        pivot_matrix_reciprocal,
        cells,
        well_transfer_speed.reshape(1, wells),
        well_reach.reshape(1, wells),
        parts,
    )

    def swapped(value, mask):
        return lax.ppermute(value, "depth", [(i, i ^ mask) for i in range(depth_count)])

    pieces = [swapped(pieces[m], m) for m in reversed(range(1, parts))][::-1] + [pieces[0]]
    pieces = [pieces[-1]] + pieces[:-1]
    mine, fl_all = first_half(where, pieces, slabs)
    other = swapped(mine, parts)
    *uv, info_all = second_half(where, fl_all, mine, other, slabs)
    uv_own = [swapped(uv[m], m) for m in reversed(range(1, parts))][::-1]
    uv_own = [uv[0]] + uv_own

    solved_wells, outer, leaving = extras(
        where,
        info_all,
        source,
        flux,
        pivot_matrix_reciprocal,
        entering_warmth.reshape(1, wells),
        well_holder_sequence.reshape(1, wells),
    )
    solved = solve(where, right, uv_own, pivot_matrix_reciprocal, place_row, solved_wells, outer)
    return solved, leaving.reshape(owned)


def solution(mesh):
    in_specs = (
        P("depth", "strip", None),
        P("depth", "strip", None),
        P(),
        P("depth", None),
        P("depth"),
        P("strip"),
        P("strip"),
        P("strip"),
        P("strip"),
        P("strip"),
    )
    out_specs = (P("depth", "strip", None), P(("strip", "depth")))
    return jax.shard_map(body, mesh=mesh, in_specs=in_specs, out_specs=out_specs, check_vma=False)
```

```python
import functools

import jax
import jax.numpy as jnp
from jax import lax
from jax.experimental import pallas as pl
from jax.experimental.pallas import tpu as pltpu
from jax.sharding import PartitionSpec as P

backward_euler_advance = 0.2
storage_volume = 2.0
flux_scale = 0.5 * backward_euler_advance
LANES = 128
ROWS = 8
EDGE_VMEM = 56 * 1024 * 1024
VMEM_LIMIT = 40 * 1024 * 1024
SOLVE_VMEM = 24 * 1024 * 1024
SMALL_VMEM = 12 * 1024 * 1024
HIGHEST = lax.Precision.HIGHEST


def select_tree(category, entries):
    values = list(entries)
    bit = 1
    while len(values) > 1:
        odd = (category & bit) != 0
        values = [
            jnp.where(odd, values[k + 1], values[k]) if k + 1 < len(values) else values[k]
            for k in range(0, len(values), 2)
        ]
        bit *= 2
    return values[0]


def crossed(mask):
    return mask & ~3 | (mask & 1) << 1 | (mask & 2) >> 1


def partner(where, mask, blocks):
    odd = where[1] & 1 if blocks >= 4 else 0
    return (where[0] & (blocks - 1)) ^ (mask + odd * (crossed(mask) - mask))


def split_bf16(value, pieces):
    out = []
    for k in range(pieces):
        part = value.astype(jnp.bfloat16)
        out.append(part)
        if k + 1 < pieces:
            value = value - part.astype(jnp.float32)
    return out


def edge_kernel(table, w_first, cat_first, w_last, cat_last, first, last):
    slabs, rows, span = w_first.shape
    entries = [flux_scale * table[k] for k in range(table.shape[0])]
    sub = lax.broadcasted_iota(jnp.int32, (ROWS, span), 0)

    def gathered(ref, start, row):
        value = jnp.broadcast_to(ref[start, row : row + 1, :], (ROWS, span))
        for k in range(1, ROWS):
            value = jnp.where(sub == k, ref[start + k, row : row + 1, :], value)
        return value

    for w_ref, cat_ref, row, out in ((w_first, cat_first, 0, first), (w_last, cat_last, rows - 1, last)):
        for start in range(0, slabs, ROWS):
            out[0, start : start + ROWS] = gathered(w_ref, start, row)
            out[1, start : start + ROWS] = select_tree(gathered(cat_ref, start, row), entries)


def edge_rows(w, cat, table):
    slabs, lines, span = w.shape
    top = pl.BlockSpec((slabs, ROWS, span), lambda i: (0, 0, 0))
    end = pl.BlockSpec((slabs, ROWS, span), lambda i: (0, lines // ROWS - 1, 0))
    out = pl.BlockSpec((2, slabs, span), lambda i: (0, 0, 0))
    return pl.pallas_call(
        edge_kernel,
        grid=(1,),
        in_specs=[pl.BlockSpec(memory_space=pltpu.SMEM), top, top, end, end],
        out_specs=[out, out],
        out_shape=[jax.ShapeDtypeStruct((2, slabs, span), jnp.float32)] * 2,
        compiler_params=pltpu.CompilerParams(vmem_limit_bytes=EDGE_VMEM),
        cost_estimate=pl.CostEstimate(flops=10**6, bytes_accessed=w.size, transcendentals=0),
        name="edge_rows",
    )(table, w, cat, w, cat)


def stencil_kernel(
    table,
    ends,
    w_ref,
    cat_ref,
    place,
    right_ref,
    acc,
    cells_ref,
    ws,
    cs,
    fs,
    base,
    pieces,
    shift,
    pick,
    found,
):
    step = pl.program_id(0)
    planes, lines, span = w_ref.shape
    tiles = span // LANES
    groups = lines // ROWS
    wells = place.shape[1]
    entries = [flux_scale * table[k] for k in range(table.shape[0])]
    lane = lax.broadcasted_iota(jnp.int32, (lines, LANES), 1)
    own_line = lax.broadcasted_iota(jnp.int32, (lines, wells), 0) == place[...] // span
    top, end = ROWS, ROWS + lines
    dot = functools.partial(jnp.dot, preferred_element_type=jnp.float32)

    @pl.when(step == 0)
    def _():
        acc[...] = jnp.zeros_like(acc)
        base[...] = jnp.zeros_like(base)
        pieces[...] = jnp.zeros_like(pieces)
        source = lax.broadcasted_iota(jnp.int32, shift.shape, 0) % (2 * LANES)
        target = lax.broadcasted_iota(jnp.int32, shift.shape, 1)
        shift[...] = (source == target + 1).astype(jnp.float32).astype(jnp.bfloat16)
        column = lax.broadcasted_iota(jnp.int32, (span, wells), 0)
        pick[...] = (column == place[...] % span).astype(jnp.float32).astype(jnp.bfloat16)

    def keep_face(slot, t, face):
        for n, part in enumerate(split_bf16(face, 2)):
            pieces[slot, n, t] = part

    def faces(k, slot):
        left_w = left_c = jnp.zeros((lines, LANES), jnp.float32)
        for t in range(tiles):
            cols = slice(t * LANES, (t + 1) * LANES)
            w = w_ref[k, :, cols]
            c = select_tree(cat_ref[k, :, cols], entries)
            for ref, value in ((ws, w), (cs, c)):
                ref[t, top:end] = value
                ref[t, top - 1 : top] = value[0:1]
            roll_w, roll_c = pltpu.roll(w, 1, 1), pltpu.roll(c, 1, 1)
            west_w = jnp.where(lane == 0, left_w, roll_w)
            west_c = jnp.where(lane == 0, left_c, roll_c)
            left_w, left_c = roll_w, roll_c
            face = (c + west_c) * (w - west_w)
            keep_face(slot, t, face)
            if t == tiles - 1:
                keep_face(slot, tiles, pltpu.roll(-c * w, 1, 1))
            north = (c + cs[t, top - 1 : end - 1]) * (w - ws[t, top - 1 : end - 1])
            fs[t, top:end] = north
            fs[t, end : end + 1] = jnp.zeros((1, LANES), jnp.float32)
            base[slot, t] = w - face - north + fs[t, top + 1 : end + 1]

    def well_cells(k):
        upper, lower = split_bf16(w_ref[k], 2)
        kinds = cat_ref[k].astype(jnp.float32).astype(jnp.bfloat16)
        sums = dot(jnp.concatenate([upper, lower, kinds], axis=0), pick[...])
        for n, value in enumerate((sums[:lines] + sums[lines : 2 * lines], sums[2 * lines :])):
            mine = jnp.where(own_line, value, 0.0)
            found[k, n : n + 1, :] = jnp.sum(mine, axis=0, keepdims=True)

    def finish(k, slot, on):
        z = step * planes + k
        end_first = jnp.where(on, ends[0, z], 0.0)
        end_last = jnp.where(on, ends[ends.shape[0] - 1, z], 0.0)
        parts = [
            pieces[slot, n, d : d + tiles].reshape(tiles * lines, LANES)
            for n in range(2)
            for d in range(2)
        ]
        east = dot(jnp.concatenate(parts, axis=1), shift[...])
        for t in range(tiles):
            cols = slice(t * LANES, (t + 1) * LANES)
            value = base[slot, t] + east[t * lines : (t + 1) * lines]
            right_ref[:, k, :, cols] = value.reshape(groups, ROWS, LANES)
            acc[0, :, cols] += end_first * value
            acc[1, :, cols] += end_last * value

    def two_planes(m, carry):
        k = 2 * m
        finish(jnp.maximum(k - 1, 0), 1, m > 0)
        faces(k, 0)
        well_cells(k)
        finish(k, 0, True)
        faces(k + 1, 1)
        well_cells(k + 1)
        return carry

    lax.fori_loop(0, planes // 2, two_planes, 0)
    finish(planes - 1, 1, True)
    for k in range(planes):
        for n in range(2):
            cells_ref[n, k : k + 1, :] = found[k, n : n + 1, :]


def stencil(w, cat, table, inverse, place_row):
    slabs, lines, span = w.shape
    planes, groups = 8, lines // ROWS
    wells = place_row.shape[1]
    block = pl.BlockSpec((planes, lines, span), lambda i: (i, 0, 0))
    smem = pl.BlockSpec(memory_space=pltpu.SMEM)
    shifted = pltpu.VMEM((span // LANES, lines + 2 * ROWS, LANES), jnp.float32)
    return pl.pallas_call(
        stencil_kernel,
        grid=(slabs // planes,),
        in_specs=[smem, smem, block, block, pl.BlockSpec((1, wells), lambda i: (0, 0))],
        out_specs=[
            pl.BlockSpec((groups, planes, ROWS, span), lambda i: (0, i, 0, 0)),
            pl.BlockSpec((2, lines, span), lambda i: (0, 0, 0)),
            pl.BlockSpec((2, planes, wells), lambda i: (0, i, 0)),
        ],
        out_shape=[
            jax.ShapeDtypeStruct((groups, slabs, ROWS, span), jnp.float32),
            jax.ShapeDtypeStruct((2, lines, span), jnp.float32),
            jax.ShapeDtypeStruct((2, slabs, wells), jnp.float32),
        ],
        scratch_shapes=[
            shifted,
            shifted,
            shifted,
            pltpu.VMEM((2, span // LANES, lines, LANES), jnp.float32),
            pltpu.VMEM((2, 2, span // LANES + 1, lines, LANES), jnp.bfloat16),
            pltpu.VMEM((4 * LANES, LANES), jnp.bfloat16),
            pltpu.VMEM((span, wells), jnp.bfloat16),
            pltpu.VMEM((planes, 2, wells), jnp.float32),
        ],
        compiler_params=pltpu.CompilerParams(vmem_limit_bytes=VMEM_LIMIT),
        cost_estimate=pl.CostEstimate(flops=40 * w.size, bytes_accessed=12 * w.size, transcendentals=0),
        name="stencil",
    )(table, inverse, w, cat, place_row)


META = 11
META_ROWS = 16


def payload_kernel(
    ratio,
    table,
    where_am_i,
    sums,
    first,
    last,
    before,
    after,
    inverse,
    cells,
    speed,
    reach,
    *refs,
):
    out_refs, (flux_ref, source_ref, keep, force, paths, totals) = refs[:-6], refs[-6:]
    copies = len(out_refs)
    share = out_refs[0].shape[1]
    _, lines, span = sums.shape
    _, slabs, wells = cells.shape
    dot = functools.partial(jnp.dot, precision=HIGHEST, preferred_element_type=jnp.float32)
    ends = jnp.concatenate([inverse[0:1], inverse[slabs - 1 : slabs]], axis=0)
    meta = 2 * lines

    entries = [table[k] for k in range(table.shape[0])]
    level = lax.broadcasted_iota(jnp.int32, (slabs, wells), 0) + where_am_i[0] * slabs
    rock = cells[0]
    cond = select_tree(cells[1].astype(jnp.int32), entries)
    rate = jnp.where(level < reach[...], speed[...] * cond / (1.0 + cond), 0.0)
    keep[...] = 1.0 - rate
    force[...] = rate * rock
    ones, zeros = jnp.ones((1, wells), jnp.float32), jnp.zeros((1, wells), jnp.float32)
    ways = []
    for n, order in enumerate((range(slabs), reversed(range(slabs)))):
        scale, shift = ones, zeros
        for z in order:
            paths[n, 0, z : z + 1] = scale
            paths[n, 1, z : z + 1] = shift
            scale, shift = keep[z : z + 1] * scale, keep[z : z + 1] * shift + force[z : z + 1]
        ways.append((scale, shift))
    source_ref[0] = -storage_volume * rate * (2.0 * rock - paths[0, 1] - paths[1, 1])
    source_ref[1] = storage_volume * rate * paths[0, 0]
    source_ref[2] = storage_volume * rate * paths[1, 0]
    own_sums = [dot(ends, source_ref[n]) for n in range(3)]

    rows = [ways[0][0], ways[0][1], ways[1][1]]
    rows += [own_sums[n][q : q + 1] for q in range(2) for n in range(3)]
    extras = []
    for own, other, line, n in ((first, before, 0, 0), (last, after, lines - 1, 1)):
        flux = (own[1] + other[1]) * (other[0] - own[0])
        flux_ref[n] = flux
        extras.append((line, dot(ends, flux)))
    totals[...] = sums[...]
    for line, extra in extras:
        for q in range(2):
            totals[q, line : line + 1, :] += extra[q : q + 1]
    for m, out_ref in enumerate(out_refs):
        cols = pl.ds(pl.multiple_of(partner(where_am_i, m, copies) * share, share), share)
        for q in range(2):
            out_ref[q * lines : (q + 1) * lines] = totals[q, :, cols]
        out_ref[meta : meta + META_ROWS] = jnp.zeros((META_ROWS, share), jnp.float32)
        out_ref[meta : meta + 2, :slabs] = ends
        out_ref[meta : meta + 1, slabs : slabs + 1] = jnp.full((1, 1), ratio[0])
        for n, row in enumerate(rows):
            out_ref[meta + 2 + n : meta + 3 + n, :wells] = row


def payload(ratio, table, where, sums, edges, inverse, cells, speed, reach, copies):
    _, lines, span = sums.shape
    _, slabs, wells = cells.shape
    share = span // copies
    smem = pl.BlockSpec(memory_space=pltpu.SMEM)
    vmem = pl.BlockSpec(memory_space=pltpu.VMEM)
    column = pltpu.VMEM((slabs, wells), jnp.float32)
    return pl.pallas_call(
        payload_kernel,
        in_specs=[smem] * 3 + [vmem] * 9,
        out_specs=[vmem] * (copies + 2),
        out_shape=[jax.ShapeDtypeStruct((2 * lines + META_ROWS, share), jnp.float32)] * copies
        + [
            jax.ShapeDtypeStruct((2, slabs, span), jnp.float32),
            jax.ShapeDtypeStruct((3, slabs, wells), jnp.float32),
        ],
        scratch_shapes=[
            column,
            column,
            pltpu.VMEM((2, 2, slabs, wells), jnp.float32),
            pltpu.VMEM((2, lines, span), jnp.float32),
        ],
        compiler_params=pltpu.CompilerParams(vmem_limit_bytes=SMALL_VMEM),
        cost_estimate=pl.CostEstimate(flops=10**6, bytes_accessed=10**6, transcendentals=0),
        name="payload",
    )(ratio, table, where, sums, *edges, inverse, cells, speed, reach)


CORNERS = ((0, 0), (0, 1), (1, 0), (1, 1))


def block_scalars(tile, slabs, shape, flipped=None):
    at = lambda row, lane: jnp.broadcast_to(tile[row : row + 1, lane : lane + 1], shape)
    corner = {(r, c): at(r, c * (slabs - 1)) for r, c in CORNERS}
    if flipped is not None:
        corner = {(r, c): jnp.where(flipped, corner[1 - r, 1 - c], corner[r, c]) for r, c in CORNERS}
    return corner, at(0, slabs)


def coupling(ratio, one, other, slabs):
    return ratio * (slabs / (slabs + 1.0)) / jnp.sqrt(one * other)


def chain(corners, couple, q=None):
    out = []
    q = jnp.zeros_like(couple[0])
    for k, corner in enumerate(corners):
        vf, vl = couple[k] * corner[0, 0], couple[k] * corner[1, 0]
        wf, wl = couple[k + 1] * corner[0, 1], couple[k + 1] * corner[1, 1]
        inverse = 1.0 / (1.0 - vf * q)
        out.append(
            dict(
                p_first=vl * q * inverse,
                p_before=vl * inverse,
                a_first=inverse,
                a_before=vf * inverse,
                a_after=wf * inverse,
                couple=couple[k],
                couple_after=couple[k + 1],
                q=q,
            )
        )
        q = wl + vl * q * wf * inverse
    return out, q


KINDS = ("p_first", "p_before", "a_first", "a_before", "a_after", "couple", "couple_after", "q")


def forward(coef, firsts, lasts):
    before = [jnp.zeros_like(firsts[0])]
    for j in range(len(firsts)):
        before.append(
            lasts[j] + coef("p_first", j) * firsts[j] + coef("p_before", j) * before[j]
        )
    return before


def backward(coef, firsts, before, after):
    blocks = len(firsts)
    above, below = [None] * blocks, [None] * blocks
    for j in reversed(range(blocks)):
        below[j] = coef("couple_after", j) * after
        here = (
            coef("a_first", j) * firsts[j]
            + coef("a_before", j) * before[j]
            + coef("a_after", j) * after
        )
        above[j] = coef("couple", j) * (before[j] + coef("q", j) * here)
        after = here
    return above, below


def half_chain(tiles, slabs, flipped, middle):
    shape = (ROWS, LANES)
    scalars = [block_scalars(tile, slabs, shape, flipped) for tile in tiles]
    couple = [jnp.zeros(shape, jnp.float32)]
    for k in range(1, len(tiles)):
        ratio = jnp.where(flipped, scalars[k - 1][1], scalars[k][1])
        couple.append(coupling(ratio, scalars[k - 1][0][1, 1], scalars[k][0][0, 0], slabs))
    couple.append(middle)
    return chain([corner for corner, _ in scalars], couple)


def meta_place(j, lines, share):
    side = share // LANES
    row = lines + j // side * META
    return slice(row, row + META), slice(j % side * LANES, (j % side + 1) * LANES)


def first_kernel(slabs, where, *refs):
    piece_refs, (out_ref, fl_ref, table) = refs[:-3], refs[-3:]
    blocks, rows, share = fl_ref.shape
    lines = (rows - META_ROWS) // 2
    for m, piece in enumerate(piece_refs):
        fl_ref[partner(where, m, blocks)] = piece[...]
    flip = where[0] // blocks
    flipped = flip == 1
    block = [k + flip * (blocks - 1 - 2 * k) for k in range(blocks)]
    entries, _ = half_chain(
        [fl_ref[block[k], 2 * lines : 2 * lines + ROWS, :LANES] for k in range(blocks)],
        slabs,
        flipped,
        jnp.zeros((ROWS, LANES), jnp.float32),
    )
    for k, entry in enumerate(entries):
        for n, kind in enumerate(KINDS[:2]):
            table[k, n] = entry[kind]
    coef = lambda kind, k: table[k, KINDS.index(kind)]

    def group(g, carry):
        rows = pl.ds(pl.multiple_of(g * ROWS, ROWS), ROWS)
        outer = pl.ds(pl.multiple_of(flip * lines + g * ROWS, ROWS), ROWS)
        inner = pl.ds(pl.multiple_of((1 - flip) * lines + g * ROWS, ROWS), ROWS)
        for t in range(share // LANES):
            cols = slice(t * LANES, (t + 1) * LANES)
            before = forward(
                coef,
                [fl_ref[block[k], outer, cols] for k in range(blocks)],
                [fl_ref[block[k], inner, cols] for k in range(blocks)],
            )
            out_ref[rows, cols] = before[blocks]
        return carry

    lax.fori_loop(0, lines // ROWS, group, 0)
    out_ref[lines:, :] = jnp.zeros((out_ref.shape[0] - lines, share), jnp.float32)
    for j in range(blocks):
        rows, cols = meta_place(j, lines, share)
        out_ref[rows, cols] = fl_ref[j, 2 * lines : 2 * lines + META, :LANES]


def first_half(where, pieces, slabs):
    parts = len(pieces)
    rows, share = pieces[0].shape
    lines = (rows - META_ROWS) // 2
    vmem = pl.BlockSpec(memory_space=pltpu.VMEM)
    crossing = -(-meta_place(parts - 1, lines, share)[0].stop // ROWS) * ROWS
    return pl.pallas_call(
        functools.partial(first_kernel, slabs),
        in_specs=[pl.BlockSpec(memory_space=pltpu.SMEM)] + [vmem] * parts,
        out_specs=[vmem, vmem],
        out_shape=[
            jax.ShapeDtypeStruct((crossing, share), jnp.float32),
            jax.ShapeDtypeStruct((parts, rows, share), jnp.float32),
        ],
        scratch_shapes=[pltpu.VMEM((parts, 2, ROWS, LANES), jnp.float32)],
        compiler_params=pltpu.CompilerParams(vmem_limit_bytes=SMALL_VMEM),
        cost_estimate=pl.CostEstimate(flops=10**6, bytes_accessed=10**6, transcendentals=0),
        name="reduced_in",
    )(where, *pieces)


def second_kernel(slabs, where, fl_ref, mine, other, *refs):
    out_refs, (info_ref, table, uv_ref) = refs[:-3], refs[-3:]
    blocks, _, lines, share = uv_ref.shape
    flip = where[0] // blocks
    flipped = flip == 1
    block = [k + flip * (blocks - 1 - 2 * k) for k in range(blocks)]
    for j in range(blocks):
        rows, cols = meta_place(j, lines, share)
        info_ref[flip * blocks + j] = fl_ref[j, 2 * lines :, :LANES]
        info_ref[(1 - flip) * blocks + j] = jnp.zeros((META_ROWS, LANES), jnp.float32)
        info_ref[(1 - flip) * blocks + j, :META] = other[rows, cols]
    shape = (ROWS, LANES)
    above, above_ratio = block_scalars(info_ref[blocks - 1], slabs, shape)
    below, below_ratio = block_scalars(info_ref[blocks], slabs, shape)
    middle = coupling(below_ratio, above[1, 1], below[0, 0], slabs)
    tiles = lambda flip: [
        info_ref[flip * blocks + k + flip * (blocks - 1 - 2 * k)] for k in range(blocks)
    ]
    entries, q_own = half_chain(tiles(flip), slabs, flipped, middle)
    _, q_other = half_chain(tiles(1 - flip), slabs, jnp.logical_not(flipped), middle)
    for k, entry in enumerate(entries):
        for n, kind in enumerate(KINDS):
            table[k, n] = entry[kind]
    table[blocks, 0] = 1.0 / (1.0 - q_own * q_other)
    table[blocks, 1] = q_other
    coef = lambda kind, k: table[k, KINDS.index(kind)]

    def group(g, carry):
        rows = pl.ds(pl.multiple_of(g * ROWS, ROWS), ROWS)
        outside = pl.ds(pl.multiple_of(flip * lines + g * ROWS, ROWS), ROWS)
        inside = pl.ds(pl.multiple_of((1 - flip) * lines + g * ROWS, ROWS), ROWS)
        for t in range(share // LANES):
            cols = slice(t * LANES, (t + 1) * LANES)
            firsts = [fl_ref[block[k], outside, cols] for k in range(blocks)]
            lasts = [fl_ref[block[k], inside, cols] for k in range(blocks - 1)]
            before = forward(coef, firsts[:-1], lasts)
            across = table[blocks, 0] * (other[rows, cols] + table[blocks, 1] * mine[rows, cols])
            outer, inner = backward(coef, firsts, before, across)
            for k in range(blocks):
                uv_ref[block[k], flip, rows, cols] = outer[k]
                uv_ref[block[k], 1 - flip, rows, cols] = inner[k]
        return carry

    lax.fori_loop(0, lines // ROWS, group, 0)
    for m, out_ref in enumerate(out_refs):
        out_ref[...] = uv_ref[partner(where, m, blocks)]


def second_half(where, fl, mine, other, slabs):
    parts, rows, share = fl.shape
    lines = (rows - META_ROWS) // 2
    vmem = pl.BlockSpec(memory_space=pltpu.VMEM)
    return pl.pallas_call(
        functools.partial(second_kernel, slabs),
        in_specs=[pl.BlockSpec(memory_space=pltpu.SMEM), vmem, vmem, vmem],
        out_specs=[vmem] * (parts + 1),
        out_shape=[jax.ShapeDtypeStruct((2, lines, share), jnp.float32)] * parts
        + [jax.ShapeDtypeStruct((2 * parts, META_ROWS, LANES), jnp.float32)],
        scratch_shapes=[
            pltpu.VMEM((parts + 1, len(KINDS), ROWS, LANES), jnp.float32),
            pltpu.VMEM((parts, 2, lines, share), jnp.float32),
        ],
        compiler_params=pltpu.CompilerParams(vmem_limit_bytes=SMALL_VMEM),
        cost_estimate=pl.CostEstimate(flops=10 * fl.size, bytes_accessed=9 * fl.size, transcendentals=0),
        name="reduced_out",
    )(where, fl, mine, other)


def extras_kernel(where_am_i, info, source, flux, inverse, inlet, holders, wells_ref, rows_ref, leaving, found):
    blocks = info.shape[0]
    slabs, wells = wells_ref.shape
    d = where_am_i[0]
    dot = functools.partial(jnp.dot, precision=HIGHEST, preferred_element_type=jnp.float32)
    row_of = lambda j, n: info[j, 2 + n : 3 + n, :wells]
    down, rise = [None] * blocks, [None] * blocks
    value = inlet[...]
    for j in range(blocks):
        down[j] = value
        value = row_of(j, 0) * value + row_of(j, 1)
    for j in reversed(range(blocks)):
        rise[j] = value
        value = row_of(j, 0) * value + row_of(j, 2)
    held = holders[...] == lax.broadcasted_iota(jnp.int32, (wells, wells), 0)
    ordered = dot(jnp.broadcast_to(value, (ROWS, wells)), held.astype(jnp.float32))
    owned = leaving.shape[1]
    source_lane = lax.broadcasted_iota(jnp.int32, (wells, owned), 0)
    mine = source_lane == d * owned + lax.broadcasted_iota(jnp.int32, (wells, owned), 1)
    leaving[...] = dot(ordered, mine.astype(jnp.float32))[0:1]

    ends = [
        [row_of(j, n) + row_of(j, n + 1) * down[j] + row_of(j, n + 2) * rise[j] for j in range(blocks)]
        for n in (3, 6)
    ]
    scalars = [block_scalars(info[j], slabs, (1, wells)) for j in range(blocks)]
    zero = jnp.zeros((1, wells), jnp.float32)
    couple = [zero]
    for j in range(1, blocks):
        couple.append(
            coupling(scalars[j][1], scalars[j - 1][0][1, 1], scalars[j][0][0, 0], slabs)
        )
    couple.append(zero)
    coefs, _ = chain([corner for corner, _ in scalars], couple)
    coef = lambda kind, j: coefs[j][kind]
    above, below = backward(coef, ends[0], forward(coef, *ends), zero)
    for j in range(blocks):
        for n, value in enumerate((down[j], rise[j], above[j], below[j])):
            found[j, n : n + 1] = value
    mine = found[d]
    row = lax.broadcasted_iota(jnp.int32, (slabs, wells), 0)
    own = source[0] + source[1] * mine[0:1] + source[2] * mine[1:2]
    own = own + jnp.where(row == 0, mine[2:3], 0.0) + jnp.where(row == slabs - 1, mine[3:4], 0.0)
    wells_ref[...] = dot(inverse[...], own)
    for n in range(2):
        rows_ref[n] = dot(inverse[...], flux[n])


def extras(where, info, source, flux, inverse, inlet, holders):
    blocks = info.shape[0]
    _, slabs, span = flux.shape
    wells = source.shape[-1]
    vmem = pl.BlockSpec(memory_space=pltpu.VMEM)
    return pl.pallas_call(
        extras_kernel,
        in_specs=[pl.BlockSpec(memory_space=pltpu.SMEM)] + [vmem] * 6,
        out_specs=[vmem] * 3,
        out_shape=[
            jax.ShapeDtypeStruct((slabs, wells), jnp.float32),
            jax.ShapeDtypeStruct((2, slabs, span), jnp.float32),
            jax.ShapeDtypeStruct((1, wells // blocks), jnp.float32),
        ],
        scratch_shapes=[pltpu.VMEM((blocks, ROWS, wells), jnp.float32)],
        compiler_params=pltpu.CompilerParams(vmem_limit_bytes=SMALL_VMEM),
        cost_estimate=pl.CostEstimate(flops=10**7, bytes_accessed=10**6, transcendentals=0),
        name="extras",
    )(where, info, source, flux, inverse, inlet, holders)


def solve_kernel(where, right, inverse, place_row, solved_wells, outer, *refs):
    uv_refs, (out, factor, pick, uv) = refs[:-4], refs[-4:]
    for m, piece in enumerate(uv_refs):
        uv[partner(where, m, len(uv_refs))] = piece[...]
    _, slabs, rows, span = right.shape
    together = out.shape[1] // rows
    wells = place_row.shape[1]
    step = pl.program_id(0)
    size = slabs * rows

    @pl.when(step == 0)
    def _():
        spread = (
            lax.broadcasted_iota(jnp.int32, (size, slabs), 0) // rows
            == lax.broadcasted_iota(jnp.int32, (size, slabs), 1)
        ).astype(jnp.float32).astype(jnp.bfloat16)
        spread_t = (
            lax.broadcasted_iota(jnp.int32, (slabs, size), 1) // rows
            == lax.broadcasted_iota(jnp.int32, (slabs, size), 0)
        ).astype(jnp.float32).astype(jnp.bfloat16)
        same = (
            lax.broadcasted_iota(jnp.int32, (size, size), 0) % rows
            == lax.broadcasted_iota(jnp.int32, (size, size), 1) % rows
        )
        for n, part in enumerate(split_bf16(inverse[...], 2)):
            tall = jnp.dot(spread, part, preferred_element_type=jnp.float32).astype(jnp.bfloat16)
            wide = jnp.dot(tall, spread_t, preferred_element_type=jnp.float32)
            wide = jnp.where(same, wide, 0.0).astype(jnp.bfloat16)
            if n == 0:
                factor[:, :size] = wide
                factor[:, size : 2 * size] = wide
            else:
                factor[:, 2 * size : 3 * size] = wide
        across = lax.broadcasted_iota(jnp.int32, (wells, wells), 1)
        diagonal = lax.broadcasted_iota(jnp.int32, (wells, wells), 0) == across
        place = jnp.where(diagonal, (place_row[...] % span).astype(jnp.float32), 0.0)
        place = jnp.sum(place, axis=1, keepdims=True)
        column = lax.broadcasted_iota(jnp.int32, (wells, span), 1).astype(jnp.float32)
        chosen = (column == place).astype(jnp.float32).astype(jnp.bfloat16)
        pick[:wells] = chosen
        pick[wells:] = chosen

    tile = min(span, 256)
    for n in range(together):
        group = step * together + n
        line = lax.broadcasted_iota(jnp.int32, (slabs, rows, wells), 1) + group * rows
        at_wells = jnp.where(line == (place_row[...] // span)[None], solved_wells[...][:, None, :], 0.0)
        at_wells = jnp.concatenate(split_bf16(at_wells.reshape(size, wells), 2), axis=1)
        factor[:, 3 * size :] = at_wells
        lines = slice(n * rows, (n + 1) * rows)
        above = jnp.concatenate([uv[d, 0, lines] for d in range(uv.shape[0])], axis=1)
        below = jnp.concatenate([uv[d, 1, lines] for d in range(uv.shape[0])], axis=1)
        for t in range(span // tile):
            cols = slice(t * tile, (t + 1) * tile)
            value = jnp.concatenate(
                [
                    right[group, 0:1, :, cols] + above[None, :, cols],
                    right[group, 1 : slabs - 1, :, cols],
                    right[group, slabs - 1 :, :, cols] + below[None, :, cols],
                ],
                axis=0,
            ).reshape(size, tile)
            upper, lower = split_bf16(value, 2)
            result = jnp.dot(
                factor[...],
                jnp.concatenate([upper, lower, upper, pick[:, cols]], axis=0),
                preferred_element_type=jnp.float32,
            )
            out[:, lines, cols] = result.reshape(slabs, rows, tile)

    for n, (when, line) in enumerate(((0, 0), (pl.num_programs(0) - 1, together * rows - 1))):

        @pl.when(step == when)
        def _():
            for z in range(slabs):
                out[z, line : line + 1, :] += outer[n, z : z + 1, :]


def solve(where, right, uv, inverse, place_row, solved_wells, outer):
    groups, slabs, _, span = right.shape
    wells = place_row.shape[1]
    together = 2
    lines = together * ROWS
    _, _, share = uv[0].shape
    whole = lambda *shape: pl.BlockSpec(shape, lambda g: (0,) * len(shape))
    size = slabs * ROWS
    return pl.pallas_call(
        solve_kernel,
        grid=(groups // together,),
        in_specs=[
            pl.BlockSpec(memory_space=pltpu.SMEM),
            pl.BlockSpec(memory_space=pltpu.VMEM),
            whole(slabs, slabs),
            whole(1, wells),
            whole(slabs, wells),
            whole(*outer.shape),
        ]
        + [pl.BlockSpec((2, lines, share), lambda g: (0, g, 0))] * len(uv),
        out_specs=pl.BlockSpec((slabs, lines, span), lambda g: (0, g, 0)),
        out_shape=jax.ShapeDtypeStruct((slabs, groups * ROWS, span), jnp.float32),
        scratch_shapes=[
            pltpu.VMEM((size, 3 * size + 2 * wells), jnp.bfloat16),
            pltpu.VMEM((2 * wells, span), jnp.bfloat16),
            pltpu.VMEM((len(uv), 2, lines, share), jnp.float32),
        ],
        compiler_params=pltpu.CompilerParams(vmem_limit_bytes=SOLVE_VMEM),
        cost_estimate=pl.CostEstimate(
            flops=8 * size * right.size, bytes_accessed=8 * right.size, transcendentals=0
        ),
        name="depth_solve",
    )(where, right, inverse, place_row, solved_wells, outer, *uv)


def body(
    warmth_before,
    stratum_category,
    conductance_catalogue,
    pivot_matrix_reciprocal,
    linkage_factor,
    well_position_inside,
    well_holder_sequence,
    well_reach,
    entering_warmth,
    well_transfer_speed,
):
    slabs, lines, span = warmth_before.shape
    depth_index = lax.axis_index("depth")
    depth_count = lax.axis_size("depth")
    wells = well_position_inside.shape[0]
    owned = wells // depth_count
    table = conductance_catalogue

    parts = depth_count // 2

    place_row = well_position_inside.reshape(1, wells)
    where = jnp.stack([depth_index, lax.axis_index("strip")])
    first, last = edge_rows(warmth_before, stratum_category, table)
    first, last, place_row, where = lax.optimization_barrier((first, last, place_row, where))
    count = lax.axis_size("strip")
    up = [(i, i + 1) for i in range(count - 1)]
    down = [(j, i) for i, j in up]
    before = lax.ppermute(last, "strip", up)
    after = lax.ppermute(first, "strip", down)
    right, sums, cells = stencil(
        warmth_before, stratum_category, table, pivot_matrix_reciprocal, place_row
    )
    *pieces, flux, source = payload(
        linkage_factor,
        table,
        where,
        sums,
        (first, last, before, after),
        pivot_matrix_reciprocal,
        cells,
        well_transfer_speed.reshape(1, wells),
        well_reach.reshape(1, wells),
        parts,
    )

    def swapped(value, mask):
        return lax.ppermute(value, "depth", [(i, i ^ mask) for i in range(depth_count)])

    def with_partner(value, mask):
        perm = []
        for strip in range(count):
            step = crossed(mask) if strip % 2 and parts >= 4 else mask
            start = strip * depth_count
            perm += [(start + i, start + (i ^ step)) for i in range(depth_count)]
        return lax.ppermute(value, ("strip", "depth"), perm)

    pieces = [with_partner(pieces[m], m) for m in reversed(range(1, parts))][::-1] + [pieces[0]]
    pieces = [pieces[-1]] + pieces[:-1]
    mine, fl_all = first_half(where, pieces, slabs)
    other = swapped(mine, parts)
    *uv, info_all = second_half(where, fl_all, mine, other, slabs)
    uv_own = [with_partner(uv[m], m) for m in reversed(range(1, parts))][::-1]
    uv_own = [uv[0]] + uv_own

    solved_wells, outer, leaving = extras(
        where,
        info_all,
        source,
        flux,
        pivot_matrix_reciprocal,
        entering_warmth.reshape(1, wells),
        well_holder_sequence.reshape(1, wells),
    )
    solved = solve(where, right, uv_own, pivot_matrix_reciprocal, place_row, solved_wells, outer)
    return solved, leaving.reshape(owned)


def solution(mesh):
    in_specs = (
        P("depth", "strip", None),
        P("depth", "strip", None),
        P(),
        P("depth", None),
        P("depth"),
        P("strip"),
        P("strip"),
        P("strip"),
        P("strip"),
        P("strip"),
    )
    out_specs = (P("depth", "strip", None), P(("strip", "depth")))
    return jax.shard_map(body, mesh=mesh, in_specs=in_specs, out_specs=out_specs, check_vma=False)
```

```python
import functools

import jax
import jax.numpy as jnp
from jax import lax
from jax.experimental import pallas as pl
from jax.experimental.pallas import tpu as pltpu
from jax.sharding import PartitionSpec as P

backward_euler_advance = 0.2
storage_volume = 2.0
flux_scale = 0.5 * backward_euler_advance
LANES = 128
ROWS = 8
EDGE_VMEM = 56 * 1024 * 1024
VMEM_LIMIT = 40 * 1024 * 1024
SOLVE_VMEM = 24 * 1024 * 1024
SMALL_VMEM = 12 * 1024 * 1024
HIGHEST = lax.Precision.HIGHEST


def select_tree(category, entries):
    values = list(entries)
    bit = 1
    while len(values) > 1:
        odd = (category & bit) != 0
        values = [
            jnp.where(odd, values[k + 1], values[k]) if k + 1 < len(values) else values[k]
            for k in range(0, len(values), 2)
        ]
        bit *= 2
    return values[0]


def crossed(mask):
    return mask & ~3 | (mask & 1) << 1 | (mask & 2) >> 1


def depth_of(where, count):
    return where[0] & (count - 1)


def partner(where, mask, blocks):
    odd = where[0] // (2 * blocks) & 1 if blocks >= 4 else 0
    return (where[0] & (blocks - 1)) ^ (mask + odd * (crossed(mask) - mask))


def split_bf16(value, pieces):
    out = []
    for k in range(pieces):
        part = value.astype(jnp.bfloat16)
        out.append(part)
        if k + 1 < pieces:
            value = value - part.astype(jnp.float32)
    return out


def edge_kernel(table, w_first, cat_first, w_last, cat_last, first, last):
    slabs, rows, span = w_first.shape
    entries = [flux_scale * table[k] for k in range(table.shape[0])]
    sub = lax.broadcasted_iota(jnp.int32, (ROWS, span), 0)

    def gathered(ref, start, row):
        value = jnp.broadcast_to(ref[start, row : row + 1, :], (ROWS, span))
        for k in range(1, ROWS):
            value = jnp.where(sub == k, ref[start + k, row : row + 1, :], value)
        return value

    for w_ref, cat_ref, row, out in ((w_first, cat_first, 0, first), (w_last, cat_last, rows - 1, last)):
        for start in range(0, slabs, ROWS):
            out[0, start : start + ROWS] = gathered(w_ref, start, row)
            out[1, start : start + ROWS] = select_tree(gathered(cat_ref, start, row), entries)


def edge_rows(w, cat, table):
    slabs, lines, span = w.shape
    top = pl.BlockSpec((slabs, ROWS, span), lambda i: (0, 0, 0))
    end = pl.BlockSpec((slabs, ROWS, span), lambda i: (0, lines // ROWS - 1, 0))
    out = pl.BlockSpec((2, slabs, span), lambda i: (0, 0, 0))
    return pl.pallas_call(
        edge_kernel,
        grid=(1,),
        in_specs=[pl.BlockSpec(memory_space=pltpu.SMEM), top, top, end, end],
        out_specs=[out, out],
        out_shape=[jax.ShapeDtypeStruct((2, slabs, span), jnp.float32)] * 2,
        compiler_params=pltpu.CompilerParams(vmem_limit_bytes=EDGE_VMEM),
        cost_estimate=pl.CostEstimate(flops=10**6, bytes_accessed=w.size, transcendentals=0),
        name="edge_rows",
    )(table, w, cat, w, cat)


def stencil_kernel(
    table,
    ends,
    w_ref,
    cat_ref,
    place,
    right_ref,
    acc,
    cells_ref,
    ws,
    cs,
    fs,
    base,
    pieces,
    shift,
    pick,
    found,
):
    step = pl.program_id(0)
    planes, lines, span = w_ref.shape
    tiles = span // LANES
    groups = lines // ROWS
    wells = place.shape[1]
    entries = [flux_scale * table[k] for k in range(table.shape[0])]
    lane = lax.broadcasted_iota(jnp.int32, (lines, LANES), 1)
    own_line = lax.broadcasted_iota(jnp.int32, (lines, wells), 0) == place[...] // span
    top, end = ROWS, ROWS + lines
    dot = functools.partial(jnp.dot, preferred_element_type=jnp.float32)

    @pl.when(step == 0)
    def _():
        acc[...] = jnp.zeros_like(acc)
        base[...] = jnp.zeros_like(base)
        pieces[...] = jnp.zeros_like(pieces)
        source = lax.broadcasted_iota(jnp.int32, shift.shape, 0) % (2 * LANES)
        target = lax.broadcasted_iota(jnp.int32, shift.shape, 1)
        shift[...] = (source == target + 1).astype(jnp.float32).astype(jnp.bfloat16)
        column = lax.broadcasted_iota(jnp.int32, (span, wells), 0)
        pick[...] = (column == place[...] % span).astype(jnp.float32).astype(jnp.bfloat16)

    def keep_face(slot, t, face):
        for n, part in enumerate(split_bf16(face, 2)):
            pieces[slot, n, t] = part

    def faces(k, slot):
        left_w = left_c = jnp.zeros((lines, LANES), jnp.float32)
        for t in range(tiles):
            cols = slice(t * LANES, (t + 1) * LANES)
            w = w_ref[k, :, cols]
            c = select_tree(cat_ref[k, :, cols], entries)
            for ref, value in ((ws, w), (cs, c)):
                ref[t, top:end] = value
                ref[t, top - 1 : top] = value[0:1]
            roll_w, roll_c = pltpu.roll(w, 1, 1), pltpu.roll(c, 1, 1)
            west_w = jnp.where(lane == 0, left_w, roll_w)
            west_c = jnp.where(lane == 0, left_c, roll_c)
            left_w, left_c = roll_w, roll_c
            face = (c + west_c) * (w - west_w)
            keep_face(slot, t, face)
            if t == tiles - 1:
                keep_face(slot, tiles, pltpu.roll(-c * w, 1, 1))
            north = (c + cs[t, top - 1 : end - 1]) * (w - ws[t, top - 1 : end - 1])
            fs[t, top:end] = north
            fs[t, end : end + 1] = jnp.zeros((1, LANES), jnp.float32)
            base[slot, t] = w - face - north + fs[t, top + 1 : end + 1]

    def well_cells(k):
        upper, lower = split_bf16(w_ref[k], 2)
        kinds = cat_ref[k].astype(jnp.float32).astype(jnp.bfloat16)
        sums = dot(jnp.concatenate([upper, lower, kinds], axis=0), pick[...])
        for n, value in enumerate((sums[:lines] + sums[lines : 2 * lines], sums[2 * lines :])):
            mine = jnp.where(own_line, value, 0.0)
            found[k, n : n + 1, :] = jnp.sum(mine, axis=0, keepdims=True)

    def finish(k, slot, on):
        z = step * planes + k
        end_first = jnp.where(on, ends[0, z], 0.0)
        end_last = jnp.where(on, ends[ends.shape[0] - 1, z], 0.0)
        parts = [
            pieces[slot, n, d : d + tiles].reshape(tiles * lines, LANES)
            for n in range(2)
            for d in range(2)
        ]
        east = dot(jnp.concatenate(parts, axis=1), shift[...])
        for t in range(tiles):
            cols = slice(t * LANES, (t + 1) * LANES)
            value = base[slot, t] + east[t * lines : (t + 1) * lines]
            right_ref[:, k, :, cols] = value.reshape(groups, ROWS, LANES)
            acc[0, :, cols] += end_first * value
            acc[1, :, cols] += end_last * value

    def two_planes(m, carry):
        k = 2 * m
        finish(jnp.maximum(k - 1, 0), 1, m > 0)
        faces(k, 0)
        well_cells(k)
        finish(k, 0, True)
        faces(k + 1, 1)
        well_cells(k + 1)
        return carry

    lax.fori_loop(0, planes // 2, two_planes, 0)
    finish(planes - 1, 1, True)
    for k in range(planes):
        for n in range(2):
            cells_ref[n, k : k + 1, :] = found[k, n : n + 1, :]


def stencil(w, cat, table, inverse, place_row):
    slabs, lines, span = w.shape
    planes, groups = 8, lines // ROWS
    wells = place_row.shape[1]
    block = pl.BlockSpec((planes, lines, span), lambda i: (i, 0, 0))
    smem = pl.BlockSpec(memory_space=pltpu.SMEM)
    shifted = pltpu.VMEM((span // LANES, lines + 2 * ROWS, LANES), jnp.float32)
    return pl.pallas_call(
        stencil_kernel,
        grid=(slabs // planes,),
        in_specs=[smem, smem, block, block, pl.BlockSpec((1, wells), lambda i: (0, 0))],
        out_specs=[
            pl.BlockSpec((groups, planes, ROWS, span), lambda i: (0, i, 0, 0)),
            pl.BlockSpec((2, lines, span), lambda i: (0, 0, 0)),
            pl.BlockSpec((2, planes, wells), lambda i: (0, i, 0)),
        ],
        out_shape=[
            jax.ShapeDtypeStruct((groups, slabs, ROWS, span), jnp.float32),
            jax.ShapeDtypeStruct((2, lines, span), jnp.float32),
            jax.ShapeDtypeStruct((2, slabs, wells), jnp.float32),
        ],
        scratch_shapes=[
            shifted,
            shifted,
            shifted,
            pltpu.VMEM((2, span // LANES, lines, LANES), jnp.float32),
            pltpu.VMEM((2, 2, span // LANES + 1, lines, LANES), jnp.bfloat16),
            pltpu.VMEM((4 * LANES, LANES), jnp.bfloat16),
            pltpu.VMEM((span, wells), jnp.bfloat16),
            pltpu.VMEM((planes, 2, wells), jnp.float32),
        ],
        compiler_params=pltpu.CompilerParams(vmem_limit_bytes=VMEM_LIMIT),
        cost_estimate=pl.CostEstimate(flops=40 * w.size, bytes_accessed=12 * w.size, transcendentals=0),
        name="stencil",
    )(table, inverse, w, cat, place_row)


META = 11
META_ROWS = 16


def payload_kernel(
    ratio,
    table,
    where_am_i,
    sums,
    first,
    last,
    before,
    after,
    inverse,
    cells,
    speed,
    reach,
    *refs,
):
    out_refs, (flux_ref, source_ref, keep, force, paths, totals) = refs[:-6], refs[-6:]
    copies = len(out_refs)
    share = out_refs[0].shape[1]
    _, lines, span = sums.shape
    _, slabs, wells = cells.shape
    dot = functools.partial(jnp.dot, precision=HIGHEST, preferred_element_type=jnp.float32)
    ends = jnp.concatenate([inverse[0:1], inverse[slabs - 1 : slabs]], axis=0)
    meta = 2 * lines

    entries = [table[k] for k in range(table.shape[0])]
    level = lax.broadcasted_iota(jnp.int32, (slabs, wells), 0) + depth_of(where_am_i, 2 * copies) * slabs
    rock = cells[0]
    cond = select_tree(cells[1].astype(jnp.int32), entries)
    rate = jnp.where(level < reach[...], speed[...] * cond / (1.0 + cond), 0.0)
    keep[...] = 1.0 - rate
    force[...] = rate * rock
    ones, zeros = jnp.ones((1, wells), jnp.float32), jnp.zeros((1, wells), jnp.float32)
    ways = []
    for n, order in enumerate((range(slabs), reversed(range(slabs)))):
        scale, shift = ones, zeros
        for z in order:
            paths[n, 0, z : z + 1] = scale
            paths[n, 1, z : z + 1] = shift
            scale, shift = keep[z : z + 1] * scale, keep[z : z + 1] * shift + force[z : z + 1]
        ways.append((scale, shift))
    source_ref[0] = -storage_volume * rate * (2.0 * rock - paths[0, 1] - paths[1, 1])
    source_ref[1] = storage_volume * rate * paths[0, 0]
    source_ref[2] = storage_volume * rate * paths[1, 0]
    own_sums = [dot(ends, source_ref[n]) for n in range(3)]

    rows = [ways[0][0], ways[0][1], ways[1][1]]
    rows += [own_sums[n][q : q + 1] for q in range(2) for n in range(3)]
    extras = []
    for own, other, line, n in ((first, before, 0, 0), (last, after, lines - 1, 1)):
        flux = (own[1] + other[1]) * (other[0] - own[0])
        flux_ref[n] = flux
        extras.append((line, dot(ends, flux)))
    totals[...] = sums[...]
    for line, extra in extras:
        for q in range(2):
            totals[q, line : line + 1, :] += extra[q : q + 1]
    for m, out_ref in enumerate(out_refs):
        cols = pl.ds(pl.multiple_of(partner(where_am_i, m, copies) * share, share), share)
        for q in range(2):
            out_ref[q * lines : (q + 1) * lines] = totals[q, :, cols]
        out_ref[meta : meta + META_ROWS] = jnp.zeros((META_ROWS, share), jnp.float32)
        out_ref[meta : meta + 2, :slabs] = ends
        out_ref[meta : meta + 1, slabs : slabs + 1] = jnp.full((1, 1), ratio[0])
        for n, row in enumerate(rows):
            out_ref[meta + 2 + n : meta + 3 + n, :wells] = row


def payload(ratio, table, where, sums, edges, inverse, cells, speed, reach, copies):
    _, lines, span = sums.shape
    _, slabs, wells = cells.shape
    share = span // copies
    smem = pl.BlockSpec(memory_space=pltpu.SMEM)
    vmem = pl.BlockSpec(memory_space=pltpu.VMEM)
    column = pltpu.VMEM((slabs, wells), jnp.float32)
    return pl.pallas_call(
        payload_kernel,
        in_specs=[smem] * 3 + [vmem] * 9,
        out_specs=[vmem] * (copies + 2),
        out_shape=[jax.ShapeDtypeStruct((2 * lines + META_ROWS, share), jnp.float32)] * copies
        + [
            jax.ShapeDtypeStruct((2, slabs, span), jnp.float32),
            jax.ShapeDtypeStruct((3, slabs, wells), jnp.float32),
        ],
        scratch_shapes=[
            column,
            column,
            pltpu.VMEM((2, 2, slabs, wells), jnp.float32),
            pltpu.VMEM((2, lines, span), jnp.float32),
        ],
        compiler_params=pltpu.CompilerParams(vmem_limit_bytes=SMALL_VMEM),
        cost_estimate=pl.CostEstimate(flops=10**6, bytes_accessed=10**6, transcendentals=0),
        name="payload",
    )(ratio, table, where, sums, *edges, inverse, cells, speed, reach)


CORNERS = ((0, 0), (0, 1), (1, 0), (1, 1))


def block_scalars(tile, slabs, shape, flipped=None):
    at = lambda row, lane: jnp.broadcast_to(tile[row : row + 1, lane : lane + 1], shape)
    corner = {(r, c): at(r, c * (slabs - 1)) for r, c in CORNERS}
    if flipped is not None:
        corner = {(r, c): jnp.where(flipped, corner[1 - r, 1 - c], corner[r, c]) for r, c in CORNERS}
    return corner, at(0, slabs)


def coupling(ratio, one, other, slabs):
    return ratio * (slabs / (slabs + 1.0)) / jnp.sqrt(one * other)


def chain(corners, couple, q=None):
    out = []
    q = jnp.zeros_like(couple[0])
    for k, corner in enumerate(corners):
        vf, vl = couple[k] * corner[0, 0], couple[k] * corner[1, 0]
        wf, wl = couple[k + 1] * corner[0, 1], couple[k + 1] * corner[1, 1]
        inverse = 1.0 / (1.0 - vf * q)
        out.append(
            dict(
                p_first=vl * q * inverse,
                p_before=vl * inverse,
                a_first=inverse,
                a_before=vf * inverse,
                a_after=wf * inverse,
                couple=couple[k],
                couple_after=couple[k + 1],
                q=q,
            )
        )
        q = wl + vl * q * wf * inverse
    return out, q


KINDS = ("p_first", "p_before", "a_first", "a_before", "a_after", "couple", "couple_after", "q")


def forward(coef, firsts, lasts):
    before = [jnp.zeros_like(firsts[0])]
    for j in range(len(firsts)):
        before.append(
            lasts[j] + coef("p_first", j) * firsts[j] + coef("p_before", j) * before[j]
        )
    return before


def backward(coef, firsts, before, after):
    blocks = len(firsts)
    above, below = [None] * blocks, [None] * blocks
    for j in reversed(range(blocks)):
        below[j] = coef("couple_after", j) * after
        here = (
            coef("a_first", j) * firsts[j]
            + coef("a_before", j) * before[j]
            + coef("a_after", j) * after
        )
        above[j] = coef("couple", j) * (before[j] + coef("q", j) * here)
        after = here
    return above, below


def half_chain(tiles, slabs, flipped, middle):
    shape = (ROWS, LANES)
    scalars = [block_scalars(tile, slabs, shape, flipped) for tile in tiles]
    couple = [jnp.zeros(shape, jnp.float32)]
    for k in range(1, len(tiles)):
        ratio = jnp.where(flipped, scalars[k - 1][1], scalars[k][1])
        couple.append(coupling(ratio, scalars[k - 1][0][1, 1], scalars[k][0][0, 0], slabs))
    couple.append(middle)
    return chain([corner for corner, _ in scalars], couple)


def meta_place(j, lines, share):
    side = share // LANES
    row = lines + j // side * META
    return slice(row, row + META), slice(j % side * LANES, (j % side + 1) * LANES)


def first_kernel(slabs, where, *refs):
    piece_refs, (out_ref, fl_ref, table) = refs[:-3], refs[-3:]
    blocks, rows, share = fl_ref.shape
    lines = (rows - META_ROWS) // 2
    for m, piece in enumerate(piece_refs):
        fl_ref[partner(where, m, blocks)] = piece[...]
    flip = depth_of(where, 2 * blocks) // blocks
    flipped = flip == 1
    block = [k + flip * (blocks - 1 - 2 * k) for k in range(blocks)]
    entries, _ = half_chain(
        [fl_ref[block[k], 2 * lines : 2 * lines + ROWS, :LANES] for k in range(blocks)],
        slabs,
        flipped,
        jnp.zeros((ROWS, LANES), jnp.float32),
    )
    for k, entry in enumerate(entries):
        for n, kind in enumerate(KINDS[:2]):
            table[k, n] = entry[kind]
    coef = lambda kind, k: table[k, KINDS.index(kind)]

    def group(g, carry):
        rows = pl.ds(pl.multiple_of(g * ROWS, ROWS), ROWS)
        outer = pl.ds(pl.multiple_of(flip * lines + g * ROWS, ROWS), ROWS)
        inner = pl.ds(pl.multiple_of((1 - flip) * lines + g * ROWS, ROWS), ROWS)
        for t in range(share // LANES):
            cols = slice(t * LANES, (t + 1) * LANES)
            before = forward(
                coef,
                [fl_ref[block[k], outer, cols] for k in range(blocks)],
                [fl_ref[block[k], inner, cols] for k in range(blocks)],
            )
            out_ref[rows, cols] = before[blocks]
        return carry

    lax.fori_loop(0, lines // ROWS, group, 0)
    out_ref[lines:, :] = jnp.zeros((out_ref.shape[0] - lines, share), jnp.float32)
    for j in range(blocks):
        rows, cols = meta_place(j, lines, share)
        out_ref[rows, cols] = fl_ref[j, 2 * lines : 2 * lines + META, :LANES]


def first_half(where, pieces, slabs):
    parts = len(pieces)
    rows, share = pieces[0].shape
    lines = (rows - META_ROWS) // 2
    vmem = pl.BlockSpec(memory_space=pltpu.VMEM)
    crossing = -(-meta_place(parts - 1, lines, share)[0].stop // ROWS) * ROWS
    return pl.pallas_call(
        functools.partial(first_kernel, slabs),
        in_specs=[pl.BlockSpec(memory_space=pltpu.SMEM)] + [vmem] * parts,
        out_specs=[vmem, vmem],
        out_shape=[
            jax.ShapeDtypeStruct((crossing, share), jnp.float32),
            jax.ShapeDtypeStruct((parts, rows, share), jnp.float32),
        ],
        scratch_shapes=[pltpu.VMEM((parts, 2, ROWS, LANES), jnp.float32)],
        compiler_params=pltpu.CompilerParams(vmem_limit_bytes=SMALL_VMEM),
        cost_estimate=pl.CostEstimate(flops=10**6, bytes_accessed=10**6, transcendentals=0),
        name="reduced_in",
    )(where, *pieces)


def second_kernel(slabs, where, fl_ref, mine, other, *refs):
    out_refs, (info_ref, table, uv_ref) = refs[:-3], refs[-3:]
    blocks, _, lines, share = uv_ref.shape
    flip = depth_of(where, 2 * blocks) // blocks
    flipped = flip == 1
    block = [k + flip * (blocks - 1 - 2 * k) for k in range(blocks)]
    for j in range(blocks):
        rows, cols = meta_place(j, lines, share)
        info_ref[flip * blocks + j] = fl_ref[j, 2 * lines :, :LANES]
        info_ref[(1 - flip) * blocks + j] = jnp.zeros((META_ROWS, LANES), jnp.float32)
        info_ref[(1 - flip) * blocks + j, :META] = other[rows, cols]
    shape = (ROWS, LANES)
    above, above_ratio = block_scalars(info_ref[blocks - 1], slabs, shape)
    below, below_ratio = block_scalars(info_ref[blocks], slabs, shape)
    middle = coupling(below_ratio, above[1, 1], below[0, 0], slabs)
    tiles = lambda flip: [
        info_ref[flip * blocks + k + flip * (blocks - 1 - 2 * k)] for k in range(blocks)
    ]
    entries, q_own = half_chain(tiles(flip), slabs, flipped, middle)
    _, q_other = half_chain(tiles(1 - flip), slabs, jnp.logical_not(flipped), middle)
    for k, entry in enumerate(entries):
        for n, kind in enumerate(KINDS):
            table[k, n] = entry[kind]
    table[blocks, 0] = 1.0 / (1.0 - q_own * q_other)
    table[blocks, 1] = q_other
    coef = lambda kind, k: table[k, KINDS.index(kind)]

    def group(g, carry):
        rows = pl.ds(pl.multiple_of(g * ROWS, ROWS), ROWS)
        outside = pl.ds(pl.multiple_of(flip * lines + g * ROWS, ROWS), ROWS)
        inside = pl.ds(pl.multiple_of((1 - flip) * lines + g * ROWS, ROWS), ROWS)
        for t in range(share // LANES):
            cols = slice(t * LANES, (t + 1) * LANES)
            firsts = [fl_ref[block[k], outside, cols] for k in range(blocks)]
            lasts = [fl_ref[block[k], inside, cols] for k in range(blocks - 1)]
            before = forward(coef, firsts[:-1], lasts)
            across = table[blocks, 0] * (other[rows, cols] + table[blocks, 1] * mine[rows, cols])
            outer, inner = backward(coef, firsts, before, across)
            for k in range(blocks):
                uv_ref[block[k], flip, rows, cols] = outer[k]
                uv_ref[block[k], 1 - flip, rows, cols] = inner[k]
        return carry

    lax.fori_loop(0, lines // ROWS, group, 0)
    for m, out_ref in enumerate(out_refs):
        out_ref[...] = uv_ref[partner(where, m, blocks)]


def second_half(where, fl, mine, other, slabs):
    parts, rows, share = fl.shape
    lines = (rows - META_ROWS) // 2
    vmem = pl.BlockSpec(memory_space=pltpu.VMEM)
    return pl.pallas_call(
        functools.partial(second_kernel, slabs),
        in_specs=[pl.BlockSpec(memory_space=pltpu.SMEM), vmem, vmem, vmem],
        out_specs=[vmem] * (parts + 1),
        out_shape=[jax.ShapeDtypeStruct((2, lines, share), jnp.float32)] * parts
        + [jax.ShapeDtypeStruct((2 * parts, META_ROWS, LANES), jnp.float32)],
        scratch_shapes=[
            pltpu.VMEM((parts + 1, len(KINDS), ROWS, LANES), jnp.float32),
            pltpu.VMEM((parts, 2, lines, share), jnp.float32),
        ],
        compiler_params=pltpu.CompilerParams(vmem_limit_bytes=SMALL_VMEM),
        cost_estimate=pl.CostEstimate(flops=10 * fl.size, bytes_accessed=9 * fl.size, transcendentals=0),
        name="reduced_out",
    )(where, fl, mine, other)


def extras_kernel(where_am_i, info, source, flux, inverse, inlet, holders, wells_ref, rows_ref, leaving, found):
    blocks = info.shape[0]
    slabs, wells = wells_ref.shape
    d = depth_of(where_am_i, blocks)
    dot = functools.partial(jnp.dot, precision=HIGHEST, preferred_element_type=jnp.float32)
    row_of = lambda j, n: info[j, 2 + n : 3 + n, :wells]
    down, rise = [None] * blocks, [None] * blocks
    value = inlet[...]
    for j in range(blocks):
        down[j] = value
        value = row_of(j, 0) * value + row_of(j, 1)
    for j in reversed(range(blocks)):
        rise[j] = value
        value = row_of(j, 0) * value + row_of(j, 2)
    held = holders[...] == lax.broadcasted_iota(jnp.int32, (wells, wells), 0)
    ordered = dot(jnp.broadcast_to(value, (ROWS, wells)), held.astype(jnp.float32))
    owned = leaving.shape[1]
    source_lane = lax.broadcasted_iota(jnp.int32, (wells, owned), 0)
    mine = source_lane == d * owned + lax.broadcasted_iota(jnp.int32, (wells, owned), 1)
    leaving[...] = dot(ordered, mine.astype(jnp.float32))[0:1]

    ends = [
        [row_of(j, n) + row_of(j, n + 1) * down[j] + row_of(j, n + 2) * rise[j] for j in range(blocks)]
        for n in (3, 6)
    ]
    scalars = [block_scalars(info[j], slabs, (1, wells)) for j in range(blocks)]
    zero = jnp.zeros((1, wells), jnp.float32)
    couple = [zero]
    for j in range(1, blocks):
        couple.append(
            coupling(scalars[j][1], scalars[j - 1][0][1, 1], scalars[j][0][0, 0], slabs)
        )
    couple.append(zero)
    coefs, _ = chain([corner for corner, _ in scalars], couple)
    coef = lambda kind, j: coefs[j][kind]
    above, below = backward(coef, ends[0], forward(coef, *ends), zero)
    for j in range(blocks):
        for n, value in enumerate((down[j], rise[j], above[j], below[j])):
            found[j, n : n + 1] = value
    mine = found[d]
    row = lax.broadcasted_iota(jnp.int32, (slabs, wells), 0)
    own = source[0] + source[1] * mine[0:1] + source[2] * mine[1:2]
    own = own + jnp.where(row == 0, mine[2:3], 0.0) + jnp.where(row == slabs - 1, mine[3:4], 0.0)
    wells_ref[...] = dot(inverse[...], own)
    for n in range(2):
        rows_ref[n] = dot(inverse[...], flux[n])


def extras(where, info, source, flux, inverse, inlet, holders):
    blocks = info.shape[0]
    _, slabs, span = flux.shape
    wells = source.shape[-1]
    vmem = pl.BlockSpec(memory_space=pltpu.VMEM)
    return pl.pallas_call(
        extras_kernel,
        in_specs=[pl.BlockSpec(memory_space=pltpu.SMEM)] + [vmem] * 6,
        out_specs=[vmem] * 3,
        out_shape=[
            jax.ShapeDtypeStruct((slabs, wells), jnp.float32),
            jax.ShapeDtypeStruct((2, slabs, span), jnp.float32),
            jax.ShapeDtypeStruct((1, wells // blocks), jnp.float32),
        ],
        scratch_shapes=[pltpu.VMEM((blocks, ROWS, wells), jnp.float32)],
        compiler_params=pltpu.CompilerParams(vmem_limit_bytes=SMALL_VMEM),
        cost_estimate=pl.CostEstimate(flops=10**7, bytes_accessed=10**6, transcendentals=0),
        name="extras",
    )(where, info, source, flux, inverse, inlet, holders)


def solve_kernel(where, right, inverse, place_row, solved_wells, outer, *refs):
    uv_refs, (out, factor, pick, uv) = refs[:-4], refs[-4:]
    for m, piece in enumerate(uv_refs):
        uv[partner(where, m, len(uv_refs))] = piece[...]
    _, slabs, rows, span = right.shape
    together = out.shape[1] // rows
    wells = place_row.shape[1]
    step = pl.program_id(0)
    size = slabs * rows

    @pl.when(step == 0)
    def _():
        spread = (
            lax.broadcasted_iota(jnp.int32, (size, slabs), 0) // rows
            == lax.broadcasted_iota(jnp.int32, (size, slabs), 1)
        ).astype(jnp.float32).astype(jnp.bfloat16)
        spread_t = (
            lax.broadcasted_iota(jnp.int32, (slabs, size), 1) // rows
            == lax.broadcasted_iota(jnp.int32, (slabs, size), 0)
        ).astype(jnp.float32).astype(jnp.bfloat16)
        same = (
            lax.broadcasted_iota(jnp.int32, (size, size), 0) % rows
            == lax.broadcasted_iota(jnp.int32, (size, size), 1) % rows
        )
        for n, part in enumerate(split_bf16(inverse[...], 2)):
            tall = jnp.dot(spread, part, preferred_element_type=jnp.float32).astype(jnp.bfloat16)
            wide = jnp.dot(tall, spread_t, preferred_element_type=jnp.float32)
            wide = jnp.where(same, wide, 0.0).astype(jnp.bfloat16)
            if n == 0:
                factor[:, :size] = wide
                factor[:, size : 2 * size] = wide
            else:
                factor[:, 2 * size : 3 * size] = wide
        across = lax.broadcasted_iota(jnp.int32, (wells, wells), 1)
        diagonal = lax.broadcasted_iota(jnp.int32, (wells, wells), 0) == across
        place = jnp.where(diagonal, (place_row[...] % span).astype(jnp.float32), 0.0)
        place = jnp.sum(place, axis=1, keepdims=True)
        column = lax.broadcasted_iota(jnp.int32, (wells, span), 1).astype(jnp.float32)
        chosen = (column == place).astype(jnp.float32).astype(jnp.bfloat16)
        pick[:wells] = chosen
        pick[wells:] = chosen

    tile = min(span, 256)
    for n in range(together):
        group = step * together + n
        line = lax.broadcasted_iota(jnp.int32, (slabs, rows, wells), 1) + group * rows
        at_wells = jnp.where(line == (place_row[...] // span)[None], solved_wells[...][:, None, :], 0.0)
        at_wells = jnp.concatenate(split_bf16(at_wells.reshape(size, wells), 2), axis=1)
        factor[:, 3 * size :] = at_wells
        lines = slice(n * rows, (n + 1) * rows)
        above = jnp.concatenate([uv[d, 0, lines] for d in range(uv.shape[0])], axis=1)
        below = jnp.concatenate([uv[d, 1, lines] for d in range(uv.shape[0])], axis=1)
        for t in range(span // tile):
            cols = slice(t * tile, (t + 1) * tile)
            value = jnp.concatenate(
                [
                    right[group, 0:1, :, cols] + above[None, :, cols],
                    right[group, 1 : slabs - 1, :, cols],
                    right[group, slabs - 1 :, :, cols] + below[None, :, cols],
                ],
                axis=0,
            ).reshape(size, tile)
            upper, lower = split_bf16(value, 2)
            result = jnp.dot(
                factor[...],
                jnp.concatenate([upper, lower, upper, pick[:, cols]], axis=0),
                preferred_element_type=jnp.float32,
            )
            out[:, lines, cols] = result.reshape(slabs, rows, tile)

    for n, (when, line) in enumerate(((0, 0), (pl.num_programs(0) - 1, together * rows - 1))):

        @pl.when(step == when)
        def _():
            for z in range(slabs):
                out[z, line : line + 1, :] += outer[n, z : z + 1, :]


def solve(where, right, uv, inverse, place_row, solved_wells, outer):
    groups, slabs, _, span = right.shape
    wells = place_row.shape[1]
    together = 2
    lines = together * ROWS
    _, _, share = uv[0].shape
    whole = lambda *shape: pl.BlockSpec(shape, lambda g: (0,) * len(shape))
    size = slabs * ROWS
    return pl.pallas_call(
        solve_kernel,
        grid=(groups // together,),
        in_specs=[
            pl.BlockSpec(memory_space=pltpu.SMEM),
            pl.BlockSpec(memory_space=pltpu.VMEM),
            whole(slabs, slabs),
            whole(1, wells),
            whole(slabs, wells),
            whole(*outer.shape),
        ]
        + [pl.BlockSpec((2, lines, share), lambda g: (0, g, 0))] * len(uv),
        out_specs=pl.BlockSpec((slabs, lines, span), lambda g: (0, g, 0)),
        out_shape=jax.ShapeDtypeStruct((slabs, groups * ROWS, span), jnp.float32),
        scratch_shapes=[
            pltpu.VMEM((size, 3 * size + 2 * wells), jnp.bfloat16),
            pltpu.VMEM((2 * wells, span), jnp.bfloat16),
            pltpu.VMEM((len(uv), 2, lines, share), jnp.float32),
        ],
        compiler_params=pltpu.CompilerParams(vmem_limit_bytes=SOLVE_VMEM),
        cost_estimate=pl.CostEstimate(
            flops=8 * size * right.size, bytes_accessed=8 * right.size, transcendentals=0
        ),
        name="depth_solve",
    )(where, right, inverse, place_row, solved_wells, outer, *uv)


def body(
    warmth_before,
    stratum_category,
    conductance_catalogue,
    pivot_matrix_reciprocal,
    linkage_factor,
    well_position_inside,
    well_holder_sequence,
    well_reach,
    entering_warmth,
    well_transfer_speed,
):
    slabs, lines, span = warmth_before.shape
    depth_index = lax.axis_index("depth")
    depth_count = lax.axis_size("depth")
    wells = well_position_inside.shape[0]
    owned = wells // depth_count
    table = conductance_catalogue

    parts = depth_count // 2

    place_row = well_position_inside.reshape(1, wells)
    where = lax.axis_index(("strip", "depth")).reshape(1)
    first, last = edge_rows(warmth_before, stratum_category, table)
    first, last, place_row, where = lax.optimization_barrier((first, last, place_row, where))
    count = lax.axis_size("strip")
    up = [(i, i + 1) for i in range(count - 1)]
    down = [(j, i) for i, j in up]
    before = lax.ppermute(last, "strip", up)
    after = lax.ppermute(first, "strip", down)
    right, sums, cells = stencil(
        warmth_before, stratum_category, table, pivot_matrix_reciprocal, place_row
    )
    *pieces, flux, source = payload(
        linkage_factor,
        table,
        where,
        sums,
        (first, last, before, after),
        pivot_matrix_reciprocal,
        cells,
        well_transfer_speed.reshape(1, wells),
        well_reach.reshape(1, wells),
        parts,
    )

    def swapped(value, mask):
        return lax.ppermute(value, "depth", [(i, i ^ mask) for i in range(depth_count)])

    def with_partner(value, mask):
        perm = []
        for strip in range(count):
            step = crossed(mask) if strip % 2 and parts >= 4 else mask
            start = strip * depth_count
            perm += [(start + i, start + (i ^ step)) for i in range(depth_count)]
        return lax.ppermute(value, ("strip", "depth"), perm)

    pieces = [with_partner(pieces[m], m) for m in reversed(range(1, parts))][::-1] + [pieces[0]]
    pieces = [pieces[-1]] + pieces[:-1]
    mine, fl_all = first_half(where, pieces, slabs)
    other = swapped(mine, parts)
    *uv, info_all = second_half(where, fl_all, mine, other, slabs)
    uv_own = [with_partner(uv[m], m) for m in reversed(range(1, parts))][::-1]
    uv_own = [uv[0]] + uv_own

    solved_wells, outer, leaving = extras(
        where,
        info_all,
        source,
        flux,
        pivot_matrix_reciprocal,
        entering_warmth.reshape(1, wells),
        well_holder_sequence.reshape(1, wells),
    )
    solved = solve(where, right, uv_own, pivot_matrix_reciprocal, place_row, solved_wells, outer)
    return solved, leaving.reshape(owned)


def solution(mesh):
    in_specs = (
        P("depth", "strip", None),
        P("depth", "strip", None),
        P(),
        P("depth", None),
        P("depth"),
        P("strip"),
        P("strip"),
        P("strip"),
        P("strip"),
        P("strip"),
    )
    out_specs = (P("depth", "strip", None), P(("strip", "depth")))
    return jax.shard_map(body, mesh=mesh, in_specs=in_specs, out_specs=out_specs, check_vma=False)
```
